32 devices in a mesh: row: 16 (over z, y, core), col: 2 (over x).
Axes of the slice: x: 2, y: 2, z: 4, core: 2. Of those that a mesh axis runs over, the one named last changes fastest.
Arguments:
- velocity: float32 [6, 3, 2048], P(None, None, ('row', 'col')), may hold values from -3 to 3
- points: float32 [3, 2048], P(None, ('row', 'col')), may hold values from -1 to 1
- panel_area: float32 [2048], P(('row', 'col')), may hold values from 0.00390625 to 0.0390625
- self_term: float32 [2048], P(('row', 'col')), may hold values from 0.5 to 4
- near_index: int32 [2048, 32], P('row', 'col'), may hold values from 0 to 1023
- near_weight: float32 [2048, 32], P('row', 'col'), may hold values from -0.5 to 0.5
Outputs:
- density: float32 [6, 3, 2048], P(None, None, ('row', 'col'))
The draws below stay inside these ranges and needn't reach their ends.
Inputs may be any that keep to these rules, and one draw needn't show every extreme that they name: `near_index`: each entry is a place in the source block of its column of 16 entries; places may repeat, and every listing counts.
All inputs are finite; a program needn't handle non-finite values.
Results may differ from the reference program's by a relative error of at most 0.0003.
Values sent between devices are 32-bit elements; how exact they have to be, the bound alone decides.
No kernel may reach another device: no remote copies, remote signals or barrier semaphores. Data moves between devices by JAX's collectives and lax.ppermute only.
A program may use at most 128 MiB of HBM per device.

```python
import math
import jax
import jax.numpy as jnp
from jax import lax

PAN_DEV = 64
RHS = 6
NEAR = 16
ITERS = 3
PANELS = 2048
SRC = 1024
N_COL = 2


def panel_centres(key):
    return jax.random.uniform(jax.random.fold_in(key, 11), (3, PANELS), jnp.float32, -1.0, 1.0)


def draw_points(key, part):
    return panel_centres(key)


def draw_velocity(key, part):
    centres = panel_centres(key)
    zeros_row = jnp.zeros((PANELS,), jnp.float32)
    ones_row = jnp.ones((PANELS,), jnp.float32)
    first = centres[0]
    second = centres[1]
    third = centres[2]
    motions = jnp.stack([jnp.stack([ones_row, zeros_row, zeros_row]), jnp.stack([zeros_row, ones_row, zeros_row]), jnp.stack([zeros_row, zeros_row, ones_row]), jnp.stack([zeros_row, -third, second]), jnp.stack([third, zeros_row, -first]), jnp.stack([-second, first, zeros_row])])
    noise_key = jax.random.fold_in(key, 12)
    rough = 0.5 * jax.random.normal(noise_key, (RHS, 3, PANELS), jnp.float32)
    field = motions + rough
    return jnp.clip(field, -3.0, 3.0)


def touch_ends(array, rng, least, high):
    shape = array.shape
    place = [jax.random.randint(jax.random.fold_in(rng, axis), (), 0, shape[axis]) for axis in range(len(shape))]
    array = array.at[tuple(place)].set(least)
    longest = shape.index(max(shape))
    place[longest] = (place[longest] + 1) % shape[longest]
    return array.at[tuple(place)].set(high)


def block_scale(stream_key, shape, pieces, smallest, largest):
    factor_of, own = 1.0, jax.random.fold_in(stream_key, 6)
    for axis_at, shards_of in pieces:
        steps = jnp.exp(jax.random.uniform(jax.random.fold_in(own, axis_at), (shards_of,), jnp.float32, smallest / len(pieces), largest / len(pieces)))
        factor_of = factor_of * jnp.repeat(steps, shape[axis_at] // shards_of).reshape([-1 if axis == axis_at else 1 for axis in range(len(shape))])
    return factor_of


def normal_values(rng, extent, width, bound, shards=(), dtype=jnp.bfloat16):
    level = block_scale(rng, extent, shards, -0.22, 0.18) if shards else 1.0
    array = jax.random.normal(rng, extent, jnp.float32) * width * level
    return jnp.minimum(jnp.maximum(array, -bound), bound).astype(dtype)


def setup_inputs(seed: int = 0) -> dict:
    keys = jax.random.split(jax.random.key(seed), 7)
    velocity = draw_velocity(jax.random.fold_in(keys[6], 71), 0)
    points = draw_points(jax.random.fold_in(keys[6], 71), 0)
    panel_area = jnp.clip(jnp.exp(math.log(0.0390625) - 2.3025851 * jax.random.uniform(keys[2], (PANELS,), jnp.float32) ** block_scale(keys[2], (PANELS,), ((0, 32),), -0.2, 0.2)), 0.00390625, 0.0390625)
    self_term = jnp.clip(jnp.exp(math.log(4.0) - 2.0794415 * jax.random.uniform(keys[3], (PANELS,), jnp.float32) ** block_scale(keys[3], (PANELS,), ((0, 32),), -0.2, 0.2)), 0.5, 4.0)
    near_index = touch_ends(jax.random.randint(keys[4], (PANELS, N_COL * NEAR), 0, SRC), jax.random.fold_in(keys[4], 1), 0, SRC - 1).astype(jnp.int32)
    near_weight = normal_values(keys[5], (PANELS, N_COL * NEAR), 0.1, 0.5, ((0, 16), (1, 2)), jnp.float32)
    return dict(velocity=velocity, points=points, panel_area=panel_area, self_term=self_term, near_index=near_index, near_weight=near_weight)


BLOB_SQ = 0.0025
INV_EIGHT_PI = 1.0 / (8.0 * math.pi)

def build_columns(values, src_points):
    rhs_count = values.shape[0]
    count = values.shape[2]
    inner_prod = lax.optimization_barrier(jnp.sum(src_points[None] * values, axis=1))
    direct_cols = values.reshape(rhs_count * 3, count)
    outer_cols = (src_points[None, :, None, :] * values[:, None, :, :]).reshape(rhs_count * 9, count)
    scaled = (src_points[None] * inner_prod[:, None]).reshape(rhs_count * 3, count)
    return (direct_cols, jnp.concatenate([direct_cols, inner_prod, outer_cols, scaled], axis=0))

def tile_terms(tgt_points, src_points, src_area, direct_cols, columns):
    offsets = tgt_points[:, :, None] - src_points[:, None, :]
    dist_sq = lax.optimization_barrier(jnp.sum(offsets * offsets, axis=0))
    inv_root = lax.rsqrt(dist_sq + BLOB_SQ)
    kernel_two = src_area[None, :] * inv_root * inv_root * inv_root * INV_EIGHT_PI
    kernel_one = (dist_sq + 2.0 * BLOB_SQ) * kernel_two
    dims = (((1,), (1,)), ((), ()))
    near_one = lax.dot_general(direct_cols, kernel_one, dims, precision=lax.Precision.HIGHEST)
    products = lax.dot_general(columns, kernel_two, dims, precision=lax.Precision.HIGHEST)
    rhs_count = direct_cols.shape[0] // 3
    tgt_count = tgt_points.shape[1]
    direct = near_one.reshape(rhs_count, 3, tgt_count)
    along_f = products[:3 * rhs_count].reshape(rhs_count, 3, tgt_count)
    along_g = products[3 * rhs_count:4 * rhs_count]
    along_yf = products[4 * rhs_count:13 * rhs_count].reshape(rhs_count, 3, 3, tgt_count)
    along_yg = products[13 * rhs_count:].reshape(rhs_count, 3, tgt_count)
    x_dot = lax.optimization_barrier(jnp.sum(tgt_points[None] * along_f, axis=1))
    cross_term = lax.optimization_barrier(jnp.sum(tgt_points[None, None] * along_yf, axis=2))
    return direct + tgt_points[None] * (x_dot - along_g)[:, None] - cross_term + along_yg

def solve_small(hessen, start_norm, count):
    zero = jnp.zeros_like(start_norm)
    target = [start_norm] + [zero] * count
    cosines = []
    sines = []
    triangle = {}
    for k in range(count):
        column = [hessen[i, k] for i in range(k + 2)]
        for j in range(k):
            first_val = column[j]
            second_val = column[j + 1]
            column[j] = cosines[j] * first_val + sines[j] * second_val
            column[j + 1] = cosines[j] * second_val - sines[j] * first_val
        radius = jnp.sqrt(column[k] * column[k] + column[k + 1] * column[k + 1])
        cosine = column[k] / radius
        sine = column[k + 1] / radius
        cosines.append(cosine)
        sines.append(sine)
        for i in range(k):
            triangle[i, k] = column[i]
        triangle[k, k] = radius
        target[k + 1] = -sine * target[k]
        target[k] = cosine * target[k]
    coeffs = [None] * count
    for k in range(count - 1, -1, -1):
        accum = target[k]
        for i in range(k + 1, count):
            accum = accum - triangle[k, i] * coeffs[i]
        coeffs[k] = accum / triangle[k, k]
    return coeffs

def reference(velocity, points, panel_area, self_term, near_index, near_weight):
    rhs_count = velocity.shape[0]
    blocks = PANELS // PAN_DEV
    tgt_blocks = points.reshape(3, blocks, PAN_DEV).transpose(1, 0, 2)
    column_id = (jnp.arange(N_COL * NEAR) // NEAR).astype(jnp.int32)
    glob = ((near_index // PAN_DEV * N_COL + column_id[None]) * PAN_DEV + near_index % PAN_DEV).astype(jnp.int32)

    def apply(vector):
        direct_cols, columns = build_columns(vector, points)

        def one_block(tgt):
            return tile_terms(tgt, points, panel_area, direct_cols, columns)
        distant = lax.map(one_block, tgt_blocks)
        distant = distant.transpose(1, 2, 0, 3).reshape(rhs_count, 3, PANELS)
        nearby = lax.optimization_barrier(jnp.sum(vector[:, :, glob] * near_weight[None, None], axis=-1))
        return self_term[None, None] * vector + distant + nearby

    def norm_of(field):
        return jnp.sqrt(lax.optimization_barrier(jnp.sum(field * field, axis=(1, 2))))
    start_norm = norm_of(velocity)
    basis = [velocity / start_norm[:, None, None]]
    hessen = {}
    for k in range(ITERS):
        image = apply(basis[k])
        for j in range(k + 1):
            value = lax.optimization_barrier(jnp.sum(basis[j] * image, axis=(1, 2)))
            hessen[j, k] = value
            image = image - value[:, None, None] * basis[j]
        length = norm_of(image)
        hessen[k + 1, k] = length
        if k + 1 < ITERS:
            basis.append(image / length[:, None, None])
    coeffs = solve_small(hessen, start_norm, ITERS)
    density = coeffs[0][:, None, None] * basis[0]
    for k in range(1, ITERS):
        density = density + coeffs[k][:, None, None] * basis[k]
    return density
```

```python
import functools
import math

import jax
import jax.numpy as jnp
from jax import lax
from jax.experimental import pallas as pl
from jax.experimental.pallas import tpu as pltpu
from jax.sharding import PartitionSpec as P

ITERS = 3
BLOB_SQ = 0.0025
INV_EIGHT_PI = 1.0 / (8.0 * math.pi)
ROWS = 8
AXES = ("row", "col")
F32 = jnp.float32
BF16 = jnp.bfloat16


def low_half(shape):
    return lax.broadcasted_iota(jnp.int32, shape, len(shape) - 1) < 64


def pack(rows):
    return jnp.concatenate([rows[..., :4, :], rows[..., 4:, :]], axis=-1)


def xor_perm(n, m):
    return [(d, d ^ m) for d in range(n)]


def exchange(piece, n, mode):
    if mode == "gather" or n > 64:
        return [lax.all_gather(piece, AXES, axis=0)], None
    if mode == "alltoall":
        wide = jnp.broadcast_to(piece[None], (n,) + piece.shape)
        return [lax.all_to_all(wide, AXES, 0, 0, tiled=True)], None
    if mode == "direct":
        arrays = [piece[None]]
        for m in range(1, n):
            arrays.append(lax.ppermute(piece[None], AXES, xor_perm(n, m)))
        return arrays, [(m, 0) for m in range(n)]
    if mode == "double":
        held = piece[None]
        m = 1
        while m < n:
            other = lax.ppermute(held, AXES, xor_perm(n, m))
            if 2 * m == n:
                return [held, other], [(i // m, i % m) for i in range(n)]
            held = jnp.concatenate([held, other], axis=0)
            m *= 2
    raise ValueError(mode)


def assemble(piece_refs, where, slots, me):
    n = slots.shape[0]
    if where is None:

        @pl.loop(0, n)
        def _(m):
            slots[m] = piece_refs[0][me ^ m]
    else:
        for m, (k, i) in enumerate(where):
            slots[m] = piece_refs[k][i]


def chunk_parts(slots, chunk, n_row, n_col, part):
    half = n_row // 2
    o = chunk // half
    u = chunk % half
    even = slots[(2 * u) * n_col + o, part]
    odd = slots[(2 * u + 1) * n_col + o, part]
    low = low_half((4, 128))
    first = jnp.where(low, even, pltpu.roll(odd, 64, 1))
    second = jnp.where(low, pltpu.roll(even, 64, 1), odd)
    return first, second


def row_sum(acc):
    return jnp.sum(acc, axis=1, keepdims=True)


def dot_of(left, right, n_chunk):
    def step(chunk, acc):
        return acc + jnp.sum(left[chunk] * right[chunk], axis=0)

    acc = lax.fori_loop(0, n_chunk, step, jnp.zeros((ROWS, 128), F32), unroll=4)
    return row_sum(acc)


def write_columns(cols, places, chunk, vec):
    y = places[chunk]
    ys = [y[a : a + 1] for a in range(3)]
    f = [vec[a] for a in range(3)]
    g = ys[0] * f[0] + ys[1] * f[1] + ys[2] * f[2]
    groups = f + [g]
    groups += [ys[p] * f[v] for p in range(3) for v in range(3)]
    groups += [ys[a] * g for a in range(3)]
    full = jnp.concatenate(groups, axis=0)
    high = full.astype(BF16)
    low = (full - high.astype(F32)).astype(BF16)
    at = pl.ds(pl.multiple_of(chunk * 128, 128), 128)
    cols[0:128, at] = high
    cols[128:256, at] = low


def apply_rows(cols, kernels, targets, self_row, own, out):
    total = cols.shape[1]
    step = min(total, 2048)

    def turn(i, acc):
        at = pl.ds(pl.multiple_of(i * step, step), step)
        return acc + jnp.dot(cols[:, at], kernels[at, :], preferred_element_type=F32)

    if total == step:
        prod = jnp.dot(cols[...], kernels[...], preferred_element_type=F32)
    else:
        prod = lax.fori_loop(0, total // step, turn, jnp.zeros((256, 256), F32))
    both = prod[:128, :128] + (prod[128:, :128] + prod[:128, 128:])
    two = pltpu.roll(both, 64, 1)

    def group(k):
        return two[8 * k : 8 * k + 8]

    x = [targets[a : a + 1] for a in range(3)]
    along = x[0] * group(0) + x[1] * group(1) + x[2] * group(2) - group(3)
    for a in range(3):
        cross = sum(x[b] * group(4 + 3 * a + b) for b in range(3))
        image = both[8 * a : 8 * a + 8] + x[a] * along - cross + group(13 + a)
        image = image + self_row * own[a]
        top, bottom = image[:4], pltpu.roll(image[4:], 64, 1)
        out[a] = jnp.where(low_half((4, 128)), top, bottom)


def first_kernel(n_row, n_col, where, n_pieces, *refs):
    pieces = refs[:n_pieces]
    near = refs[n_pieces : n_pieces + n_col]
    tgt, me_ref = refs[n_pieces + n_col : n_pieces + n_col + 2]
    kernels, places, basis, norm_out, out, slots, cols = refs[n_pieces + n_col + 2 :]
    n_chunk = n_row * n_col // 2
    half = n_row // 2
    assemble(pieces, where, slots, me_ref[0])

    def unpack(chunk, acc):
        first, _ = chunk_parts(slots, chunk, n_row, n_col, 3)
        places[chunk] = jnp.concatenate([first, first], axis=0)
        for a in range(3):
            vec = jnp.concatenate(chunk_parts(slots, chunk, n_row, n_col, a), axis=0)
            basis[chunk, a] = vec
            acc = acc + vec * vec
        return acc

    acc = lax.fori_loop(0, n_chunk, unpack, jnp.zeros((ROWS, 128), F32))
    norm = jnp.sqrt(row_sum(acc))
    norm_out[...] = jnp.broadcast_to(norm, (ROWS, 128))

    low = low_half((128, 128))
    x = [tgt[a : a + 1] for a in range(3)]
    lines = lax.broadcasted_iota(jnp.int32, (128, 128), 0)

    for o in range(n_col):
        index = near[o][0]
        weight = near[o][1]
        count = index.shape[0]

        def build(u, carry):
            chunk = o * half + u
            vec = [basis[chunk, a] / norm for a in range(3)]
            for a in range(3):
                basis[chunk, a] = vec[a]
            write_columns(cols, places, chunk, vec)
            col = places[chunk].T
            d = [x[a] - col[:, a : a + 1] for a in range(3)]
            dist = d[0] * d[0] + d[1] * d[1] + d[2] * d[2]
            root = lax.rsqrt(dist + BLOB_SQ)
            two = col[:, 3:4] * root * root * root * INV_EIGHT_PI
            one = (dist + 2.0 * BLOB_SQ) * two
            line = (lines + u * 128).astype(F32)
            extra = jnp.zeros((128, 128), F32)
            for k in range(count):
                extra = extra + jnp.where(line == index[k : k + 1], weight[k : k + 1], 0.0)
            one = one + (extra + pltpu.roll(extra, 64, 1))
            value = jnp.where(low, one, two)
            high = value.astype(BF16)
            at = pl.ds(pl.multiple_of(chunk * 128, 128), 128)
            kernels[at, 0:128] = high
            kernels[at, 128:256] = (value - high.astype(F32)).astype(BF16)
            return carry

        lax.fori_loop(0, half, build, 0)

    apply_rows(cols, kernels, tgt, tgt[3:4], basis[0], out)


def load_image(pieces, where, slots, image, me, n_row, n_col):
    assemble(pieces, where, slots, me)

    def unpack(chunk, carry):
        for a in range(3):
            image[chunk, a] = jnp.concatenate(
                chunk_parts(slots, chunk, n_row, n_col, a), axis=0
            )
        return carry

    lax.fori_loop(0, n_row * n_col // 2, unpack, 0)


def orthogonalize(image, bases, n_chunk):
    column = []
    for base in bases:
        h = dot_of(image, base, n_chunk)
        column.append(h)

        def take(chunk, carry):
            image[chunk] = image[chunk] - h[None] * base[chunk]
            return carry

        lax.fori_loop(0, n_chunk, take, 0, unroll=4)
    column.append(jnp.sqrt(dot_of(image, image, n_chunk)))
    return column


def middle_kernel(n_row, n_col, where, n_pieces, n_base, *refs):
    pieces = refs[:n_pieces]
    bases = refs[n_pieces : n_pieces + n_base]
    kernels, places, tgt, me_ref, basis, h_out, out, slots, cols = refs[n_pieces + n_base :]
    n_chunk = n_row * n_col // 2
    load_image(pieces, where, slots, basis, me_ref[0], n_row, n_col)
    column = orthogonalize(basis, bases, n_chunk)
    for j, h in enumerate(column):
        h_out[j] = jnp.broadcast_to(h, (ROWS, 128))

    def scale(chunk, carry):
        vec = [basis[chunk, a] / column[-1] for a in range(3)]
        for a in range(3):
            basis[chunk, a] = vec[a]
        write_columns(cols, places, chunk, vec)
        return carry

    lax.fori_loop(0, n_chunk, scale, 0)
    apply_rows(cols, kernels, tgt, tgt[3:4], basis[0], out)


def solve_small(hessen, start_norm, count):
    zero = jnp.zeros_like(start_norm)
    target = [start_norm] + [zero] * count
    cosines = []
    sines = []
    triangle = {}
    for k in range(count):
        column = [hessen[i, k] for i in range(k + 2)]
        for j in range(k):
            first_val = column[j]
            second_val = column[j + 1]
            column[j] = cosines[j] * first_val + sines[j] * second_val
            column[j + 1] = cosines[j] * second_val - sines[j] * first_val
        radius = jnp.sqrt(column[k] * column[k] + column[k + 1] * column[k + 1])
        cosine = column[k] / radius
        sine = column[k + 1] / radius
        cosines.append(cosine)
        sines.append(sine)
        for i in range(k):
            triangle[i, k] = column[i]
        triangle[k, k] = radius
        target[k + 1] = -sine * target[k]
        target[k] = cosine * target[k]
    coeffs = [None] * count
    for k in range(count - 1, -1, -1):
        accum = target[k]
        for i in range(k + 1, count):
            accum = accum - triangle[k, i] * coeffs[i]
        coeffs[k] = accum / triangle[k, k]
    return coeffs


def last_kernel(n_row, n_col, where, n_pieces, *refs):
    pieces = refs[:n_pieces]
    bases = refs[n_pieces : n_pieces + ITERS]
    columns = refs[n_pieces + ITERS : n_pieces + 2 * ITERS - 1]
    norm, me_ref, out, slots, image = refs[n_pieces + 2 * ITERS - 1 :]
    n_chunk = n_row * n_col // 2
    load_image(pieces, where, slots, image, me_ref[0], n_row, n_col)
    last = orthogonalize(image, bases, n_chunk)
    hessen = {}
    for k in range(ITERS - 1):
        for j in range(k + 2):
            hessen[j, k] = columns[k][j]
    for j in range(ITERS + 1):
        hessen[j, ITERS - 1] = jnp.broadcast_to(last[j], (ROWS, 128))
    coeffs = solve_small(hessen, norm[...], ITERS)
    for a in range(3):
        out[a] = sum(coeffs[k] * bases[k][0, a] for k in range(ITERS))


def call(kernel, outs, scratch, operands, n_smem):
    vmem = pl.BlockSpec(memory_space=pltpu.VMEM)
    smem = pl.BlockSpec(memory_space=pltpu.SMEM)
    count = len(operands)
    specs = [smem if i in n_smem else vmem for i in range(count)]
    return pl.pallas_call(
        kernel,
        out_shape=[jax.ShapeDtypeStruct(s, t) for s, t in outs],
        in_specs=specs,
        out_specs=[vmem] * len(outs),
        scratch_shapes=[pltpu.VMEM(s, t) for s, t in scratch],
        compiler_params=pltpu.CompilerParams(vmem_limit_bytes=48 * 1024 * 1024),
    )(*operands)


def body(n_row, n_col, velocity, points, panel_area, self_term, near_index, near_weight):
    n = n_row * n_col
    n_chunk = n // 2
    total = n * 64
    row = lax.axis_index("row")
    col = lax.axis_index("col")
    me = (row * n_col + col).astype(jnp.int32).reshape(1)
    rhs = velocity.shape[0]
    vec = velocity.transpose(1, 0, 2)
    vec = jnp.concatenate([vec, vec[:, : ROWS - rhs]], axis=1)
    place = jnp.concatenate([points, panel_area[None]], axis=0)
    place = jnp.concatenate([place, jnp.zeros_like(place)], axis=0)
    piece = jnp.concatenate([pack(vec), pack(place)[None]], axis=0)

    tgt = jnp.concatenate([points, self_term[None]], axis=0)
    tgt = jnp.concatenate([tgt, tgt], axis=1)
    tgt = jnp.concatenate([tgt, tgt], axis=0)

    near = []
    count = near_index.shape[1] // 2
    for o in range(n_col):
        begin = (col ^ o) * 64
        index = lax.dynamic_slice_in_dim(near_index, begin, 64, 0)
        index = ((index // 64) ^ row) * 64 + index % 64
        weight = lax.dynamic_slice_in_dim(near_weight, begin, 64, 0)
        pair = jnp.stack([index.astype(F32), weight]).transpose(0, 2, 1)
        pair = jnp.concatenate([pair[:, :count], pair[:, count:]], axis=-1)
        if o:
            pair = lax.ppermute(pair, "col", xor_perm(n_col, o))
        near.append(pair)

    vec_shape = (n_chunk, 3, ROWS, 128)
    out_piece = ((3, 4, 128), F32)
    cols = ((256, total), BF16)

    arrays, where = exchange(piece, n, "gather")
    kernels, places, basis, norm, image = call(
        functools.partial(first_kernel, n_row, n_col, where, len(arrays)),
        [
            ((total, 256), BF16),
            ((n_chunk, ROWS, 128), F32),
            (vec_shape, F32),
            ((ROWS, 128), F32),
            out_piece,
        ],
        [((n, 4, 4, 128), F32), cols],
        [*arrays, *near, tgt, me],
        {len(arrays) + n_col + 1},
    )
    bases = [basis]
    columns = []
    for k, mode in ((1, "double"), (2, "direct")):
        arrays, where = exchange(image, n, mode)
        basis, column, image = call(
            functools.partial(middle_kernel, n_row, n_col, where, len(arrays), k),
            [(vec_shape, F32), ((k + 1, ROWS, 128), F32), out_piece],
            [((n, 3, 4, 128), F32), cols],
            [*arrays, *bases, kernels, places, tgt, me],
            {len(arrays) + k + 3},
        )
        bases.append(basis)
        columns.append(column)
    arrays, where = exchange(image, n, "alltoall")
    (density,) = call(
        functools.partial(last_kernel, n_row, n_col, where, len(arrays)),
        [((3, ROWS, 128), F32)],
        [((n, 3, 4, 128), F32), (vec_shape, F32)],
        [*arrays, *bases, *columns, norm, me],
        {len(arrays) + 2 * ITERS},
    )
    return density[:, :rhs, :64].transpose(1, 0, 2)


def solution(mesh):
    n_row, n_col = mesh.shape["row"], mesh.shape["col"]
    return jax.shard_map(
        functools.partial(body, n_row, n_col),
        mesh=mesh,
        in_specs=(
            P(None, None, AXES),
            P(None, AXES),
            P(AXES),
            P(AXES),
            P("row", "col"),
            P("row", "col"),
        ),
        out_specs=P(None, None, AXES),
        check_vma=False,
    )
```

```python
import functools
import math

import jax
import jax.numpy as jnp
from jax import lax
from jax.experimental import pallas as pl
from jax.experimental.pallas import tpu as pltpu
from jax.sharding import PartitionSpec as P

ITERS = 3
BLOB_SQ = 0.0025
INV_EIGHT_PI = 1.0 / (8.0 * math.pi)
ROWS = 8
AXES = ("top", "mid", "core", "col")
F32 = jnp.float32
BF16 = jnp.bfloat16


def low_half(shape):
    return lax.broadcasted_iota(jnp.int32, shape, len(shape) - 1) < 64


def pack(rows):
    return jnp.concatenate([rows[..., :4, :], rows[..., 4:, :]], axis=-1)


def xor_perm(n, m):
    return [(d, d ^ m) for d in range(n)]


def spread(piece, axes, size):
    wide = jnp.broadcast_to(piece[None], (size,) + piece.shape)
    return lax.all_to_all(wide, axes, 0, 0, tiled=True)


def exchange(piece, sizes, mode):
    top, mid, core, col = sizes
    n = top * mid * core * col
    if mode == "all":
        return [spread(piece, AXES, n)], lambda m, me: (0, me ^ m)
    if mode == "two":
        near = spread(piece, AXES[1:], n // top)
        far = spread(near, AXES[0], top)
        return [far.reshape((n,) + piece.shape)], lambda m, me: (0, me ^ m)
    if mode == "chips":
        own = spread(piece, ("top", "mid", "col"), n // 2)
        other = lax.ppermute(own, "core", xor_perm(2, 1))

        def where(m, me):
            dev = me ^ m
            chip = dev // (2 * col) * col + dev % col
            return (m // col) % 2, chip

        return [own, other], where
    raise ValueError(mode)


def assemble(piece_refs, where, slots, me):
    for m in range(slots.shape[0]):
        k, i = where(m, me)
        slots[m] = piece_refs[k][i]


def chunk_parts(slots, chunk, n_row, n_col, part):
    half = n_row // 2
    o = chunk // half
    u = chunk % half
    even = slots[(2 * u) * n_col + o, part]
    odd = slots[(2 * u + 1) * n_col + o, part]
    low = low_half((4, 128))
    first = jnp.where(low, even, pltpu.roll(odd, 64, 1))
    second = jnp.where(low, pltpu.roll(even, 64, 1), odd)
    return first, second


PAIRS = [(i, j) for i in range(ITERS) for j in range(i, ITERS)]


def place_of(j):
    lane = lax.broadcasted_iota(jnp.int32, (ROWS, 128), 1)
    return lane == lax.broadcasted_iota(jnp.int32, (ROWS, 128), 0) * (ITERS + 1) + j


def row_sum(acc):
    return jnp.sum(acc, axis=1, keepdims=True)


def dot_of(left, right, n_chunk):
    def step(chunk, acc):
        return acc + jnp.sum(left[chunk] * right[chunk], axis=0)

    acc = lax.fori_loop(0, n_chunk, step, jnp.zeros((ROWS, 128), F32), unroll=4)
    return row_sum(acc)


def write_columns(cols, places, chunk, vec):
    y = places[chunk]
    ys = [y[a : a + 1] for a in range(3)]
    f = [vec[a] for a in range(3)]
    g = ys[0] * f[0] + ys[1] * f[1] + ys[2] * f[2]
    groups = f + [g]
    groups += [ys[p] * f[v] for p in range(3) for v in range(3)]
    groups += [ys[a] * g for a in range(3)]
    full = jnp.concatenate(groups, axis=0)
    high = full.astype(BF16)
    low = (full - high.astype(F32)).astype(BF16)
    at = pl.ds(pl.multiple_of(chunk * 128, 128), 128)
    cols[0:128, at] = high
    cols[128:256, at] = low


def apply_rows(cols, kernels, targets, own):
    total = cols.shape[1]
    step = min(total, 2048)

    def turn(i, acc):
        at = pl.ds(pl.multiple_of(i * step, step), step)
        return acc + jnp.dot(cols[:, at], kernels[at, :], preferred_element_type=F32)

    if total == step:
        prod = jnp.dot(cols[...], kernels[...], preferred_element_type=F32)
    else:
        prod = lax.fori_loop(0, total // step, turn, jnp.zeros((256, 256), F32))
    both = prod[:128, :128] + (prod[128:, :128] + prod[:128, 128:])
    two = pltpu.roll(both, 64, 1)

    def group(k):
        return two[8 * k : 8 * k + 8]

    x = [targets[a : a + 1] for a in range(3)]
    images = []
    along = x[0] * group(0) + x[1] * group(1) + x[2] * group(2) - group(3)
    for a in range(3):
        cross = sum(x[b] * group(4 + 3 * a + b) for b in range(3))
        image = both[8 * a : 8 * a + 8] + x[a] * along - cross + group(13 + a)
        images.append(image + targets[3:4] * own[a])
    return images


def write_piece(images, out):
    for a, image in enumerate(images):
        top, bottom = image[:4], pltpu.roll(image[4:], 64, 1)
        out[a] = jnp.where(low_half((4, 128)), top, bottom)


def first_kernel(n_row, n_col, where, n_pieces, *refs):
    pieces = refs[:n_pieces]
    near = refs[n_pieces : n_pieces + n_col]
    tgt, me_ref = refs[n_pieces + n_col : n_pieces + n_col + 2]
    kernels, places, basis, norm_out, out, slots, cols = refs[n_pieces + n_col + 2 :]
    n_chunk = n_row * n_col // 2
    half = n_row // 2
    assemble(pieces, where, slots, me_ref[0])

    def unpack(chunk, acc):
        first, _ = chunk_parts(slots, chunk, n_row, n_col, 3)
        places[chunk] = jnp.concatenate([first, first], axis=0)
        for a in range(3):
            vec = jnp.concatenate(chunk_parts(slots, chunk, n_row, n_col, a), axis=0)
            basis[chunk, a] = vec
            acc = acc + vec * vec
        return acc

    acc = lax.fori_loop(0, n_chunk, unpack, jnp.zeros((ROWS, 128), F32))
    norm = jnp.sqrt(row_sum(acc))
    norm_out[...] = jnp.broadcast_to(norm, (ROWS, 128))

    low = low_half((128, 128))
    x = [tgt[a : a + 1] for a in range(3)]
    lines = lax.broadcasted_iota(jnp.int32, (128, 128), 0)

    for o in range(n_col):
        index = near[o][0]
        weight = near[o][1]
        count = index.shape[0]

        def build(u, carry):
            chunk = o * half + u
            vec = [basis[chunk, a] / norm for a in range(3)]
            for a in range(3):
                basis[chunk, a] = vec[a]
            write_columns(cols, places, chunk, vec)
            col = places[chunk].T
            d = [x[a] - col[:, a : a + 1] for a in range(3)]
            dist = d[0] * d[0] + d[1] * d[1] + d[2] * d[2]
            root = lax.rsqrt(dist + BLOB_SQ)
            two = col[:, 3:4] * root * root * root * INV_EIGHT_PI
            one = (dist + 2.0 * BLOB_SQ) * two
            line = (lines + u * 128).astype(F32)
            extra = jnp.zeros((128, 128), F32)
            for k in range(count):
                extra = extra + jnp.where(line == index[k : k + 1], weight[k : k + 1], 0.0)
            one = one + (extra + pltpu.roll(extra, 64, 1))
            value = jnp.where(low, one, two)
            high = value.astype(BF16)
            at = pl.ds(pl.multiple_of(chunk * 128, 128), 128)
            kernels[at, 0:128] = high
            kernels[at, 128:256] = (value - high.astype(F32)).astype(BF16)
            return carry

        lax.fori_loop(0, half, build, 0)

    write_piece(apply_rows(cols, kernels, tgt, basis[0]), out)


def load_image(pieces, where, slots, image, me, n_row, n_col):
    assemble(pieces, where, slots, me)

    def unpack(chunk, carry):
        for a in range(3):
            image[chunk, a] = jnp.concatenate(
                chunk_parts(slots, chunk, n_row, n_col, a), axis=0
            )
        return carry

    lax.fori_loop(0, n_row * n_col // 2, unpack, 0)


def orthogonalize(image, bases, n_chunk):
    column = []
    for base in bases:
        h = dot_of(image, base, n_chunk)
        column.append(h)

        def take(chunk, carry):
            image[chunk] = image[chunk] - h[None] * base[chunk]
            return carry

        lax.fori_loop(0, n_chunk, take, 0, unroll=4)
    column.append(jnp.sqrt(dot_of(image, image, n_chunk)))
    return column


def middle_kernel(n_row, n_col, where, n_pieces, n_base, final, *refs):
    pieces = refs[:n_pieces]
    bases = refs[n_pieces : n_pieces + n_base]
    kernels, places, tgt, me_ref, basis, h_out, out, slots, cols = refs[n_pieces + n_base :]
    n_chunk = n_row * n_col // 2
    load_image(pieces, where, slots, basis, me_ref[0], n_row, n_col)
    column = orthogonalize(basis, bases, n_chunk)
    for j, h in enumerate(column):
        h_out[j] = jnp.broadcast_to(h, (ROWS, 128))

    def scale(chunk, carry):
        vec = [basis[chunk, a] / column[-1] for a in range(3)]
        for a in range(3):
            basis[chunk, a] = vec[a]
        write_columns(cols, places, chunk, vec)
        return carry

    lax.fori_loop(0, n_chunk, scale, 0)
    images = apply_rows(cols, kernels, tgt, basis[0])
    if not final:
        write_piece(images, out)
        return
    every = [*bases, basis]
    for at, (i, j) in enumerate(PAIRS):
        gram = dot_of(every[i], every[j], n_chunk)
        h_out[len(column) + at] = jnp.broadcast_to(gram, (ROWS, 128))
    low = low_half((ROWS, 128))
    row = jnp.zeros((ROWS, 128), F32)
    for j in range(ITERS + 1):
        other = images if j == ITERS else [every[j][0, a] for a in range(3)]
        part = sum(images[a] * other[a] for a in range(3))
        part = row_sum(jnp.where(low, part, 0.0))
        row = row + jnp.where(place_of(j), part, 0.0)
    out[...] = jnp.sum(row, axis=0, keepdims=True)


def solve_small(hessen, start_norm, count):
    zero = jnp.zeros_like(start_norm)
    target = [start_norm] + [zero] * count
    cosines = []
    sines = []
    triangle = {}
    for k in range(count):
        column = [hessen[i, k] for i in range(k + 2)]
        for j in range(k):
            first_val = column[j]
            second_val = column[j + 1]
            column[j] = cosines[j] * first_val + sines[j] * second_val
            column[j + 1] = cosines[j] * second_val - sines[j] * first_val
        radius = jnp.sqrt(column[k] * column[k] + column[k + 1] * column[k + 1])
        cosine = column[k] / radius
        sine = column[k + 1] / radius
        cosines.append(cosine)
        sines.append(sine)
        for i in range(k):
            triangle[i, k] = column[i]
        triangle[k, k] = radius
        target[k + 1] = -sine * target[k]
        target[k] = cosine * target[k]
    coeffs = [None] * count
    for k in range(count - 1, -1, -1):
        accum = target[k]
        for i in range(k + 1, count):
            accum = accum - triangle[k, i] * coeffs[i]
        coeffs[k] = accum / triangle[k, k]
    return coeffs


def last_kernel(sums, *refs):
    bases = refs[:ITERS]
    columns = refs[ITERS : 2 * ITERS - 1]
    norm, out = refs[2 * ITERS - 1 :]
    hessen = {}
    for k in range(ITERS - 1):
        for j in range(k + 2):
            hessen[j, k] = columns[k][j]
    gram = {}
    for at, (i, j) in enumerate(PAIRS):
        gram[i, j] = gram[j, i] = columns[-1][ITERS + at]
    row = jnp.broadcast_to(jnp.sum(sums[...], axis=0), (ROWS, 128))
    inner = [
        jnp.broadcast_to(row_sum(jnp.where(place_of(j), row, 0.0)), (ROWS, 128))
        for j in range(ITERS + 1)
    ]
    square = inner[ITERS]
    for j in range(ITERS):
        h = inner[j]
        for i in range(j):
            h = h - hessen[i, ITERS - 1] * gram[i, j]
        hessen[j, ITERS - 1] = h
    for j in range(ITERS):
        rest = -2.0 * inner[j]
        for i in range(ITERS):
            rest = rest + hessen[i, ITERS - 1] * gram[i, j]
        square = square + hessen[j, ITERS - 1] * rest
    hessen[ITERS, ITERS - 1] = jnp.sqrt(jnp.maximum(square, 0.0))
    coeffs = solve_small(hessen, norm[...], ITERS)
    for a in range(3):
        out[a] = sum(coeffs[k] * bases[k][a] for k in range(ITERS))


def call(kernel, outs, scratch, operands, n_smem):
    vmem = pl.BlockSpec(memory_space=pltpu.VMEM)
    smem = pl.BlockSpec(memory_space=pltpu.SMEM)
    count = len(operands)
    specs = [smem if i in n_smem else vmem for i in range(count)]
    return pl.pallas_call(
        kernel,
        out_shape=[jax.ShapeDtypeStruct(s, t) for s, t in outs],
        in_specs=specs,
        out_specs=[vmem] * len(outs),
        scratch_shapes=[pltpu.VMEM(s, t) for s, t in scratch],
        compiler_params=pltpu.CompilerParams(vmem_limit_bytes=48 * 1024 * 1024),
    )(*operands)


def body(sizes, velocity, points, panel_area, self_term, near_index, near_weight):
    n_row, n_col = sizes[0] * sizes[1] * sizes[2], sizes[3]
    n = n_row * n_col
    n_chunk = n // 2
    total = n * 64
    row = lax.axis_index(AXES[:3])
    col = lax.axis_index("col")
    me = (row * n_col + col).astype(jnp.int32).reshape(1)
    rhs = velocity.shape[0]
    vec = velocity.transpose(1, 0, 2)
    vec = jnp.concatenate([vec, vec[:, : ROWS - rhs]], axis=1)
    place = jnp.concatenate([points, panel_area[None]], axis=0)
    place = jnp.concatenate([place, jnp.zeros_like(place)], axis=0)
    piece = jnp.concatenate([pack(vec), pack(place)[None]], axis=0)

    tgt = jnp.concatenate([points, self_term[None]], axis=0)
    tgt = jnp.concatenate([tgt, tgt], axis=1)
    tgt = jnp.concatenate([tgt, tgt], axis=0)

    near = []
    count = near_index.shape[1] // 2
    for o in range(n_col):
        begin = (col ^ o) * 64
        index = lax.dynamic_slice_in_dim(near_index, begin, 64, 0)
        index = ((index // 64) ^ row) * 64 + index % 64
        weight = lax.dynamic_slice_in_dim(near_weight, begin, 64, 0)
        pair = jnp.stack([index.astype(F32), weight]).transpose(0, 2, 1)
        pair = jnp.concatenate([pair[:, :count], pair[:, count:]], axis=-1)
        if o:
            pair = lax.ppermute(pair, "col", xor_perm(n_col, o))
        near.append(pair)

    vec_shape = (n_chunk, 3, ROWS, 128)
    out_piece = ((3, 4, 128), F32)
    cols = ((256, total), BF16)

    arrays, where = exchange(piece, sizes, "all")
    kernels, places, basis, norm, image = call(
        functools.partial(first_kernel, n_row, n_col, where, len(arrays)),
        [
            ((total, 256), BF16),
            ((n_chunk, ROWS, 128), F32),
            (vec_shape, F32),
            ((ROWS, 128), F32),
            out_piece,
        ],
        [((n, 4, 4, 128), F32), cols],
        [*arrays, *near, tgt, me],
        {len(arrays) + n_col + 1},
    )
    bases = [basis]
    columns = []
    for k, mode in ((1, "chips"), (2, "two")):
        arrays, where = exchange(image, sizes, mode)
        final = k == ITERS - 1
        basis, column, image = call(
            functools.partial(middle_kernel, n_row, n_col, where, len(arrays), k, final),
            [
                (vec_shape, F32),
                ((k + 1 + (6 if final else 0), ROWS, 128), F32),
                ((1, 128), F32) if final else out_piece,
            ],
            [((n, 3, 4, 128), F32), cols],
            [*arrays, *bases, kernels, places, tgt, me],
            {len(arrays) + k + 3},
        )
        bases.append(basis)
        columns.append(column)
    sums = spread(image, AXES, n)
    (density,) = call(
        last_kernel,
        [((3, ROWS, 128), F32)],
        [],
        [sums, *[base[0] for base in bases], *columns, norm],
        {},
    )
    return density[:, :rhs, :64].transpose(1, 0, 2)


def solution(mesh):
    n_row, n_col = mesh.shape["row"], mesh.shape["col"]
    sizes = (n_row // 4, 2, 2, n_col)
    split = jax.sharding.Mesh(mesh.devices.reshape(sizes), AXES)
    return jax.shard_map(
        functools.partial(body, sizes),
        mesh=split,
        in_specs=(
            P(None, None, AXES),
            P(None, AXES),
            P(AXES),
            P(AXES),
            P(AXES[:3], "col"),
            P(AXES[:3], "col"),
        ),
        out_specs=P(None, None, AXES),
        check_vma=False,
    )
```

```python
import functools
import math

import jax
import jax.numpy as jnp
from jax import lax
from jax.experimental import pallas as pl
from jax.experimental.pallas import tpu as pltpu
from jax.sharding import PartitionSpec as P

ITERS = 3
BLOB_SQ = 0.0025
INV_EIGHT_PI = 1.0 / (8.0 * math.pi)
ROWS = 8
AXES = ("top", "mid", "core", "col")
F32 = jnp.float32
BF16 = jnp.bfloat16


def low_half(shape):
    return lax.broadcasted_iota(jnp.int32, shape, len(shape) - 1) < 64


def pack(rows):
    return jnp.concatenate([rows[..., :4, :], rows[..., 4:, :]], axis=-1)


def xor_perm(n, m):
    return [(d, d ^ m) for d in range(n)]


def spread(piece, axes, size):
    wide = jnp.broadcast_to(piece[None], (size,) + piece.shape)
    return lax.all_to_all(wide, axes, 0, 0, tiled=True)


def each(count, step):
    if count <= 16:
        for i in range(count):
            step(i)
    else:
        pl.loop(0, count)(step)


def dots(pairs, n_chunk):
    lanes = 4
    zero = jnp.zeros((ROWS, 128), F32)

    def step(chunk, accs):
        slot = chunk % lanes if isinstance(chunk, int) else 0
        for at, (left, right) in enumerate(pairs):
            part = sum(left[chunk, a] * right[chunk, a] for a in range(3))
            accs[at][slot] = accs[at][slot] + part
        return accs

    accs = [[zero] * lanes for _ in pairs]
    if n_chunk <= 16:
        for chunk in range(n_chunk):
            accs = step(chunk, accs)
    else:
        accs = lax.fori_loop(0, n_chunk, step, accs)
    sums = [(acc[0] + acc[1]) + (acc[2] + acc[3]) for acc in accs]
    return [jnp.sum(acc, axis=1, keepdims=True) for acc in sums]


def chunk_parts(piece, chunk, me, n_row, n_col, part):
    half = n_row // 2
    o = chunk // half
    u = chunk % half
    even = piece[me ^ ((2 * u) * n_col + o), part]
    odd = piece[me ^ ((2 * u + 1) * n_col + o), part]
    low = low_half((4, 128))
    first = jnp.where(low, even, pltpu.roll(odd, 64, 1))
    second = jnp.where(low, pltpu.roll(even, 64, 1), odd)
    return first, second


PAIRS = [(i, j) for i in range(ITERS) for j in range(i, ITERS)]


def place_of(j):
    lane = lax.broadcasted_iota(jnp.int32, (ROWS, 128), 1)
    return lane == lax.broadcasted_iota(jnp.int32, (ROWS, 128), 0) * (ITERS + 1) + j


def row_sum(acc):
    return jnp.sum(acc, axis=1, keepdims=True)


def lines_of(chunk):
    if isinstance(chunk, int):
        return pl.ds(chunk * 128, 128)
    return pl.ds(pl.multiple_of(chunk * 128, 128), 128)


def write_columns(cols, places, chunk, vec):
    y = places[chunk]
    ys = [y[a : a + 1] for a in range(3)]
    f = [vec[a] for a in range(3)]
    g = ys[0] * f[0] + ys[1] * f[1] + ys[2] * f[2]
    groups = f + [g]
    groups += [ys[p] * f[v] for p in range(3) for v in range(3)]
    groups += [ys[a] * g for a in range(3)]
    full = jnp.concatenate(groups, axis=0)
    high = full.astype(BF16)
    low = (full - high.astype(F32)).astype(BF16)
    at = lines_of(chunk)
    cols[0:128, at] = high
    cols[128:256, at] = low


def apply_rows(cols, kernels, targets, own):
    total = cols.shape[1]
    step = min(total, 2048)

    def turn(i, acc):
        at = pl.ds(pl.multiple_of(i * step, step), step)
        return acc + jnp.dot(cols[:, at], kernels[at, :], preferred_element_type=F32)

    if total == step:
        prod = jnp.dot(cols[...], kernels[...], preferred_element_type=F32)
    else:
        prod = lax.fori_loop(0, total // step, turn, jnp.zeros((256, 256), F32))
    both = prod[:128, :128] + (prod[128:, :128] + prod[:128, 128:])
    two = pltpu.roll(both, 64, 1)

    def group(k):
        return two[8 * k : 8 * k + 8]

    x = [targets[a : a + 1] for a in range(3)]
    images = []
    along = x[0] * group(0) + x[1] * group(1) + x[2] * group(2) - group(3)
    for a in range(3):
        cross = sum(x[b] * group(4 + 3 * a + b) for b in range(3))
        image = both[8 * a : 8 * a + 8] + x[a] * along - cross + group(13 + a)
        images.append(image + targets[3:4] * own[a])
    return images


def write_piece(images, out):
    rows = []
    for image in images:
        top, bottom = image[:4], pltpu.roll(image[4:], 64, 1)
        rows.append(jnp.where(low_half((4, 128)), top, bottom))

    def put(m):
        for a in range(3):
            out[m, a] = rows[a]

    each_wide(out.shape[0], put)


def each_wide(count, put):
    if count <= 64:
        for m in range(count):
            put(m)
    else:
        pl.loop(0, count)(put)


def pack_kernel(velocity, points, area, self_term, out, tgt):
    rhs = velocity.shape[0]
    field = velocity[...]
    rows = []
    for a in range(3):
        vec = field[:, a, :]
        rows.append(jnp.concatenate([vec[:4], jnp.concatenate([vec[4:], vec[: ROWS - rhs]], axis=0)], axis=1))
    where = points[...]
    place = jnp.concatenate([where, area[...]], axis=0)
    rows.append(jnp.concatenate([place, place], axis=1))
    mine = jnp.concatenate([where, self_term[...]], axis=0)
    mine = jnp.concatenate([mine, mine], axis=1)
    tgt[...] = jnp.concatenate([mine, mine], axis=0)

    def put(m):
        for a in range(4):
            out[m, a] = rows[a]

    each_wide(out.shape[0], put)


def near_kernel(index, weight, me, *outs):
    row, col = me[1], me[2]
    half = index.shape[0] // 2
    low = low_half((half, 128))
    for o, out in enumerate(outs):
        to = col ^ o
        at = lines_of(to // 2)
        odd = to % 2 == 1
        place = index[:, at]
        place = (((place // 64) ^ row) * 64 + place % 64).astype(F32)
        for i, value in enumerate((place, weight[:, at])):
            top, bottom = value[:half], value[half:]
            lower = jnp.where(low, top, pltpu.roll(bottom, 64, 1))
            upper = jnp.where(low, pltpu.roll(top, 64, 1), bottom)
            out[i] = jnp.where(odd, upper, lower)


def extra_kernel(half_chunks, *refs):
    near, out = refs[:-1], refs[-1]
    low = low_half((128, 128))
    lines = lax.broadcasted_iota(jnp.int32, (128, 128), 0)
    for o, pair in enumerate(near):
        index, weight = pair[0], pair[1]

        def build(u):
            line = (lines + u * 128).astype(F32)
            total = jnp.zeros((128, 128), F32)
            for k in range(index.shape[0]):
                total = total + jnp.where(line == index[k : k + 1], weight[k : k + 1], 0.0)
            total = total + pltpu.roll(total, 64, 1)
            out[o * half_chunks + u] = jnp.where(low, total, 0.0)

        pl.loop(0, half_chunks)(build)


def first_kernel(n_row, n_col, piece, extra, tgt, me_ref, kernels, places, basis, norm_out, out, cols):
    n_chunk = n_row * n_col // 2
    me = me_ref[0]

    def unpack(chunk):
        first, _ = chunk_parts(piece, chunk, me, n_row, n_col, 3)
        places[chunk] = jnp.concatenate([first, first], axis=0)
        for a in range(3):
            parts = chunk_parts(piece, chunk, me, n_row, n_col, a)
            basis[chunk, a] = jnp.concatenate(parts, axis=0)

    each(n_chunk, unpack)
    (square,) = dots([(basis, basis)], n_chunk)
    norm = jnp.sqrt(square)
    norm_out[...] = jnp.broadcast_to(norm, (ROWS, 128))
    scale = jnp.broadcast_to(1.0 / norm, (ROWS, 128))
    low = low_half((128, 128))
    x = [tgt[a : a + 1] for a in range(3)]

    def build(chunk):
        vec = [basis[chunk, a] * scale for a in range(3)]
        for a in range(3):
            basis[chunk, a] = vec[a]
        write_columns(cols, places, chunk, vec)
        col = places[chunk].T
        d = [x[a] - col[:, a : a + 1] for a in range(3)]
        dist = d[0] * d[0] + d[1] * d[1] + d[2] * d[2]
        root = lax.rsqrt(dist + BLOB_SQ)
        two = (col[:, 3:4] * INV_EIGHT_PI) * root * root * root
        one = (dist + 2.0 * BLOB_SQ) * two
        value = jnp.where(low, one, two) + extra[chunk]
        high = value.astype(BF16)
        at = lines_of(chunk)
        kernels[at, 0:128] = high
        kernels[at, 128:256] = (value - high.astype(F32)).astype(BF16)

    each(n_chunk, build)
    write_piece(apply_rows(cols, kernels, tgt, basis[0]), out)


def middle_kernel(n_row, n_col, n_base, final, piece, *refs):
    bases = refs[:n_base]
    kernels, places, tgt, me_ref, basis, h_out, out, own, cols = refs[n_base:]
    n_chunk = n_row * n_col // 2
    me = me_ref[0]

    def unpack(chunk):
        for a in range(3):
            parts = chunk_parts(piece, chunk, me, n_row, n_col, a)
            basis[chunk, a] = jnp.concatenate(parts, axis=0)

    each(n_chunk, unpack)
    column = []
    for base in bases:
        (h,) = dots([(basis, base)], n_chunk)
        h = jnp.broadcast_to(h, (ROWS, 128))
        column.append(h)

        def take(chunk):
            for a in range(3):
                basis[chunk, a] = basis[chunk, a] - h * base[chunk, a]

        each(n_chunk, take)
    (square,) = dots([(basis, basis)], n_chunk)
    length = jnp.broadcast_to(jnp.sqrt(square), (ROWS, 128))
    column.append(length)
    for j, h in enumerate(column):
        h_out[j] = h
    scale = 1.0 / length

    def columns(chunk):
        vec = [basis[chunk, a] * scale for a in range(3)]
        for a in range(3):
            basis[chunk, a] = vec[a]
        write_columns(cols, places, chunk, vec)

    each(n_chunk, columns)
    images = apply_rows(cols, kernels, tgt, basis[0])
    every = [*bases, basis]
    for j, base in enumerate(every):
        own[j] = base[0]
    if not final:
        write_piece(images, out)
        return
    grams = dots([(every[i], every[j]) for i, j in PAIRS], n_chunk)
    for at, gram in enumerate(grams):
        h_out[len(column) + at] = jnp.broadcast_to(gram, (ROWS, 128))
    low = low_half((ROWS, 128))
    row = jnp.zeros((ROWS, 128), F32)
    for j in range(ITERS + 1):
        other = images if j == ITERS else [every[j][0, a] for a in range(3)]
        part = sum(images[a] * other[a] for a in range(3))
        part = row_sum(jnp.where(low, part, 0.0))
        row = row + jnp.where(place_of(j), part, 0.0)
    row = jnp.sum(row, axis=0, keepdims=True)

    def put(m):
        out[m] = row

    each_wide(out.shape[0], put)


def solve_small(hessen, start_norm, count):
    zero = jnp.zeros_like(start_norm)
    target = [start_norm] + [zero] * count
    cosines = []
    sines = []
    triangle = {}
    for k in range(count):
        column = [hessen[i, k] for i in range(k + 2)]
        for j in range(k):
            first_val = column[j]
            second_val = column[j + 1]
            column[j] = cosines[j] * first_val + sines[j] * second_val
            column[j + 1] = cosines[j] * second_val - sines[j] * first_val
        radius = jnp.sqrt(column[k] * column[k] + column[k + 1] * column[k + 1])
        cosine = column[k] / radius
        sine = column[k + 1] / radius
        cosines.append(cosine)
        sines.append(sine)
        for i in range(k):
            triangle[i, k] = column[i]
        triangle[k, k] = radius
        target[k + 1] = -sine * target[k]
        target[k] = cosine * target[k]
    coeffs = [None] * count
    for k in range(count - 1, -1, -1):
        accum = target[k]
        for i in range(k + 1, count):
            accum = accum - triangle[k, i] * coeffs[i]
        coeffs[k] = accum / triangle[k, k]
    return coeffs


def last_kernel(sums, own, *refs):
    columns = refs[: ITERS - 1]
    norm, out = refs[ITERS - 1 :]
    hessen = {}
    for k in range(ITERS - 1):
        for j in range(k + 2):
            hessen[j, k] = columns[k][j]
    gram = {}
    for at, (i, j) in enumerate(PAIRS):
        gram[i, j] = gram[j, i] = columns[-1][ITERS + at]
    row = jnp.broadcast_to(jnp.sum(sums[...], axis=0), (ROWS, 128))
    inner = [
        jnp.broadcast_to(row_sum(jnp.where(place_of(j), row, 0.0)), (ROWS, 128))
        for j in range(ITERS + 1)
    ]
    square = inner[ITERS]
    for j in range(ITERS):
        h = inner[j]
        for i in range(j):
            h = h - hessen[i, ITERS - 1] * gram[i, j]
        hessen[j, ITERS - 1] = h
    for j in range(ITERS):
        rest = -2.0 * inner[j]
        for i in range(ITERS):
            rest = rest + hessen[i, ITERS - 1] * gram[i, j]
        square = square + hessen[j, ITERS - 1] * rest
    hessen[ITERS, ITERS - 1] = jnp.sqrt(jnp.maximum(square, 0.0))
    coeffs = solve_small(hessen, norm[...], ITERS)
    for a in range(3):
        density = sum(coeffs[k] * own[k, a] for k in range(ITERS))
        out[:, a, :] = density[: out.shape[0], :64]


def call(kernel, outs, scratch, operands, scalars=(), flops=0):
    vmem = pl.BlockSpec(memory_space=pltpu.VMEM)
    smem = pl.BlockSpec(memory_space=pltpu.SMEM)
    count = len(operands)
    specs = [smem if i in scalars else vmem for i in range(count)]
    moved = sum(x.size * x.dtype.itemsize for x in operands)
    return pl.pallas_call(
        kernel,
        out_shape=[jax.ShapeDtypeStruct(s, t) for s, t in outs],
        in_specs=specs,
        out_specs=[vmem] * len(outs),
        scratch_shapes=[pltpu.VMEM(s, t) for s, t in scratch],
        cost_estimate=pl.CostEstimate(flops=flops, bytes_accessed=moved, transcendentals=0),
        compiler_params=pltpu.CompilerParams(vmem_limit_bytes=48 * 1024 * 1024),
    )(*operands)


def body(sizes, velocity, points, panel_area, self_term, near_index, near_weight):
    n_row, n_col = sizes[0] * sizes[1] * sizes[2], sizes[3]
    n = n_row * n_col
    n_chunk = n // 2
    total = n * 64
    row = lax.axis_index(AXES[:3])
    col = lax.axis_index("col")
    me = jnp.stack([row * n_col + col, row, col]).astype(jnp.int32)
    rhs = velocity.shape[0]

    wide, tgt = call(
        pack_kernel,
        [((n, 4, 4, 128), F32), ((8, 128), F32)],
        [],
        [velocity, points, panel_area[None], self_term[None]],
    )
    piece = lax.all_to_all(wide, AXES, 0, 0, tiled=True)

    near = call(
        near_kernel,
        [((2, near_index.shape[1] // 2, 128), F32)] * n_col,
        [],
        [near_index.T, near_weight.T, me],
        {2},
    )
    near = [
        lax.ppermute(pair, "col", xor_perm(n_col, o)) if o else pair
        for o, pair in enumerate(near)
    ]
    (extra,) = call(
        functools.partial(extra_kernel, n_row // 2),
        [((n_chunk, 128, 128), F32)],
        [],
        near,
        flops=10**9,
    )

    vec_shape = (n_chunk, 3, ROWS, 128)
    cols = ((256, total), BF16)
    kernels, places, basis, norm, wide = call(
        functools.partial(first_kernel, n_row, n_col),
        [
            ((total, 256), BF16),
            ((n_chunk, ROWS, 128), F32),
            (vec_shape, F32),
            ((ROWS, 128), F32),
            ((n, 3, 4, 128), F32),
        ],
        [cols],
        [piece, extra, tgt, me],
        {3},
    )
    bases = [basis]
    columns = []
    for k in range(1, ITERS):
        final = k == ITERS - 1
        piece = lax.all_to_all(wide, AXES, 0, 0, tiled=True)
        basis, column, wide, own = call(
            functools.partial(middle_kernel, n_row, n_col, k, final),
            [
                (vec_shape, F32),
                ((k + 1 + (len(PAIRS) if final else 0), ROWS, 128), F32),
                ((n, 1, 128) if final else (n, 3, 4, 128), F32),
                ((k + 1, 3, ROWS, 128), F32),
            ],
            [cols],
            [piece, *bases, kernels, places, tgt, me],
            {k + 4},
        )
        bases.append(basis)
        columns.append(column)
    sums = lax.all_to_all(wide, AXES, 0, 0, tiled=True)
    (density,) = call(
        last_kernel, [((rhs, 3, 64), F32)], [], [sums, own, *columns, norm]
    )
    return density


def solution(mesh):
    n_row, n_col = mesh.shape["row"], mesh.shape["col"]
    sizes = (n_row // 4, 2, 2, n_col)
    split = jax.sharding.Mesh(mesh.devices.reshape(sizes), AXES)
    return jax.shard_map(
        functools.partial(body, sizes),
        mesh=split,
        in_specs=(
            P(None, None, AXES),
            P(None, AXES),
            P(AXES),
            P(AXES),
            P(AXES[:3], "col"),
            P(AXES[:3], "col"),
        ),
        out_specs=P(None, None, AXES),
        check_vma=False,
    )
```

```python
import functools
import math

import jax
import jax.numpy as jnp
from jax import lax
from jax.experimental import pallas as pl
from jax.experimental.pallas import tpu as pltpu
from jax.sharding import PartitionSpec as P

ITERS = 3
BLOB_SQ = 0.0025
INV_EIGHT_PI = 1.0 / (8.0 * math.pi)
ROWS = 8
AXES = ("top", "mid", "core", "col")
F32 = jnp.float32
BF16 = jnp.bfloat16


def low_half(shape):
    return lax.broadcasted_iota(jnp.int32, shape, len(shape) - 1) < 64


def pack(rows):
    return jnp.concatenate([rows[..., :4, :], rows[..., 4:, :]], axis=-1)


def xor_perm(n, m):
    return [(d, d ^ m) for d in range(n)]


def spread(piece, axes, size):
    wide = jnp.broadcast_to(piece[None], (size,) + piece.shape)
    return lax.all_to_all(wide, axes, 0, 0, tiled=True)


def each(count, step):
    if count <= 16:
        for i in range(count):
            step(i)
    else:
        pl.loop(0, count)(step)


class Sums:
    def __init__(self, count, refs):
        self.refs = refs
        self.parts = [[None] * 4 for _ in range(count)]
        if refs is not None:
            for at in range(count):
                refs[at] = jnp.zeros((ROWS, 128), F32)

    def add(self, chunk, at, left, right):
        part = sum(left[a] * right[a] for a in range(3))
        if self.refs is not None:
            self.refs[at] = self.refs[at] + part
            return
        held = self.parts[at]
        slot = chunk % 4
        held[slot] = part if held[slot] is None else held[slot] + part

    def get(self, at):
        if self.refs is not None:
            total = self.refs[at]
        else:
            held = self.parts[at]
            total = (held[0] + held[1]) + (held[2] + held[3])
        return jnp.broadcast_to(jnp.sum(total, axis=1, keepdims=True), (ROWS, 128))


def chunk_parts(piece, chunk, me, n_row, n_col, part):
    half = n_row // 2
    o = chunk // half
    u = chunk % half
    even = piece[me ^ ((2 * u) * n_col + o), part]
    odd = piece[me ^ ((2 * u + 1) * n_col + o), part]
    low = low_half((4, 128))
    first = jnp.where(low, even, pltpu.roll(odd, 64, 1))
    second = jnp.where(low, pltpu.roll(even, 64, 1), odd)
    return first, second


PAIRS = [(i, j) for i in range(ITERS) for j in range(i + 1, ITERS)]


def place_of(j):
    lane = lax.broadcasted_iota(jnp.int32, (ROWS, 128), 1)
    return lane == lax.broadcasted_iota(jnp.int32, (ROWS, 128), 0) * (ITERS + 1) + j


def row_sum(acc):
    return jnp.sum(acc, axis=1, keepdims=True)


def lines_of(chunk):
    if isinstance(chunk, int):
        return pl.ds(chunk * 128, 128)
    return pl.ds(pl.multiple_of(chunk * 128, 128), 128)


def write_columns(cols, y, chunk, vec):
    ys = [y[a : a + 1] for a in range(3)]
    f = [vec[a] for a in range(3)]
    g = ys[0] * f[0] + ys[1] * f[1] + ys[2] * f[2]
    groups = f + [g]
    groups += [ys[p] * f[v] for p in range(3) for v in range(3)]
    groups += [ys[a] * g for a in range(3)]
    full = jnp.concatenate(groups, axis=0)
    high = full.astype(BF16)
    low = (full - high.astype(F32)).astype(BF16)
    at = lines_of(chunk)
    cols[0:128, at] = high
    cols[128:256, at] = low


def apply_rows(cols, kernels, targets, own, scale):
    total = cols.shape[1]
    step = min(total, 2048)

    def turn(i, acc):
        at = pl.ds(pl.multiple_of(i * step, step), step)
        return acc + jnp.dot(cols[:, at], kernels[at, :], preferred_element_type=F32)

    if total == step:
        prod = jnp.dot(cols[...], kernels[...], preferred_element_type=F32)
    else:
        prod = lax.fori_loop(0, total // step, turn, jnp.zeros((256, 256), F32))
    both = prod[:128, :128] + (prod[128:, :128] + prod[:128, 128:])
    two = pltpu.roll(both, 64, 1)

    def group(k):
        return two[8 * k : 8 * k + 8]

    x = [targets[a : a + 1] for a in range(3)]
    images = []
    along = x[0] * group(0) + x[1] * group(1) + x[2] * group(2) - group(3)
    for a in range(3):
        cross = sum(x[b] * group(4 + 3 * a + b) for b in range(3))
        image = both[8 * a : 8 * a + 8] + x[a] * along - cross + group(13 + a)
        images.append((image + targets[3:4] * own[a]) * scale)
    return images


def write_piece(images, out):
    rows = []
    for image in images:
        top, bottom = image[:4], pltpu.roll(image[4:], 64, 1)
        rows.append(jnp.where(low_half((4, 128)), top, bottom))

    def put(m):
        for a in range(3):
            out[m, a] = rows[a]

    each_wide(out.shape[0], put)


def each_wide(count, put):
    if count <= 64:
        for m in range(count):
            put(m)
    else:
        pl.loop(0, count)(put)


def pack_kernel(n_col, *refs):
    sources, me = refs[:6], refs[6]
    out, tgt = refs[7:9]
    near = refs[9 : 9 + n_col]
    held, sems = refs[9 + n_col : 15 + n_col], refs[15 + n_col]
    copies = [
        pltpu.make_async_copy(src, dst, sems.at[i])
        for i, (src, dst) in enumerate(zip(sources, held))
    ]
    for copy in copies:
        copy.start()
    for copy in copies:
        copy.wait()
    velocity, points, area, self_term, index, weight = held
    rhs = velocity.shape[0]
    field = velocity[...]
    spot = points[...]
    place = [jnp.concatenate([spot[2:3], area[...]], axis=0) if a == 1 else spot[:2] for a in range(3)]
    rows = []
    for a in range(3):
        vec = field[:, a, :]
        rows.append(jnp.concatenate([vec[:4], jnp.concatenate([vec[4:], place[a]], axis=0)], axis=1))
    mine = jnp.concatenate([spot, self_term[...]], axis=0)
    mine = jnp.concatenate([mine, mine], axis=1)
    tgt[...] = jnp.concatenate([mine, mine], axis=0)

    def put(m):
        for a in range(3):
            out[m, a] = rows[a]

    each_wide(out.shape[0], put)

    row, col = me[1], me[2]
    half = index.shape[0] // 2
    low = low_half((half, 128))
    for o in range(n_col):
        to = col ^ o
        at = lines_of(to // 2)
        odd = to % 2 == 1
        at_source = index[:, at]
        at_source = (((at_source // 64) ^ row) * 64 + at_source % 64).astype(F32)
        for i, value in enumerate((at_source, weight[:, at])):
            top, bottom = value[:half], value[half:]
            lower = jnp.where(low, top, pltpu.roll(bottom, 64, 1))
            upper = jnp.where(low, pltpu.roll(top, 64, 1), bottom)
            near[o][i] = jnp.where(odd, upper, lower)


def extra_kernel(half_chunks, *refs):
    near, out = refs[:-1], refs[-1]
    low = low_half((128, 128))
    lines = lax.broadcasted_iota(jnp.int32, (128, 128), 0)
    for o, pair in enumerate(near):
        index, weight = pair[0], pair[1]

        def build(u):
            line = (lines + u * 128).astype(F32)
            total = jnp.zeros((128, 128), F32)
            for k in range(index.shape[0]):
                total = total + jnp.where(line == index[k : k + 1], weight[k : k + 1], 0.0)
            total = total + pltpu.roll(total, 64, 1)
            out[o * half_chunks + u] = jnp.where(low, total, 0.0)

        pl.loop(0, half_chunks)(build)


def first_kernel(
    n_row, n_col, piece, extra, tgt, me_ref, kernels, places, basis, norm_out, out, cols, *sums
):
    n_chunk = n_row * n_col // 2
    me = me_ref[0]
    low = low_half((128, 128))
    x = [tgt[a : a + 1] for a in range(3)]
    total = Sums(1, sums[0] if sums else None)

    def build(chunk):
        vec = [
            jnp.concatenate(chunk_parts(piece, chunk, me, n_row, n_col, a), axis=0)
            for a in range(3)
        ]
        spot = jnp.concatenate([vec[0][6:8], vec[1][6:8]], axis=0)
        spot = jnp.concatenate([spot, spot], axis=0)
        places[chunk] = spot
        for a in range(3):
            basis[chunk, a] = vec[a]
        total.add(chunk, 0, vec, vec)
        write_columns(cols, spot, chunk, vec)
        col = spot.T
        d = [x[a] - col[:, a : a + 1] for a in range(3)]
        dist = d[0] * d[0] + d[1] * d[1] + d[2] * d[2]
        root = lax.rsqrt(dist + BLOB_SQ)
        two = (col[:, 3:4] * INV_EIGHT_PI) * root * root * root
        one = (dist + 2.0 * BLOB_SQ) * two
        value = jnp.where(low, one, two) + extra[chunk]
        high = value.astype(BF16)
        at = lines_of(chunk)
        kernels[at, 0:128] = high
        kernels[at, 128:256] = (value - high.astype(F32)).astype(BF16)

    each(n_chunk, build)
    norm = jnp.sqrt(total.get(0))
    scale = 1.0 / norm
    norm_out[0] = norm
    norm_out[1] = scale
    write_piece(apply_rows(cols, kernels, tgt, basis[0], scale), out)


def middle_kernel(n_row, n_col, n_base, final, piece, *refs):
    bases, norms = refs[:n_base], refs[n_base : 2 * n_base]
    kernels, places, tgt, me_ref, basis, h_out, out, own, cols, *held = refs[2 * n_base :]
    n_chunk = n_row * n_col // 2
    me = me_ref[0]
    scales = [norm[norm.shape[0] - 1] for norm in norms]
    cross = [(i, j) for i in range(n_base) for j in range(i)]
    sums = Sums(2 * n_base + 1 + len(cross), held[0] if held else None)

    def unpack(chunk):
        vec = [
            jnp.concatenate(chunk_parts(piece, chunk, me, n_row, n_col, a), axis=0)
            for a in range(3)
        ]
        old = [[base[chunk, a] for a in range(3)] for base in bases]
        for a in range(3):
            basis[chunk, a] = vec[a]
        for j in range(n_base):
            sums.add(chunk, j, vec, old[j])
        for at, (i, j) in enumerate(cross):
            sums.add(chunk, 2 * n_base + 1 + at, old[i], old[j])

    each(n_chunk, unpack)
    gram = {}
    for at, (i, j) in enumerate(cross):
        gram[j, i] = sums.get(2 * n_base + 1 + at) * (scales[i] * scales[j])
    column = []
    for j in range(n_base):
        h = sums.get(j) * scales[j]
        for i in range(j):
            h = h - column[i] * gram[i, j]
        column.append(h)
        h_out[j] = h
    factors = [h * scale for h, scale in zip(column, scales)]

    def columns(chunk):
        old = [[base[chunk, a] for a in range(3)] for base in bases]
        vec = []
        for a in range(3):
            value = basis[chunk, a]
            for j in range(n_base):
                value = value - factors[j] * old[j][a]
            vec.append(value)
            basis[chunk, a] = value
        sums.add(chunk, n_base, vec, vec)
        write_columns(cols, places[chunk], chunk, vec)
        if final:
            for j in range(n_base):
                sums.add(chunk, n_base + 1 + j, vec, old[j])

    each(n_chunk, columns)
    norm = jnp.sqrt(sums.get(n_base))
    scale = 1.0 / norm
    h_out[n_base] = norm
    images = apply_rows(cols, kernels, tgt, basis[0], scale)
    every = [*bases, basis]
    scales = [*scales, scale]
    for j, base in enumerate(every):
        for a in range(3):
            own[j, a] = base[0, a] * scales[j]
    if not final:
        h_out[n_base + 1] = scale
        write_piece(images, out)
        return
    for j in range(n_base):
        gram[j, n_base] = sums.get(n_base + 1 + j) * (scale * scales[j])
    for at, pair in enumerate(PAIRS):
        h_out[n_base + 1 + at] = gram[pair]
    low = low_half((ROWS, 128))
    row = jnp.zeros((ROWS, 128), F32)
    for j in range(ITERS + 1):
        other = images if j == ITERS else [own[j, a] for a in range(3)]
        part = sum(images[a] * other[a] for a in range(3))
        part = row_sum(jnp.where(low, part, 0.0))
        row = row + jnp.where(place_of(j), part, 0.0)
    row = jnp.sum(row, axis=0, keepdims=True)

    def put(m):
        out[m] = row

    each_wide(out.shape[0], put)


def solve_small(hessen, start_norm, count):
    zero = jnp.zeros_like(start_norm)
    target = [start_norm] + [zero] * count
    cosines = []
    sines = []
    triangle = {}
    for k in range(count):
        column = [hessen[i, k] for i in range(k + 2)]
        for j in range(k):
            first_val = column[j]
            second_val = column[j + 1]
            column[j] = cosines[j] * first_val + sines[j] * second_val
            column[j + 1] = cosines[j] * second_val - sines[j] * first_val
        radius = jnp.sqrt(column[k] * column[k] + column[k + 1] * column[k + 1])
        cosine = column[k] / radius
        sine = column[k + 1] / radius
        cosines.append(cosine)
        sines.append(sine)
        for i in range(k):
            triangle[i, k] = column[i]
        triangle[k, k] = radius
        target[k + 1] = -sine * target[k]
        target[k] = cosine * target[k]
    coeffs = [None] * count
    for k in range(count - 1, -1, -1):
        accum = target[k]
        for i in range(k + 1, count):
            accum = accum - triangle[k, i] * coeffs[i]
        coeffs[k] = accum / triangle[k, k]
    return coeffs


def last_kernel(sums, own, *refs):
    columns = refs[: ITERS - 1]
    norm, out = refs[ITERS - 1 :]
    hessen = {}
    for k in range(ITERS - 1):
        for j in range(k + 2):
            hessen[j, k] = columns[k][j]
    gram = {(j, j): 1.0 for j in range(ITERS)}
    for at, (i, j) in enumerate(PAIRS):
        gram[i, j] = gram[j, i] = columns[-1][ITERS + at]
    row = jnp.broadcast_to(jnp.sum(sums[...], axis=0), (ROWS, 128))
    inner = [
        jnp.broadcast_to(row_sum(jnp.where(place_of(j), row, 0.0)), (ROWS, 128))
        for j in range(ITERS + 1)
    ]
    square = inner[ITERS]
    for j in range(ITERS):
        h = inner[j]
        for i in range(j):
            h = h - hessen[i, ITERS - 1] * gram[i, j]
        hessen[j, ITERS - 1] = h
    for j in range(ITERS):
        rest = -2.0 * inner[j]
        for i in range(ITERS):
            rest = rest + hessen[i, ITERS - 1] * gram[i, j]
        square = square + hessen[j, ITERS - 1] * rest
    hessen[ITERS, ITERS - 1] = jnp.sqrt(jnp.maximum(square, 0.0))
    coeffs = solve_small(hessen, norm[0], ITERS)
    for a in range(3):
        density = sum(coeffs[k] * own[k, a] for k in range(ITERS))
        out[:, a, :] = density[: out.shape[0], :64]


def call(kernel, outs, scratch, operands, scalars=(), far=(), flops=0):
    vmem = pl.BlockSpec(memory_space=pltpu.VMEM)
    smem = pl.BlockSpec(memory_space=pltpu.SMEM)
    anywhere = pl.BlockSpec(memory_space=pl.ANY)
    count = len(operands)
    specs = [smem if i in scalars else anywhere if i in far else vmem for i in range(count)]
    moved = sum(x.size * x.dtype.itemsize for x in operands)
    return pl.pallas_call(
        kernel,
        out_shape=[jax.ShapeDtypeStruct(s, t) for s, t in outs],
        in_specs=specs,
        out_specs=[vmem] * len(outs),
        scratch_shapes=scratch,
        cost_estimate=pl.CostEstimate(flops=flops, bytes_accessed=moved, transcendentals=0),
        compiler_params=pltpu.CompilerParams(vmem_limit_bytes=48 * 1024 * 1024),
    )(*operands)


def body(sizes, velocity, points, panel_area, self_term, near_index, near_weight):
    n_row, n_col = sizes[0] * sizes[1] * sizes[2], sizes[3]
    n = n_row * n_col
    n_chunk = n // 2
    total = n * 64
    row = lax.axis_index(AXES[:3])
    col = lax.axis_index("col")
    me = jnp.stack([row * n_col + col, row, col]).astype(jnp.int32)
    rhs = velocity.shape[0]

    sources = [
        velocity,
        points,
        panel_area[None],
        self_term[None],
        near_index.T,
        near_weight.T,
    ]
    message = ((n, 3, 4, 128), F32)
    wide, tgt, *near = call(
        functools.partial(pack_kernel, n_col),
        [message, ((8, 128), F32)]
        + [((2, near_index.shape[1] // 2, 128), F32)] * n_col,
        [pltpu.VMEM(x.shape, x.dtype) for x in sources] + [pltpu.SemaphoreType.DMA((6,))],
        [*sources, me],
        {6},
        range(6),
    )
    near = [
        lax.ppermute(pair, "col", xor_perm(n_col, o)) if o else pair
        for o, pair in enumerate(near)
    ]
    piece = lax.all_to_all(wide, AXES, 0, 0, tiled=True)
    (extra,) = call(
        functools.partial(extra_kernel, n_row // 2),
        [((n_chunk, 128, 128), F32)],
        [],
        near,
        flops=10**9,
    )

    vec_shape = (n_chunk, 3, ROWS, 128)
    cols = pltpu.VMEM((256, total), BF16)
    held = [] if n_chunk <= 16 else [pltpu.VMEM((8, ROWS, 128), F32)]
    kernels, places, basis, norm, wide = call(
        functools.partial(first_kernel, n_row, n_col),
        [
            ((total, 256), BF16),
            ((n_chunk, ROWS, 128), F32),
            (vec_shape, F32),
            ((2, ROWS, 128), F32),
            message,
        ],
        [cols, *held],
        [piece, extra, tgt, me],
        {3},
    )
    bases = [basis]
    columns = [norm]
    for k in range(1, ITERS):
        final = k == ITERS - 1
        piece = lax.all_to_all(wide, AXES, 0, 0, tiled=True)
        basis, column, wide, own = call(
            functools.partial(middle_kernel, n_row, n_col, k, final),
            [
                (vec_shape, F32),
                ((k + 1 + (len(PAIRS) if final else 1), ROWS, 128), F32),
                ((n, 1, 128), F32) if final else message,
                ((k + 1, 3, ROWS, 128), F32),
            ],
            [cols, *held],
            [piece, *bases, *columns, kernels, places, tgt, me],
            {2 * k + 4},
        )
        bases.append(basis)
        columns.append(column)
    sums = lax.all_to_all(wide, AXES, 0, 0, tiled=True)
    (density,) = call(
        last_kernel, [((rhs, 3, 64), F32)], [], [sums, own, *columns[1:], columns[0]]
    )
    return density


def solution(mesh):
    n_row, n_col = mesh.shape["row"], mesh.shape["col"]
    sizes = (n_row // 4, 2, 2, n_col)
    split = jax.sharding.Mesh(mesh.devices.reshape(sizes), AXES)
    return jax.shard_map(
        functools.partial(body, sizes),
        mesh=split,
        in_specs=(
            P(None, None, AXES),
            P(None, AXES),
            P(AXES),
            P(AXES),
            P(AXES[:3], "col"),
            P(AXES[:3], "col"),
        ),
        out_specs=P(None, None, AXES),
        check_vma=False,
    )
```

```python
import functools
import math

import jax
import jax.numpy as jnp
from jax import lax
from jax.experimental import pallas as pl
from jax.experimental.pallas import tpu as pltpu
from jax.sharding import PartitionSpec as P

ITERS = 3
BLOB_SQ = 0.0025
INV_EIGHT_PI = 1.0 / (8.0 * math.pi)
ROWS = 8
AXES = ("top", "mid", "core", "col")
F32 = jnp.float32
BF16 = jnp.bfloat16


def low_half(shape):
    return lax.broadcasted_iota(jnp.int32, shape, len(shape) - 1) < 64


def pack(rows):
    return jnp.concatenate([rows[..., :4, :], rows[..., 4:, :]], axis=-1)


def xor_perm(n, m):
    return [(d, d ^ m) for d in range(n)]


def spread(piece, axes, size):
    wide = jnp.broadcast_to(piece[None], (size,) + piece.shape)
    return lax.all_to_all(wide, axes, 0, 0, tiled=True)


def each(count, step):
    if count <= 16:
        for i in range(count):
            step(i)
    else:
        pl.loop(0, count)(step)


class Sums:
    def __init__(self, count, refs):
        self.refs = refs
        self.parts = [[None] * 4 for _ in range(count)]
        if refs is not None:
            for at in range(count):
                refs[at] = jnp.zeros((ROWS, 128), F32)

    def add(self, chunk, at, left, right):
        part = sum(left[a] * right[a] for a in range(3))
        if self.refs is not None:
            self.refs[at] = self.refs[at] + part
            return
        held = self.parts[at]
        slot = chunk % 4
        held[slot] = part if held[slot] is None else held[slot] + part

    def get(self, at):
        if self.refs is not None:
            total = self.refs[at]
        else:
            held = self.parts[at]
            total = (held[0] + held[1]) + (held[2] + held[3])
        return jnp.broadcast_to(jnp.sum(total, axis=1, keepdims=True), (ROWS, 128))


def chunk_parts(piece, chunk, me, n_row, n_col, part):
    half = n_row // 2
    o = chunk // half
    u = chunk % half
    even = piece[me ^ ((2 * u) * n_col + o), part]
    odd = piece[me ^ ((2 * u + 1) * n_col + o), part]
    low = low_half((4, 128))
    first = jnp.where(low, even, pltpu.roll(odd, 64, 1))
    second = jnp.where(low, pltpu.roll(even, 64, 1), odd)
    return first, second


PAIRS = [(i, j) for i in range(ITERS) for j in range(i + 1, ITERS)]


def place_of(j):
    lane = lax.broadcasted_iota(jnp.int32, (ROWS, 128), 1)
    return lane == lax.broadcasted_iota(jnp.int32, (ROWS, 128), 0) * (ITERS + 1) + j


def row_sum(acc):
    return jnp.sum(acc, axis=1, keepdims=True)


def lines_of(chunk):
    if isinstance(chunk, int):
        return pl.ds(chunk * 128, 128)
    return pl.ds(pl.multiple_of(chunk * 128, 128), 128)


def write_columns(cols, y, chunk, vec):
    ys = [y[a : a + 1] for a in range(3)]
    f = [vec[a] for a in range(3)]
    g = ys[0] * f[0] + ys[1] * f[1] + ys[2] * f[2]
    groups = f + [g]
    groups += [ys[p] * f[v] for p in range(3) for v in range(3)]
    groups += [ys[a] * g for a in range(3)]
    full = jnp.concatenate(groups, axis=0)
    high = full.astype(BF16)
    low = (full - high.astype(F32)).astype(BF16)
    at = lines_of(chunk)
    cols[0:128, at] = high
    cols[128:256, at] = low


def contract(left, right):
    dims = (((1,), (1,)), ((), ()))
    return lax.dot_general(left, right, dims, preferred_element_type=F32)


def apply_rows(cols, kernels, targets, own, scale):
    total = cols.shape[1]
    step = min(total, 2048)

    def turn(i, acc):
        at = pl.ds(pl.multiple_of(i * step, step), step)
        return acc + contract(cols[:, at], kernels[:, at])

    if total == step:
        prod = contract(cols[...], kernels[...])
    else:
        prod = lax.fori_loop(0, total // step, turn, jnp.zeros((256, 256), F32))
    both = prod[:128, :128] + (prod[128:, :128] + prod[:128, 128:])
    two = pltpu.roll(both, 64, 1)

    def group(k):
        return two[8 * k : 8 * k + 8]

    x = [targets[a : a + 1] for a in range(3)]
    images = []
    along = x[0] * group(0) + x[1] * group(1) + x[2] * group(2) - group(3)
    for a in range(3):
        cross = sum(x[b] * group(4 + 3 * a + b) for b in range(3))
        image = both[8 * a : 8 * a + 8] + x[a] * along - cross + group(13 + a)
        images.append((image + targets[3:4] * own[a]) * scale)
    return images


def write_piece(images, out):
    rows = []
    for image in images:
        top, bottom = image[:4], pltpu.roll(image[4:], 64, 1)
        rows.append(jnp.where(low_half((4, 128)), top, bottom))

    def put(m):
        for a in range(3):
            out[m, a] = rows[a]

    each_wide(out.shape[0], put)


def each_wide(count, put):
    if count <= 64:
        for m in range(count):
            put(m)
    else:
        pl.loop(0, count)(put)


def pack_kernel(n_col, *refs):
    velocity, points, area, self_term, index, weight, me, out, tgt = refs[:9]
    near = refs[9:]
    rhs = velocity.shape[0]
    field = velocity[...]
    spot = points[...]
    place = [jnp.concatenate([spot[2:3], area[...]], axis=0) if a == 1 else spot[:2] for a in range(3)]
    rows = []
    for a in range(3):
        vec = field[:, a, :]
        rows.append(jnp.concatenate([vec[:4], jnp.concatenate([vec[4:], place[a]], axis=0)], axis=1))
    mine = jnp.concatenate([spot, self_term[...]], axis=0)
    mine = jnp.concatenate([mine, mine], axis=1)
    tgt[...] = jnp.concatenate([mine, mine], axis=0)

    def put(m):
        for a in range(3):
            out[m, a] = rows[a]

    each_wide(out.shape[0], put)

    row, col = me[1], me[2]
    half = index.shape[0] // 2
    low = low_half((half, 128))
    for o in range(n_col):
        to = col ^ o
        at = lines_of(to // 2)
        odd = to % 2 == 1
        at_source = index[:, at]
        at_source = (((at_source // 64) ^ row) * 64 + at_source % 64).astype(F32)
        for i, value in enumerate((at_source, weight[:, at])):
            top, bottom = value[:half], value[half:]
            lower = jnp.where(low, top, pltpu.roll(bottom, 64, 1))
            upper = jnp.where(low, pltpu.roll(top, 64, 1), bottom)
            near[o][i] = jnp.where(odd, upper, lower)


def extra_kernel(half_chunks, *refs):
    near, out = refs[:-1], refs[-1]
    lines = lax.broadcasted_iota(jnp.int32, (128, 128), 0)
    for o, pair in enumerate(near):
        index, weight = pair[0], pair[1]

        def build(u):
            line = (lines + u * 128).astype(F32)
            total = jnp.zeros((128, 128), F32)
            for k in range(index.shape[0]):
                total = total + jnp.where(line == index[k : k + 1], weight[k : k + 1], 0.0)
            turned = total.T
            out[o * half_chunks + u] = turned[:64] + turned[64:]

        pl.loop(0, half_chunks)(build)


def first_kernel(
    n_row, n_col, piece, extra, tgt, me_ref, kernels, places, basis, norm_out, out, cols, *sums
):
    n_chunk = n_row * n_col // 2
    me = me_ref[0]
    total = Sums(1, sums[0] if sums else None)

    def unpack(chunk):
        vec = [
            jnp.concatenate(chunk_parts(piece, chunk, me, n_row, n_col, a), axis=0)
            for a in range(3)
        ]
        spot = jnp.concatenate([vec[0][6:8], vec[1][6:8]], axis=0)
        spot = jnp.concatenate([spot, spot], axis=0)
        places[chunk] = spot
        for a in range(3):
            basis[chunk, a] = vec[a]
        total.add(chunk, 0, vec, vec)
        write_columns(cols, spot, chunk, vec)

    each(n_chunk, unpack)
    turned = tgt[...].T
    x = [jnp.broadcast_to(turned[:64, a : a + 1], (64, 128)) for a in range(3)]

    def build(chunk):
        y = places[chunk]
        d = [x[a] - y[a : a + 1] for a in range(3)]
        dist = d[0] * d[0] + d[1] * d[1] + d[2] * d[2]
        root = lax.rsqrt(dist + BLOB_SQ)
        two = (y[3:4] * INV_EIGHT_PI) * root * root * root
        one = (dist + 2.0 * BLOB_SQ) * two + extra[chunk]
        value = jnp.concatenate([one, two], axis=0)
        high = value.astype(BF16)
        at = lines_of(chunk)
        kernels[0:128, at] = high
        kernels[128:256, at] = (value - high.astype(F32)).astype(BF16)

    each(n_chunk, build)
    norm = jnp.sqrt(total.get(0))
    scale = 1.0 / norm
    norm_out[0] = norm
    norm_out[1] = scale
    write_piece(apply_rows(cols, kernels, tgt, basis[0], scale), out)


def middle_kernel(n_row, n_col, n_base, final, piece, *refs):
    bases, norms = refs[:n_base], refs[n_base : 2 * n_base]
    kernels, places, tgt, me_ref, basis, h_out, out, own, cols, *held = refs[2 * n_base :]
    n_chunk = n_row * n_col // 2
    me = me_ref[0]
    scales = [norm[norm.shape[0] - 1] for norm in norms]
    cross = [(i, j) for i in range(n_base) for j in range(i)]
    sums = Sums(2 * n_base + 1 + len(cross), held[0] if held else None)

    def unpack(chunk):
        vec = [
            jnp.concatenate(chunk_parts(piece, chunk, me, n_row, n_col, a), axis=0)
            for a in range(3)
        ]
        old = [[base[chunk, a] for a in range(3)] for base in bases]
        for a in range(3):
            basis[chunk, a] = vec[a]
        for j in range(n_base):
            sums.add(chunk, j, vec, old[j])
        for at, (i, j) in enumerate(cross):
            sums.add(chunk, 2 * n_base + 1 + at, old[i], old[j])

    each(n_chunk, unpack)
    gram = {}
    for at, (i, j) in enumerate(cross):
        gram[j, i] = sums.get(2 * n_base + 1 + at) * (scales[i] * scales[j])
    column = []
    for j in range(n_base):
        h = sums.get(j) * scales[j]
        for i in range(j):
            h = h - column[i] * gram[i, j]
        column.append(h)
        h_out[j] = h
    factors = [h * scale for h, scale in zip(column, scales)]

    def columns(chunk):
        old = [[base[chunk, a] for a in range(3)] for base in bases]
        vec = []
        for a in range(3):
            value = basis[chunk, a]
            for j in range(n_base):
                value = value - factors[j] * old[j][a]
            vec.append(value)
            basis[chunk, a] = value
        sums.add(chunk, n_base, vec, vec)
        write_columns(cols, places[chunk], chunk, vec)
        if final:
            for j in range(n_base):
                sums.add(chunk, n_base + 1 + j, vec, old[j])

    each(n_chunk, columns)
    norm = jnp.sqrt(sums.get(n_base))
    scale = 1.0 / norm
    h_out[n_base] = norm
    images = apply_rows(cols, kernels, tgt, basis[0], scale)
    every = [*bases, basis]
    scales = [*scales, scale]
    for j, base in enumerate(every):
        for a in range(3):
            own[j, a] = base[0, a] * scales[j]
    if not final:
        h_out[n_base + 1] = scale
        write_piece(images, out)
        return
    for j in range(n_base):
        gram[j, n_base] = sums.get(n_base + 1 + j) * (scale * scales[j])
    for at, pair in enumerate(PAIRS):
        h_out[n_base + 1 + at] = gram[pair]
    low = low_half((ROWS, 128))
    row = jnp.zeros((ROWS, 128), F32)
    for j in range(ITERS + 1):
        other = images if j == ITERS else [own[j, a] for a in range(3)]
        part = sum(images[a] * other[a] for a in range(3))
        part = row_sum(jnp.where(low, part, 0.0))
        row = row + jnp.where(place_of(j), part, 0.0)
    row = jnp.sum(row, axis=0, keepdims=True)

    def put(m):
        out[m] = row

    each_wide(out.shape[0], put)


def solve_small(hessen, start_norm, count):
    zero = jnp.zeros_like(start_norm)
    target = [start_norm] + [zero] * count
    cosines = []
    sines = []
    triangle = {}
    for k in range(count):
        column = [hessen[i, k] for i in range(k + 2)]
        for j in range(k):
            first_val = column[j]
            second_val = column[j + 1]
            column[j] = cosines[j] * first_val + sines[j] * second_val
            column[j + 1] = cosines[j] * second_val - sines[j] * first_val
        radius = jnp.sqrt(column[k] * column[k] + column[k + 1] * column[k + 1])
        cosine = column[k] / radius
        sine = column[k + 1] / radius
        cosines.append(cosine)
        sines.append(sine)
        for i in range(k):
            triangle[i, k] = column[i]
        triangle[k, k] = radius
        target[k + 1] = -sine * target[k]
        target[k] = cosine * target[k]
    coeffs = [None] * count
    for k in range(count - 1, -1, -1):
        accum = target[k]
        for i in range(k + 1, count):
            accum = accum - triangle[k, i] * coeffs[i]
        coeffs[k] = accum / triangle[k, k]
    return coeffs


def last_kernel(sums, own, *refs):
    columns = refs[: ITERS - 1]
    norm, out = refs[ITERS - 1 :]
    hessen = {}
    for k in range(ITERS - 1):
        for j in range(k + 2):
            hessen[j, k] = columns[k][j]
    gram = {(j, j): 1.0 for j in range(ITERS)}
    for at, (i, j) in enumerate(PAIRS):
        gram[i, j] = gram[j, i] = columns[-1][ITERS + at]
    row = jnp.broadcast_to(jnp.sum(sums[...], axis=0), (ROWS, 128))
    inner = [
        jnp.broadcast_to(row_sum(jnp.where(place_of(j), row, 0.0)), (ROWS, 128))
        for j in range(ITERS + 1)
    ]
    square = inner[ITERS]
    for j in range(ITERS):
        h = inner[j]
        for i in range(j):
            h = h - hessen[i, ITERS - 1] * gram[i, j]
        hessen[j, ITERS - 1] = h
    for j in range(ITERS):
        rest = -2.0 * inner[j]
        for i in range(ITERS):
            rest = rest + hessen[i, ITERS - 1] * gram[i, j]
        square = square + hessen[j, ITERS - 1] * rest
    hessen[ITERS, ITERS - 1] = jnp.sqrt(jnp.maximum(square, 0.0))
    coeffs = solve_small(hessen, norm[0], ITERS)
    for a in range(3):
        density = sum(coeffs[k] * own[k, a] for k in range(ITERS))
        out[:, a, :] = density[: out.shape[0], :64]


def call(kernel, outs, scratch, operands, scalars=(), flops=0):
    vmem = pl.BlockSpec(memory_space=pltpu.VMEM)
    smem = pl.BlockSpec(memory_space=pltpu.SMEM)
    count = len(operands)
    specs = [smem if i in scalars else vmem for i in range(count)]
    moved = sum(x.size * x.dtype.itemsize for x in operands)
    return pl.pallas_call(
        kernel,
        out_shape=[jax.ShapeDtypeStruct(s, t) for s, t in outs],
        in_specs=specs,
        out_specs=[vmem] * len(outs),
        scratch_shapes=scratch,
        cost_estimate=pl.CostEstimate(flops=flops, bytes_accessed=moved, transcendentals=0),
        compiler_params=pltpu.CompilerParams(vmem_limit_bytes=48 * 1024 * 1024),
    )(*operands)


def body(sizes, velocity, points, panel_area, self_term, near_index, near_weight):
    n_row, n_col = sizes[0] * sizes[1] * sizes[2], sizes[3]
    n = n_row * n_col
    n_chunk = n // 2
    total = n * 64
    row = lax.axis_index(AXES[:3])
    col = lax.axis_index("col")
    me = jnp.stack([row * n_col + col, row, col]).astype(jnp.int32)
    rhs = velocity.shape[0]

    sources = [
        velocity,
        points,
        panel_area[None],
        self_term[None],
        near_index.T,
        near_weight.T,
    ]
    message = ((n, 3, 4, 128), F32)
    wide, tgt, *near = call(
        functools.partial(pack_kernel, n_col),
        [message, ((8, 128), F32)]
        + [((2, near_index.shape[1] // 2, 128), F32)] * n_col,
        [],
        [*sources, me],
        {6},
    )
    near = [
        lax.ppermute(pair, "col", xor_perm(n_col, o)) if o else pair
        for o, pair in enumerate(near)
    ]
    piece = lax.all_to_all(wide, AXES, 0, 0, tiled=True)
    (extra,) = call(
        functools.partial(extra_kernel, n_row // 2),
        [((n_chunk, 64, 128), F32)],
        [],
        near,
        flops=10**9,
    )

    vec_shape = (n_chunk, 3, ROWS, 128)
    cols = pltpu.VMEM((256, total), BF16)
    held = [] if n_chunk <= 16 else [pltpu.VMEM((8, ROWS, 128), F32)]
    kernels, places, basis, norm, wide = call(
        functools.partial(first_kernel, n_row, n_col),
        [
            ((256, total), BF16),
            ((n_chunk, ROWS, 128), F32),
            (vec_shape, F32),
            ((2, ROWS, 128), F32),
            message,
        ],
        [cols, *held],
        [piece, extra, tgt, me],
        {3},
    )
    bases = [basis]
    columns = [norm]
    for k in range(1, ITERS):
        final = k == ITERS - 1
        piece = lax.all_to_all(wide, AXES, 0, 0, tiled=True)
        basis, column, wide, own = call(
            functools.partial(middle_kernel, n_row, n_col, k, final),
            [
                (vec_shape, F32),
                ((k + 1 + (len(PAIRS) if final else 1), ROWS, 128), F32),
                ((n, 1, 128), F32) if final else message,
                ((k + 1, 3, ROWS, 128), F32),
            ],
            [cols, *held],
            [piece, *bases, *columns, kernels, places, tgt, me],
            {2 * k + 4},
        )
        bases.append(basis)
        columns.append(column)
    sums = lax.all_to_all(wide, AXES, 0, 0, tiled=True)
    (density,) = call(
        last_kernel, [((rhs, 3, 64), F32)], [], [sums, own, *columns[1:], columns[0]]
    )
    return density


def solution(mesh):
    n_row, n_col = mesh.shape["row"], mesh.shape["col"]
    sizes = (n_row // 4, 2, 2, n_col)
    split = jax.sharding.Mesh(mesh.devices.reshape(sizes), AXES)
    return jax.shard_map(
        functools.partial(body, sizes),
        mesh=split,
        in_specs=(
            P(None, None, AXES),
            P(None, AXES),
            P(AXES),
            P(AXES),
            P(AXES[:3], "col"),
            P(AXES[:3], "col"),
        ),
        out_specs=P(None, None, AXES),
        check_vma=False,
    )
```

```python
import functools
import math

import jax
import jax.numpy as jnp
from jax import lax
from jax.experimental import pallas as pl
from jax.experimental.pallas import tpu as pltpu
from jax.sharding import PartitionSpec as P

ITERS = 3
BLOB_SQ = 0.0025
INV_EIGHT_PI = 1.0 / (8.0 * math.pi)
ROWS = 8
HALF = 3
FIRST, LATER = 11, 10
ORDER = (0, 2, 1)
AXES = ("top", "mid", "core", "col")
F32 = jnp.float32
BF16 = jnp.bfloat16


def low_half(shape):
    return lax.broadcasted_iota(jnp.int32, shape, len(shape) - 1) < 64


def xor_perm(n, m):
    return [(d, d ^ m) for d in range(n)]


def spread(rows, n):
    wide = rows.reshape(n, -1, 1, 128)
    return lax.all_to_all(wide, AXES, 0, 0, tiled=True).reshape(rows.shape)


def each(count, step):
    if count <= 16:
        for i in range(count):
            step(i)
    else:
        pl.loop(0, count)(step)


class Sums:
    def __init__(self, count, refs):
        self.refs = refs
        self.parts = [[None] * 4 for _ in range(count)]
        if refs is not None:
            for at in range(count):
                refs[at] = jnp.zeros((ROWS, 128), F32)

    def add(self, chunk, at, left, right):
        part = sum(left[a] * right[a] for a in range(3))
        if self.refs is not None:
            self.refs[at] = self.refs[at] + part
            return
        held = self.parts[at]
        slot = chunk % 4
        held[slot] = part if held[slot] is None else held[slot] + part

    def get(self, at):
        if self.refs is not None:
            total = self.refs[at]
        else:
            held = self.parts[at]
            total = (held[0] + held[1]) + (held[2] + held[3])
        return jnp.broadcast_to(jnp.sum(total, axis=1, keepdims=True), (ROWS, 128))


def chunk_parts(piece, chunk, me, n_row, n_col, size, at, count):
    half = n_row // 2
    o = chunk // half
    u = chunk % half
    even = piece[pl.ds((me ^ ((2 * u) * n_col + o)) * size + at, count)]
    odd = piece[pl.ds((me ^ ((2 * u + 1) * n_col + o)) * size + at, count)]
    low = low_half((count, 128))
    first = jnp.where(low, even, pltpu.roll(odd, 64, 1))
    second = jnp.where(low, pltpu.roll(even, 64, 1), odd)
    return jnp.concatenate([first, second], axis=0)


PAIRS = [(i, j) for i in range(ITERS) for j in range(i + 1, ITERS)]


def place_of(j):
    lane = lax.broadcasted_iota(jnp.int32, (ROWS, 128), 1)
    return lane == lax.broadcasted_iota(jnp.int32, (ROWS, 128), 0) * (ITERS + 1) + j


def row_sum(acc):
    return jnp.sum(acc, axis=1, keepdims=True)


def lines_of(chunk):
    if isinstance(chunk, int):
        return pl.ds(chunk * 128, 128)
    return pl.ds(pl.multiple_of(chunk * 128, 128), 128)


def write_columns(cols, y, chunk, vec):
    ys = [y[a : a + 1] for a in ORDER]
    f = [vec[a] for a in range(3)]
    g = ys[0] * f[0] + ys[1] * f[1] + ys[2] * f[2]
    groups = f + [g]
    groups += [ys[p] * f[v] for p in range(3) for v in range(3)]
    groups += [ys[a] * g for a in range(3)]
    full = jnp.concatenate(groups, axis=0)
    high = full.astype(BF16)
    low = (full - high.astype(F32)).astype(BF16)
    at = lines_of(chunk)
    cols[0:128, at] = high
    cols[128:256, at] = low


def contract(left, right):
    dims = (((1,), (1,)), ((), ()))
    return lax.dot_general(left, right, dims, preferred_element_type=F32)


def apply_rows(cols, kernels, targets, own, scale):
    total = cols.shape[1]
    step = min(total, 2048)

    def turn(i, acc):
        at = pl.ds(pl.multiple_of(i * step, step), step)
        return acc + contract(cols[:, at], kernels[:, at])

    if total == step:
        prod = contract(cols[...], kernels[...])
    else:
        prod = lax.fori_loop(0, total // step, turn, jnp.zeros((256, 256), F32))
    both = prod[:128, :128] + (prod[128:, :128] + prod[:128, 128:])
    two = pltpu.roll(both, 64, 1)

    def group(k):
        return two[8 * k : 8 * k + 8]

    x = [targets[a : a + 1] for a in range(3)]
    images = []
    along = x[0] * group(0) + x[1] * group(1) + x[2] * group(2) - group(3)
    for a in range(3):
        cross = sum(x[b] * group(4 + 3 * a + b) for b in range(3))
        image = both[8 * a : 8 * a + 8] + x[a] * along - cross + group(13 + a)
        images.append((image + targets[3:4] * own[a]) * scale)
    return images


def write_piece(images, out):
    rows = []
    for image in images:
        top, bottom = image[:4], pltpu.roll(image[4:], 64, 1)
        rows.append(jnp.where(low_half((4, 128)), top, bottom))

    def put(m):
        for a in range(3):
            out[pl.ds(m * LATER + HALF * a, 4)] = rows[a]

    each_wide(out.shape[0] // LATER, put)


def each_wide(count, put):
    if count <= 64:
        for m in range(count):
            put(m)
    else:
        pl.loop(0, count)(put)


def pack_kernel(n_col, *refs):
    velocity, points, area, self_term, index, weight, me, out, tgt = refs[:9]
    near = refs[9:]
    field = velocity[...]
    spot = points[...]
    rows = []
    for a in range(3):
        vec = field[:, a, :]
        rows.append(jnp.concatenate([vec[:HALF], vec[HALF:]], axis=1))
    mine = jnp.concatenate([spot, self_term[...]], axis=0)
    mine = jnp.concatenate([mine, mine], axis=1)
    tgt[...] = jnp.concatenate([mine, mine], axis=0)
    left = jnp.concatenate([spot[0:1], spot[2:3]], axis=0)
    right = jnp.concatenate([spot[1:2], area[...]], axis=0)
    rows.append(jnp.concatenate([left, right], axis=1))
    message = jnp.concatenate(rows, axis=0)

    def put(m):
        out[pl.ds(m * FIRST, FIRST)] = message

    each_wide(out.shape[0] // FIRST, put)

    row, col = me[1], me[2]
    half = index.shape[0] // 2
    low = low_half((half, 128))
    for o in range(n_col):
        to = col ^ o
        at = lines_of(to // 2)
        odd = to % 2 == 1
        at_source = index[:, at]
        at_source = (((at_source // 64) ^ row) * 64 + at_source % 64).astype(F32)
        for i, value in enumerate((at_source, weight[:, at])):
            top, bottom = value[:half], value[half:]
            lower = jnp.where(low, top, pltpu.roll(bottom, 64, 1))
            upper = jnp.where(low, pltpu.roll(top, 64, 1), bottom)
            near[o][i] = jnp.where(odd, upper, lower)


def extra_kernel(half_chunks, *refs):
    near, out = refs[:-1], refs[-1]
    lines = lax.broadcasted_iota(jnp.int32, (128, 128), 0)
    for o, pair in enumerate(near):
        index, weight = pair[0], pair[1]

        def build(u):
            line = (lines + u * 128).astype(F32)
            total = jnp.zeros((128, 128), F32)
            for k in range(index.shape[0]):
                total = total + jnp.where(line == index[k : k + 1], weight[k : k + 1], 0.0)
            turned = total.T
            out[o * half_chunks + u] = turned[:64] + turned[64:]

        pl.loop(0, half_chunks)(build)


def first_kernel(
    n_row, n_col, piece, extra, tgt, me_ref, kernels, places, basis, norm_out, out, cols, *sums
):
    n_chunk = n_row * n_col // 2
    me = me_ref[0]
    total = Sums(1, sums[0] if sums else None)

    def unpack(chunk):
        vec = [
            chunk_parts(piece, chunk, me, n_row, n_col, FIRST, HALF * a, 4)
            for a in range(3)
        ]
        spot = chunk_parts(piece, chunk, me, n_row, n_col, FIRST, 3 * HALF, 2)
        places[chunk] = spot
        for a in range(3):
            basis[chunk, a] = vec[a]
        total.add(chunk, 0, vec, vec)
        write_columns(cols, spot, chunk, vec)

    each(n_chunk, unpack)
    turned = tgt[...].T
    x = [jnp.broadcast_to(turned[:64, a : a + 1], (64, 128)) for a in range(3)]

    def build(chunk):
        y = places[chunk]
        d = [x[a] - y[k : k + 1] for a, k in enumerate(ORDER)]
        dist = d[0] * d[0] + d[1] * d[1] + d[2] * d[2]
        root = lax.rsqrt(dist + BLOB_SQ)
        two = (y[3:4] * INV_EIGHT_PI) * root * root * root
        one = (dist + 2.0 * BLOB_SQ) * two + extra[chunk]
        value = jnp.concatenate([one, two], axis=0)
        high = value.astype(BF16)
        at = lines_of(chunk)
        kernels[0:128, at] = high
        kernels[128:256, at] = (value - high.astype(F32)).astype(BF16)

    each(n_chunk, build)
    norm = jnp.sqrt(total.get(0))
    scale = 1.0 / norm
    norm_out[0] = norm
    norm_out[1] = scale
    write_piece(apply_rows(cols, kernels, tgt, basis[0], scale), out)


def middle_kernel(n_row, n_col, n_base, final, piece, *refs):
    bases, norms = refs[:n_base], refs[n_base : 2 * n_base]
    kernels, places, tgt, me_ref, basis, h_out, out, own, cols, *held = refs[2 * n_base :]
    n_chunk = n_row * n_col // 2
    me = me_ref[0]
    scales = [norm[norm.shape[0] - 1] for norm in norms]
    cross = [(i, j) for i in range(n_base) for j in range(i)]
    sums = Sums(2 * n_base + 1 + len(cross), held[0] if held else None)

    def unpack(chunk):
        vec = [
            chunk_parts(piece, chunk, me, n_row, n_col, LATER, HALF * a, 4)
            for a in range(3)
        ]
        old = [[base[chunk, a] for a in range(3)] for base in bases]
        for a in range(3):
            basis[chunk, a] = vec[a]
        for j in range(n_base):
            sums.add(chunk, j, vec, old[j])
        for at, (i, j) in enumerate(cross):
            sums.add(chunk, 2 * n_base + 1 + at, old[i], old[j])

    each(n_chunk, unpack)
    gram = {}
    for at, (i, j) in enumerate(cross):
        gram[j, i] = sums.get(2 * n_base + 1 + at) * (scales[i] * scales[j])
    column = []
    for j in range(n_base):
        h = sums.get(j) * scales[j]
        for i in range(j):
            h = h - column[i] * gram[i, j]
        column.append(h)
        h_out[j] = h
    factors = [h * scale for h, scale in zip(column, scales)]

    def columns(chunk):
        old = [[base[chunk, a] for a in range(3)] for base in bases]
        vec = []
        for a in range(3):
            value = basis[chunk, a]
            for j in range(n_base):
                value = value - factors[j] * old[j][a]
            vec.append(value)
            basis[chunk, a] = value
        sums.add(chunk, n_base, vec, vec)
        write_columns(cols, places[chunk], chunk, vec)
        if final:
            for j in range(n_base):
                sums.add(chunk, n_base + 1 + j, vec, old[j])

    each(n_chunk, columns)
    norm = jnp.sqrt(sums.get(n_base))
    scale = 1.0 / norm
    h_out[n_base] = norm
    images = apply_rows(cols, kernels, tgt, basis[0], scale)
    every = [*bases, basis]
    scales = [*scales, scale]
    for j, base in enumerate(every):
        for a in range(3):
            own[j, a] = base[0, a] * scales[j]
    if not final:
        h_out[n_base + 1] = scale
        write_piece(images, out)
        return
    for j in range(n_base):
        gram[j, n_base] = sums.get(n_base + 1 + j) * (scale * scales[j])
    for at, pair in enumerate(PAIRS):
        h_out[n_base + 1 + at] = gram[pair]
    low = low_half((ROWS, 128))
    row = jnp.zeros((ROWS, 128), F32)
    for j in range(ITERS + 1):
        other = images if j == ITERS else [own[j, a] for a in range(3)]
        part = sum(images[a] * other[a] for a in range(3))
        part = row_sum(jnp.where(low, part, 0.0))
        row = row + jnp.where(place_of(j), part, 0.0)
    row = jnp.sum(row, axis=0, keepdims=True)

    def put(m):
        out[pl.ds(m, 1)] = row

    each_wide(out.shape[0], put)


def solve_small(hessen, start_norm, count):
    zero = jnp.zeros_like(start_norm)
    target = [start_norm] + [zero] * count
    cosines = []
    sines = []
    triangle = {}
    for k in range(count):
        column = [hessen[i, k] for i in range(k + 2)]
        for j in range(k):
            first_val = column[j]
            second_val = column[j + 1]
            column[j] = cosines[j] * first_val + sines[j] * second_val
            column[j + 1] = cosines[j] * second_val - sines[j] * first_val
        radius = jnp.sqrt(column[k] * column[k] + column[k + 1] * column[k + 1])
        cosine = column[k] / radius
        sine = column[k + 1] / radius
        cosines.append(cosine)
        sines.append(sine)
        for i in range(k):
            triangle[i, k] = column[i]
        triangle[k, k] = radius
        target[k + 1] = -sine * target[k]
        target[k] = cosine * target[k]
    coeffs = [None] * count
    for k in range(count - 1, -1, -1):
        accum = target[k]
        for i in range(k + 1, count):
            accum = accum - triangle[k, i] * coeffs[i]
        coeffs[k] = accum / triangle[k, k]
    return coeffs


def last_kernel(sums, own, *refs):
    columns = refs[: ITERS - 1]
    norm, out = refs[ITERS - 1 :]
    hessen = {}
    for k in range(ITERS - 1):
        for j in range(k + 2):
            hessen[j, k] = columns[k][j]
    gram = {(j, j): 1.0 for j in range(ITERS)}
    for at, (i, j) in enumerate(PAIRS):
        gram[i, j] = gram[j, i] = columns[-1][ITERS + at]
    row = jnp.broadcast_to(jnp.sum(sums[...], axis=0, keepdims=True), (ROWS, 128))
    inner = [
        jnp.broadcast_to(row_sum(jnp.where(place_of(j), row, 0.0)), (ROWS, 128))
        for j in range(ITERS + 1)
    ]
    square = inner[ITERS]
    for j in range(ITERS):
        h = inner[j]
        for i in range(j):
            h = h - hessen[i, ITERS - 1] * gram[i, j]
        hessen[j, ITERS - 1] = h
    for j in range(ITERS):
        rest = -2.0 * inner[j]
        for i in range(ITERS):
            rest = rest + hessen[i, ITERS - 1] * gram[i, j]
        square = square + hessen[j, ITERS - 1] * rest
    hessen[ITERS, ITERS - 1] = jnp.sqrt(jnp.maximum(square, 0.0))
    coeffs = solve_small(hessen, norm[0], ITERS)
    for a in range(3):
        density = sum(coeffs[k] * own[k, a] for k in range(ITERS))
        out[:HALF, a, :] = density[:HALF, :64]
        out[HALF:, a, :] = density[4 : 4 + HALF, :64]


def call(kernel, outs, scratch, operands, scalars=(), flops=0):
    vmem = pl.BlockSpec(memory_space=pltpu.VMEM)
    smem = pl.BlockSpec(memory_space=pltpu.SMEM)
    count = len(operands)
    specs = [smem if i in scalars else vmem for i in range(count)]
    moved = sum(x.size * x.dtype.itemsize for x in operands)
    return pl.pallas_call(
        kernel,
        out_shape=[jax.ShapeDtypeStruct(s, t) for s, t in outs],
        in_specs=specs,
        out_specs=[vmem] * len(outs),
        scratch_shapes=scratch,
        cost_estimate=pl.CostEstimate(flops=flops, bytes_accessed=moved, transcendentals=0),
        compiler_params=pltpu.CompilerParams(vmem_limit_bytes=48 * 1024 * 1024),
    )(*operands)


def body(sizes, velocity, points, panel_area, self_term, near_index, near_weight):
    n_row, n_col = sizes[0] * sizes[1] * sizes[2], sizes[3]
    n = n_row * n_col
    n_chunk = n // 2
    total = n * 64
    row = lax.axis_index(AXES[:3])
    col = lax.axis_index("col")
    me = jnp.stack([row * n_col + col, row, col]).astype(jnp.int32)
    rhs = velocity.shape[0]

    sources = [
        velocity,
        points,
        panel_area[None],
        self_term[None],
        near_index.T,
        near_weight.T,
    ]
    message = ((n * LATER, 128), F32)
    wide, tgt, *near = call(
        functools.partial(pack_kernel, n_col),
        [((n * FIRST, 128), F32), ((8, 128), F32)]
        + [((2, near_index.shape[1] // 2, 128), F32)] * n_col,
        [],
        [*sources, me],
        {6},
    )
    near = [
        lax.ppermute(pair, "col", xor_perm(n_col, o)) if o else pair
        for o, pair in enumerate(near)
    ]
    piece = spread(wide, n)
    (extra,) = call(
        functools.partial(extra_kernel, n_row // 2),
        [((n_chunk, 64, 128), F32)],
        [],
        near,
        flops=10**9,
    )

    vec_shape = (n_chunk, 3, ROWS, 128)
    cols = pltpu.VMEM((256, total), BF16)
    held = [] if n_chunk <= 16 else [pltpu.VMEM((8, ROWS, 128), F32)]
    kernels, places, basis, norm, wide = call(
        functools.partial(first_kernel, n_row, n_col),
        [
            ((256, total), BF16),
            ((n_chunk, 4, 128), F32),
            (vec_shape, F32),
            ((2, ROWS, 128), F32),
            message,
        ],
        [cols, *held],
        [piece, extra, tgt, me],
        {3},
    )
    bases = [basis]
    columns = [norm]
    for k in range(1, ITERS):
        final = k == ITERS - 1
        piece = spread(wide, n)
        basis, column, wide, own = call(
            functools.partial(middle_kernel, n_row, n_col, k, final),
            [
                (vec_shape, F32),
                ((k + 1 + (len(PAIRS) if final else 1), ROWS, 128), F32),
                ((n, 128), F32) if final else message,
                ((k + 1, 3, ROWS, 128), F32),
            ],
            [cols, *held],
            [piece, *bases, *columns, kernels, places, tgt, me],
            {2 * k + 4},
        )
        bases.append(basis)
        columns.append(column)
    sums = spread(wide, n)
    (density,) = call(
        last_kernel, [((rhs, 3, 64), F32)], [], [sums, own, *columns[1:], columns[0]]
    )
    return density


def solution(mesh):
    n_row, n_col = mesh.shape["row"], mesh.shape["col"]
    sizes = (n_row // 4, 2, 2, n_col)
    split = jax.sharding.Mesh(mesh.devices.reshape(sizes), AXES)
    return jax.shard_map(
        functools.partial(body, sizes),
        mesh=split,
        in_specs=(
            P(None, None, AXES),
            P(None, AXES),
            P(AXES),
            P(AXES),
            P(AXES[:3], "col"),
            P(AXES[:3], "col"),
        ),
        out_specs=P(None, None, AXES),
        check_vma=False,
    )
```

```python
import functools
import math

import jax
import jax.numpy as jnp
from jax import lax
from jax.experimental import pallas as pl
from jax.experimental.pallas import tpu as pltpu
from jax.sharding import PartitionSpec as P

ITERS = 3
BLOB_SQ = 0.0025
INV_EIGHT_PI = 1.0 / (8.0 * math.pi)
ROWS = 8
HALF = 3
FIRST, LATER = 11, 10
ORDER = (0, 2, 1)
AXES = ("top", "mid", "core", "col")
F32 = jnp.float32
BF16 = jnp.bfloat16


def low_half(shape):
    return lax.broadcasted_iota(jnp.int32, shape, len(shape) - 1) < 64


def xor_perm(n, m):
    return [(d, d ^ m) for d in range(n)]


def spread(rows, n):
    wide = rows.reshape(n, -1, 1, 128)
    return lax.all_to_all(wide, AXES, 0, 0, tiled=True).reshape(rows.shape)


def each(count, step):
    if count <= 16:
        for i in range(count):
            step(i)
    else:
        pl.loop(0, count)(step)


class Sums:
    def __init__(self, count, refs):
        self.refs = refs
        self.parts = [[None] * 4 for _ in range(count)]
        if refs is not None:
            for at in range(count):
                refs[at] = jnp.zeros((ROWS, 128), F32)

    def add(self, chunk, at, left, right):
        part = sum(left[a] * right[a] for a in range(3))
        if self.refs is not None:
            self.refs[at] = self.refs[at] + part
            return
        held = self.parts[at]
        slot = chunk % 4
        held[slot] = part if held[slot] is None else held[slot] + part

    def get(self, at):
        if self.refs is not None:
            total = self.refs[at]
        else:
            held = self.parts[at]
            total = (held[0] + held[1]) + (held[2] + held[3])
        return jnp.broadcast_to(jnp.sum(total, axis=1, keepdims=True), (ROWS, 128))


def chunk_parts(piece, chunk, me, n_row, n_col, size, at, count):
    half = n_row // 2
    o = chunk // half
    u = chunk % half
    even = piece[pl.ds((me ^ ((2 * u) * n_col + o)) * size + at, count)]
    odd = piece[pl.ds((me ^ ((2 * u + 1) * n_col + o)) * size + at, count)]
    low = low_half((count, 128))
    first = jnp.where(low, even, pltpu.roll(odd, 64, 1))
    second = jnp.where(low, pltpu.roll(even, 64, 1), odd)
    return jnp.concatenate([first, second], axis=0)


PAIRS = [(i, j) for i in range(ITERS) for j in range(i + 1, ITERS)]


def place_of(j):
    lane = lax.broadcasted_iota(jnp.int32, (ROWS, 128), 1)
    return lane == lax.broadcasted_iota(jnp.int32, (ROWS, 128), 0) * (ITERS + 1) + j


def row_sum(acc):
    return jnp.sum(acc, axis=1, keepdims=True)


def lines_of(chunk):
    if isinstance(chunk, int):
        return pl.ds(chunk * 128, 128)
    return pl.ds(pl.multiple_of(chunk * 128, 128), 128)


def write_columns(cols, y, chunk, vec):
    ys = [y[a : a + 1] for a in ORDER]
    f = [vec[a] for a in range(3)]
    g = ys[0] * f[0] + ys[1] * f[1] + ys[2] * f[2]
    groups = f + [g]
    groups += [ys[p] * f[v] for p in range(3) for v in range(3)]
    groups += [ys[a] * g for a in range(3)]
    full = jnp.concatenate(groups, axis=0)
    high = full.astype(BF16)
    low = (full - high.astype(F32)).astype(BF16)
    at = lines_of(chunk)
    cols[0:128, at] = high
    cols[128:256, at] = low


def contract(left, right):
    dims = (((1,), (1,)), ((), ()))
    return lax.dot_general(left, right, dims, preferred_element_type=F32)


def products(n_chunk, columns, cols, kernels):
    if n_chunk <= 16:
        group = n_chunk // 4
        prod = None
        for begin in range(0, n_chunk, group):
            for chunk in range(begin, begin + group):
                columns(chunk)
            at = pl.ds(begin * 128, group * 128)
            part = contract(cols[:, at], kernels[:, at])
            prod = part if prod is None else prod + part
        return prod
    pl.loop(0, n_chunk)(columns)

    def turn(i, acc):
        at = pl.ds(pl.multiple_of(i * 2048, 2048), 2048)
        return acc + contract(cols[:, at], kernels[:, at])

    return lax.fori_loop(0, n_chunk // 16, turn, jnp.zeros((256, 256), F32))


def image_rows(prod, targets, own, scale):
    both = prod[:128, :128] + (prod[128:, :128] + prod[:128, 128:])
    two = pltpu.roll(both, 64, 1)

    def group(k):
        return two[8 * k : 8 * k + 8]

    x = [targets[a : a + 1] for a in range(3)]
    images = []
    along = x[0] * group(0) + x[1] * group(1) + x[2] * group(2) - group(3)
    for a in range(3):
        cross = sum(x[b] * group(4 + 3 * a + b) for b in range(3))
        image = both[8 * a : 8 * a + 8] + x[a] * along - cross + group(13 + a)
        images.append((image + targets[3:4] * own[a]) * scale)
    return images


def write_piece(images, out):
    rows = []
    for image in images:
        top, bottom = image[:4], pltpu.roll(image[4:], 64, 1)
        rows.append(jnp.where(low_half((4, 128)), top, bottom))

    def put(m):
        for a in range(3):
            out[pl.ds(m * LATER + HALF * a, 4)] = rows[a]

    each_wide(out.shape[0] // LATER, put)


def each_wide(count, put):
    if count <= 64:
        for m in range(count):
            put(m)
    else:
        pl.loop(0, count)(put)


def pack_kernel(velocity, points, area, self_term, out, tgt):
    field = velocity[...]
    spot = points[...]
    rows = []
    for a in range(3):
        vec = field[:, a, :]
        rows.append(jnp.concatenate([vec[:HALF], vec[HALF:]], axis=1))
    mine = jnp.concatenate([spot, self_term[...]], axis=0)
    mine = jnp.concatenate([mine, mine], axis=1)
    tgt[...] = jnp.concatenate([mine, mine], axis=0)
    left = jnp.concatenate([spot[0:1], spot[2:3]], axis=0)
    right = jnp.concatenate([spot[1:2], area[...]], axis=0)
    rows.append(jnp.concatenate([left, right], axis=1))
    message = jnp.concatenate(rows, axis=0)

    def put(m):
        out[pl.ds(m * FIRST, FIRST)] = message

    each_wide(out.shape[0] // FIRST, put)


def extra_kernel(half_chunks, me, *refs):
    near, out = refs[:-1], refs[-1]
    row, col = me[1], me[2]
    lines = lax.broadcasted_iota(jnp.int32, (128, 128), 0).astype(F32)
    for o, lists in enumerate(near):
        count = lists.shape[0] // 2
        half = count // 2
        low = low_half((half, 128))
        odd = col % 2 == 1
        both = lists[:, lines_of(col // 2)]
        place = both[:count].astype(jnp.int32)
        place = (((place // 64) ^ row) * 64 + place % 64).astype(F32)
        packed = []
        for value in (place, both[count:]):
            top, bottom = value[:half], value[half:]
            lower = jnp.where(low, top, pltpu.roll(bottom, 64, 1))
            upper = jnp.where(low, pltpu.roll(top, 64, 1), bottom)
            packed.append(jnp.where(odd, upper, lower))
        index, weight = packed

        def build(u):
            line = lines + (u * 128.0 if isinstance(u, int) else (u * 128).astype(F32))
            total = jnp.zeros((128, 128), F32)
            for k in range(half):
                total = total + jnp.where(line == index[k : k + 1], weight[k : k + 1], 0.0)
            turned = total.T
            out[o * half_chunks + u] = turned[:64] + turned[64:]

        each(half_chunks, build)


def first_kernel(
    n_row, n_col, piece, extra, tgt, me_ref, kernels, places, basis, norm_out, out, cols, *sums
):
    n_chunk = n_row * n_col // 2
    me = me_ref[0]
    total = Sums(1, sums[0] if sums else None)

    def unpack(chunk):
        vec = [
            chunk_parts(piece, chunk, me, n_row, n_col, FIRST, HALF * a, 4)
            for a in range(3)
        ]
        spot = chunk_parts(piece, chunk, me, n_row, n_col, FIRST, 3 * HALF, 2)
        places[chunk] = spot
        for a in range(3):
            basis[chunk, a] = vec[a]
        total.add(chunk, 0, vec, vec)
        write_columns(cols, spot, chunk, vec)

    turned = tgt[...].T
    x = [jnp.broadcast_to(turned[:64, a : a + 1], (64, 128)) for a in range(3)]

    def build(chunk):
        unpack(chunk)
        y = places[chunk]
        d = [x[a] - y[k : k + 1] for a, k in enumerate(ORDER)]
        dist = d[0] * d[0] + d[1] * d[1] + d[2] * d[2]
        root = lax.rsqrt(dist + BLOB_SQ)
        two = (y[3:4] * INV_EIGHT_PI) * root * root * root
        one = (dist + 2.0 * BLOB_SQ) * two + extra[chunk]
        value = jnp.concatenate([one, two], axis=0)
        high = value.astype(BF16)
        at = lines_of(chunk)
        kernels[0:128, at] = high
        kernels[128:256, at] = (value - high.astype(F32)).astype(BF16)

    prod = products(n_chunk, build, cols, kernels)
    norm = jnp.sqrt(total.get(0))
    scale = 1.0 / norm
    norm_out[0] = norm
    norm_out[1] = scale
    write_piece(image_rows(prod, tgt, basis[0], scale), out)


def middle_kernel(n_row, n_col, n_base, final, piece, *refs):
    bases, norms = refs[:n_base], refs[n_base : 2 * n_base]
    kernels, places, tgt, me_ref, basis, h_out, out, own, cols, *held = refs[2 * n_base :]
    n_chunk = n_row * n_col // 2
    me = me_ref[0]
    scales = [norm[norm.shape[0] - 1] for norm in norms]
    cross = [(i, j) for i in range(n_base) for j in range(i)]
    sums = Sums(2 * n_base + 1 + len(cross), held[0] if held else None)

    def unpack(chunk):
        vec = [
            chunk_parts(piece, chunk, me, n_row, n_col, LATER, HALF * a, 4)
            for a in range(3)
        ]
        old = [[base[chunk, a] for a in range(3)] for base in bases]
        for a in range(3):
            basis[chunk, a] = vec[a]
        for j in range(n_base):
            sums.add(chunk, j, vec, old[j])
        for at, (i, j) in enumerate(cross):
            sums.add(chunk, 2 * n_base + 1 + at, old[i], old[j])

    each(n_chunk, unpack)
    gram = {}
    for at, (i, j) in enumerate(cross):
        gram[j, i] = sums.get(2 * n_base + 1 + at) * (scales[i] * scales[j])
    column = []
    for j in range(n_base):
        h = sums.get(j) * scales[j]
        for i in range(j):
            h = h - column[i] * gram[i, j]
        column.append(h)
        h_out[j] = h
    factors = [h * scale for h, scale in zip(column, scales)]

    def columns(chunk):
        old = [[base[chunk, a] for a in range(3)] for base in bases]
        vec = []
        for a in range(3):
            value = basis[chunk, a]
            for j in range(n_base):
                value = value - factors[j] * old[j][a]
            vec.append(value)
            basis[chunk, a] = value
        sums.add(chunk, n_base, vec, vec)
        write_columns(cols, places[chunk], chunk, vec)
        if final:
            for j in range(n_base):
                sums.add(chunk, n_base + 1 + j, vec, old[j])

    prod = products(n_chunk, columns, cols, kernels)
    norm = jnp.sqrt(sums.get(n_base))
    scale = 1.0 / norm
    h_out[n_base] = norm
    images = image_rows(prod, tgt, basis[0], scale)
    every = [*bases, basis]
    scales = [*scales, scale]
    for j, base in enumerate(every):
        for a in range(3):
            own[j, a] = base[0, a] * scales[j]
    if not final:
        h_out[n_base + 1] = scale
        write_piece(images, out)
        return
    for j in range(n_base):
        gram[j, n_base] = sums.get(n_base + 1 + j) * (scale * scales[j])
    for at, pair in enumerate(PAIRS):
        h_out[n_base + 1 + at] = gram[pair]
    low = low_half((ROWS, 128))
    row = jnp.zeros((ROWS, 128), F32)
    for j in range(ITERS + 1):
        other = images if j == ITERS else [own[j, a] for a in range(3)]
        part = sum(images[a] * other[a] for a in range(3))
        part = row_sum(jnp.where(low, part, 0.0))
        row = row + jnp.where(place_of(j), part, 0.0)
    row = jnp.sum(row, axis=0, keepdims=True)

    def put(m):
        out[pl.ds(m, 1)] = row

    each_wide(out.shape[0], put)


def solve_small(hessen, start_norm, count):
    zero = jnp.zeros_like(start_norm)
    target = [start_norm] + [zero] * count
    cosines = []
    sines = []
    triangle = {}
    for k in range(count):
        column = [hessen[i, k] for i in range(k + 2)]
        for j in range(k):
            first_val = column[j]
            second_val = column[j + 1]
            column[j] = cosines[j] * first_val + sines[j] * second_val
            column[j + 1] = cosines[j] * second_val - sines[j] * first_val
        radius = jnp.sqrt(column[k] * column[k] + column[k + 1] * column[k + 1])
        cosine = column[k] / radius
        sine = column[k + 1] / radius
        cosines.append(cosine)
        sines.append(sine)
        for i in range(k):
            triangle[i, k] = column[i]
        triangle[k, k] = radius
        target[k + 1] = -sine * target[k]
        target[k] = cosine * target[k]
    coeffs = [None] * count
    for k in range(count - 1, -1, -1):
        accum = target[k]
        for i in range(k + 1, count):
            accum = accum - triangle[k, i] * coeffs[i]
        coeffs[k] = accum / triangle[k, k]
    return coeffs


def last_kernel(sums, own, *refs):
    columns = refs[: ITERS - 1]
    norm, out = refs[ITERS - 1 :]
    hessen = {}
    for k in range(ITERS - 1):
        for j in range(k + 2):
            hessen[j, k] = columns[k][j]
    gram = {(j, j): 1.0 for j in range(ITERS)}
    for at, (i, j) in enumerate(PAIRS):
        gram[i, j] = gram[j, i] = columns[-1][ITERS + at]
    row = jnp.broadcast_to(jnp.sum(sums[...], axis=0, keepdims=True), (ROWS, 128))
    inner = [
        jnp.broadcast_to(row_sum(jnp.where(place_of(j), row, 0.0)), (ROWS, 128))
        for j in range(ITERS + 1)
    ]
    square = inner[ITERS]
    for j in range(ITERS):
        h = inner[j]
        for i in range(j):
            h = h - hessen[i, ITERS - 1] * gram[i, j]
        hessen[j, ITERS - 1] = h
    for j in range(ITERS):
        rest = -2.0 * inner[j]
        for i in range(ITERS):
            rest = rest + hessen[i, ITERS - 1] * gram[i, j]
        square = square + hessen[j, ITERS - 1] * rest
    hessen[ITERS, ITERS - 1] = jnp.sqrt(jnp.maximum(square, 0.0))
    coeffs = solve_small(hessen, norm[0], ITERS)
    for a in range(3):
        density = sum(coeffs[k] * own[k, a] for k in range(ITERS))
        out[:HALF, a, :] = density[:HALF, :64]
        out[HALF:, a, :] = density[4 : 4 + HALF, :64]


def call(kernel, outs, scratch, operands, scalars=(), resident=(), flops=0):
    vmem = pl.BlockSpec(memory_space=pltpu.VMEM)
    smem = pl.BlockSpec(memory_space=pltpu.SMEM)
    count = len(operands)
    specs = [smem if i in scalars else vmem for i in range(count)]
    moved = sum(x.size * x.dtype.itemsize for x in operands)
    return pl.pallas_call(
        kernel,
        out_shape=[
            pltpu.VMEM(s, t) if i in resident else jax.ShapeDtypeStruct(s, t)
            for i, (s, t) in enumerate(outs)
        ],
        in_specs=specs,
        out_specs=[vmem] * len(outs),
        scratch_shapes=scratch,
        cost_estimate=pl.CostEstimate(flops=flops, bytes_accessed=moved, transcendentals=0),
        compiler_params=pltpu.CompilerParams(vmem_limit_bytes=48 * 1024 * 1024),
    )(*operands)


def body(sizes, velocity, points, panel_area, self_term, near_index, near_weight):
    n_row, n_col = sizes[0] * sizes[1] * sizes[2], sizes[3]
    n = n_row * n_col
    n_chunk = n // 2
    total = n * 64
    row = lax.axis_index(AXES[:3])
    col = lax.axis_index("col")
    me = jnp.stack([row * n_col + col, row, col]).astype(jnp.int32)
    rhs = velocity.shape[0]

    message = ((n * LATER, 128), F32)
    wide, tgt = call(
        pack_kernel,
        [((n * FIRST, 128), F32), ((8, 128), F32)],
        [],
        [velocity, points, panel_area[None], self_term[None]],
        resident={0},
    )
    piece = spread(wide, n)
    lists = jnp.concatenate([near_index.T.astype(F32), near_weight.T], axis=0)
    near = [lists] + [lax.ppermute(lists, "col", xor_perm(n_col, o)) for o in range(1, n_col)]
    (extra,) = call(
        functools.partial(extra_kernel, n_row // 2),
        [((n_chunk, 64, 128), F32)],
        [],
        [me, *near],
        {0},
        flops=10**9,
    )

    vec_shape = (n_chunk, 3, ROWS, 128)
    cols = pltpu.VMEM((256, total), BF16)
    held = [] if n_chunk <= 16 else [pltpu.VMEM((8, ROWS, 128), F32)]
    kernels, places, basis, norm, wide = call(
        functools.partial(first_kernel, n_row, n_col),
        [
            ((256, total), BF16),
            ((n_chunk, 4, 128), F32),
            (vec_shape, F32),
            ((2, ROWS, 128), F32),
            message,
        ],
        [cols, *held],
        [piece, extra, tgt, me],
        {3},
    )
    bases = [basis]
    columns = [norm]
    for k in range(1, ITERS):
        final = k == ITERS - 1
        piece = spread(wide, n)
        basis, column, wide, own = call(
            functools.partial(middle_kernel, n_row, n_col, k, final),
            [
                (vec_shape, F32),
                ((k + 1 + (len(PAIRS) if final else 1), ROWS, 128), F32),
                ((n, 128), F32) if final else message,
                ((k + 1, 3, ROWS, 128), F32),
            ],
            [cols, *held],
            [piece, *bases, *columns, kernels, places, tgt, me],
            {2 * k + 4},
        )
        bases.append(basis)
        columns.append(column)
    sums = spread(wide, n)
    (density,) = call(
        last_kernel, [((rhs, 3, 64), F32)], [], [sums, own, *columns[1:], columns[0]]
    )
    return density


def solution(mesh):
    n_row, n_col = mesh.shape["row"], mesh.shape["col"]
    sizes = (n_row // 4, 2, 2, n_col)
    split = jax.sharding.Mesh(mesh.devices.reshape(sizes), AXES)
    return jax.shard_map(
        functools.partial(body, sizes),
        mesh=split,
        in_specs=(
            P(None, None, AXES),
            P(None, AXES),
            P(AXES),
            P(AXES),
            P(AXES[:3], "col"),
            P(AXES[:3], "col"),
        ),
        out_specs=P(None, None, AXES),
        check_vma=False,
    )
```

```python
import functools
import math

import jax
import jax.numpy as jnp
from jax import lax
from jax.experimental import pallas as pl
from jax.experimental.pallas import tpu as pltpu
from jax.sharding import PartitionSpec as P

ITERS = 3
BLOB_SQ = 0.0025
INV_EIGHT_PI = 1.0 / (8.0 * math.pi)
ROWS = 8
HALF = 3
FIRST, LATER = 11, 10
ORDER = (0, 2, 1)
AXES = ("top", "mid", "core", "col")
F32 = jnp.float32
BF16 = jnp.bfloat16


def low_half(shape):
    return lax.broadcasted_iota(jnp.int32, shape, len(shape) - 1) < 64


def xor_perm(n, m):
    return [(d, d ^ m) for d in range(n)]


def spread(rows, n):
    wide = rows.reshape(n, -1, 1, 128)
    return lax.all_to_all(wide, AXES, 0, 0, tiled=True).reshape(rows.shape)


def each(count, step):
    if count <= 16:
        for i in range(count):
            step(i)
    else:
        pl.loop(0, count)(step)


class Sums:
    def __init__(self, count, refs):
        self.refs = refs
        self.parts = [[None] * 4 for _ in range(count)]
        if refs is not None:
            for at in range(count):
                refs[at] = jnp.zeros((ROWS, 128), F32)

    def add(self, chunk, at, left, right):
        part = sum(left[a] * right[a] for a in range(3))
        if self.refs is not None:
            self.refs[at] = self.refs[at] + part
            return
        held = self.parts[at]
        slot = chunk % 4
        held[slot] = part if held[slot] is None else held[slot] + part

    def get(self, at):
        if self.refs is not None:
            total = self.refs[at]
        else:
            held = self.parts[at]
            total = (held[0] + held[1]) + (held[2] + held[3])
        return jnp.broadcast_to(jnp.sum(total, axis=1, keepdims=True), (ROWS, 128))


def chunk_parts(piece, chunk, me, n_row, n_col, size, at, count):
    half = n_row // 2
    o = chunk // half
    u = chunk % half
    even = piece[pl.ds((me ^ ((2 * u) * n_col + o)) * size + at, count)]
    odd = piece[pl.ds((me ^ ((2 * u + 1) * n_col + o)) * size + at, count)]
    low = low_half((count, 128))
    first = jnp.where(low, even, pltpu.roll(odd, 64, 1))
    second = jnp.where(low, pltpu.roll(even, 64, 1), odd)
    return jnp.concatenate([first, second], axis=0)


PAIRS = [(i, j) for i in range(ITERS) for j in range(i + 1, ITERS)]


def place_of(j):
    lane = lax.broadcasted_iota(jnp.int32, (ROWS, 128), 1)
    return lane == lax.broadcasted_iota(jnp.int32, (ROWS, 128), 0) * (ITERS + 1) + j


def row_sum(acc):
    return jnp.sum(acc, axis=1, keepdims=True)


def lines_of(chunk):
    if isinstance(chunk, int):
        return pl.ds(chunk * 128, 128)
    return pl.ds(pl.multiple_of(chunk * 128, 128), 128)


def write_columns(cols, y, chunk, vec):
    ys = [y[a : a + 1] for a in ORDER]
    f = [vec[a] for a in range(3)]
    g = ys[0] * f[0] + ys[1] * f[1] + ys[2] * f[2]
    groups = f + [g]
    groups += [ys[p] * f[v] for p in range(3) for v in range(3)]
    groups += [ys[a] * g for a in range(3)]
    full = jnp.concatenate(groups, axis=0)
    high = full.astype(BF16)
    low = (full - high.astype(F32)).astype(BF16)
    at = lines_of(chunk)
    cols[0:128, at] = high
    cols[128:256, at] = low


def contract(left, right):
    dims = (((1,), (1,)), ((), ()))
    return lax.dot_general(left, right, dims, preferred_element_type=F32)


def products(n_chunk, columns, cols, kernels):
    if n_chunk <= 16:
        group = n_chunk // 4
        prod = None
        for begin in range(0, n_chunk, group):
            for chunk in range(begin, begin + group):
                columns(chunk)
            at = pl.ds(begin * 128, group * 128)
            part = contract(cols[:, at], kernels[:, at])
            prod = part if prod is None else prod + part
        return prod
    pl.loop(0, n_chunk)(columns)

    def turn(i, acc):
        at = pl.ds(pl.multiple_of(i * 2048, 2048), 2048)
        return acc + contract(cols[:, at], kernels[:, at])

    return lax.fori_loop(0, n_chunk // 16, turn, jnp.zeros((256, 256), F32))


def image_rows(prod, targets, own, scale):
    both = prod[:128, :128] + (prod[128:, :128] + prod[:128, 128:])
    two = pltpu.roll(both, 64, 1)

    def group(k):
        return two[8 * k : 8 * k + 8]

    x = [targets[a : a + 1] for a in range(3)]
    images = []
    along = x[0] * group(0) + x[1] * group(1) + x[2] * group(2) - group(3)
    for a in range(3):
        cross = sum(x[b] * group(4 + 3 * a + b) for b in range(3))
        image = both[8 * a : 8 * a + 8] + x[a] * along - cross + group(13 + a)
        images.append((image + targets[3:4] * own[a]) * scale)
    return images


def write_piece(images, out):
    rows = []
    for image in images:
        top, bottom = image[:4], pltpu.roll(image[4:], 64, 1)
        rows.append(jnp.where(low_half((4, 128)), top, bottom))

    def put(m):
        for a in range(3):
            out[pl.ds(m * LATER + HALF * a, 4)] = rows[a]

    each_wide(out.shape[0] // LATER, put)


def each_wide(count, put):
    if count <= 64:
        for m in range(count):
            put(m)
    else:
        pl.loop(0, count)(put)


def pack_kernel(*refs):
    sources, outs, held, sems = refs[:6], refs[6:9], refs[9:15], refs[15]
    out, tgt, lists = outs
    copies = [
        pltpu.make_async_copy(src, dst, sems.at[i])
        for i, (src, dst) in enumerate(zip(sources, held))
    ]
    for copy in copies:
        copy.start()
    for copy in copies:
        copy.wait()
    velocity, points, area, self_term, index, weight = held
    count = index.shape[0]
    lists[:count] = index[...].astype(F32)
    lists[count:] = weight[...]
    field = velocity[...]
    spot = points[...]
    rows = []
    for a in range(3):
        vec = field[:, a, :]
        rows.append(jnp.concatenate([vec[:HALF], vec[HALF:]], axis=1))
    mine = jnp.concatenate([spot, self_term[...]], axis=0)
    mine = jnp.concatenate([mine, mine], axis=1)
    tgt[...] = jnp.concatenate([mine, mine], axis=0)
    left = jnp.concatenate([spot[0:1], spot[2:3]], axis=0)
    right = jnp.concatenate([spot[1:2], area[...]], axis=0)
    rows.append(jnp.concatenate([left, right], axis=1))
    message = jnp.concatenate(rows, axis=0)

    def put(m):
        out[pl.ds(m * FIRST, FIRST)] = message

    each_wide(out.shape[0] // FIRST, put)


def extra_kernel(half_chunks, me, *refs):
    near, out = refs[:-1], refs[-1]
    row, col = me[1], me[2]
    lines = lax.broadcasted_iota(jnp.int32, (128, 128), 0).astype(F32)
    for o, lists in enumerate(near):
        count = lists.shape[0] // 2
        half = count // 2
        low = low_half((half, 128))
        odd = col % 2 == 1
        both = lists[:, lines_of(col // 2)]
        place = both[:count].astype(jnp.int32)
        place = (((place // 64) ^ row) * 64 + place % 64).astype(F32)
        packed = []
        for value in (place, both[count:]):
            top, bottom = value[:half], value[half:]
            lower = jnp.where(low, top, pltpu.roll(bottom, 64, 1))
            upper = jnp.where(low, pltpu.roll(top, 64, 1), bottom)
            packed.append(jnp.where(odd, upper, lower))
        index, weight = packed

        def build(u):
            line = lines + (u * 128.0 if isinstance(u, int) else (u * 128).astype(F32))
            total = jnp.zeros((128, 128), F32)
            for k in range(half):
                total = total + jnp.where(line == index[k : k + 1], weight[k : k + 1], 0.0)
            turned = total.T
            out[o * half_chunks + u] = turned[:64] + turned[64:]

        each(half_chunks, build)


def first_kernel(
    n_row, n_col, piece, extra, tgt, me_ref, kernels, places, basis, norm_out, out, cols, *sums
):
    n_chunk = n_row * n_col // 2
    me = me_ref[0]
    total = Sums(1, sums[0] if sums else None)

    def unpack(chunk):
        vec = [
            chunk_parts(piece, chunk, me, n_row, n_col, FIRST, HALF * a, 4)
            for a in range(3)
        ]
        spot = chunk_parts(piece, chunk, me, n_row, n_col, FIRST, 3 * HALF, 2)
        places[chunk] = spot
        for a in range(3):
            basis[chunk, a] = vec[a]
        total.add(chunk, 0, vec, vec)
        write_columns(cols, spot, chunk, vec)

    turned = tgt[...].T
    x = [jnp.broadcast_to(turned[:64, a : a + 1], (64, 128)) for a in range(3)]

    def build(chunk):
        unpack(chunk)
        y = places[chunk]
        d = [x[a] - y[k : k + 1] for a, k in enumerate(ORDER)]
        dist = d[0] * d[0] + d[1] * d[1] + d[2] * d[2]
        root = lax.rsqrt(dist + BLOB_SQ)
        two = (y[3:4] * INV_EIGHT_PI) * root * root * root
        one = (dist + 2.0 * BLOB_SQ) * two + extra[chunk]
        value = jnp.concatenate([one, two], axis=0)
        high = value.astype(BF16)
        at = lines_of(chunk)
        kernels[0:128, at] = high
        kernels[128:256, at] = (value - high.astype(F32)).astype(BF16)

    prod = products(n_chunk, build, cols, kernels)
    norm = jnp.sqrt(total.get(0))
    scale = 1.0 / norm
    norm_out[0] = norm
    norm_out[1] = scale
    write_piece(image_rows(prod, tgt, basis[0], scale), out)


def middle_kernel(n_row, n_col, n_base, final, piece, *refs):
    bases, norms = refs[:n_base], refs[n_base : 2 * n_base]
    if final:
        kernels, places, tgt, me_ref, own, h_out, out, basis, cols, *held = refs[2 * n_base :]
    else:
        kernels, places, tgt, me_ref, basis, h_out, out, cols, *held = refs[2 * n_base :]
    n_chunk = n_row * n_col // 2
    me = me_ref[0]
    scales = [norm[norm.shape[0] - 1] for norm in norms]
    cross = [(i, j) for i in range(n_base) for j in range(i)]
    sums = Sums(2 * n_base + 1 + len(cross), held[0] if held else None)

    def unpack(chunk):
        vec = [
            chunk_parts(piece, chunk, me, n_row, n_col, LATER, HALF * a, 4)
            for a in range(3)
        ]
        old = [[base[chunk, a] for a in range(3)] for base in bases]
        for a in range(3):
            basis[chunk, a] = vec[a]
        for j in range(n_base):
            sums.add(chunk, j, vec, old[j])
        for at, (i, j) in enumerate(cross):
            sums.add(chunk, 2 * n_base + 1 + at, old[i], old[j])

    each(n_chunk, unpack)
    gram = {}
    for at, (i, j) in enumerate(cross):
        gram[j, i] = sums.get(2 * n_base + 1 + at) * (scales[i] * scales[j])
    column = []
    for j in range(n_base):
        h = sums.get(j) * scales[j]
        for i in range(j):
            h = h - column[i] * gram[i, j]
        column.append(h)
        h_out[j] = h
    factors = [h * scale for h, scale in zip(column, scales)]

    def columns(chunk):
        old = [[base[chunk, a] for a in range(3)] for base in bases]
        vec = []
        for a in range(3):
            value = basis[chunk, a]
            for j in range(n_base):
                value = value - factors[j] * old[j][a]
            vec.append(value)
            basis[chunk, a] = value
        sums.add(chunk, n_base, vec, vec)
        write_columns(cols, places[chunk], chunk, vec)
        if final:
            for j in range(n_base):
                sums.add(chunk, n_base + 1 + j, vec, old[j])

    prod = products(n_chunk, columns, cols, kernels)
    norm = jnp.sqrt(sums.get(n_base))
    scale = 1.0 / norm
    h_out[n_base] = norm
    images = image_rows(prod, tgt, basis[0], scale)
    if not final:
        h_out[n_base + 1] = scale
        write_piece(images, out)
        return
    every = [*bases, basis]
    for j, base in enumerate(every):
        for a in range(3):
            own[j, a] = base[0, a] * [*scales, scale][j]
    for j in range(n_base):
        gram[j, n_base] = sums.get(n_base + 1 + j) * (scale * scales[j])
    for at, pair in enumerate(PAIRS):
        h_out[n_base + 1 + at] = gram[pair]
    low = low_half((ROWS, 128))
    row = jnp.zeros((ROWS, 128), F32)
    for j in range(ITERS + 1):
        other = images if j == ITERS else [own[j, a] for a in range(3)]
        part = sum(images[a] * other[a] for a in range(3))
        part = row_sum(jnp.where(low, part, 0.0))
        row = row + jnp.where(place_of(j), part, 0.0)
    row = jnp.sum(row, axis=0, keepdims=True)

    def put(m):
        out[pl.ds(m, 1)] = row

    each_wide(out.shape[0], put)


def solve_small(hessen, start_norm, count):
    zero = jnp.zeros_like(start_norm)
    target = [start_norm] + [zero] * count
    cosines = []
    sines = []
    triangle = {}
    for k in range(count):
        column = [hessen[i, k] for i in range(k + 2)]
        for j in range(k):
            first_val = column[j]
            second_val = column[j + 1]
            column[j] = cosines[j] * first_val + sines[j] * second_val
            column[j + 1] = cosines[j] * second_val - sines[j] * first_val
        radius = jnp.sqrt(column[k] * column[k] + column[k + 1] * column[k + 1])
        cosine = column[k] / radius
        sine = column[k + 1] / radius
        cosines.append(cosine)
        sines.append(sine)
        for i in range(k):
            triangle[i, k] = column[i]
        triangle[k, k] = radius
        target[k + 1] = -sine * target[k]
        target[k] = cosine * target[k]
    coeffs = [None] * count
    for k in range(count - 1, -1, -1):
        accum = target[k]
        for i in range(k + 1, count):
            accum = accum - triangle[k, i] * coeffs[i]
        coeffs[k] = accum / triangle[k, k]
    return coeffs


def last_kernel(sums, own, *refs):
    columns = refs[: ITERS - 1]
    norm, out = refs[ITERS - 1 :]
    hessen = {}
    for k in range(ITERS - 1):
        for j in range(k + 2):
            hessen[j, k] = columns[k][j]
    gram = {(j, j): 1.0 for j in range(ITERS)}
    for at, (i, j) in enumerate(PAIRS):
        gram[i, j] = gram[j, i] = columns[-1][ITERS + at]
    row = jnp.broadcast_to(jnp.sum(sums[...], axis=0, keepdims=True), (ROWS, 128))
    inner = [
        jnp.broadcast_to(row_sum(jnp.where(place_of(j), row, 0.0)), (ROWS, 128))
        for j in range(ITERS + 1)
    ]
    square = inner[ITERS]
    for j in range(ITERS):
        h = inner[j]
        for i in range(j):
            h = h - hessen[i, ITERS - 1] * gram[i, j]
        hessen[j, ITERS - 1] = h
    for j in range(ITERS):
        rest = -2.0 * inner[j]
        for i in range(ITERS):
            rest = rest + hessen[i, ITERS - 1] * gram[i, j]
        square = square + hessen[j, ITERS - 1] * rest
    hessen[ITERS, ITERS - 1] = jnp.sqrt(jnp.maximum(square, 0.0))
    coeffs = solve_small(hessen, norm[0], ITERS)
    for a in range(3):
        density = sum(coeffs[k] * own[k, a] for k in range(ITERS))
        out[:HALF, a, :] = density[:HALF, :64]
        out[HALF:, a, :] = density[4 : 4 + HALF, :64]


def call(kernel, outs, scratch, operands, scalars=(), far=(), flops=0):
    vmem = pl.BlockSpec(memory_space=pltpu.VMEM)
    smem = pl.BlockSpec(memory_space=pltpu.SMEM)
    count = len(operands)
    hbm = pl.BlockSpec(memory_space=pltpu.HBM)
    specs = [smem if i in scalars else hbm if i in far else vmem for i in range(count)]
    moved = sum(x.size * x.dtype.itemsize for x in operands)
    return pl.pallas_call(
        kernel,
        out_shape=[jax.ShapeDtypeStruct(s, t) for s, t in outs],
        in_specs=specs,
        out_specs=[vmem] * len(outs),
        scratch_shapes=scratch,
        cost_estimate=pl.CostEstimate(flops=flops, bytes_accessed=moved, transcendentals=0),
        compiler_params=pltpu.CompilerParams(vmem_limit_bytes=48 * 1024 * 1024),
    )(*operands)


def body(sizes, velocity, points, panel_area, self_term, near_index, near_weight):
    n_row, n_col = sizes[0] * sizes[1] * sizes[2], sizes[3]
    n = n_row * n_col
    n_chunk = n // 2
    total = n * 64
    row = lax.axis_index(AXES[:3])
    col = lax.axis_index("col")
    me = jnp.stack([row * n_col + col, row, col]).astype(jnp.int32)
    rhs = velocity.shape[0]

    message = ((n * LATER, 128), F32)
    sources = [
        velocity,
        points,
        panel_area[None],
        self_term[None],
        near_index.T,
        near_weight.T,
    ]
    wide, tgt, lists = call(
        pack_kernel,
        [
            ((n * FIRST, 128), F32),
            ((8, 128), F32),
            ((2 * near_index.shape[1], near_index.shape[0]), F32),
        ],
        [pltpu.VMEM(x.shape, x.dtype) for x in sources] + [pltpu.SemaphoreType.DMA((6,))],
        [pltpu.with_memory_space_constraint(x, pltpu.HBM) for x in sources],
        far=range(6),
    )
    piece = spread(wide, n)
    near = [lists] + [lax.ppermute(lists, "col", xor_perm(n_col, o)) for o in range(1, n_col)]
    (extra,) = call(
        functools.partial(extra_kernel, n_row // 2),
        [((n_chunk, 64, 128), F32)],
        [],
        [me, *near],
        {0},
        flops=10**9,
    )

    vec_shape = (n_chunk, 3, ROWS, 128)
    cols = pltpu.VMEM((256, total), BF16)
    held = [] if n_chunk <= 16 else [pltpu.VMEM((8, ROWS, 128), F32)]
    kernels, places, basis, norm, wide = call(
        functools.partial(first_kernel, n_row, n_col),
        [
            ((256, total), BF16),
            ((n_chunk, 4, 128), F32),
            (vec_shape, F32),
            ((2, ROWS, 128), F32),
            message,
        ],
        [cols, *held],
        [piece, extra, tgt, me],
        {3},
    )
    bases = [basis]
    columns = [norm]
    for k in range(1, ITERS):
        final = k == ITERS - 1
        piece = spread(wide, n)
        main, column, wide = call(
            functools.partial(middle_kernel, n_row, n_col, k, final),
            [
                ((ITERS, 3, ROWS, 128) if final else vec_shape, F32),
                ((k + 1 + (len(PAIRS) if final else 1), ROWS, 128), F32),
                ((n, 128), F32) if final else message,
            ],
            [*([pltpu.VMEM(vec_shape, F32)] if final else []), cols, *held],
            [piece, *bases, *columns, kernels, places, tgt, me],
            {2 * k + 4},
        )
        bases.append(main)
        columns.append(column)
    sums = spread(wide, n)
    (density,) = call(
        last_kernel, [((rhs, 3, 64), F32)], [], [sums, bases[-1], *columns[1:], columns[0]]
    )
    return density


def solution(mesh):
    n_row, n_col = mesh.shape["row"], mesh.shape["col"]
    sizes = (n_row // 4, 2, 2, n_col)
    split = jax.sharding.Mesh(mesh.devices.reshape(sizes), AXES)
    return jax.shard_map(
        functools.partial(body, sizes),
        mesh=split,
        in_specs=(
            P(None, None, AXES),
            P(None, AXES),
            P(AXES),
            P(AXES),
            P(AXES[:3], "col"),
            P(AXES[:3], "col"),
        ),
        out_specs=P(None, None, AXES),
        check_vma=False,
    )
```

```python
import functools
import math

import jax
import jax.numpy as jnp
from jax import lax
from jax.experimental import pallas as pl
from jax.experimental.pallas import tpu as pltpu
from jax.sharding import PartitionSpec as P

ITERS = 3
BLOB_SQ = 0.0025
INV_EIGHT_PI = 1.0 / (8.0 * math.pi)
ROWS = 8
HALF = 3
FIRST, LATER = 11, 10
ORDER = (0, 2, 1)
AXES = ("top", "mid", "core", "col")
F32 = jnp.float32
BF16 = jnp.bfloat16


def low_half(shape):
    return lax.broadcasted_iota(jnp.int32, shape, len(shape) - 1) < 64


def xor_perm(n, m):
    return [(d, d ^ m) for d in range(n)]


def spread(rows, n):
    wide = rows.reshape(n, -1, 1, 128)
    return lax.all_to_all(wide, AXES, 0, 0, tiled=True).reshape(rows.shape)


def each(count, step):
    if count <= 16:
        for i in range(count):
            step(i)
    else:
        pl.loop(0, count)(step)


class Sums:
    def __init__(self, count, refs):
        self.refs = refs
        self.parts = [[None] * 4 for _ in range(count)]
        if refs is not None:
            for at in range(count):
                refs[at] = jnp.zeros((ROWS, 128), F32)

    def add(self, chunk, at, left, right):
        part = sum(left[a] * right[a] for a in range(3))
        if self.refs is not None:
            self.refs[at] = self.refs[at] + part
            return
        held = self.parts[at]
        slot = chunk % 4
        held[slot] = part if held[slot] is None else held[slot] + part

    def get(self, at):
        if self.refs is not None:
            total = self.refs[at]
        else:
            held = self.parts[at]
            total = (held[0] + held[1]) + (held[2] + held[3])
        return jnp.broadcast_to(jnp.sum(total, axis=1, keepdims=True), (ROWS, 128))


def chunk_parts(piece, chunk, me, n_row, n_col, size, at, count):
    half = n_row // 2
    o = chunk // half
    u = chunk % half
    even = piece[pl.ds((me ^ ((2 * u) * n_col + o)) * size + at, count)]
    odd = piece[pl.ds((me ^ ((2 * u + 1) * n_col + o)) * size + at, count)]
    low = low_half((count, 128))
    first = jnp.where(low, even, pltpu.roll(odd, 64, 1))
    second = jnp.where(low, pltpu.roll(even, 64, 1), odd)
    return jnp.concatenate([first, second], axis=0)


PAIRS = [(i, j) for i in range(ITERS) for j in range(i + 1, ITERS)]


def place_of(j):
    lane = lax.broadcasted_iota(jnp.int32, (ROWS, 128), 1)
    return lane == lax.broadcasted_iota(jnp.int32, (ROWS, 128), 0) * (ITERS + 1) + j


def row_sum(acc):
    return jnp.sum(acc, axis=1, keepdims=True)


def lines_of(chunk):
    if isinstance(chunk, int):
        return pl.ds(chunk * 128, 128)
    return pl.ds(pl.multiple_of(chunk * 128, 128), 128)


def write_columns(cols, y, chunk, vec):
    ys = [y[a : a + 1] for a in ORDER]
    f = [vec[a] for a in range(3)]
    g = ys[0] * f[0] + ys[1] * f[1] + ys[2] * f[2]
    groups = f + [g]
    groups += [ys[p] * f[v] for p in range(3) for v in range(3)]
    groups += [ys[a] * g for a in range(3)]
    full = jnp.concatenate(groups, axis=0)
    high = full.astype(BF16)
    low = (full - high.astype(F32)).astype(BF16)
    at = lines_of(chunk)
    cols[0:128, at] = high
    cols[128:256, at] = low


def contract(left, right):
    dims = (((1,), (1,)), ((), ()))
    return lax.dot_general(left, right, dims, preferred_element_type=F32)


def products(n_chunk, columns, cols, kernels):
    if n_chunk <= 16:
        for chunk in range(n_chunk):
            columns(chunk)
        return contract(cols[...], kernels[...])
    pl.loop(0, n_chunk)(columns)

    def turn(i, acc):
        at = pl.ds(pl.multiple_of(i * 2048, 2048), 2048)
        return acc + contract(cols[:, at], kernels[:, at])

    return lax.fori_loop(0, n_chunk // 16, turn, jnp.zeros((256, 256), F32))


def image_rows(prod, targets, own):
    both = prod[:128, :128] + (prod[128:, :128] + prod[:128, 128:])
    two = pltpu.roll(both, 64, 1)

    def group(k):
        return two[8 * k : 8 * k + 8]

    x = [targets[a : a + 1] for a in range(3)]
    images = []
    along = x[0] * group(0) + x[1] * group(1) + x[2] * group(2) - group(3)
    for a in range(3):
        cross = sum(x[b] * group(4 + 3 * a + b) for b in range(3))
        image = both[8 * a : 8 * a + 8] + x[a] * along - cross + group(13 + a)
        images.append(image + targets[3:4] * own[a])
    return images


def write_piece(images, out):
    rows = []
    for image in images:
        top, bottom = image[:4], pltpu.roll(image[4:], 64, 1)
        rows.append(jnp.where(low_half((4, 128)), top, bottom))

    def put(m):
        for a in range(3):
            out[pl.ds(m * LATER + HALF * a, 4)] = rows[a]

    each_wide(out.shape[0] // LATER, put)


def each_wide(count, put):
    if count <= 64:
        for m in range(count):
            put(m)
    else:
        pl.loop(0, count)(put)


def pack_kernel(*refs):
    sources, outs, held, sems = refs[:6], refs[6:9], refs[9:15], refs[15]
    out, tgt, lists = outs
    copies = [
        pltpu.make_async_copy(src, dst, sems.at[i])
        for i, (src, dst) in enumerate(zip(sources, held))
    ]
    for copy in copies:
        copy.start()
    for copy in copies:
        copy.wait()
    velocity, points, area, self_term, index, weight = held
    count = index.shape[0]
    lists[:count] = index[...].astype(F32)
    lists[count:] = weight[...]
    field = velocity[...]
    spot = points[...]
    rows = []
    for a in range(3):
        vec = field[:, a, :]
        rows.append(jnp.concatenate([vec[:HALF], vec[HALF:]], axis=1))
    mine = jnp.concatenate([spot, self_term[...]], axis=0)
    mine = jnp.concatenate([mine, mine], axis=1)
    tgt[...] = jnp.concatenate([mine, mine], axis=0)
    left = jnp.concatenate([spot[0:1], spot[2:3]], axis=0)
    right = jnp.concatenate([spot[1:2], area[...]], axis=0)
    rows.append(jnp.concatenate([left, right], axis=1))
    message = jnp.concatenate(rows, axis=0)

    def put(m):
        out[pl.ds(m * FIRST, FIRST)] = message

    each_wide(out.shape[0] // FIRST, put)


def extra_kernel(half_chunks, me, *refs):
    near, out = refs[:-1], refs[-1]
    row, col = me[1], me[2]
    lines = lax.broadcasted_iota(jnp.int32, (128, 128), 0).astype(F32)
    for o, lists in enumerate(near):
        count = lists.shape[0] // 2
        half = count // 2
        low = low_half((half, 128))
        odd = col % 2 == 1
        both = lists[:, lines_of(col // 2)]
        place = both[:count].astype(jnp.int32)
        place = (((place // 64) ^ row) * 64 + place % 64).astype(F32)
        packed = []
        for value in (place, both[count:]):
            top, bottom = value[:half], value[half:]
            lower = jnp.where(low, top, pltpu.roll(bottom, 64, 1))
            upper = jnp.where(low, pltpu.roll(top, 64, 1), bottom)
            packed.append(jnp.where(odd, upper, lower))
        index, weight = packed

        def build(u):
            line = lines + (u * 128.0 if isinstance(u, int) else (u * 128).astype(F32))
            total = jnp.zeros((128, 128), F32)
            for k in range(half):
                total = total + jnp.where(line == index[k : k + 1], weight[k : k + 1], 0.0)
            turned = total.T
            out[o * half_chunks + u] = turned[:64] + turned[64:]

        each(half_chunks, build)


def first_kernel(
    n_row, n_col, piece, extra, tgt, me_ref, kernels, places, basis, mine, norm_out, out, cols, *sums
):
    n_chunk = n_row * n_col // 2
    me = me_ref[0]
    total = Sums(1, sums[0] if sums else None)

    def unpack(chunk):
        vec = [
            chunk_parts(piece, chunk, me, n_row, n_col, FIRST, HALF * a, 4)
            for a in range(3)
        ]
        spot = chunk_parts(piece, chunk, me, n_row, n_col, FIRST, 3 * HALF, 2)
        places[chunk] = spot
        for a in range(3):
            basis[chunk, a] = vec[a]
        total.add(chunk, 0, vec, vec)
        write_columns(cols, spot, chunk, vec)

    turned = tgt[...].T
    x = [jnp.broadcast_to(turned[:64, a : a + 1], (64, 128)) for a in range(3)]

    def build(chunk):
        unpack(chunk)
        y = places[chunk]
        d = [x[a] - y[k : k + 1] for a, k in enumerate(ORDER)]
        dist = d[0] * d[0] + d[1] * d[1] + d[2] * d[2]
        root = lax.rsqrt(dist + BLOB_SQ)
        two = (y[3:4] * INV_EIGHT_PI) * root * root * root
        one = (dist + 2.0 * BLOB_SQ) * two + extra[chunk]
        value = jnp.concatenate([one, two], axis=0)
        high = value.astype(BF16)
        at = lines_of(chunk)
        kernels[0:128, at] = high
        kernels[128:256, at] = (value - high.astype(F32)).astype(BF16)

    prod = products(n_chunk, build, cols, kernels)
    norm = jnp.sqrt(total.get(0))
    scale = 1.0 / norm
    norm_out[0] = norm
    norm_out[1] = scale
    images = [image * scale for image in image_rows(prod, tgt, basis[0])]
    for a in range(3):
        mine[a] = images[a]
    write_piece(images, out)


def middle_kernel(n_row, n_col, n_base, final, piece, *refs):
    bases, norms, before = (refs[i * n_base : (i + 1) * n_base] for i in range(3))
    kernels, places, tgt, me_ref, *rest = refs[3 * n_base :]
    if final:
        own, h_out, out, basis, cols, *held = rest
    else:
        basis, mine, h_out, out, cols, *held = rest
    n_chunk = n_row * n_col // 2
    me = me_ref[0]
    scales = [norm[norm.shape[0] - 1] for norm in norms]
    cross = [(i, j) for i in range(n_base) for j in range(i)]
    sums = Sums(2 * n_base + 1 + len(cross), held[0] if held else None)

    def unpack(chunk):
        vec = [
            chunk_parts(piece, chunk, me, n_row, n_col, LATER, HALF * a, 4)
            for a in range(3)
        ]
        old = [[base[chunk, a] for a in range(3)] for base in bases]
        for a in range(3):
            basis[chunk, a] = vec[a]
        write_columns(cols, places[chunk], chunk, vec)
        for j in range(n_base):
            sums.add(chunk, j, vec, old[j])
        for at, (i, j) in enumerate(cross):
            sums.add(chunk, 2 * n_base + 1 + at, old[i], old[j])

    prod = products(n_chunk, unpack, cols, kernels)
    raw = image_rows(prod, tgt, basis[0])
    gram = {}
    for at, (i, j) in enumerate(cross):
        gram[j, i] = sums.get(2 * n_base + 1 + at) * (scales[i] * scales[j])
    column = []
    for j in range(n_base):
        h = sums.get(j) * scales[j]
        for i in range(j):
            h = h - column[i] * gram[i, j]
        column.append(h)
        h_out[j] = h
    factors = [h * scale for h, scale in zip(column, scales)]

    def take(chunk):
        old = [[base[chunk, a] for a in range(3)] for base in bases]
        vec = []
        for a in range(3):
            value = basis[chunk, a]
            for j in range(n_base):
                value = value - factors[j] * old[j][a]
            vec.append(value)
            basis[chunk, a] = value
        sums.add(chunk, n_base, vec, vec)
        if final:
            for j in range(n_base):
                sums.add(chunk, n_base + 1 + j, vec, old[j])

    each(n_chunk, take)
    norm = jnp.sqrt(sums.get(n_base))
    scale = 1.0 / norm
    h_out[n_base] = norm
    images = [
        (raw[a] - sum(column[j] * before[j][a] for j in range(n_base))) * scale
        for a in range(3)
    ]
    if not final:
        for a in range(3):
            mine[a] = images[a]
        h_out[n_base + 1] = scale
        write_piece(images, out)
        return
    every = [*bases, basis]
    for j, base in enumerate(every):
        for a in range(3):
            own[j, a] = base[0, a] * [*scales, scale][j]
    for j in range(n_base):
        gram[j, n_base] = sums.get(n_base + 1 + j) * (scale * scales[j])
    for at, pair in enumerate(PAIRS):
        h_out[n_base + 1 + at] = gram[pair]
    low = low_half((ROWS, 128))
    row = jnp.zeros((ROWS, 128), F32)
    for j in range(ITERS + 1):
        other = images if j == ITERS else [own[j, a] for a in range(3)]
        part = sum(images[a] * other[a] for a in range(3))
        part = row_sum(jnp.where(low, part, 0.0))
        row = row + jnp.where(place_of(j), part, 0.0)
    row = jnp.sum(row, axis=0, keepdims=True)

    def put(m):
        out[pl.ds(m, 1)] = row

    each_wide(out.shape[0], put)


def solve_small(hessen, start_norm, count):
    zero = jnp.zeros_like(start_norm)
    target = [start_norm] + [zero] * count
    cosines = []
    sines = []
    triangle = {}
    for k in range(count):
        column = [hessen[i, k] for i in range(k + 2)]
        for j in range(k):
            first_val = column[j]
            second_val = column[j + 1]
            column[j] = cosines[j] * first_val + sines[j] * second_val
            column[j + 1] = cosines[j] * second_val - sines[j] * first_val
        radius = jnp.sqrt(column[k] * column[k] + column[k + 1] * column[k + 1])
        cosine = column[k] / radius
        sine = column[k + 1] / radius
        cosines.append(cosine)
        sines.append(sine)
        for i in range(k):
            triangle[i, k] = column[i]
        triangle[k, k] = radius
        target[k + 1] = -sine * target[k]
        target[k] = cosine * target[k]
    coeffs = [None] * count
    for k in range(count - 1, -1, -1):
        accum = target[k]
        for i in range(k + 1, count):
            accum = accum - triangle[k, i] * coeffs[i]
        coeffs[k] = accum / triangle[k, k]
    return coeffs


def last_kernel(sums, own, *refs):
    columns = refs[: ITERS - 1]
    norm, out = refs[ITERS - 1 :]
    hessen = {}
    for k in range(ITERS - 1):
        for j in range(k + 2):
            hessen[j, k] = columns[k][j]
    gram = {(j, j): 1.0 for j in range(ITERS)}
    for at, (i, j) in enumerate(PAIRS):
        gram[i, j] = gram[j, i] = columns[-1][ITERS + at]
    row = jnp.broadcast_to(jnp.sum(sums[...], axis=0, keepdims=True), (ROWS, 128))
    inner = [
        jnp.broadcast_to(row_sum(jnp.where(place_of(j), row, 0.0)), (ROWS, 128))
        for j in range(ITERS + 1)
    ]
    square = inner[ITERS]
    for j in range(ITERS):
        h = inner[j]
        for i in range(j):
            h = h - hessen[i, ITERS - 1] * gram[i, j]
        hessen[j, ITERS - 1] = h
    for j in range(ITERS):
        rest = -2.0 * inner[j]
        for i in range(ITERS):
            rest = rest + hessen[i, ITERS - 1] * gram[i, j]
        square = square + hessen[j, ITERS - 1] * rest
    hessen[ITERS, ITERS - 1] = jnp.sqrt(jnp.maximum(square, 0.0))
    coeffs = solve_small(hessen, norm[0], ITERS)
    for a in range(3):
        density = sum(coeffs[k] * own[k, a] for k in range(ITERS))
        out[:HALF, a, :] = density[:HALF, :64]
        out[HALF:, a, :] = density[4 : 4 + HALF, :64]


def call(kernel, outs, scratch, operands, scalars=(), far=(), flops=0):
    vmem = pl.BlockSpec(memory_space=pltpu.VMEM)
    smem = pl.BlockSpec(memory_space=pltpu.SMEM)
    count = len(operands)
    hbm = pl.BlockSpec(memory_space=pltpu.HBM)
    specs = [smem if i in scalars else hbm if i in far else vmem for i in range(count)]
    moved = sum(x.size * x.dtype.itemsize for x in operands)
    return pl.pallas_call(
        kernel,
        out_shape=[jax.ShapeDtypeStruct(s, t) for s, t in outs],
        in_specs=specs,
        out_specs=[vmem] * len(outs),
        scratch_shapes=scratch,
        cost_estimate=pl.CostEstimate(flops=flops, bytes_accessed=moved, transcendentals=0),
        compiler_params=pltpu.CompilerParams(vmem_limit_bytes=48 * 1024 * 1024),
    )(*operands)


def body(sizes, velocity, points, panel_area, self_term, near_index, near_weight):
    n_row, n_col = sizes[0] * sizes[1] * sizes[2], sizes[3]
    n = n_row * n_col
    n_chunk = n // 2
    total = n * 64
    row = lax.axis_index(AXES[:3])
    col = lax.axis_index("col")
    me = jnp.stack([row * n_col + col, row, col]).astype(jnp.int32)
    rhs = velocity.shape[0]

    message = ((n * LATER, 128), F32)
    sources = [
        velocity,
        points,
        panel_area[None],
        self_term[None],
        near_index.T,
        near_weight.T,
    ]
    wide, tgt, lists = call(
        pack_kernel,
        [
            ((n * FIRST, 128), F32),
            ((8, 128), F32),
            ((2 * near_index.shape[1], near_index.shape[0]), F32),
        ],
        [pltpu.VMEM(x.shape, x.dtype) for x in sources] + [pltpu.SemaphoreType.DMA((6,))],
        [pltpu.with_memory_space_constraint(x, pltpu.HBM) for x in sources],
        far=range(6),
    )
    piece = spread(wide, n)
    near = [lists] + [lax.ppermute(lists, "col", xor_perm(n_col, o)) for o in range(1, n_col)]
    (extra,) = call(
        functools.partial(extra_kernel, n_row // 2),
        [((n_chunk, 64, 128), F32)],
        [],
        [me, *near],
        {0},
        flops=10**9,
    )

    vec_shape = (n_chunk, 3, ROWS, 128)
    cols = pltpu.VMEM((256, total), BF16)
    held = [] if n_chunk <= 16 else [pltpu.VMEM((8, ROWS, 128), F32)]
    kernels, places, basis, image, norm, wide = call(
        functools.partial(first_kernel, n_row, n_col),
        [
            ((256, total), BF16),
            ((n_chunk, 4, 128), F32),
            (vec_shape, F32),
            ((3, ROWS, 128), F32),
            ((2, ROWS, 128), F32),
            message,
        ],
        [cols, *held],
        [piece, extra, tgt, me],
        {3},
    )
    bases = [basis]
    columns = [norm]
    images = [image]
    for k in range(1, ITERS):
        final = k == ITERS - 1
        piece = spread(wide, n)
        main, *image, column, wide = call(
            functools.partial(middle_kernel, n_row, n_col, k, final),
            [
                ((ITERS, 3, ROWS, 128) if final else vec_shape, F32),
                *([] if final else [((3, ROWS, 128), F32)]),
                ((k + 1 + (len(PAIRS) if final else 1), ROWS, 128), F32),
                ((n, 128), F32) if final else message,
            ],
            [*([pltpu.VMEM(vec_shape, F32)] if final else []), cols, *held],
            [piece, *bases, *columns, *images, kernels, places, tgt, me],
            {3 * k + 4},
        )
        bases.append(main)
        columns.append(column)
        images += image
    sums = spread(wide, n)
    (density,) = call(
        last_kernel, [((rhs, 3, 64), F32)], [], [sums, bases[-1], *columns[1:], columns[0]]
    )
    return density


def solution(mesh):
    n_row, n_col = mesh.shape["row"], mesh.shape["col"]
    sizes = (n_row // 4, 2, 2, n_col)
    split = jax.sharding.Mesh(mesh.devices.reshape(sizes), AXES)
    return jax.shard_map(
        functools.partial(body, sizes),
        mesh=split,
        in_specs=(
            P(None, None, AXES),
            P(None, AXES),
            P(AXES),
            P(AXES),
            P(AXES[:3], "col"),
            P(AXES[:3], "col"),
        ),
        out_specs=P(None, None, AXES),
        check_vma=False,
    )
```

```python
import functools
import math

import jax
import jax.numpy as jnp
from jax import lax
from jax.experimental import pallas as pl
from jax.experimental.pallas import tpu as pltpu
from jax.sharding import PartitionSpec as P

ITERS = 3
BLOB_SQ = 0.0025
INV_EIGHT_PI = 1.0 / (8.0 * math.pi)
ROWS = 8
HALF = 3
FIRST, LATER = 11, 10
ORDER = (0, 2, 1)
AXES = ("top", "mid", "core", "col")
F32 = jnp.float32
BF16 = jnp.bfloat16


def low_half(shape):
    return lax.broadcasted_iota(jnp.int32, shape, len(shape) - 1) < 64


def xor_perm(n, m):
    return [(d, d ^ m) for d in range(n)]


def spread(rows, n):
    wide = rows.reshape(n, -1, 1, 128)
    return lax.all_to_all(wide, AXES, 0, 0, tiled=True).reshape(rows.shape)


def each(count, step):
    if count <= 16:
        for i in range(count):
            step(i)
    else:
        pl.loop(0, count)(step)


class Sums:
    def __init__(self, count, refs):
        self.refs = refs
        self.parts = [[None] * 4 for _ in range(count)]
        if refs is not None:
            for at in range(count):
                refs[at] = jnp.zeros((ROWS, 128), F32)

    def add(self, chunk, at, left, right):
        part = sum(left[a] * right[a] for a in range(3))
        if self.refs is not None:
            self.refs[at] = self.refs[at] + part
            return
        held = self.parts[at]
        slot = chunk % 4
        held[slot] = part if held[slot] is None else held[slot] + part

    def get(self, at):
        if self.refs is not None:
            total = self.refs[at]
        else:
            held = self.parts[at]
            total = (held[0] + held[1]) + (held[2] + held[3])
        return jnp.broadcast_to(jnp.sum(total, axis=1, keepdims=True), (ROWS, 128))


def chunk_parts(piece, chunk, me, n_row, n_col, size, at, count):
    half = n_row // 2
    o = chunk // half
    u = chunk % half
    even = piece[pl.ds((me ^ ((2 * u) * n_col + o)) * size + at, count)]
    odd = piece[pl.ds((me ^ ((2 * u + 1) * n_col + o)) * size + at, count)]
    low = low_half((count, 128))
    first = jnp.where(low, even, pltpu.roll(odd, 64, 1))
    second = jnp.where(low, pltpu.roll(even, 64, 1), odd)
    return jnp.concatenate([first, second], axis=0)


PAIRS = [(i, j) for i in range(ITERS) for j in range(i + 1, ITERS)]


def place_of(j):
    lane = lax.broadcasted_iota(jnp.int32, (ROWS, 128), 1)
    return lane == lax.broadcasted_iota(jnp.int32, (ROWS, 128), 0) * (ITERS + 1) + j


def row_sum(acc):
    return jnp.sum(acc, axis=1, keepdims=True)


def lines_of(chunk):
    if isinstance(chunk, int):
        return pl.ds(chunk * 128, 128)
    return pl.ds(pl.multiple_of(chunk * 128, 128), 128)


def write_columns(cols, y, chunk, vec):
    ys = [y[a : a + 1] for a in ORDER]
    f = [vec[a] for a in range(3)]
    g = ys[0] * f[0] + ys[1] * f[1] + ys[2] * f[2]
    groups = f + [g]
    groups += [ys[p] * f[v] for p in range(3) for v in range(3)]
    groups += [ys[a] * g for a in range(3)]
    full = jnp.concatenate(groups, axis=0)
    high = full.astype(BF16)
    low = (full - high.astype(F32)).astype(BF16)
    at = lines_of(chunk)
    cols[0:128, at] = high
    cols[128:256, at] = low


def contract(cols, kernels):
    first = jnp.dot(cols[:128], kernels, preferred_element_type=F32)
    second = jnp.dot(cols[128:], kernels[:, :128], preferred_element_type=F32)
    return first[:, :128] + (second + first[:, 128:])


def products(n_chunk, columns, cols, kernels):
    if n_chunk <= 16:
        for chunk in range(n_chunk):
            columns(chunk)
        return contract(cols[...], kernels[...])
    pl.loop(0, n_chunk)(columns)

    def turn(i, acc):
        at = pl.ds(pl.multiple_of(i * 2048, 2048), 2048)
        return acc + contract(cols[:, at], kernels[at, :])

    return lax.fori_loop(0, n_chunk // 16, turn, jnp.zeros((128, 128), F32))


def image_rows(prod, targets, own, scale):
    both = prod
    two = pltpu.roll(both, 64, 1)

    def group(k):
        return two[8 * k : 8 * k + 8]

    x = [targets[a : a + 1] for a in range(3)]
    images = []
    along = x[0] * group(0) + x[1] * group(1) + x[2] * group(2) - group(3)
    for a in range(3):
        cross = sum(x[b] * group(4 + 3 * a + b) for b in range(3))
        image = both[8 * a : 8 * a + 8] + x[a] * along - cross + group(13 + a)
        images.append((image + targets[3:4] * own[a]) * scale)
    return images


def write_piece(images, out):
    rows = []
    for image in images:
        top, bottom = image[:4], pltpu.roll(image[4:], 64, 1)
        rows.append(jnp.where(low_half((4, 128)), top, bottom))

    def put(m):
        for a in range(3):
            out[pl.ds(m * LATER + HALF * a, 4)] = rows[a]

    each_wide(out.shape[0] // LATER, put)


def each_wide(count, put):
    if count <= 64:
        for m in range(count):
            put(m)
    else:
        pl.loop(0, count)(put)


def pack_kernel(*refs):
    sources, outs, held, sems = refs[:6], refs[6:9], refs[9:15], refs[15]
    out, tgt, lists = outs
    copies = [
        pltpu.make_async_copy(src, dst, sems.at[i])
        for i, (src, dst) in enumerate(zip(sources, held))
    ]
    for copy in copies:
        copy.start()
    for copy in copies:
        copy.wait()
    velocity, points, area, self_term, index, weight = held
    count = index.shape[0]
    lists[:count] = index[...].astype(F32)
    lists[count:] = weight[...]
    field = velocity[...]
    spot = points[...]
    rows = []
    for a in range(3):
        vec = field[:, a, :]
        rows.append(jnp.concatenate([vec[:HALF], vec[HALF:]], axis=1))
    mine = jnp.concatenate([spot, self_term[...]], axis=0)
    mine = jnp.concatenate([mine, mine], axis=1)
    tgt[...] = jnp.concatenate([mine, mine], axis=0)
    left = jnp.concatenate([spot[0:1], spot[2:3]], axis=0)
    right = jnp.concatenate([spot[1:2], area[...]], axis=0)
    rows.append(jnp.concatenate([left, right], axis=1))
    message = jnp.concatenate(rows, axis=0)

    def put(m):
        out[pl.ds(m * FIRST, FIRST)] = message

    each_wide(out.shape[0] // FIRST, put)


def extra_kernel(half_chunks, me, *refs):
    near, out = refs[:-1], refs[-1]
    row, col = me[1], me[2]
    lines = lax.broadcasted_iota(jnp.int32, (128, 128), 0).astype(F32)
    for o, lists in enumerate(near):
        count = lists.shape[0] // 2
        half = count // 2
        low = low_half((half, 128))
        odd = col % 2 == 1
        both = lists[:, lines_of(col // 2)]
        place = both[:count].astype(jnp.int32)
        place = (((place // 64) ^ row) * 64 + place % 64).astype(F32)
        packed = []
        for value in (place, both[count:]):
            top, bottom = value[:half], value[half:]
            lower = jnp.where(low, top, pltpu.roll(bottom, 64, 1))
            upper = jnp.where(low, pltpu.roll(top, 64, 1), bottom)
            packed.append(jnp.where(odd, upper, lower))
        index, weight = packed

        def build(u):
            line = lines + (u * 128.0 if isinstance(u, int) else (u * 128).astype(F32))
            total = jnp.zeros((128, 128), F32)
            for k in range(half):
                total = total + jnp.where(line == index[k : k + 1], weight[k : k + 1], 0.0)
            turned = total.T
            out[o * half_chunks + u] = turned[:64] + turned[64:]

        each(half_chunks, build)


def first_kernel(
    n_row, n_col, piece, extra, tgt, me_ref, kernels, places, basis, norm_out, out, cols, *sums
):
    n_chunk = n_row * n_col // 2
    me = me_ref[0]
    total = Sums(1, sums[0] if sums else None)

    def unpack(chunk):
        vec = [
            chunk_parts(piece, chunk, me, n_row, n_col, FIRST, HALF * a, 4)
            for a in range(3)
        ]
        spot = chunk_parts(piece, chunk, me, n_row, n_col, FIRST, 3 * HALF, 2)
        places[chunk] = spot
        for a in range(3):
            basis[chunk, a] = vec[a]
        total.add(chunk, 0, vec, vec)
        write_columns(cols, spot, chunk, vec)

    turned = tgt[...].T
    x = [jnp.broadcast_to(turned[:64, a : a + 1], (64, 128)) for a in range(3)]

    def build(chunk):
        unpack(chunk)
        y = places[chunk]
        d = [x[a] - y[k : k + 1] for a, k in enumerate(ORDER)]
        dist = d[0] * d[0] + d[1] * d[1] + d[2] * d[2]
        root = lax.rsqrt(dist + BLOB_SQ)
        two = (y[3:4] * INV_EIGHT_PI) * root * root * root
        one = (dist + 2.0 * BLOB_SQ) * two + extra[chunk]
        value = jnp.concatenate([one, two], axis=0).T
        high = value.astype(BF16)
        at = lines_of(chunk)
        kernels[at, 0:128] = high
        kernels[at, 128:256] = (value - high.astype(F32)).astype(BF16)

    prod = products(n_chunk, build, cols, kernels)
    norm = jnp.sqrt(total.get(0))
    scale = 1.0 / norm
    norm_out[0] = norm
    norm_out[1] = scale
    write_piece(image_rows(prod, tgt, basis[0], scale), out)


def middle_kernel(n_row, n_col, n_base, final, piece, *refs):
    bases, norms = refs[:n_base], refs[n_base : 2 * n_base]
    if final:
        kernels, places, tgt, me_ref, own, h_out, out, basis, cols, *held = refs[2 * n_base :]
    else:
        kernels, places, tgt, me_ref, basis, h_out, out, cols, *held = refs[2 * n_base :]
    n_chunk = n_row * n_col // 2
    me = me_ref[0]
    scales = [norm[norm.shape[0] - 1] for norm in norms]
    cross = [(i, j) for i in range(n_base) for j in range(i)]
    sums = Sums(2 * n_base + 1 + len(cross), held[0] if held else None)

    def unpack(chunk):
        vec = [
            chunk_parts(piece, chunk, me, n_row, n_col, LATER, HALF * a, 4)
            for a in range(3)
        ]
        old = [[base[chunk, a] for a in range(3)] for base in bases]
        for a in range(3):
            basis[chunk, a] = vec[a]
        for j in range(n_base):
            sums.add(chunk, j, vec, old[j])
        for at, (i, j) in enumerate(cross):
            sums.add(chunk, 2 * n_base + 1 + at, old[i], old[j])

    each(n_chunk, unpack)
    gram = {}
    for at, (i, j) in enumerate(cross):
        gram[j, i] = sums.get(2 * n_base + 1 + at) * (scales[i] * scales[j])
    column = []
    for j in range(n_base):
        h = sums.get(j) * scales[j]
        for i in range(j):
            h = h - column[i] * gram[i, j]
        column.append(h)
        h_out[j] = h
    factors = [h * scale for h, scale in zip(column, scales)]

    def columns(chunk):
        old = [[base[chunk, a] for a in range(3)] for base in bases]
        vec = []
        for a in range(3):
            value = basis[chunk, a]
            for j in range(n_base):
                value = value - factors[j] * old[j][a]
            vec.append(value)
            basis[chunk, a] = value
        sums.add(chunk, n_base, vec, vec)
        write_columns(cols, places[chunk], chunk, vec)
        if final:
            for j in range(n_base):
                sums.add(chunk, n_base + 1 + j, vec, old[j])

    prod = products(n_chunk, columns, cols, kernels)
    norm = jnp.sqrt(sums.get(n_base))
    scale = 1.0 / norm
    h_out[n_base] = norm
    images = image_rows(prod, tgt, basis[0], scale)
    if not final:
        h_out[n_base + 1] = scale
        write_piece(images, out)
        return
    every = [*bases, basis]
    for j, base in enumerate(every):
        for a in range(3):
            own[j, a] = base[0, a] * [*scales, scale][j]
    for j in range(n_base):
        gram[j, n_base] = sums.get(n_base + 1 + j) * (scale * scales[j])
    for at, pair in enumerate(PAIRS):
        h_out[n_base + 1 + at] = gram[pair]
    low = low_half((ROWS, 128))
    row = jnp.zeros((ROWS, 128), F32)
    for j in range(ITERS + 1):
        other = images if j == ITERS else [own[j, a] for a in range(3)]
        part = sum(images[a] * other[a] for a in range(3))
        part = row_sum(jnp.where(low, part, 0.0))
        row = row + jnp.where(place_of(j), part, 0.0)
    row = jnp.sum(row, axis=0, keepdims=True)

    def put(m):
        out[pl.ds(m, 1)] = row

    each_wide(out.shape[0], put)


def solve_small(hessen, start_norm, count):
    zero = jnp.zeros_like(start_norm)
    target = [start_norm] + [zero] * count
    cosines = []
    sines = []
    triangle = {}
    for k in range(count):
        column = [hessen[i, k] for i in range(k + 2)]
        for j in range(k):
            first_val = column[j]
            second_val = column[j + 1]
            column[j] = cosines[j] * first_val + sines[j] * second_val
            column[j + 1] = cosines[j] * second_val - sines[j] * first_val
        radius = jnp.sqrt(column[k] * column[k] + column[k + 1] * column[k + 1])
        cosine = column[k] / radius
        sine = column[k + 1] / radius
        cosines.append(cosine)
        sines.append(sine)
        for i in range(k):
            triangle[i, k] = column[i]
        triangle[k, k] = radius
        target[k + 1] = -sine * target[k]
        target[k] = cosine * target[k]
    coeffs = [None] * count
    for k in range(count - 1, -1, -1):
        accum = target[k]
        for i in range(k + 1, count):
            accum = accum - triangle[k, i] * coeffs[i]
        coeffs[k] = accum / triangle[k, k]
    return coeffs


def last_kernel(sums, own, *refs):
    columns = refs[: ITERS - 1]
    norm, out = refs[ITERS - 1 :]
    hessen = {}
    for k in range(ITERS - 1):
        for j in range(k + 2):
            hessen[j, k] = columns[k][j]
    gram = {(j, j): 1.0 for j in range(ITERS)}
    for at, (i, j) in enumerate(PAIRS):
        gram[i, j] = gram[j, i] = columns[-1][ITERS + at]
    row = jnp.broadcast_to(jnp.sum(sums[...], axis=0, keepdims=True), (ROWS, 128))
    inner = [
        jnp.broadcast_to(row_sum(jnp.where(place_of(j), row, 0.0)), (ROWS, 128))
        for j in range(ITERS + 1)
    ]
    square = inner[ITERS]
    for j in range(ITERS):
        h = inner[j]
        for i in range(j):
            h = h - hessen[i, ITERS - 1] * gram[i, j]
        hessen[j, ITERS - 1] = h
    for j in range(ITERS):
        rest = -2.0 * inner[j]
        for i in range(ITERS):
            rest = rest + hessen[i, ITERS - 1] * gram[i, j]
        square = square + hessen[j, ITERS - 1] * rest
    hessen[ITERS, ITERS - 1] = jnp.sqrt(jnp.maximum(square, 0.0))
    coeffs = solve_small(hessen, norm[0], ITERS)
    for a in range(3):
        density = sum(coeffs[k] * own[k, a] for k in range(ITERS))
        out[:HALF, a, :] = density[:HALF, :64]
        out[HALF:, a, :] = density[4 : 4 + HALF, :64]


def call(kernel, outs, scratch, operands, scalars=(), far=(), flops=0):
    vmem = pl.BlockSpec(memory_space=pltpu.VMEM)
    smem = pl.BlockSpec(memory_space=pltpu.SMEM)
    count = len(operands)
    hbm = pl.BlockSpec(memory_space=pltpu.HBM)
    specs = [smem if i in scalars else hbm if i in far else vmem for i in range(count)]
    moved = sum(x.size * x.dtype.itemsize for x in operands)
    return pl.pallas_call(
        kernel,
        out_shape=[jax.ShapeDtypeStruct(s, t) for s, t in outs],
        in_specs=specs,
        out_specs=[vmem] * len(outs),
        scratch_shapes=scratch,
        cost_estimate=pl.CostEstimate(flops=flops, bytes_accessed=moved, transcendentals=0),
        compiler_params=pltpu.CompilerParams(vmem_limit_bytes=48 * 1024 * 1024),
    )(*operands)


def body(sizes, velocity, points, panel_area, self_term, near_index, near_weight):
    n_row, n_col = sizes[0] * sizes[1] * sizes[2], sizes[3]
    n = n_row * n_col
    n_chunk = n // 2
    total = n * 64
    row = lax.axis_index(AXES[:3])
    col = lax.axis_index("col")
    me = jnp.stack([row * n_col + col, row, col]).astype(jnp.int32)
    rhs = velocity.shape[0]

    message = ((n * LATER, 128), F32)
    sources = [
        velocity,
        points,
        panel_area[None],
        self_term[None],
        near_index.T,
        near_weight.T,
    ]
    wide, tgt, lists = call(
        pack_kernel,
        [
            ((n * FIRST, 128), F32),
            ((8, 128), F32),
            ((2 * near_index.shape[1], near_index.shape[0]), F32),
        ],
        [pltpu.VMEM(x.shape, x.dtype) for x in sources] + [pltpu.SemaphoreType.DMA((6,))],
        [pltpu.with_memory_space_constraint(x, pltpu.HBM) for x in sources],
        far=range(6),
    )
    piece = spread(wide, n)
    near = [lists] + [lax.ppermute(lists, "col", xor_perm(n_col, o)) for o in range(1, n_col)]
    (extra,) = call(
        functools.partial(extra_kernel, n_row // 2),
        [((n_chunk, 64, 128), F32)],
        [],
        [me, *near],
        {0},
        flops=10**9,
    )

    vec_shape = (n_chunk, 3, ROWS, 128)
    cols = pltpu.VMEM((256, total), BF16)
    held = [] if n_chunk <= 16 else [pltpu.VMEM((8, ROWS, 128), F32)]
    kernels, places, basis, norm, wide = call(
        functools.partial(first_kernel, n_row, n_col),
        [
            ((total, 256), BF16),
            ((n_chunk, 4, 128), F32),
            (vec_shape, F32),
            ((2, ROWS, 128), F32),
            message,
        ],
        [cols, *held],
        [piece, extra, tgt, me],
        {3},
    )
    bases = [basis]
    columns = [norm]
    for k in range(1, ITERS):
        final = k == ITERS - 1
        piece = spread(wide, n)
        main, column, wide = call(
            functools.partial(middle_kernel, n_row, n_col, k, final),
            [
                ((ITERS, 3, ROWS, 128) if final else vec_shape, F32),
                ((k + 1 + (len(PAIRS) if final else 1), ROWS, 128), F32),
                ((n, 128), F32) if final else message,
            ],
            [*([pltpu.VMEM(vec_shape, F32)] if final else []), cols, *held],
            [piece, *bases, *columns, kernels, places, tgt, me],
            {2 * k + 4},
        )
        bases.append(main)
        columns.append(column)
    sums = spread(wide, n)
    (density,) = call(
        last_kernel, [((rhs, 3, 64), F32)], [], [sums, bases[-1], *columns[1:], columns[0]]
    )
    return density


def solution(mesh):
    n_row, n_col = mesh.shape["row"], mesh.shape["col"]
    sizes = (n_row // 4, 2, 2, n_col)
    split = jax.sharding.Mesh(mesh.devices.reshape(sizes), AXES)
    return jax.shard_map(
        functools.partial(body, sizes),
        mesh=split,
        in_specs=(
            P(None, None, AXES),
            P(None, AXES),
            P(AXES),
            P(AXES),
            P(AXES[:3], "col"),
            P(AXES[:3], "col"),
        ),
        out_specs=P(None, None, AXES),
        check_vma=False,
    )
```

```python
import functools
import math

import jax
import jax.numpy as jnp
from jax import lax
from jax.experimental import pallas as pl
from jax.experimental.pallas import tpu as pltpu
from jax.sharding import PartitionSpec as P

ITERS = 3
BLOB_SQ = 0.0025
INV_EIGHT_PI = 1.0 / (8.0 * math.pi)
ROWS = 8
HALF = 3
FIRST, LATER = 11, 10
ORDER = (0, 2, 1)
AXES = ("top", "mid", "core", "col")
F32 = jnp.float32
BF16 = jnp.bfloat16


def low_half(shape):
    return lax.broadcasted_iota(jnp.int32, shape, len(shape) - 1) < 64


def xor_perm(n, m):
    return [(d, d ^ m) for d in range(n)]


def spread(rows, n):
    wide = rows.reshape(n, -1, 1, 128)
    return lax.all_to_all(wide, AXES, 0, 0, tiled=True).reshape(rows.shape)


def each(count, step):
    if count <= 16:
        for i in range(count):
            step(i)
    else:
        pl.loop(0, count)(step)


class Sums:
    def __init__(self, count, refs):
        self.refs = refs
        self.parts = [[None] * 4 for _ in range(count)]
        if refs is not None:
            for at in range(count):
                refs[at] = jnp.zeros((ROWS, 128), F32)

    def add(self, chunk, at, left, right):
        part = sum(left[a] * right[a] for a in range(3))
        if self.refs is not None:
            self.refs[at] = self.refs[at] + part
            return
        held = self.parts[at]
        slot = chunk % 4
        held[slot] = part if held[slot] is None else held[slot] + part

    def get(self, at):
        if self.refs is not None:
            total = self.refs[at]
        else:
            held = self.parts[at]
            total = (held[0] + held[1]) + (held[2] + held[3])
        return jnp.broadcast_to(jnp.sum(total, axis=1, keepdims=True), (ROWS, 128))


def chunk_parts(piece, chunk, me, n_row, n_col, size, at, count):
    half = n_row // 2
    o = chunk // half
    u = chunk % half
    even = piece[pl.ds((me ^ ((2 * u) * n_col + o)) * size + at, count)]
    odd = piece[pl.ds((me ^ ((2 * u + 1) * n_col + o)) * size + at, count)]
    low = low_half((count, 128))
    first = jnp.where(low, even, pltpu.roll(odd, 64, 1))
    second = jnp.where(low, pltpu.roll(even, 64, 1), odd)
    return jnp.concatenate([first, second], axis=0)


PAIRS = [(i, j) for i in range(ITERS) for j in range(i + 1, ITERS)]


def place_of(j):
    lane = lax.broadcasted_iota(jnp.int32, (ROWS, 128), 1)
    return lane == lax.broadcasted_iota(jnp.int32, (ROWS, 128), 0) * (ITERS + 1) + j


def row_sum(acc):
    return jnp.sum(acc, axis=1, keepdims=True)


def lines_of(chunk):
    if isinstance(chunk, int):
        return pl.ds(chunk * 128, 128)
    return pl.ds(pl.multiple_of(chunk * 128, 128), 128)


def halves(value):
    scaled = value * 65537.0
    high = scaled - (scaled - value)
    return high.astype(BF16), (value - high).astype(BF16)


def write_columns(cols, y, chunk, vec):
    ys = [y[a : a + 1] for a in ORDER]
    f = [vec[a] for a in range(3)]
    g = ys[0] * f[0] + ys[1] * f[1] + ys[2] * f[2]
    groups = f + [g]
    groups += [ys[p] * f[v] for p in range(3) for v in range(3)]
    groups += [ys[a] * g for a in range(3)]
    full = jnp.concatenate(groups, axis=0)
    high, low = halves(full)
    at = lines_of(chunk)
    cols[0:128, at] = high
    cols[128:256, at] = low


def contract(cols, kernels):
    first = jnp.dot(cols[:128], kernels, preferred_element_type=F32)
    second = jnp.dot(cols[128:], kernels[:, :128], preferred_element_type=F32)
    return first[:, :128] + (second + first[:, 128:])


def products(n_chunk, columns, cols, kernels):
    if n_chunk <= 16:
        for chunk in range(n_chunk):
            columns(chunk)
        return contract(cols[...], kernels[...])
    pl.loop(0, n_chunk)(columns)

    def turn(i, acc):
        at = pl.ds(pl.multiple_of(i * 2048, 2048), 2048)
        return acc + contract(cols[:, at], kernels[at, :])

    return lax.fori_loop(0, n_chunk // 16, turn, jnp.zeros((128, 128), F32))


def image_rows(prod, targets, own, scale):
    both = prod
    two = pltpu.roll(both, 64, 1)

    def group(k):
        return two[8 * k : 8 * k + 8]

    x = [targets[a : a + 1] for a in range(3)]
    images = []
    along = x[0] * group(0) + x[1] * group(1) + x[2] * group(2) - group(3)
    for a in range(3):
        cross = sum(x[b] * group(4 + 3 * a + b) for b in range(3))
        image = both[8 * a : 8 * a + 8] + x[a] * along - cross + group(13 + a)
        images.append((image + targets[3:4] * own[a]) * scale)
    return images


def write_piece(images, out):
    rows = []
    for image in images:
        top, bottom = image[:4], pltpu.roll(image[4:], 64, 1)
        rows.append(jnp.where(low_half((4, 128)), top, bottom))

    def put(m):
        for a in range(3):
            out[pl.ds(m * LATER + HALF * a, 4)] = rows[a]

    each_wide(out.shape[0] // LATER, put)


def each_wide(count, put):
    if count <= 64:
        for m in range(count):
            put(m)
    else:
        pl.loop(0, count)(put)


def pack_kernel(*refs):
    sources, outs, held, sems = refs[:6], refs[6:9], refs[9:15], refs[15]
    out, tgt, lists = outs
    copies = [
        pltpu.make_async_copy(src, dst, sems.at[i])
        for i, (src, dst) in enumerate(zip(sources, held))
    ]
    for copy in copies:
        copy.start()
    for copy in copies:
        copy.wait()
    velocity, points, area, self_term, index, weight = held
    count = index.shape[0]
    lists[:count] = index[...].astype(F32)
    lists[count:] = weight[...]
    field = velocity[...]
    spot = points[...]
    rows = []
    for a in range(3):
        vec = field[:, a, :]
        rows.append(jnp.concatenate([vec[:HALF], vec[HALF:]], axis=1))
    mine = jnp.concatenate([spot, self_term[...]], axis=0)
    mine = jnp.concatenate([mine, mine], axis=1)
    tgt[...] = jnp.concatenate([mine, mine], axis=0)
    left = jnp.concatenate([spot[0:1], spot[2:3]], axis=0)
    right = jnp.concatenate([spot[1:2], area[...]], axis=0)
    rows.append(jnp.concatenate([left, right], axis=1))
    message = jnp.concatenate(rows, axis=0)

    def put(m):
        out[pl.ds(m * FIRST, FIRST)] = message

    each_wide(out.shape[0] // FIRST, put)


def extra_kernel(half_chunks, me, *refs):
    near, out = refs[:-1], refs[-1]
    row, col = me[1], me[2]
    lines = lax.broadcasted_iota(jnp.int32, (128, 128), 0).astype(F32)
    for o, lists in enumerate(near):
        count = lists.shape[0] // 2
        half = count // 2
        low = low_half((half, 128))
        odd = col % 2 == 1
        both = lists[:, lines_of(col // 2)]
        place = both[:count].astype(jnp.int32)
        place = (((place // 64) ^ row) * 64 + place % 64).astype(F32)
        packed = []
        for value in (place, both[count:]):
            top, bottom = value[:half], value[half:]
            lower = jnp.where(low, top, pltpu.roll(bottom, 64, 1))
            upper = jnp.where(low, pltpu.roll(top, 64, 1), bottom)
            packed.append(jnp.where(odd, upper, lower))
        index, weight = packed

        def build(u):
            line = lines + (u * 128.0 if isinstance(u, int) else (u * 128).astype(F32))
            total = jnp.zeros((128, 128), F32)
            for k in range(half):
                total = total + jnp.where(line == index[k : k + 1], weight[k : k + 1], 0.0)
            turned = total.T
            out[o * half_chunks + u] = turned[:64] + turned[64:]

        each(half_chunks, build)


def first_kernel(
    n_row, n_col, piece, extra, tgt, me_ref, kernels, places, basis, norm_out, out, cols, *sums
):
    n_chunk = n_row * n_col // 2
    me = me_ref[0]
    total = Sums(1, sums[0] if sums else None)

    def unpack(chunk):
        vec = [
            chunk_parts(piece, chunk, me, n_row, n_col, FIRST, HALF * a, 4)
            for a in range(3)
        ]
        spot = chunk_parts(piece, chunk, me, n_row, n_col, FIRST, 3 * HALF, 2)
        places[chunk] = spot
        for a in range(3):
            basis[chunk, a] = vec[a]
        total.add(chunk, 0, vec, vec)
        write_columns(cols, spot, chunk, vec)

    turned = tgt[...].T
    x = [jnp.broadcast_to(turned[:64, a : a + 1], (64, 128)) for a in range(3)]

    def build(chunk):
        unpack(chunk)
        y = places[chunk]
        d = [x[a] - y[k : k + 1] for a, k in enumerate(ORDER)]
        dist = d[0] * d[0] + d[1] * d[1] + d[2] * d[2]
        root = lax.rsqrt(dist + BLOB_SQ)
        two = (y[3:4] * INV_EIGHT_PI) * root * root * root
        one = (dist + 2.0 * BLOB_SQ) * two + extra[chunk]
        value = jnp.concatenate([one, two], axis=0).T
        high, low = halves(value)
        at = lines_of(chunk)
        kernels[at, 0:128] = high
        kernels[at, 128:256] = low

    prod = products(n_chunk, build, cols, kernels)
    norm = jnp.sqrt(total.get(0))
    scale = 1.0 / norm
    norm_out[0] = norm
    norm_out[1] = scale
    write_piece(image_rows(prod, tgt, basis[0], scale), out)


def middle_kernel(n_row, n_col, n_base, final, piece, *refs):
    bases, norms = refs[:n_base], refs[n_base : 2 * n_base]
    if final:
        kernels, places, tgt, me_ref, own, h_out, out, basis, cols, *held = refs[2 * n_base :]
    else:
        kernels, places, tgt, me_ref, basis, h_out, out, cols, *held = refs[2 * n_base :]
    n_chunk = n_row * n_col // 2
    me = me_ref[0]
    scales = [norm[norm.shape[0] - 1] for norm in norms]
    cross = [(i, j) for i in range(n_base) for j in range(i)]
    sums = Sums(2 * n_base + 1 + len(cross), held[0] if held else None)

    def unpack(chunk):
        vec = [
            chunk_parts(piece, chunk, me, n_row, n_col, LATER, HALF * a, 4)
            for a in range(3)
        ]
        old = [[base[chunk, a] for a in range(3)] for base in bases]
        for a in range(3):
            basis[chunk, a] = vec[a]
        for j in range(n_base):
            sums.add(chunk, j, vec, old[j])
        for at, (i, j) in enumerate(cross):
            sums.add(chunk, 2 * n_base + 1 + at, old[i], old[j])

    each(n_chunk, unpack)
    gram = {}
    for at, (i, j) in enumerate(cross):
        gram[j, i] = sums.get(2 * n_base + 1 + at) * (scales[i] * scales[j])
    column = []
    for j in range(n_base):
        h = sums.get(j) * scales[j]
        for i in range(j):
            h = h - column[i] * gram[i, j]
        column.append(h)
        h_out[j] = h
    factors = [h * scale for h, scale in zip(column, scales)]

    def columns(chunk):
        old = [[base[chunk, a] for a in range(3)] for base in bases]
        vec = []
        for a in range(3):
            value = basis[chunk, a]
            for j in range(n_base):
                value = value - factors[j] * old[j][a]
            vec.append(value)
            basis[chunk, a] = value
        sums.add(chunk, n_base, vec, vec)
        write_columns(cols, places[chunk], chunk, vec)
        if final:
            for j in range(n_base):
                sums.add(chunk, n_base + 1 + j, vec, old[j])

    prod = products(n_chunk, columns, cols, kernels)
    norm = jnp.sqrt(sums.get(n_base))
    scale = 1.0 / norm
    h_out[n_base] = norm
    images = image_rows(prod, tgt, basis[0], scale)
    if not final:
        h_out[n_base + 1] = scale
        write_piece(images, out)
        return
    every = [*bases, basis]
    for j, base in enumerate(every):
        for a in range(3):
            own[j, a] = base[0, a] * [*scales, scale][j]
    for j in range(n_base):
        gram[j, n_base] = sums.get(n_base + 1 + j) * (scale * scales[j])
    for at, pair in enumerate(PAIRS):
        h_out[n_base + 1 + at] = gram[pair]
    low = low_half((ROWS, 128))
    row = jnp.zeros((ROWS, 128), F32)
    for j in range(ITERS + 1):
        other = images if j == ITERS else [own[j, a] for a in range(3)]
        part = sum(images[a] * other[a] for a in range(3))
        part = row_sum(jnp.where(low, part, 0.0))
        row = row + jnp.where(place_of(j), part, 0.0)
    row = jnp.sum(row, axis=0, keepdims=True)

    def put(m):
        out[pl.ds(m, 1)] = row

    each_wide(out.shape[0], put)


def solve_small(hessen, start_norm, count):
    zero = jnp.zeros_like(start_norm)
    target = [start_norm] + [zero] * count
    cosines = []
    sines = []
    triangle = {}
    for k in range(count):
        column = [hessen[i, k] for i in range(k + 2)]
        for j in range(k):
            first_val = column[j]
            second_val = column[j + 1]
            column[j] = cosines[j] * first_val + sines[j] * second_val
            column[j + 1] = cosines[j] * second_val - sines[j] * first_val
        radius = jnp.sqrt(column[k] * column[k] + column[k + 1] * column[k + 1])
        cosine = column[k] / radius
        sine = column[k + 1] / radius
        cosines.append(cosine)
        sines.append(sine)
        for i in range(k):
            triangle[i, k] = column[i]
        triangle[k, k] = radius
        target[k + 1] = -sine * target[k]
        target[k] = cosine * target[k]
    coeffs = [None] * count
    for k in range(count - 1, -1, -1):
        accum = target[k]
        for i in range(k + 1, count):
            accum = accum - triangle[k, i] * coeffs[i]
        coeffs[k] = accum / triangle[k, k]
    return coeffs


def last_kernel(sums, own, *refs):
    columns = refs[: ITERS - 1]
    norm, out = refs[ITERS - 1 :]
    hessen = {}
    for k in range(ITERS - 1):
        for j in range(k + 2):
            hessen[j, k] = columns[k][j]
    gram = {(j, j): 1.0 for j in range(ITERS)}
    for at, (i, j) in enumerate(PAIRS):
        gram[i, j] = gram[j, i] = columns[-1][ITERS + at]
    row = jnp.broadcast_to(jnp.sum(sums[...], axis=0, keepdims=True), (ROWS, 128))
    inner = [
        jnp.broadcast_to(row_sum(jnp.where(place_of(j), row, 0.0)), (ROWS, 128))
        for j in range(ITERS + 1)
    ]
    square = inner[ITERS]
    for j in range(ITERS):
        h = inner[j]
        for i in range(j):
            h = h - hessen[i, ITERS - 1] * gram[i, j]
        hessen[j, ITERS - 1] = h
    for j in range(ITERS):
        rest = -2.0 * inner[j]
        for i in range(ITERS):
            rest = rest + hessen[i, ITERS - 1] * gram[i, j]
        square = square + hessen[j, ITERS - 1] * rest
    hessen[ITERS, ITERS - 1] = jnp.sqrt(jnp.maximum(square, 0.0))
    coeffs = solve_small(hessen, norm[0], ITERS)
    for a in range(3):
        density = sum(coeffs[k] * own[k, a] for k in range(ITERS))
        out[:HALF, a, :] = density[:HALF, :64]
        out[HALF:, a, :] = density[4 : 4 + HALF, :64]


def call(kernel, outs, scratch, operands, scalars=(), far=(), flops=0):
    vmem = pl.BlockSpec(memory_space=pltpu.VMEM)
    smem = pl.BlockSpec(memory_space=pltpu.SMEM)
    count = len(operands)
    hbm = pl.BlockSpec(memory_space=pltpu.HBM)
    specs = [smem if i in scalars else hbm if i in far else vmem for i in range(count)]
    moved = sum(x.size * x.dtype.itemsize for x in operands)
    return pl.pallas_call(
        kernel,
        out_shape=[jax.ShapeDtypeStruct(s, t) for s, t in outs],
        in_specs=specs,
        out_specs=[vmem] * len(outs),
        scratch_shapes=scratch,
        cost_estimate=pl.CostEstimate(flops=flops, bytes_accessed=moved, transcendentals=0),
        compiler_params=pltpu.CompilerParams(vmem_limit_bytes=48 * 1024 * 1024),
    )(*operands)


def body(sizes, velocity, points, panel_area, self_term, near_index, near_weight):
    n_row, n_col = sizes[0] * sizes[1] * sizes[2], sizes[3]
    n = n_row * n_col
    n_chunk = n // 2
    total = n * 64
    row = lax.axis_index(AXES[:3])
    col = lax.axis_index("col")
    me = jnp.stack([row * n_col + col, row, col]).astype(jnp.int32)
    rhs = velocity.shape[0]

    message = ((n * LATER, 128), F32)
    sources = [
        velocity,
        points,
        panel_area[None],
        self_term[None],
        near_index.T,
        near_weight.T,
    ]
    wide, tgt, lists = call(
        pack_kernel,
        [
            ((n * FIRST, 128), F32),
            ((8, 128), F32),
            ((2 * near_index.shape[1], near_index.shape[0]), F32),
        ],
        [pltpu.VMEM(x.shape, x.dtype) for x in sources] + [pltpu.SemaphoreType.DMA((6,))],
        [pltpu.with_memory_space_constraint(x, pltpu.HBM) for x in sources],
        far=range(6),
    )
    piece = spread(wide, n)
    near = [lists] + [lax.ppermute(lists, "col", xor_perm(n_col, o)) for o in range(1, n_col)]
    (extra,) = call(
        functools.partial(extra_kernel, n_row // 2),
        [((n_chunk, 64, 128), F32)],
        [],
        [me, *near],
        {0},
        flops=10**9,
    )

    vec_shape = (n_chunk, 3, ROWS, 128)
    cols = pltpu.VMEM((256, total), BF16)
    held = [] if n_chunk <= 16 else [pltpu.VMEM((8, ROWS, 128), F32)]
    kernels, places, basis, norm, wide = call(
        functools.partial(first_kernel, n_row, n_col),
        [
            ((total, 256), BF16),
            ((n_chunk, 4, 128), F32),
            (vec_shape, F32),
            ((2, ROWS, 128), F32),
            message,
        ],
        [cols, *held],
        [piece, extra, tgt, me],
        {3},
    )
    bases = [basis]
    columns = [norm]
    for k in range(1, ITERS):
        final = k == ITERS - 1
        piece = spread(wide, n)
        main, column, wide = call(
            functools.partial(middle_kernel, n_row, n_col, k, final),
            [
                ((ITERS, 3, ROWS, 128) if final else vec_shape, F32),
                ((k + 1 + (len(PAIRS) if final else 1), ROWS, 128), F32),
                ((n, 128), F32) if final else message,
            ],
            [*([pltpu.VMEM(vec_shape, F32)] if final else []), cols, *held],
            [piece, *bases, *columns, kernels, places, tgt, me],
            {2 * k + 4},
        )
        bases.append(main)
        columns.append(column)
    sums = spread(wide, n)
    (density,) = call(
        last_kernel, [((rhs, 3, 64), F32)], [], [sums, bases[-1], *columns[1:], columns[0]]
    )
    return density


def solution(mesh):
    n_row, n_col = mesh.shape["row"], mesh.shape["col"]
    sizes = (n_row // 4, 2, 2, n_col)
    split = jax.sharding.Mesh(mesh.devices.reshape(sizes), AXES)
    return jax.shard_map(
        functools.partial(body, sizes),
        mesh=split,
        in_specs=(
            P(None, None, AXES),
            P(None, AXES),
            P(AXES),
            P(AXES),
            P(AXES[:3], "col"),
            P(AXES[:3], "col"),
        ),
        out_specs=P(None, None, AXES),
        check_vma=False,
    )
```

```python
import functools
import math

import jax
import jax.numpy as jnp
from jax import lax
from jax.experimental import pallas as pl
from jax.experimental.pallas import tpu as pltpu
from jax.sharding import PartitionSpec as P

ITERS = 3
BLOB_SQ = 0.0025
INV_EIGHT_PI = 1.0 / (8.0 * math.pi)
ROWS = 8
HALF = 3
UNROLL = 4
FIRST, LATER = 11, 10
ORDER = (0, 2, 1)
AXES = ("top", "mid", "core", "col")
F32 = jnp.float32
BF16 = jnp.bfloat16


def low_half(shape):
    return lax.broadcasted_iota(jnp.int32, shape, len(shape) - 1) < 64


def xor_perm(n, m):
    return [(d, d ^ m) for d in range(n)]


def spread(rows, n):
    wide = rows.reshape(n, -1, 1, 128)
    return lax.all_to_all(wide, AXES, 0, 0, tiled=True).reshape(rows.shape)


def each(count, step):
    if count <= 16:
        for i in range(count):
            step(i)
    else:
        pl.loop(0, count)(step)


def sweep(n_chunk, count, step):
    def turn(i, sums):
        for inner in range(UNROLL):
            parts = step(i * UNROLL + inner)
            sums = [held + part for held, part in zip(sums, parts)]
        return sums

    zeros = [jnp.zeros((ROWS, 128), F32)] * count
    sums = lax.fori_loop(0, n_chunk // UNROLL, turn, zeros)
    return [
        jnp.broadcast_to(jnp.sum(held, axis=1, keepdims=True), (ROWS, 128)) for held in sums
    ]


def along(left, right):
    return sum(left[a] * right[a] for a in range(3))


def chunk_parts(piece, chunk, me, n_row, n_col, size, at, count):
    half = n_row // 2
    o = chunk // half
    u = chunk % half
    even = piece[pl.ds((me ^ ((2 * u) * n_col + o)) * size + at, count)]
    odd = piece[pl.ds((me ^ ((2 * u + 1) * n_col + o)) * size + at, count)]
    low = low_half((count, 128))
    first = jnp.where(low, even, pltpu.roll(odd, 64, 1))
    second = jnp.where(low, pltpu.roll(even, 64, 1), odd)
    return jnp.concatenate([first, second], axis=0)


PAIRS = [(i, j) for i in range(ITERS) for j in range(i + 1, ITERS)]


def place_of(j):
    lane = lax.broadcasted_iota(jnp.int32, (ROWS, 128), 1)
    return lane == lax.broadcasted_iota(jnp.int32, (ROWS, 128), 0) * (ITERS + 1) + j


def row_sum(acc):
    return jnp.sum(acc, axis=1, keepdims=True)


def lines_of(chunk):
    if isinstance(chunk, int):
        return pl.ds(chunk * 128, 128)
    return pl.ds(pl.multiple_of(chunk * 128, 128), 128)


def write_columns(cols, y, chunk, vec):
    ys = [y[a : a + 1] for a in ORDER]
    f = [vec[a] for a in range(3)]
    g = ys[0] * f[0] + ys[1] * f[1] + ys[2] * f[2]
    groups = f + [g]
    groups += [ys[p] * f[v] for p in range(3) for v in range(3)]
    groups += [ys[a] * g for a in range(3)]
    full = jnp.concatenate(groups, axis=0)
    high = full.astype(BF16)
    low = (full - high.astype(F32)).astype(BF16)
    at = lines_of(chunk)
    cols[0:128, at] = high
    cols[128:256, at] = low


def contract(cols, kernels):
    first = jnp.dot(cols[:128], kernels, preferred_element_type=F32)
    second = jnp.dot(cols[128:], kernels[:, :128], preferred_element_type=F32)
    return first[:, :128] + (second + first[:, 128:])


def products(n_chunk, cols, kernels):
    if n_chunk <= 16:
        return contract(cols[...], kernels[...])

    def turn(i, acc):
        at = pl.ds(pl.multiple_of(i * 2048, 2048), 2048)
        return acc + contract(cols[:, at], kernels[at, :])

    return lax.fori_loop(0, n_chunk // 16, turn, jnp.zeros((128, 128), F32))


def image_rows(prod, targets, own, scale):
    both = prod
    two = pltpu.roll(both, 64, 1)

    def group(k):
        return two[8 * k : 8 * k + 8]

    x = [targets[a : a + 1] for a in range(3)]
    images = []
    along = x[0] * group(0) + x[1] * group(1) + x[2] * group(2) - group(3)
    for a in range(3):
        cross = sum(x[b] * group(4 + 3 * a + b) for b in range(3))
        image = both[8 * a : 8 * a + 8] + x[a] * along - cross + group(13 + a)
        images.append((image + targets[3:4] * own[a]) * scale)
    return images


def write_piece(images, out):
    rows = []
    for image in images:
        top, bottom = image[:4], pltpu.roll(image[4:], 64, 1)
        rows.append(jnp.where(low_half((4, 128)), top, bottom))

    def put(m):
        for a in range(3):
            out[pl.ds(m * LATER + HALF * a, 4)] = rows[a]

    each_wide(out.shape[0] // LATER, put)


def each_wide(count, put):
    if count <= 64:
        for m in range(count):
            put(m)
    else:
        pl.loop(0, count)(put)


def pack_kernel(*refs):
    sources, outs, held, sems = refs[:6], refs[6:9], refs[9:15], refs[15]
    out, tgt, lists = outs
    copies = [
        pltpu.make_async_copy(src, dst, sems.at[i])
        for i, (src, dst) in enumerate(zip(sources, held))
    ]
    for copy in copies:
        copy.start()
    for copy in copies:
        copy.wait()
    velocity, points, area, self_term, index, weight = held
    count = index.shape[0]
    lists[:count] = index[...].astype(F32)
    lists[count:] = weight[...]
    field = velocity[...]
    spot = points[...]
    rows = []
    for a in range(3):
        vec = field[:, a, :]
        rows.append(jnp.concatenate([vec[:HALF], vec[HALF:]], axis=1))
    mine = jnp.concatenate([spot, self_term[...]], axis=0)
    mine = jnp.concatenate([mine, mine], axis=1)
    tgt[...] = jnp.concatenate([mine, mine], axis=0)
    left = jnp.concatenate([spot[0:1], spot[2:3]], axis=0)
    right = jnp.concatenate([spot[1:2], area[...]], axis=0)
    rows.append(jnp.concatenate([left, right], axis=1))
    message = jnp.concatenate(rows, axis=0)

    def put(m):
        out[pl.ds(m * FIRST, FIRST)] = message

    each_wide(out.shape[0] // FIRST, put)


def extra_kernel(half_chunks, me, *refs):
    near, out = refs[:-1], refs[-1]
    row, col = me[1], me[2]
    lines = lax.broadcasted_iota(jnp.int32, (128, 128), 0).astype(F32)
    for o, lists in enumerate(near):
        count = lists.shape[0] // 2
        half = count // 2
        low = low_half((half, 128))
        odd = col % 2 == 1
        both = lists[:, lines_of(col // 2)]
        place = both[:count].astype(jnp.int32)
        place = (((place // 64) ^ row) * 64 + place % 64).astype(F32)
        packed = []
        for value in (place, both[count:]):
            top, bottom = value[:half], value[half:]
            lower = jnp.where(low, top, pltpu.roll(bottom, 64, 1))
            upper = jnp.where(low, pltpu.roll(top, 64, 1), bottom)
            packed.append(jnp.where(odd, upper, lower))
        index, weight = packed

        def build(u):
            line = lines + (u * 128.0 if isinstance(u, int) else (u * 128).astype(F32))
            total = jnp.zeros((128, 128), F32)
            for k in range(half):
                total = total + jnp.where(line == index[k : k + 1], weight[k : k + 1], 0.0)
            turned = total.T
            out[o * half_chunks + u] = turned[:64] + turned[64:]

        each(half_chunks, build)


def first_kernel(
    n_row, n_col, piece, extra, tgt, me_ref, kernels, places, basis, norm_out, out, cols
):
    n_chunk = n_row * n_col // 2
    me = me_ref[0]

    def unpack(chunk):
        vec = [
            chunk_parts(piece, chunk, me, n_row, n_col, FIRST, HALF * a, 4)
            for a in range(3)
        ]
        spot = chunk_parts(piece, chunk, me, n_row, n_col, FIRST, 3 * HALF, 2)
        places[chunk] = spot
        for a in range(3):
            basis[chunk, a] = vec[a]
        write_columns(cols, spot, chunk, vec)
        return along(vec, vec)

    turned = tgt[...].T
    x = [jnp.broadcast_to(turned[:64, a : a + 1], (64, 128)) for a in range(3)]

    def build(chunk):
        square = unpack(chunk)
        y = places[chunk]
        d = [x[a] - y[k : k + 1] for a, k in enumerate(ORDER)]
        dist = d[0] * d[0] + d[1] * d[1] + d[2] * d[2]
        root = lax.rsqrt(dist + BLOB_SQ)
        two = (y[3:4] * INV_EIGHT_PI) * root * root * root
        one = (dist + 2.0 * BLOB_SQ) * two + extra[chunk]
        value = jnp.concatenate([one, two], axis=0).T
        high = value.astype(BF16)
        at = lines_of(chunk)
        kernels[at, 0:128] = high
        kernels[at, 128:256] = (value - high.astype(F32)).astype(BF16)
        return [square]

    (square,) = sweep(n_chunk, 1, build)
    prod = products(n_chunk, cols, kernels)
    norm = jnp.sqrt(square)
    scale = 1.0 / norm
    norm_out[0] = norm
    norm_out[1] = scale
    write_piece(image_rows(prod, tgt, basis[0], scale), out)


def middle_kernel(n_row, n_col, n_base, final, piece, *refs):
    bases, norms = refs[:n_base], refs[n_base : 2 * n_base]
    if final:
        kernels, places, tgt, me_ref, own, h_out, out, basis, cols = refs[2 * n_base :]
    else:
        kernels, places, tgt, me_ref, basis, h_out, out, cols = refs[2 * n_base :]
    n_chunk = n_row * n_col // 2
    me = me_ref[0]
    scales = [norm[norm.shape[0] - 1] for norm in norms]
    cross = [(i, j) for i in range(n_base) for j in range(i)]

    def unpack(chunk):
        vec = [
            chunk_parts(piece, chunk, me, n_row, n_col, LATER, HALF * a, 4)
            for a in range(3)
        ]
        old = [[base[chunk, a] for a in range(3)] for base in bases]
        for a in range(3):
            basis[chunk, a] = vec[a]
        parts = [along(vec, old[j]) for j in range(n_base)]
        return parts + [along(old[i], old[j]) for i, j in cross]

    inner = sweep(n_chunk, n_base + len(cross), unpack)
    gram = {}
    for at, (i, j) in enumerate(cross):
        gram[j, i] = inner[n_base + at] * (scales[i] * scales[j])
    column = []
    for j in range(n_base):
        h = inner[j] * scales[j]
        for i in range(j):
            h = h - column[i] * gram[i, j]
        column.append(h)
        h_out[j] = h
    factors = [h * scale for h, scale in zip(column, scales)]

    def columns(chunk):
        old = [[base[chunk, a] for a in range(3)] for base in bases]
        vec = []
        for a in range(3):
            value = basis[chunk, a]
            for j in range(n_base):
                value = value - factors[j] * old[j][a]
            vec.append(value)
            basis[chunk, a] = value
        write_columns(cols, places[chunk], chunk, vec)
        parts = [along(vec, vec)]
        return parts + ([along(vec, old[j]) for j in range(n_base)] if final else [])

    square, *mixed = sweep(n_chunk, 1 + (n_base if final else 0), columns)
    prod = products(n_chunk, cols, kernels)
    norm = jnp.sqrt(square)
    scale = 1.0 / norm
    h_out[n_base] = norm
    images = image_rows(prod, tgt, basis[0], scale)
    if not final:
        h_out[n_base + 1] = scale
        write_piece(images, out)
        return
    every = [*bases, basis]
    for j, base in enumerate(every):
        for a in range(3):
            own[j, a] = base[0, a] * [*scales, scale][j]
    for j in range(n_base):
        gram[j, n_base] = mixed[j] * (scale * scales[j])
    for at, pair in enumerate(PAIRS):
        h_out[n_base + 1 + at] = gram[pair]
    low = low_half((ROWS, 128))
    row = jnp.zeros((ROWS, 128), F32)
    for j in range(ITERS + 1):
        other = images if j == ITERS else [own[j, a] for a in range(3)]
        part = sum(images[a] * other[a] for a in range(3))
        part = row_sum(jnp.where(low, part, 0.0))
        row = row + jnp.where(place_of(j), part, 0.0)
    row = jnp.sum(row, axis=0, keepdims=True)

    def put(m):
        out[pl.ds(m, 1)] = row

    each_wide(out.shape[0], put)


def solve_small(hessen, start_norm, count):
    zero = jnp.zeros_like(start_norm)
    target = [start_norm] + [zero] * count
    cosines = []
    sines = []
    triangle = {}
    for k in range(count):
        column = [hessen[i, k] for i in range(k + 2)]
        for j in range(k):
            first_val = column[j]
            second_val = column[j + 1]
            column[j] = cosines[j] * first_val + sines[j] * second_val
            column[j + 1] = cosines[j] * second_val - sines[j] * first_val
        radius = jnp.sqrt(column[k] * column[k] + column[k + 1] * column[k + 1])
        cosine = column[k] / radius
        sine = column[k + 1] / radius
        cosines.append(cosine)
        sines.append(sine)
        for i in range(k):
            triangle[i, k] = column[i]
        triangle[k, k] = radius
        target[k + 1] = -sine * target[k]
        target[k] = cosine * target[k]
    coeffs = [None] * count
    for k in range(count - 1, -1, -1):
        accum = target[k]
        for i in range(k + 1, count):
            accum = accum - triangle[k, i] * coeffs[i]
        coeffs[k] = accum / triangle[k, k]
    return coeffs


def last_kernel(sums, own, *refs):
    columns = refs[: ITERS - 1]
    norm, out = refs[ITERS - 1 :]
    hessen = {}
    for k in range(ITERS - 1):
        for j in range(k + 2):
            hessen[j, k] = columns[k][j]
    gram = {(j, j): 1.0 for j in range(ITERS)}
    for at, (i, j) in enumerate(PAIRS):
        gram[i, j] = gram[j, i] = columns[-1][ITERS + at]
    row = jnp.broadcast_to(jnp.sum(sums[...], axis=0, keepdims=True), (ROWS, 128))
    inner = [
        jnp.broadcast_to(row_sum(jnp.where(place_of(j), row, 0.0)), (ROWS, 128))
        for j in range(ITERS + 1)
    ]
    square = inner[ITERS]
    for j in range(ITERS):
        h = inner[j]
        for i in range(j):
            h = h - hessen[i, ITERS - 1] * gram[i, j]
        hessen[j, ITERS - 1] = h
    for j in range(ITERS):
        rest = -2.0 * inner[j]
        for i in range(ITERS):
            rest = rest + hessen[i, ITERS - 1] * gram[i, j]
        square = square + hessen[j, ITERS - 1] * rest
    hessen[ITERS, ITERS - 1] = jnp.sqrt(jnp.maximum(square, 0.0))
    coeffs = solve_small(hessen, norm[0], ITERS)
    for a in range(3):
        density = sum(coeffs[k] * own[k, a] for k in range(ITERS))
        out[:HALF, a, :] = density[:HALF, :64]
        out[HALF:, a, :] = density[4 : 4 + HALF, :64]


def call(kernel, outs, scratch, operands, scalars=(), far=(), flops=0):
    vmem = pl.BlockSpec(memory_space=pltpu.VMEM)
    smem = pl.BlockSpec(memory_space=pltpu.SMEM)
    count = len(operands)
    hbm = pl.BlockSpec(memory_space=pltpu.HBM)
    specs = [smem if i in scalars else hbm if i in far else vmem for i in range(count)]
    moved = sum(x.size * x.dtype.itemsize for x in operands)
    return pl.pallas_call(
        kernel,
        out_shape=[jax.ShapeDtypeStruct(s, t) for s, t in outs],
        in_specs=specs,
        out_specs=[vmem] * len(outs),
        scratch_shapes=scratch,
        cost_estimate=pl.CostEstimate(flops=flops, bytes_accessed=moved, transcendentals=0),
        compiler_params=pltpu.CompilerParams(vmem_limit_bytes=48 * 1024 * 1024),
    )(*operands)


def body(sizes, velocity, points, panel_area, self_term, near_index, near_weight):
    n_row, n_col = sizes[0] * sizes[1] * sizes[2], sizes[3]
    n = n_row * n_col
    n_chunk = n // 2
    total = n * 64
    row = lax.axis_index(AXES[:3])
    col = lax.axis_index("col")
    me = jnp.stack([row * n_col + col, row, col]).astype(jnp.int32)
    rhs = velocity.shape[0]

    message = ((n * LATER, 128), F32)
    sources = [
        velocity,
        points,
        panel_area[None],
        self_term[None],
        near_index.T,
        near_weight.T,
    ]
    wide, tgt, lists = call(
        pack_kernel,
        [
            ((n * FIRST, 128), F32),
            ((8, 128), F32),
            ((2 * near_index.shape[1], near_index.shape[0]), F32),
        ],
        [pltpu.VMEM(x.shape, x.dtype) for x in sources] + [pltpu.SemaphoreType.DMA((6,))],
        [pltpu.with_memory_space_constraint(x, pltpu.HBM) for x in sources],
        far=range(6),
    )
    piece = spread(wide, n)
    near = [lists] + [lax.ppermute(lists, "col", xor_perm(n_col, o)) for o in range(1, n_col)]
    (extra,) = call(
        functools.partial(extra_kernel, n_row // 2),
        [((n_chunk, 64, 128), F32)],
        [],
        [me, *near],
        {0},
        flops=10**9,
    )

    vec_shape = (n_chunk, 3, ROWS, 128)
    cols = pltpu.VMEM((256, total), BF16)
    kernels, places, basis, norm, wide = call(
        functools.partial(first_kernel, n_row, n_col),
        [
            ((total, 256), BF16),
            ((n_chunk, 4, 128), F32),
            (vec_shape, F32),
            ((2, ROWS, 128), F32),
            message,
        ],
        [cols],
        [piece, extra, tgt, me],
        {3},
    )
    bases = [basis]
    columns = [norm]
    for k in range(1, ITERS):
        final = k == ITERS - 1
        piece = spread(wide, n)
        main, column, wide = call(
            functools.partial(middle_kernel, n_row, n_col, k, final),
            [
                ((ITERS, 3, ROWS, 128) if final else vec_shape, F32),
                ((k + 1 + (len(PAIRS) if final else 1), ROWS, 128), F32),
                ((n, 128), F32) if final else message,
            ],
            [*([pltpu.VMEM(vec_shape, F32)] if final else []), cols],
            [piece, *bases, *columns, kernels, places, tgt, me],
            {2 * k + 4},
        )
        bases.append(main)
        columns.append(column)
    sums = spread(wide, n)
    (density,) = call(
        last_kernel, [((rhs, 3, 64), F32)], [], [sums, bases[-1], *columns[1:], columns[0]]
    )
    return density


def solution(mesh):
    n_row, n_col = mesh.shape["row"], mesh.shape["col"]
    sizes = (n_row // 4, 2, 2, n_col)
    split = jax.sharding.Mesh(mesh.devices.reshape(sizes), AXES)
    return jax.shard_map(
        functools.partial(body, sizes),
        mesh=split,
        in_specs=(
            P(None, None, AXES),
            P(None, AXES),
            P(AXES),
            P(AXES),
            P(AXES[:3], "col"),
            P(AXES[:3], "col"),
        ),
        out_specs=P(None, None, AXES),
        check_vma=False,
    )
```

```python
import functools
import math

import jax
import jax.numpy as jnp
from jax import lax
from jax.experimental import pallas as pl
from jax.experimental.pallas import tpu as pltpu
from jax.sharding import PartitionSpec as P

ITERS = 3
BLOB_SQ = 0.0025
INV_EIGHT_PI = 1.0 / (8.0 * math.pi)
ROWS = 8
HALF = 3
FIRST, LATER = 11, 10
ORDER = (0, 2, 1)
AXES = ("top", "mid", "core", "col")
F32 = jnp.float32
BF16 = jnp.bfloat16


def low_half(shape):
    return lax.broadcasted_iota(jnp.int32, shape, len(shape) - 1) < 64


def xor_perm(n, m):
    return [(d, d ^ m) for d in range(n)]


def spread(rows, n):
    wide = rows.reshape(n, -1, 1, 128)
    return lax.all_to_all(wide, AXES, 0, 0, tiled=True).reshape(rows.shape)


def each(count, step):
    if count <= 16:
        for i in range(count):
            step(i)
    else:
        pl.loop(0, count)(step)


class Sums:
    def __init__(self, count, refs):
        self.refs = refs
        self.parts = [[None] * 4 for _ in range(count)]
        if refs is not None:
            for at in range(count):
                refs[at] = jnp.zeros((ROWS, 128), F32)

    def add(self, chunk, at, left, right):
        part = sum(left[a] * right[a] for a in range(3))
        if self.refs is not None:
            self.refs[at] = self.refs[at] + part
            return
        held = self.parts[at]
        slot = chunk % 4
        held[slot] = part if held[slot] is None else held[slot] + part

    def get(self, at):
        if self.refs is not None:
            total = self.refs[at]
        else:
            held = self.parts[at]
            total = (held[0] + held[1]) + (held[2] + held[3])
        return jnp.broadcast_to(jnp.sum(total, axis=1, keepdims=True), (ROWS, 128))


def chunk_parts(piece, chunk, me, n_row, n_col, size, at, count):
    half = n_row // 2
    o = chunk // half
    u = chunk % half
    even = piece[pl.ds((me ^ ((2 * u) * n_col + o)) * size + at, count)]
    odd = piece[pl.ds((me ^ ((2 * u + 1) * n_col + o)) * size + at, count)]
    low = low_half((count, 128))
    first = jnp.where(low, even, pltpu.roll(odd, 64, 1))
    second = jnp.where(low, pltpu.roll(even, 64, 1), odd)
    return jnp.concatenate([first, second], axis=0)


PAIRS = [(i, j) for i in range(ITERS) for j in range(i + 1, ITERS)]


def place_of(j):
    lane = lax.broadcasted_iota(jnp.int32, (ROWS, 128), 1)
    return lane == lax.broadcasted_iota(jnp.int32, (ROWS, 128), 0) * (ITERS + 1) + j


def row_sum(acc):
    return jnp.sum(acc, axis=1, keepdims=True)


def lines_of(chunk):
    if isinstance(chunk, int):
        return pl.ds(chunk * 128, 128)
    return pl.ds(pl.multiple_of(chunk * 128, 128), 128)


def write_columns(cols, y, chunk, vec):
    ys = [y[a : a + 1] for a in ORDER]
    f = [vec[a] for a in range(3)]
    g = ys[0] * f[0] + ys[1] * f[1] + ys[2] * f[2]
    groups = f + [g]
    groups += [ys[p] * f[v] for p in range(3) for v in range(3)]
    groups += [ys[a] * g for a in range(3)]
    full = jnp.concatenate(groups, axis=0)
    high = full.astype(BF16)
    low = (full - high.astype(F32)).astype(BF16)
    at = lines_of(chunk)
    cols[0:128, at] = high
    cols[128:256, at] = low


def contract(cols, kernels):
    first = jnp.dot(cols[:128], kernels, preferred_element_type=F32)
    second = jnp.dot(cols[128:], kernels[:, :128], preferred_element_type=F32)
    return first[:, :128] + (second + first[:, 128:])


def products(n_chunk, columns, cols, kernels):
    if n_chunk <= 16:
        for chunk in range(n_chunk):
            columns(chunk)
        return contract(cols[...], kernels[...])
    pl.loop(0, n_chunk)(columns)

    def turn(i, acc):
        at = pl.ds(pl.multiple_of(i * 2048, 2048), 2048)
        return acc + contract(cols[:, at], kernels[at, :])

    return lax.fori_loop(0, n_chunk // 16, turn, jnp.zeros((128, 128), F32))


def image_rows(prod, targets, own, scale):
    both = prod
    two = pltpu.roll(both, 64, 1)

    def group(k):
        return two[8 * k : 8 * k + 8]

    x = [targets[a : a + 1] for a in range(3)]
    images = []
    along = x[0] * group(0) + x[1] * group(1) + x[2] * group(2) - group(3)
    for a in range(3):
        cross = sum(x[b] * group(4 + 3 * a + b) for b in range(3))
        image = both[8 * a : 8 * a + 8] + x[a] * along - cross + group(13 + a)
        images.append((image + targets[3:4] * own[a]) * scale)
    return images


def write_piece(images, out):
    rows = []
    for image in images:
        top, bottom = image[:4], pltpu.roll(image[4:], 64, 1)
        rows.append(jnp.where(low_half((4, 128)), top, bottom))
    message = jnp.concatenate([rows[0][:HALF], rows[1][:HALF], rows[2]], axis=0)
    block = jnp.concatenate([message] * 4, axis=0)

    def put(m):
        out[pl.ds(m * 4 * LATER, 4 * LATER)] = block

    each_wide(out.shape[0] // (4 * LATER), put)


def each_wide(count, put):
    if count <= 64:
        for m in range(count):
            put(m)
    else:
        pl.loop(0, count)(put)


def pack_kernel(*refs):
    sources, (out, tgt, lists), held = refs[:6], refs[6:9], refs[9:15]
    block, sems = refs[15:]
    copies = [
        pltpu.make_async_copy(src, dst, sems.at[i])
        for i, (src, dst) in enumerate(zip(sources, held))
    ]
    for copy in copies:
        copy.start()
    for copy in copies:
        copy.wait()
    velocity, points, area, self_term, index, weight = held
    count = index.shape[0]
    field = velocity[...]
    spot = points[...]
    rows = []
    for a in range(3):
        vec = field[:, a, :]
        rows.append(jnp.concatenate([vec[:HALF], vec[HALF:]], axis=1))
    mine = jnp.concatenate([spot, self_term[...]], axis=0)
    mine = jnp.concatenate([mine, mine], axis=1)
    tgt[...] = jnp.concatenate([mine, mine], axis=0)
    left = jnp.concatenate([spot[0:1], spot[2:3]], axis=0)
    right = jnp.concatenate([spot[1:2], area[...]], axis=0)
    rows.append(jnp.concatenate([left, right], axis=1))
    message = jnp.concatenate(rows, axis=0)
    size = block.shape[0]
    block[...] = jnp.concatenate([message] * 8, axis=0)
    copies = [
        pltpu.make_async_copy(block, out.at[pl.ds(i * size, size)], sems.at[6 + i])
        for i in range(out.shape[0] // size)
    ]
    for copy in copies:
        copy.start()
    lists[:count] = index[...].astype(F32)
    lists[count:] = weight[...]
    for copy in copies:
        copy.wait()


def extra_kernel(me, lists, out):
    row, col = me[1], me[2]
    lines = lax.broadcasted_iota(jnp.int32, (128, 128), 0).astype(F32)
    count = lists.shape[0] // 2
    half = count // 2
    low = low_half((half, 128))
    odd = col % 2 == 1
    both = lists[:, lines_of(col // 2)]
    place = both[:count].astype(jnp.int32)
    place = (((place // 64) ^ row) * 64 + place % 64).astype(F32)
    packed = []
    for value in (place, both[count:]):
        top, bottom = value[:half], value[half:]
        lower = jnp.where(low, top, pltpu.roll(bottom, 64, 1))
        upper = jnp.where(low, pltpu.roll(top, 64, 1), bottom)
        packed.append(jnp.where(odd, upper, lower))
    index, weight = packed

    def build(u):
        line = lines + (u * 128.0 if isinstance(u, int) else (u * 128).astype(F32))
        total = jnp.zeros((128, 128), F32)
        for k in range(half):
            total = total + jnp.where(line == index[k : k + 1], weight[k : k + 1], 0.0)
        turned = total.T
        out[u] = turned[:64] + turned[64:]

    each(out.shape[0], build)


def first_kernel(
    n_row, n_col, piece, *refs
):
    extra = refs[:n_col]
    tgt, me_ref, kernels, places, basis, norm_out, out, cols, *sums = refs[n_col:]
    half = n_row // 2
    n_chunk = n_row * n_col // 2
    me = me_ref[0]
    total = Sums(1, sums[0] if sums else None)

    def unpack(chunk):
        vec = [
            chunk_parts(piece, chunk, me, n_row, n_col, FIRST, HALF * a, 4)
            for a in range(3)
        ]
        spot = chunk_parts(piece, chunk, me, n_row, n_col, FIRST, 3 * HALF, 2)
        places[chunk] = spot
        for a in range(3):
            basis[chunk, a] = vec[a]
        total.add(chunk, 0, vec, vec)
        write_columns(cols, spot, chunk, vec)

    turned = tgt[...].T
    x = [jnp.broadcast_to(turned[:64, a : a + 1], (64, 128)) for a in range(3)]

    def build(chunk):
        unpack(chunk)
        y = places[chunk]
        d = [x[a] - y[k : k + 1] for a, k in enumerate(ORDER)]
        dist = d[0] * d[0] + d[1] * d[1] + d[2] * d[2]
        root = lax.rsqrt(dist + BLOB_SQ)
        two = (y[3:4] * INV_EIGHT_PI) * root * root * root
        one = (dist + 2.0 * BLOB_SQ) * two
        if isinstance(chunk, int):
            one = one + extra[chunk // half][chunk % half]
        else:
            for o in range(n_col):
                mine = extra[o][chunk % half]
                one = one + jnp.where(chunk // half == o, mine, 0.0)
        value = jnp.concatenate([one, two], axis=0).T
        high = value.astype(BF16)
        at = lines_of(chunk)
        kernels[at, 0:128] = high
        kernels[at, 128:256] = (value - high.astype(F32)).astype(BF16)

    prod = products(n_chunk, build, cols, kernels)
    norm = jnp.sqrt(total.get(0))
    scale = 1.0 / norm
    norm_out[0] = norm
    norm_out[1] = scale
    write_piece(image_rows(prod, tgt, basis[0], scale), out)


def middle_kernel(n_row, n_col, n_base, final, piece, *refs):
    bases, norms = refs[:n_base], refs[n_base : 2 * n_base]
    if final:
        kernels, places, tgt, me_ref, own, h_out, out, basis, cols, *held = refs[2 * n_base :]
    else:
        kernels, places, tgt, me_ref, basis, h_out, out, cols, *held = refs[2 * n_base :]
    n_chunk = n_row * n_col // 2
    me = me_ref[0]
    scales = [norm[norm.shape[0] - 1] for norm in norms]
    cross = [(i, j) for i in range(n_base) for j in range(i)]
    sums = Sums(2 * n_base + 1 + len(cross), held[0] if held else None)

    def unpack(chunk):
        vec = [
            chunk_parts(piece, chunk, me, n_row, n_col, LATER, HALF * a, 4)
            for a in range(3)
        ]
        old = [[base[chunk, a] for a in range(3)] for base in bases]
        for a in range(3):
            basis[chunk, a] = vec[a]
        for j in range(n_base):
            sums.add(chunk, j, vec, old[j])
        for at, (i, j) in enumerate(cross):
            sums.add(chunk, 2 * n_base + 1 + at, old[i], old[j])

    each(n_chunk, unpack)
    gram = {}
    for at, (i, j) in enumerate(cross):
        gram[j, i] = sums.get(2 * n_base + 1 + at) * (scales[i] * scales[j])
    column = []
    for j in range(n_base):
        h = sums.get(j) * scales[j]
        for i in range(j):
            h = h - column[i] * gram[i, j]
        column.append(h)
        h_out[j] = h
    factors = [h * scale for h, scale in zip(column, scales)]

    def columns(chunk):
        old = [[base[chunk, a] for a in range(3)] for base in bases]
        vec = []
        for a in range(3):
            value = basis[chunk, a]
            for j in range(n_base):
                value = value - factors[j] * old[j][a]
            vec.append(value)
            basis[chunk, a] = value
        sums.add(chunk, n_base, vec, vec)
        write_columns(cols, places[chunk], chunk, vec)
        if final:
            for j in range(n_base):
                sums.add(chunk, n_base + 1 + j, vec, old[j])

    prod = products(n_chunk, columns, cols, kernels)
    norm = jnp.sqrt(sums.get(n_base))
    scale = 1.0 / norm
    h_out[n_base] = norm
    images = image_rows(prod, tgt, basis[0], scale)
    if not final:
        h_out[n_base + 1] = scale
        write_piece(images, out)
        return
    every = [*bases, basis]
    for j, base in enumerate(every):
        for a in range(3):
            own[j, a] = base[0, a] * [*scales, scale][j]
    for j in range(n_base):
        gram[j, n_base] = sums.get(n_base + 1 + j) * (scale * scales[j])
    for at, pair in enumerate(PAIRS):
        h_out[n_base + 1 + at] = gram[pair]
    low = low_half((ROWS, 128))
    row = jnp.zeros((ROWS, 128), F32)
    for j in range(ITERS + 1):
        other = images if j == ITERS else [own[j, a] for a in range(3)]
        part = sum(images[a] * other[a] for a in range(3))
        part = row_sum(jnp.where(low, part, 0.0))
        row = row + jnp.where(place_of(j), part, 0.0)
    row = jnp.sum(row, axis=0, keepdims=True)

    def put(m):
        out[pl.ds(m, 1)] = row

    each_wide(out.shape[0], put)


def solve_small(hessen, start_norm, count):
    zero = jnp.zeros_like(start_norm)
    target = [start_norm] + [zero] * count
    cosines = []
    sines = []
    triangle = {}
    for k in range(count):
        column = [hessen[i, k] for i in range(k + 2)]
        for j in range(k):
            first_val = column[j]
            second_val = column[j + 1]
            column[j] = cosines[j] * first_val + sines[j] * second_val
            column[j + 1] = cosines[j] * second_val - sines[j] * first_val
        radius = jnp.sqrt(column[k] * column[k] + column[k + 1] * column[k + 1])
        cosine = column[k] / radius
        sine = column[k + 1] / radius
        cosines.append(cosine)
        sines.append(sine)
        for i in range(k):
            triangle[i, k] = column[i]
        triangle[k, k] = radius
        target[k + 1] = -sine * target[k]
        target[k] = cosine * target[k]
    coeffs = [None] * count
    for k in range(count - 1, -1, -1):
        accum = target[k]
        for i in range(k + 1, count):
            accum = accum - triangle[k, i] * coeffs[i]
        coeffs[k] = accum / triangle[k, k]
    return coeffs


def last_kernel(sums, own, *refs):
    columns = refs[: ITERS - 1]
    norm, out = refs[ITERS - 1 :]
    hessen = {}
    for k in range(ITERS - 1):
        for j in range(k + 2):
            hessen[j, k] = columns[k][j]
    gram = {(j, j): 1.0 for j in range(ITERS)}
    for at, (i, j) in enumerate(PAIRS):
        gram[i, j] = gram[j, i] = columns[-1][ITERS + at]
    row = jnp.broadcast_to(jnp.sum(sums[...], axis=0, keepdims=True), (ROWS, 128))
    inner = [
        jnp.broadcast_to(row_sum(jnp.where(place_of(j), row, 0.0)), (ROWS, 128))
        for j in range(ITERS + 1)
    ]
    square = inner[ITERS]
    for j in range(ITERS):
        h = inner[j]
        for i in range(j):
            h = h - hessen[i, ITERS - 1] * gram[i, j]
        hessen[j, ITERS - 1] = h
    for j in range(ITERS):
        rest = -2.0 * inner[j]
        for i in range(ITERS):
            rest = rest + hessen[i, ITERS - 1] * gram[i, j]
        square = square + hessen[j, ITERS - 1] * rest
    hessen[ITERS, ITERS - 1] = jnp.sqrt(jnp.maximum(square, 0.0))
    coeffs = solve_small(hessen, norm[0], ITERS)
    for a in range(3):
        density = sum(coeffs[k] * own[k, a] for k in range(ITERS))
        out[:HALF, a, :] = density[:HALF, :64]
        out[HALF:, a, :] = density[4 : 4 + HALF, :64]


def call(kernel, outs, scratch, operands, scalars=(), far=(), spread_out=False, flops=0):
    vmem = pl.BlockSpec(memory_space=pltpu.VMEM)
    smem = pl.BlockSpec(memory_space=pltpu.SMEM)
    count = len(operands)
    hbm = pl.BlockSpec(memory_space=pltpu.HBM)
    specs = [smem if i in scalars else hbm if i in far else vmem for i in range(count)]
    moved = sum(x.size * x.dtype.itemsize for x in operands)
    return pl.pallas_call(
        kernel,
        out_shape=[jax.ShapeDtypeStruct(s, t) for s, t in outs],
        in_specs=specs,
        out_specs=[pl.BlockSpec(memory_space=pl.ANY) if spread_out and i == 0 else vmem for i in range(len(outs))],
        scratch_shapes=scratch,
        cost_estimate=pl.CostEstimate(flops=flops, bytes_accessed=moved, transcendentals=0),
        compiler_params=pltpu.CompilerParams(vmem_limit_bytes=48 * 1024 * 1024),
    )(*operands)


def body(sizes, velocity, points, panel_area, self_term, near_index, near_weight):
    n_row, n_col = sizes[0] * sizes[1] * sizes[2], sizes[3]
    n = n_row * n_col
    n_chunk = n // 2
    total = n * 64
    row = lax.axis_index(AXES[:3])
    col = lax.axis_index("col")
    me = jnp.stack([row * n_col + col, row, col]).astype(jnp.int32)
    rhs = velocity.shape[0]

    message = ((n * LATER, 128), F32)
    sources = [
        velocity,
        points,
        panel_area[None],
        self_term[None],
        near_index.T,
        near_weight.T,
    ]
    wide, tgt, lists = call(
        pack_kernel,
        [
            ((n * FIRST, 128), F32),
            ((8, 128), F32),
            ((2 * near_index.shape[1], near_index.shape[0]), F32),
        ],
        [pltpu.VMEM(x.shape, x.dtype) for x in sources]
        + [pltpu.VMEM((8 * FIRST, 128), F32), pltpu.SemaphoreType.DMA((6 + n // 8,))],
        [pltpu.with_memory_space_constraint(x, pltpu.HBM) for x in sources],
        far=range(6),
        spread_out=True,
    )
    piece = spread(wide, n)
    near = [lists] + [lax.ppermute(lists, "col", xor_perm(n_col, o)) for o in range(1, n_col)]
    extra = [
        call(
            extra_kernel,
            [((n_row // 2, 64, 128), F32)],
            [],
            [me, pair],
            {0},
            flops=10**8,
        )[0]
        for pair in near
    ]

    vec_shape = (n_chunk, 3, ROWS, 128)
    cols = pltpu.VMEM((256, total), BF16)
    held = [] if n_chunk <= 16 else [pltpu.VMEM((8, ROWS, 128), F32)]
    kernels, places, basis, norm, wide = call(
        functools.partial(first_kernel, n_row, n_col),
        [
            ((total, 256), BF16),
            ((n_chunk, 4, 128), F32),
            (vec_shape, F32),
            ((2, ROWS, 128), F32),
            message,
        ],
        [cols, *held],
        [piece, *extra, tgt, me],
        {n_col + 2},
    )
    bases = [basis]
    columns = [norm]
    for k in range(1, ITERS):
        final = k == ITERS - 1
        piece = spread(wide, n)
        main, column, wide = call(
            functools.partial(middle_kernel, n_row, n_col, k, final),
            [
                ((ITERS, 3, ROWS, 128) if final else vec_shape, F32),
                ((k + 1 + (len(PAIRS) if final else 1), ROWS, 128), F32),
                ((n, 128), F32) if final else message,
            ],
            [*([pltpu.VMEM(vec_shape, F32)] if final else []), cols, *held],
            [piece, *bases, *columns, kernels, places, tgt, me],
            {2 * k + 4},
        )
        bases.append(main)
        columns.append(column)
    sums = spread(wide, n)
    (density,) = call(
        last_kernel, [((rhs, 3, 64), F32)], [], [sums, bases[-1], *columns[1:], columns[0]]
    )
    return density


def solution(mesh):
    n_row, n_col = mesh.shape["row"], mesh.shape["col"]
    sizes = (n_row // 4, 2, 2, n_col)
    split = jax.sharding.Mesh(mesh.devices.reshape(sizes), AXES)
    return jax.shard_map(
        functools.partial(body, sizes),
        mesh=split,
        in_specs=(
            P(None, None, AXES),
            P(None, AXES),
            P(AXES),
            P(AXES),
            P(AXES[:3], "col"),
            P(AXES[:3], "col"),
        ),
        out_specs=P(None, None, AXES),
        check_vma=False,
    )
```

```python
import functools
import math

import jax
import jax.numpy as jnp
from jax import lax
from jax.experimental import pallas as pl
from jax.experimental.pallas import tpu as pltpu
from jax.sharding import PartitionSpec as P

ITERS = 3
BLOB_SQ = 0.0025
INV_EIGHT_PI = 1.0 / (8.0 * math.pi)
ROWS = 8
HALF = 3
FIRST, LATER = 11, 9
ORDER = (0, 2, 1)
AXES = ("top", "mid", "core", "col")
F32 = jnp.float32
BF16 = jnp.bfloat16


def low_half(shape):
    return lax.broadcasted_iota(jnp.int32, shape, len(shape) - 1) < 64


def xor_perm(n, m):
    return [(d, d ^ m) for d in range(n)]


def spread(rows, n):
    wide = rows.reshape(n, -1, 1, 128)
    return lax.all_to_all(wide, AXES, 0, 0, tiled=True).reshape(rows.shape)


def each(count, step):
    if count <= 16:
        for i in range(count):
            step(i)
    else:
        pl.loop(0, count)(step)


class Sums:
    def __init__(self, count, refs):
        self.refs = refs
        self.parts = [[None] * 4 for _ in range(count)]
        if refs is not None:
            for at in range(count):
                refs[at] = jnp.zeros((ROWS, 128), F32)

    def add(self, chunk, at, left, right):
        part = sum(left[a] * right[a] for a in range(3))
        if self.refs is not None:
            self.refs[at] = self.refs[at] + part
            return
        held = self.parts[at]
        slot = chunk % 4
        held[slot] = part if held[slot] is None else held[slot] + part

    def get(self, at):
        if self.refs is not None:
            total = self.refs[at]
        else:
            held = self.parts[at]
            total = (held[0] + held[1]) + (held[2] + held[3])
        return jnp.broadcast_to(jnp.sum(total, axis=1, keepdims=True), (ROWS, 128))


def chunk_parts(piece, chunk, me, n_row, n_col, size, at, count):
    half = n_row // 2
    o = chunk // half
    u = chunk % half
    early = max(at + count - size, 0)
    even = piece[pl.ds((me ^ ((2 * u) * n_col + o)) * size + at - early, count)]
    odd = piece[pl.ds((me ^ ((2 * u + 1) * n_col + o)) * size + at - early, count)]
    low = low_half((count, 128))
    first = jnp.where(low, even, pltpu.roll(odd, 64, 1))
    second = jnp.where(low, pltpu.roll(even, 64, 1), odd)
    rows = jnp.concatenate([first, second], axis=0)
    return pltpu.roll(rows, ROWS - early, 0) if early else rows


PAIRS = [(i, j) for i in range(ITERS) for j in range(i + 1, ITERS)]


def place_of(j):
    lane = lax.broadcasted_iota(jnp.int32, (ROWS, 128), 1)
    return lane == lax.broadcasted_iota(jnp.int32, (ROWS, 128), 0) * (ITERS + 1) + j


def row_sum(acc):
    return jnp.sum(acc, axis=1, keepdims=True)


def lines_of(chunk):
    if isinstance(chunk, int):
        return pl.ds(chunk * 128, 128)
    return pl.ds(pl.multiple_of(chunk * 128, 128), 128)


def write_columns(cols, y, chunk, vec):
    ys = [y[a : a + 1] for a in ORDER]
    f = [vec[a] for a in range(3)]
    g = ys[0] * f[0] + ys[1] * f[1] + ys[2] * f[2]
    groups = f + [g]
    groups += [ys[p] * f[v] for p in range(3) for v in range(3)]
    groups += [ys[a] * g for a in range(3)]
    full = jnp.concatenate(groups, axis=0)
    high = full.astype(BF16)
    low = (full - high.astype(F32)).astype(BF16)
    at = lines_of(chunk)
    cols[0:128, at] = high
    cols[128:256, at] = low


def contract(cols, kernels):
    prod = jnp.dot(cols, kernels, preferred_element_type=F32)
    return prod[:128, :128] + (prod[128:, :128] + prod[:128, 128:])


def products(n_chunk, columns, cols, kernels):
    if n_chunk <= 16:
        for chunk in range(n_chunk):
            columns(chunk)
        return contract(cols[...], kernels[...])
    pl.loop(0, n_chunk)(columns)

    def turn(i, acc):
        at = pl.ds(pl.multiple_of(i * 2048, 2048), 2048)
        return acc + contract(cols[:, at], kernels[at, :])

    return lax.fori_loop(0, n_chunk // 16, turn, jnp.zeros((128, 128), F32))


def image_rows(prod, targets, own, scale):
    both = prod
    two = pltpu.roll(both, 64, 1)

    def group(k):
        return two[8 * k : 8 * k + 8]

    x = [targets[a : a + 1] for a in range(3)]
    images = []
    along = x[0] * group(0) + x[1] * group(1) + x[2] * group(2) - group(3)
    for a in range(3):
        cross = sum(x[b] * group(4 + 3 * a + b) for b in range(3))
        image = both[8 * a : 8 * a + 8] + x[a] * along - cross + group(13 + a)
        images.append((image + targets[3:4] * own[a]) * scale)
    return images


def write_piece(images, out):
    rows = []
    for image in images:
        top, bottom = image[:4], pltpu.roll(image[4:], 64, 1)
        rows.append(jnp.where(low_half((4, 128)), top, bottom))
    message = jnp.concatenate([row[:HALF] for row in rows], axis=0)
    block = jnp.concatenate([message] * 8, axis=0)

    def put(m):
        out[pl.ds(m * 8 * LATER, 8 * LATER)] = block

    each_wide(out.shape[0] // (8 * LATER), put)


def each_wide(count, put):
    if count <= 64:
        for m in range(count):
            put(m)
    else:
        pl.loop(0, count)(put)


def pack_kernel(*refs):
    sources, (out, tgt, lists), held = refs[:6], refs[6:9], refs[9:15]
    block, sems = refs[15:]
    copies = [
        pltpu.make_async_copy(src, dst, sems.at[i])
        for i, (src, dst) in enumerate(zip(sources, held))
    ]
    for copy in copies:
        copy.start()
    for copy in copies[:4]:
        copy.wait()
    velocity, points, area, self_term, index, weight = held
    count = index.shape[0]
    field = velocity[...]
    spot = points[...]
    rows = []
    for a in range(3):
        vec = field[:, a, :]
        rows.append(jnp.concatenate([vec[:HALF], vec[HALF:]], axis=1))
    mine = jnp.concatenate([spot, self_term[...]], axis=0)
    mine = jnp.concatenate([mine, mine], axis=1)
    tgt[...] = jnp.concatenate([mine, mine], axis=0)
    left = jnp.concatenate([spot[0:1], spot[2:3]], axis=0)
    right = jnp.concatenate([spot[1:2], area[...]], axis=0)
    rows.append(jnp.concatenate([left, right], axis=1))
    message = jnp.concatenate(rows, axis=0)
    size = block.shape[0]
    block[...] = jnp.concatenate([message] * 8, axis=0)
    leaving = [
        pltpu.make_async_copy(block, out.at[pl.ds(i * size, size)], sems.at[6 + i])
        for i in range(out.shape[0] // size)
    ]
    for copy in leaving:
        copy.start()
    for copy in copies[4:]:
        copy.wait()
    lists[:count] = index[...].astype(F32)
    lists[count:] = weight[...]
    for copy in leaving:
        copy.wait()


def extra_kernel(me, lists, out):
    row, col = me[1], me[2]
    lines = lax.broadcasted_iota(jnp.int32, (128, 128), 0).astype(F32)
    count = lists.shape[0] // 2
    half = count // 2
    low = low_half((half, 128))
    odd = col % 2 == 1
    both = lists[:, lines_of(col // 2)]
    place = both[:count].astype(jnp.int32)
    place = (((place // 64) ^ row) * 64 + place % 64).astype(F32)
    packed = []
    for value in (place, both[count:]):
        top, bottom = value[:half], value[half:]
        lower = jnp.where(low, top, pltpu.roll(bottom, 64, 1))
        upper = jnp.where(low, pltpu.roll(top, 64, 1), bottom)
        packed.append(jnp.where(odd, upper, lower))
    index, weight = packed

    def build(u):
        line = lines + (u * 128.0 if isinstance(u, int) else (u * 128).astype(F32))
        total = jnp.zeros((128, 128), F32)
        for k in range(half):
            total = total + jnp.where(line == index[k : k + 1], weight[k : k + 1], 0.0)
        turned = total.T
        out[u] = turned[:64] + turned[64:]

    each(out.shape[0], build)


def first_kernel(
    n_row, n_col, piece, *refs
):
    extra = refs[:n_col]
    tgt, me_ref, kernels, places, basis, norm_out, out, cols, *sums = refs[n_col:]
    half = n_row // 2
    n_chunk = n_row * n_col // 2
    me = me_ref[0]
    total = Sums(1, sums[0] if sums else None)

    def unpack(chunk):
        vec = [
            chunk_parts(piece, chunk, me, n_row, n_col, FIRST, HALF * a, 4)
            for a in range(3)
        ]
        spot = chunk_parts(piece, chunk, me, n_row, n_col, FIRST, 3 * HALF, 2)
        places[chunk] = spot
        for a in range(3):
            basis[chunk, a] = vec[a]
        total.add(chunk, 0, vec, vec)
        write_columns(cols, spot, chunk, vec)

    turned = tgt[...].T
    x = [jnp.broadcast_to(turned[:64, a : a + 1], (64, 128)) for a in range(3)]

    def build(chunk):
        unpack(chunk)
        y = places[chunk]
        d = [x[a] - y[k : k + 1] for a, k in enumerate(ORDER)]
        dist = d[0] * d[0] + d[1] * d[1] + d[2] * d[2]
        root = lax.rsqrt(dist + BLOB_SQ)
        two = (y[3:4] * INV_EIGHT_PI) * root * root * root
        one = (dist + 2.0 * BLOB_SQ) * two
        if isinstance(chunk, int):
            one = one + extra[chunk // half][chunk % half]
        else:
            for o in range(n_col):
                mine = extra[o][chunk % half]
                one = one + jnp.where(chunk // half == o, mine, 0.0)
        value = jnp.concatenate([one, two], axis=0).T
        high = value.astype(BF16)
        at = lines_of(chunk)
        kernels[at, 0:128] = high
        kernels[at, 128:256] = (value - high.astype(F32)).astype(BF16)

    prod = products(n_chunk, build, cols, kernels)
    norm = jnp.sqrt(total.get(0))
    scale = 1.0 / norm
    norm_out[0] = norm
    norm_out[1] = scale
    write_piece(image_rows(prod, tgt, basis[0], scale), out)


def middle_kernel(n_row, n_col, n_base, final, piece, *refs):
    bases, norms = refs[:n_base], refs[n_base : 2 * n_base]
    if final:
        kernels, places, tgt, me_ref, own, h_out, out, basis, cols, *held = refs[2 * n_base :]
    else:
        kernels, places, tgt, me_ref, basis, h_out, out, cols, *held = refs[2 * n_base :]
    n_chunk = n_row * n_col // 2
    me = me_ref[0]
    scales = [norm[norm.shape[0] - 1] for norm in norms]
    cross = [(i, j) for i in range(n_base) for j in range(i)]
    sums = Sums(2 * n_base + 1 + len(cross), held[0] if held else None)

    def unpack(chunk):
        vec = [
            chunk_parts(piece, chunk, me, n_row, n_col, LATER, HALF * a, 4)
            for a in range(3)
        ]
        old = [[base[chunk, a] for a in range(3)] for base in bases]
        for a in range(3):
            basis[chunk, a] = vec[a]
        for j in range(n_base):
            sums.add(chunk, j, vec, old[j])
        for at, (i, j) in enumerate(cross):
            sums.add(chunk, 2 * n_base + 1 + at, old[i], old[j])

    each(n_chunk, unpack)
    gram = {}
    for at, (i, j) in enumerate(cross):
        gram[j, i] = sums.get(2 * n_base + 1 + at) * (scales[i] * scales[j])
    column = []
    for j in range(n_base):
        h = sums.get(j) * scales[j]
        for i in range(j):
            h = h - column[i] * gram[i, j]
        column.append(h)
        h_out[j] = h
    factors = [h * scale for h, scale in zip(column, scales)]

    def columns(chunk):
        old = [[base[chunk, a] for a in range(3)] for base in bases]
        vec = []
        for a in range(3):
            value = basis[chunk, a]
            for j in range(n_base):
                value = value - factors[j] * old[j][a]
            vec.append(value)
            basis[chunk, a] = value
        sums.add(chunk, n_base, vec, vec)
        write_columns(cols, places[chunk], chunk, vec)
        if final:
            for j in range(n_base):
                sums.add(chunk, n_base + 1 + j, vec, old[j])

    prod = products(n_chunk, columns, cols, kernels)
    norm = jnp.sqrt(sums.get(n_base))
    scale = 1.0 / norm
    h_out[n_base] = norm
    images = image_rows(prod, tgt, basis[0], scale)
    if not final:
        h_out[n_base + 1] = scale
        write_piece(images, out)
        return
    every = [*bases, basis]
    for j, base in enumerate(every):
        for a in range(3):
            own[j, a] = base[0, a] * [*scales, scale][j]
    for j in range(n_base):
        gram[j, n_base] = sums.get(n_base + 1 + j) * (scale * scales[j])
    for at, pair in enumerate(PAIRS):
        h_out[n_base + 1 + at] = gram[pair]
    low = low_half((ROWS, 128))
    row = jnp.zeros((ROWS, 128), F32)
    for j in range(ITERS + 1):
        other = images if j == ITERS else [own[j, a] for a in range(3)]
        part = sum(images[a] * other[a] for a in range(3))
        part = row_sum(jnp.where(low, part, 0.0))
        row = row + jnp.where(place_of(j), part, 0.0)
    row = jnp.sum(row, axis=0, keepdims=True)

    def put(m):
        out[pl.ds(m, 1)] = row

    each_wide(out.shape[0], put)


def solve_small(hessen, start_norm, count):
    zero = jnp.zeros_like(start_norm)
    target = [start_norm] + [zero] * count
    cosines = []
    sines = []
    triangle = {}
    for k in range(count):
        column = [hessen[i, k] for i in range(k + 2)]
        for j in range(k):
            first_val = column[j]
            second_val = column[j + 1]
            column[j] = cosines[j] * first_val + sines[j] * second_val
            column[j + 1] = cosines[j] * second_val - sines[j] * first_val
        radius = jnp.sqrt(column[k] * column[k] + column[k + 1] * column[k + 1])
        cosine = column[k] / radius
        sine = column[k + 1] / radius
        cosines.append(cosine)
        sines.append(sine)
        for i in range(k):
            triangle[i, k] = column[i]
        triangle[k, k] = radius
        target[k + 1] = -sine * target[k]
        target[k] = cosine * target[k]
    coeffs = [None] * count
    for k in range(count - 1, -1, -1):
        accum = target[k]
        for i in range(k + 1, count):
            accum = accum - triangle[k, i] * coeffs[i]
        coeffs[k] = accum / triangle[k, k]
    return coeffs


def last_kernel(sums, own, *refs):
    columns = refs[: ITERS - 1]
    norm, out = refs[ITERS - 1 :]
    hessen = {}
    for k in range(ITERS - 1):
        for j in range(k + 2):
            hessen[j, k] = columns[k][j]
    gram = {(j, j): 1.0 for j in range(ITERS)}
    for at, (i, j) in enumerate(PAIRS):
        gram[i, j] = gram[j, i] = columns[-1][ITERS + at]
    row = jnp.broadcast_to(jnp.sum(sums[...], axis=0, keepdims=True), (ROWS, 128))
    inner = [
        jnp.broadcast_to(row_sum(jnp.where(place_of(j), row, 0.0)), (ROWS, 128))
        for j in range(ITERS + 1)
    ]
    square = inner[ITERS]
    for j in range(ITERS):
        h = inner[j]
        for i in range(j):
            h = h - hessen[i, ITERS - 1] * gram[i, j]
        hessen[j, ITERS - 1] = h
    for j in range(ITERS):
        rest = -2.0 * inner[j]
        for i in range(ITERS):
            rest = rest + hessen[i, ITERS - 1] * gram[i, j]
        square = square + hessen[j, ITERS - 1] * rest
    hessen[ITERS, ITERS - 1] = jnp.sqrt(jnp.maximum(square, 0.0))
    coeffs = solve_small(hessen, norm[0], ITERS)
    for a in range(3):
        density = sum(coeffs[k] * own[k, a] for k in range(ITERS))
        out[:HALF, a, :] = density[:HALF, :64]
        out[HALF:, a, :] = density[4 : 4 + HALF, :64]


def call(kernel, outs, scratch, operands, scalars=(), far=(), spread_out=False, flops=0):
    vmem = pl.BlockSpec(memory_space=pltpu.VMEM)
    smem = pl.BlockSpec(memory_space=pltpu.SMEM)
    count = len(operands)
    hbm = pl.BlockSpec(memory_space=pltpu.HBM)
    specs = [smem if i in scalars else hbm if i in far else vmem for i in range(count)]
    moved = sum(x.size * x.dtype.itemsize for x in operands)
    return pl.pallas_call(
        kernel,
        out_shape=[jax.ShapeDtypeStruct(s, t) for s, t in outs],
        in_specs=specs,
        out_specs=[pl.BlockSpec(memory_space=pl.ANY) if spread_out and i == 0 else vmem for i in range(len(outs))],
        scratch_shapes=scratch,
        cost_estimate=pl.CostEstimate(flops=flops, bytes_accessed=moved, transcendentals=0),
        compiler_params=pltpu.CompilerParams(vmem_limit_bytes=48 * 1024 * 1024),
    )(*operands)


def body(sizes, velocity, points, panel_area, self_term, near_index, near_weight):
    n_row, n_col = sizes[0] * sizes[1] * sizes[2], sizes[3]
    n = n_row * n_col
    n_chunk = n // 2
    total = n * 64
    row = lax.axis_index(AXES[:3])
    col = lax.axis_index("col")
    me = jnp.stack([row * n_col + col, row, col]).astype(jnp.int32)
    rhs = velocity.shape[0]

    message = ((n * LATER, 128), F32)
    sources = [
        velocity,
        points,
        panel_area[None],
        self_term[None],
        near_index.T,
        near_weight.T,
    ]
    wide, tgt, lists = call(
        pack_kernel,
        [
            ((n * FIRST, 128), F32),
            ((8, 128), F32),
            ((2 * near_index.shape[1], near_index.shape[0]), F32),
        ],
        [pltpu.VMEM(x.shape, x.dtype) for x in sources]
        + [pltpu.VMEM((8 * FIRST, 128), F32), pltpu.SemaphoreType.DMA((6 + n // 8,))],
        [pltpu.with_memory_space_constraint(x, pltpu.HBM) for x in sources],
        far=range(6),
        spread_out=True,
    )
    piece = spread(wide, n)
    near = [lists] + [lax.ppermute(lists, "col", xor_perm(n_col, o)) for o in range(1, n_col)]
    extra = [
        call(
            extra_kernel,
            [((n_row // 2, 64, 128), F32)],
            [],
            [me, pair],
            {0},
            flops=10**8,
        )[0]
        for pair in near
    ]

    vec_shape = (n_chunk, 3, ROWS, 128)
    cols = pltpu.VMEM((256, total), BF16)
    held = [] if n_chunk <= 16 else [pltpu.VMEM((8, ROWS, 128), F32)]
    kernels, places, basis, norm, wide = call(
        functools.partial(first_kernel, n_row, n_col),
        [
            ((total, 256), BF16),
            ((n_chunk, 4, 128), F32),
            (vec_shape, F32),
            ((2, ROWS, 128), F32),
            message,
        ],
        [cols, *held],
        [piece, *extra, tgt, me],
        {n_col + 2},
    )
    bases = [basis]
    columns = [norm]
    for k in range(1, ITERS):
        final = k == ITERS - 1
        piece = spread(wide, n)
        main, column, wide = call(
            functools.partial(middle_kernel, n_row, n_col, k, final),
            [
                ((ITERS, 3, ROWS, 128) if final else vec_shape, F32),
                ((k + 1 + (len(PAIRS) if final else 1), ROWS, 128), F32),
                ((n, 128), F32) if final else message,
            ],
            [*([pltpu.VMEM(vec_shape, F32)] if final else []), cols, *held],
            [piece, *bases, *columns, kernels, places, tgt, me],
            {2 * k + 4},
        )
        bases.append(main)
        columns.append(column)
    sums = spread(wide, n)
    (density,) = call(
        last_kernel, [((rhs, 3, 64), F32)], [], [sums, bases[-1], *columns[1:], columns[0]]
    )
    return density


def solution(mesh):
    n_row, n_col = mesh.shape["row"], mesh.shape["col"]
    sizes = (n_row // 4, 2, 2, n_col)
    split = jax.sharding.Mesh(mesh.devices.reshape(sizes), AXES)
    return jax.shard_map(
        functools.partial(body, sizes),
        mesh=split,
        in_specs=(
            P(None, None, AXES),
            P(None, AXES),
            P(AXES),
            P(AXES),
            P(AXES[:3], "col"),
            P(AXES[:3], "col"),
        ),
        out_specs=P(None, None, AXES),
        check_vma=False,
    )
```

```python
import functools
import math

import jax
import jax.numpy as jnp
from jax import lax
from jax.experimental import pallas as pl
from jax.experimental.pallas import tpu as pltpu
from jax.sharding import PartitionSpec as P

ITERS = 3
BLOB_SQ = 0.0025
INV_EIGHT_PI = 1.0 / (8.0 * math.pi)
ROWS = 8
HALF = 3
FIRST, LATER = 11, 9
ORDER = (0, 2, 1)
AXES = ("top", "mid", "core", "col")
F32 = jnp.float32
BF16 = jnp.bfloat16


def low_half(shape):
    return lax.broadcasted_iota(jnp.int32, shape, len(shape) - 1) < 64


def xor_perm(n, m):
    return [(d, d ^ m) for d in range(n)]


def spread(rows, n):
    wide = rows.reshape(n, -1, 1, 128)
    return lax.all_to_all(wide, AXES, 0, 0, tiled=True).reshape(rows.shape)


def each(count, step):
    if count <= 16:
        for i in range(count):
            step(i)
    else:
        pl.loop(0, count)(step)


class Sums:
    def __init__(self, count, refs):
        self.refs = refs
        self.parts = [[None] * 4 for _ in range(count)]
        if refs is not None:
            for at in range(count):
                refs[at] = jnp.zeros((ROWS, 128), F32)

    def add(self, chunk, at, left, right):
        part = sum(left[a] * right[a] for a in range(3))
        if self.refs is not None:
            self.refs[at] = self.refs[at] + part
            return
        held = self.parts[at]
        slot = chunk % 4
        held[slot] = part if held[slot] is None else held[slot] + part

    def get(self, at):
        if self.refs is not None:
            total = self.refs[at]
        else:
            held = self.parts[at]
            total = (held[0] + held[1]) + (held[2] + held[3])
        return jnp.broadcast_to(jnp.sum(total, axis=1, keepdims=True), (ROWS, 128))


def chunk_parts(piece, chunk, me, n_row, n_col, size, at, count):
    half = n_row // 2
    o = chunk // half
    u = chunk % half
    early = max(at + count - size, 0)
    even = piece[pl.ds((me ^ ((2 * u) * n_col + o)) * size + at - early, count)]
    odd = piece[pl.ds((me ^ ((2 * u + 1) * n_col + o)) * size + at - early, count)]
    low = low_half((count, 128))
    first = jnp.where(low, even, pltpu.roll(odd, 64, 1))
    second = jnp.where(low, pltpu.roll(even, 64, 1), odd)
    rows = jnp.concatenate([first, second], axis=0)
    return pltpu.roll(rows, ROWS - early, 0) if early else rows


PAIRS = [(i, j) for i in range(ITERS) for j in range(i + 1, ITERS)]


def place_of(j):
    lane = lax.broadcasted_iota(jnp.int32, (ROWS, 128), 1)
    return lane == lax.broadcasted_iota(jnp.int32, (ROWS, 128), 0) * (ITERS + 1) + j


def row_sum(acc):
    return jnp.sum(acc, axis=1, keepdims=True)


def lines_of(chunk):
    if isinstance(chunk, int):
        return pl.ds(chunk * 128, 128)
    return pl.ds(pl.multiple_of(chunk * 128, 128), 128)


def write_columns(cols, y, chunk, f):
    inner = sum(y[k : k + 1] * f[a] for a, k in enumerate(ORDER))
    full = jnp.concatenate([*f, inner], axis=0)
    high = full.astype(BF16)
    at = lines_of(chunk)
    cols[0:32, at] = high
    cols[32:64, at] = (full - high.astype(F32)).astype(BF16)


def contract(cols, kernels):
    prod = jnp.dot(cols, kernels, preferred_element_type=F32)
    return prod[:32, :256] + (prod[32:, :256] + prod[:32, 256:])


def products(n_chunk, columns, cols, kernels):
    if n_chunk <= 16:
        for chunk in range(n_chunk):
            columns(chunk)
        return contract(cols[...], kernels[...])
    pl.loop(0, n_chunk)(columns)

    def turn(i, acc):
        at = pl.ds(pl.multiple_of(i * 2048, 2048), 2048)
        return acc + contract(cols[:, at], kernels[at, :])

    return lax.fori_loop(0, n_chunk // 16, turn, jnp.zeros((32, 256), F32))


def image_rows(prod, targets, own, scale):
    left = [prod[8 * k : 8 * k + 8, :128] for k in range(4)]
    right = [prod[8 * k : 8 * k + 8, 128:] for k in range(4)]
    x = [targets[a : a + 1] for a in range(3)]
    first = x[0] * left[0] + x[1] * left[1] + x[2] * left[2] - left[3]
    other = x[0] * right[0] + x[1] * right[1] + x[2] * right[2] - right[3]
    parts = [pltpu.roll(first, 64, 1), other, pltpu.roll(other, 64, 1)]
    return [(left[a] + parts[a] + targets[3:4] * own[a]) * scale for a in range(3)]


def write_piece(images, out):
    rows = []
    for image in images:
        top, bottom = image[:4], pltpu.roll(image[4:], 64, 1)
        rows.append(jnp.where(low_half((4, 128)), top, bottom))
    message = jnp.concatenate([row[:HALF] for row in rows], axis=0)
    block = jnp.concatenate([message] * 8, axis=0)

    def put(m):
        out[pl.ds(m * 8 * LATER, 8 * LATER)] = block

    each_wide(out.shape[0] // (8 * LATER), put)


def each_wide(count, put):
    if count <= 64:
        for m in range(count):
            put(m)
    else:
        pl.loop(0, count)(put)


def pack_kernel(*refs):
    sources, (out, tgt, lists), held = refs[:6], refs[6:9], refs[9:15]
    block, sems = refs[15:]
    copies = [
        pltpu.make_async_copy(src, dst, sems.at[i])
        for i, (src, dst) in enumerate(zip(sources, held))
    ]
    for copy in copies:
        copy.start()
    for copy in copies[:4]:
        copy.wait()
    velocity, points, area, self_term, index, weight = held
    count = index.shape[0]
    field = velocity[...]
    spot = points[...]
    rows = []
    for a in range(3):
        vec = field[:, a, :]
        rows.append(jnp.concatenate([vec[:HALF], vec[HALF:]], axis=1))
    mine = jnp.concatenate([spot, self_term[...]], axis=0)
    mine = jnp.concatenate([mine, mine], axis=1)
    tgt[...] = jnp.concatenate([mine, mine], axis=0)
    left = jnp.concatenate([spot[0:1], spot[2:3]], axis=0)
    right = jnp.concatenate([spot[1:2], area[...]], axis=0)
    rows.append(jnp.concatenate([left, right], axis=1))
    message = jnp.concatenate(rows, axis=0)
    size = block.shape[0]
    block[...] = jnp.concatenate([message] * 8, axis=0)
    leaving = [
        pltpu.make_async_copy(block, out.at[pl.ds(i * size, size)], sems.at[6 + i])
        for i in range(out.shape[0] // size)
    ]
    for copy in leaving:
        copy.start()
    for copy in copies[4:]:
        copy.wait()
    lists[:count] = index[...].astype(F32)
    lists[count:] = weight[...]
    for copy in leaving:
        copy.wait()


def extra_kernel(me, lists, out):
    row, col = me[1], me[2]
    lines = lax.broadcasted_iota(jnp.int32, (128, 128), 0).astype(F32)
    count = lists.shape[0] // 2
    half = count // 2
    low = low_half((half, 128))
    odd = col % 2 == 1
    both = lists[:, lines_of(col // 2)]
    place = both[:count].astype(jnp.int32)
    place = (((place // 64) ^ row) * 64 + place % 64).astype(F32)
    packed = []
    for value in (place, both[count:]):
        top, bottom = value[:half], value[half:]
        lower = jnp.where(low, top, pltpu.roll(bottom, 64, 1))
        upper = jnp.where(low, pltpu.roll(top, 64, 1), bottom)
        packed.append(jnp.where(odd, upper, lower))
    index, weight = packed

    def build(u):
        line = lines + (u * 128.0 if isinstance(u, int) else (u * 128).astype(F32))
        total = jnp.zeros((128, 128), F32)
        for k in range(half):
            total = total + jnp.where(line == index[k : k + 1], weight[k : k + 1], 0.0)
        turned = total.T
        out[u] = turned[:64] + turned[64:]

    each(out.shape[0], build)


def first_kernel(
    n_row, n_col, piece, *refs
):
    extra = refs[:n_col]
    tgt, me_ref, kernels, places, basis, norm_out, out, cols, *sums = refs[n_col:]
    half = n_row // 2
    n_chunk = n_row * n_col // 2
    me = me_ref[0]
    total = Sums(1, sums[0] if sums else None)

    def unpack(chunk):
        vec = [
            chunk_parts(piece, chunk, me, n_row, n_col, FIRST, HALF * a, 4)
            for a in range(3)
        ]
        spot = chunk_parts(piece, chunk, me, n_row, n_col, FIRST, 3 * HALF, 2)
        places[chunk] = spot
        for a in range(3):
            basis[chunk, a] = vec[a]
        total.add(chunk, 0, vec, vec)
        write_columns(cols, spot, chunk, vec)

    turned = tgt[...].T
    x = [jnp.broadcast_to(turned[:64, a : a + 1], (64, 128)) for a in range(3)]

    def build(chunk):
        unpack(chunk)
        y = places[chunk]
        d = [x[a] - y[k : k + 1] for a, k in enumerate(ORDER)]
        dist = d[0] * d[0] + d[1] * d[1] + d[2] * d[2]
        root = lax.rsqrt(dist + BLOB_SQ)
        two = (y[3:4] * INV_EIGHT_PI) * root * root * root
        one = (dist + 2.0 * BLOB_SQ) * two
        if isinstance(chunk, int):
            one = one + extra[chunk // half][chunk % half]
        else:
            for o in range(n_col):
                mine = extra[o][chunk % half]
                one = one + jnp.where(chunk // half == o, mine, 0.0)
        moved = [two * part for part in d]
        at = lines_of(chunk)
        for k, pair in enumerate(([one, moved[0]], moved[1:])):
            value = jnp.concatenate(pair, axis=0).T
            high = value.astype(BF16)
            kernels[at, 128 * k : 128 * k + 128] = high
            kernels[at, 256 + 128 * k : 384 + 128 * k] = (value - high.astype(F32)).astype(BF16)

    prod = products(n_chunk, build, cols, kernels)
    norm = jnp.sqrt(total.get(0))
    scale = 1.0 / norm
    norm_out[0] = norm
    norm_out[1] = scale
    write_piece(image_rows(prod, tgt, basis[0], scale), out)


def middle_kernel(n_row, n_col, n_base, final, piece, *refs):
    bases, norms = refs[:n_base], refs[n_base : 2 * n_base]
    if final:
        kernels, places, tgt, me_ref, own, h_out, out, basis, cols, *held = refs[2 * n_base :]
    else:
        kernels, places, tgt, me_ref, basis, h_out, out, cols, *held = refs[2 * n_base :]
    n_chunk = n_row * n_col // 2
    me = me_ref[0]
    scales = [norm[norm.shape[0] - 1] for norm in norms]
    cross = [(i, j) for i in range(n_base) for j in range(i)]
    sums = Sums(2 * n_base + 1 + len(cross), held[0] if held else None)

    def unpack(chunk):
        vec = [
            chunk_parts(piece, chunk, me, n_row, n_col, LATER, HALF * a, 4)
            for a in range(3)
        ]
        old = [[base[chunk, a] for a in range(3)] for base in bases]
        for a in range(3):
            basis[chunk, a] = vec[a]
        for j in range(n_base):
            sums.add(chunk, j, vec, old[j])
        for at, (i, j) in enumerate(cross):
            sums.add(chunk, 2 * n_base + 1 + at, old[i], old[j])

    each(n_chunk, unpack)
    gram = {}
    for at, (i, j) in enumerate(cross):
        gram[j, i] = sums.get(2 * n_base + 1 + at) * (scales[i] * scales[j])
    column = []
    for j in range(n_base):
        h = sums.get(j) * scales[j]
        for i in range(j):
            h = h - column[i] * gram[i, j]
        column.append(h)
        h_out[j] = h
    factors = [h * scale for h, scale in zip(column, scales)]

    def columns(chunk):
        old = [[base[chunk, a] for a in range(3)] for base in bases]
        vec = []
        for a in range(3):
            value = basis[chunk, a]
            for j in range(n_base):
                value = value - factors[j] * old[j][a]
            vec.append(value)
            basis[chunk, a] = value
        sums.add(chunk, n_base, vec, vec)
        write_columns(cols, places[chunk], chunk, vec)
        if final:
            for j in range(n_base):
                sums.add(chunk, n_base + 1 + j, vec, old[j])

    prod = products(n_chunk, columns, cols, kernels)
    norm = jnp.sqrt(sums.get(n_base))
    scale = 1.0 / norm
    h_out[n_base] = norm
    images = image_rows(prod, tgt, basis[0], scale)
    if not final:
        h_out[n_base + 1] = scale
        write_piece(images, out)
        return
    every = [*bases, basis]
    for j, base in enumerate(every):
        for a in range(3):
            own[j, a] = base[0, a] * [*scales, scale][j]
    for j in range(n_base):
        gram[j, n_base] = sums.get(n_base + 1 + j) * (scale * scales[j])
    for at, pair in enumerate(PAIRS):
        h_out[n_base + 1 + at] = gram[pair]
    low = low_half((ROWS, 128))
    row = jnp.zeros((ROWS, 128), F32)
    for j in range(ITERS + 1):
        other = images if j == ITERS else [own[j, a] for a in range(3)]
        part = sum(images[a] * other[a] for a in range(3))
        part = row_sum(jnp.where(low, part, 0.0))
        row = row + jnp.where(place_of(j), part, 0.0)
    row = jnp.sum(row, axis=0, keepdims=True)

    def put(m):
        out[pl.ds(m, 1)] = row

    each_wide(out.shape[0], put)


def solve_small(hessen, start_norm, count):
    zero = jnp.zeros_like(start_norm)
    target = [start_norm] + [zero] * count
    cosines = []
    sines = []
    triangle = {}
    for k in range(count):
        column = [hessen[i, k] for i in range(k + 2)]
        for j in range(k):
            first_val = column[j]
            second_val = column[j + 1]
            column[j] = cosines[j] * first_val + sines[j] * second_val
            column[j + 1] = cosines[j] * second_val - sines[j] * first_val
        radius = jnp.sqrt(column[k] * column[k] + column[k + 1] * column[k + 1])
        cosine = column[k] / radius
        sine = column[k + 1] / radius
        cosines.append(cosine)
        sines.append(sine)
        for i in range(k):
            triangle[i, k] = column[i]
        triangle[k, k] = radius
        target[k + 1] = -sine * target[k]
        target[k] = cosine * target[k]
    coeffs = [None] * count
    for k in range(count - 1, -1, -1):
        accum = target[k]
        for i in range(k + 1, count):
            accum = accum - triangle[k, i] * coeffs[i]
        coeffs[k] = accum / triangle[k, k]
    return coeffs


def last_kernel(sums, own, *refs):
    columns = refs[: ITERS - 1]
    norm, out = refs[ITERS - 1 :]
    hessen = {}
    for k in range(ITERS - 1):
        for j in range(k + 2):
            hessen[j, k] = columns[k][j]
    gram = {(j, j): 1.0 for j in range(ITERS)}
    for at, (i, j) in enumerate(PAIRS):
        gram[i, j] = gram[j, i] = columns[-1][ITERS + at]
    row = jnp.broadcast_to(jnp.sum(sums[...], axis=0, keepdims=True), (ROWS, 128))
    inner = [
        jnp.broadcast_to(row_sum(jnp.where(place_of(j), row, 0.0)), (ROWS, 128))
        for j in range(ITERS + 1)
    ]
    square = inner[ITERS]
    for j in range(ITERS):
        h = inner[j]
        for i in range(j):
            h = h - hessen[i, ITERS - 1] * gram[i, j]
        hessen[j, ITERS - 1] = h
    for j in range(ITERS):
        rest = -2.0 * inner[j]
        for i in range(ITERS):
            rest = rest + hessen[i, ITERS - 1] * gram[i, j]
        square = square + hessen[j, ITERS - 1] * rest
    hessen[ITERS, ITERS - 1] = jnp.sqrt(jnp.maximum(square, 0.0))
    coeffs = solve_small(hessen, norm[0], ITERS)
    for a in range(3):
        density = sum(coeffs[k] * own[k, a] for k in range(ITERS))
        out[:HALF, a, :] = density[:HALF, :64]
        out[HALF:, a, :] = density[4 : 4 + HALF, :64]


def call(kernel, outs, scratch, operands, scalars=(), far=(), spread_out=False, flops=0):
    vmem = pl.BlockSpec(memory_space=pltpu.VMEM)
    smem = pl.BlockSpec(memory_space=pltpu.SMEM)
    count = len(operands)
    hbm = pl.BlockSpec(memory_space=pltpu.HBM)
    specs = [smem if i in scalars else hbm if i in far else vmem for i in range(count)]
    moved = sum(x.size * x.dtype.itemsize for x in operands)
    return pl.pallas_call(
        kernel,
        out_shape=[jax.ShapeDtypeStruct(s, t) for s, t in outs],
        in_specs=specs,
        out_specs=[pl.BlockSpec(memory_space=pl.ANY) if spread_out and i == 0 else vmem for i in range(len(outs))],
        scratch_shapes=scratch,
        cost_estimate=pl.CostEstimate(flops=flops, bytes_accessed=moved, transcendentals=0),
        compiler_params=pltpu.CompilerParams(vmem_limit_bytes=48 * 1024 * 1024),
    )(*operands)


def body(sizes, velocity, points, panel_area, self_term, near_index, near_weight):
    n_row, n_col = sizes[0] * sizes[1] * sizes[2], sizes[3]
    n = n_row * n_col
    n_chunk = n // 2
    total = n * 64
    row = lax.axis_index(AXES[:3])
    col = lax.axis_index("col")
    me = jnp.stack([row * n_col + col, row, col]).astype(jnp.int32)
    rhs = velocity.shape[0]

    message = ((n * LATER, 128), F32)
    sources = [
        velocity,
        points,
        panel_area[None],
        self_term[None],
        near_index.T,
        near_weight.T,
    ]
    wide, tgt, lists = call(
        pack_kernel,
        [
            ((n * FIRST, 128), F32),
            ((8, 128), F32),
            ((2 * near_index.shape[1], near_index.shape[0]), F32),
        ],
        [pltpu.VMEM(x.shape, x.dtype) for x in sources]
        + [pltpu.VMEM((8 * FIRST, 128), F32), pltpu.SemaphoreType.DMA((6 + n // 8,))],
        [pltpu.with_memory_space_constraint(x, pltpu.HBM) for x in sources],
        far=range(6),
        spread_out=True,
    )
    piece = spread(wide, n)
    near = [lists] + [lax.ppermute(lists, "col", xor_perm(n_col, o)) for o in range(1, n_col)]
    extra = [
        call(
            extra_kernel,
            [((n_row // 2, 64, 128), F32)],
            [],
            [me, pair],
            {0},
            flops=10**8,
        )[0]
        for pair in near
    ]

    vec_shape = (n_chunk, 3, ROWS, 128)
    cols = pltpu.VMEM((64, total), BF16)
    held = [] if n_chunk <= 16 else [pltpu.VMEM((8, ROWS, 128), F32)]
    kernels, places, basis, norm, wide = call(
        functools.partial(first_kernel, n_row, n_col),
        [
            ((total, 512), BF16),
            ((n_chunk, 4, 128), F32),
            (vec_shape, F32),
            ((2, ROWS, 128), F32),
            message,
        ],
        [cols, *held],
        [piece, *extra, tgt, me],
        {n_col + 2},
    )
    bases = [basis]
    columns = [norm]
    for k in range(1, ITERS):
        final = k == ITERS - 1
        piece = spread(wide, n)
        main, column, wide = call(
            functools.partial(middle_kernel, n_row, n_col, k, final),
            [
                ((ITERS, 3, ROWS, 128) if final else vec_shape, F32),
                ((k + 1 + (len(PAIRS) if final else 1), ROWS, 128), F32),
                ((n, 128), F32) if final else message,
            ],
            [*([pltpu.VMEM(vec_shape, F32)] if final else []), cols, *held],
            [piece, *bases, *columns, kernels, places, tgt, me],
            {2 * k + 4},
        )
        bases.append(main)
        columns.append(column)
    sums = spread(wide, n)
    (density,) = call(
        last_kernel, [((rhs, 3, 64), F32)], [], [sums, bases[-1], *columns[1:], columns[0]]
    )
    return density


def solution(mesh):
    n_row, n_col = mesh.shape["row"], mesh.shape["col"]
    sizes = (n_row // 4, 2, 2, n_col)
    split = jax.sharding.Mesh(mesh.devices.reshape(sizes), AXES)
    return jax.shard_map(
        functools.partial(body, sizes),
        mesh=split,
        in_specs=(
            P(None, None, AXES),
            P(None, AXES),
            P(AXES),
            P(AXES),
            P(AXES[:3], "col"),
            P(AXES[:3], "col"),
        ),
        out_specs=P(None, None, AXES),
        check_vma=False,
    )
```

```python
import functools
import math

import jax
import jax.numpy as jnp
from jax import lax
from jax.experimental import pallas as pl
from jax.experimental.pallas import tpu as pltpu
from jax.sharding import PartitionSpec as P

ITERS = 3
BLOB_SQ = 0.0025
INV_EIGHT_PI = 1.0 / (8.0 * math.pi)
ROWS = 8
HALF = 3
FIRST, LATER = 11, 9
ORDER = (0, 2, 1)
AXES = ("top", "mid", "core", "col")
F32 = jnp.float32
BF16 = jnp.bfloat16


def position(sizes):
    top, mid, core, col = (lax.axis_index(axis) for axis in AXES)
    row = (top * sizes[1] + mid) * sizes[2] + core
    return row * sizes[3] + col, row, col


def low_half(shape):
    return lax.broadcasted_iota(jnp.int32, shape, len(shape) - 1) < 64


def xor_perm(n, m):
    return [(d, d ^ m) for d in range(n)]


def spread(rows, n):
    wide = rows.reshape(n, -1, 1, 128)
    return lax.all_to_all(wide, AXES, 0, 0, tiled=True).reshape(rows.shape)


def each(count, step):
    if count <= 16:
        for i in range(count):
            step(i)
    else:
        pl.loop(0, count)(step)


class Sums:
    def __init__(self, count, refs):
        self.refs = refs
        self.parts = [[None] * 4 for _ in range(count)]
        if refs is not None:
            for at in range(count):
                refs[at] = jnp.zeros((ROWS, 128), F32)

    def add(self, chunk, at, left, right):
        part = sum(left[a] * right[a] for a in range(3))
        if self.refs is not None:
            self.refs[at] = self.refs[at] + part
            return
        held = self.parts[at]
        slot = chunk % 4
        held[slot] = part if held[slot] is None else held[slot] + part

    def get(self, at):
        if self.refs is not None:
            total = self.refs[at]
        else:
            held = self.parts[at]
            total = (held[0] + held[1]) + (held[2] + held[3])
        return jnp.broadcast_to(jnp.sum(total, axis=1, keepdims=True), (ROWS, 128))


def chunk_parts(piece, chunk, me, n_row, n_col, size, at, count):
    half = n_row // 2
    o = chunk // half
    u = chunk % half
    early = max(at + count - size, 0)
    even = piece[pl.ds((me ^ ((2 * u) * n_col + o)) * size + at - early, count)]
    odd = piece[pl.ds((me ^ ((2 * u + 1) * n_col + o)) * size + at - early, count)]
    low = low_half((count, 128))
    first = jnp.where(low, even, pltpu.roll(odd, 64, 1))
    second = jnp.where(low, pltpu.roll(even, 64, 1), odd)
    rows = jnp.concatenate([first, second], axis=0)
    return pltpu.roll(rows, ROWS - early, 0) if early else rows


PAIRS = [(i, j) for i in range(ITERS) for j in range(i + 1, ITERS)]


def place_of(j):
    lane = lax.broadcasted_iota(jnp.int32, (ROWS, 128), 1)
    return lane == lax.broadcasted_iota(jnp.int32, (ROWS, 128), 0) * (ITERS + 1) + j


def row_sum(acc):
    return jnp.sum(acc, axis=1, keepdims=True)


def lines_of(chunk):
    if isinstance(chunk, int):
        return pl.ds(chunk * 128, 128)
    return pl.ds(pl.multiple_of(chunk * 128, 128), 128)


def write_columns(cols, y, chunk, f):
    inner = sum(y[k : k + 1] * f[a] for a, k in enumerate(ORDER))
    full = jnp.concatenate([*f, inner], axis=0)
    high = full.astype(BF16)
    at = lines_of(chunk)
    cols[0:32, at] = high
    cols[32:64, at] = (full - high.astype(F32)).astype(BF16)


def contract(cols, kernels):
    prod = jnp.dot(cols, kernels, preferred_element_type=F32)
    return prod[:32, :256] + (prod[32:, :256] + prod[:32, 256:])


def products(n_chunk, columns, cols, kernels):
    if n_chunk <= 16:
        for chunk in range(n_chunk):
            columns(chunk)
        return contract(cols[...], kernels[...])
    pl.loop(0, n_chunk)(columns)

    def turn(i, acc):
        at = pl.ds(pl.multiple_of(i * 2048, 2048), 2048)
        return acc + contract(cols[:, at], kernels[at, :])

    return lax.fori_loop(0, n_chunk // 16, turn, jnp.zeros((32, 256), F32))


def image_rows(prod, targets, own, scale):
    left = [prod[8 * k : 8 * k + 8, :128] for k in range(4)]
    right = [prod[8 * k : 8 * k + 8, 128:] for k in range(4)]
    x = [targets[a : a + 1] for a in range(3)]
    first = x[0] * left[0] + x[1] * left[1] + x[2] * left[2] - left[3]
    other = x[0] * right[0] + x[1] * right[1] + x[2] * right[2] - right[3]
    parts = [pltpu.roll(first, 64, 1), other, pltpu.roll(other, 64, 1)]
    return [(left[a] + parts[a] + targets[3:4] * own[a]) * scale for a in range(3)]


def write_piece(images, out):
    rows = []
    for image in images:
        top, bottom = image[:4], pltpu.roll(image[4:], 64, 1)
        rows.append(jnp.where(low_half((4, 128)), top, bottom))
    message = jnp.concatenate([row[:HALF] for row in rows], axis=0)
    block = jnp.concatenate([message] * 8, axis=0)

    def put(m):
        out[pl.ds(m * 8 * LATER, 8 * LATER)] = block

    each_wide(out.shape[0] // (8 * LATER), put)


def each_wide(count, put):
    if count <= 64:
        for m in range(count):
            put(m)
    else:
        pl.loop(0, count)(put)


def pack_kernel(*refs):
    sources, (out, tgt, lists), held = refs[:6], refs[6:9], refs[9:15]
    block, sems = refs[15:]
    copies = [
        pltpu.make_async_copy(src, dst, sems.at[i])
        for i, (src, dst) in enumerate(zip(sources, held))
    ]
    for copy in copies:
        copy.start()
    for copy in copies[:4]:
        copy.wait()
    velocity, points, area, self_term, index, weight = held
    count = index.shape[0]
    field = velocity[...]
    spot = points[...]
    rows = []
    for a in range(3):
        vec = field[:, a, :]
        rows.append(jnp.concatenate([vec[:HALF], vec[HALF:]], axis=1))
    mine = jnp.concatenate([spot, self_term[...]], axis=0)
    mine = jnp.concatenate([mine, mine], axis=1)
    tgt[...] = jnp.concatenate([mine, mine], axis=0)
    left = jnp.concatenate([spot[0:1], spot[2:3]], axis=0)
    right = jnp.concatenate([spot[1:2], area[...]], axis=0)
    rows.append(jnp.concatenate([left, right], axis=1))
    message = jnp.concatenate(rows, axis=0)
    size = block.shape[0]
    block[...] = jnp.concatenate([message] * 8, axis=0)
    leaving = [
        pltpu.make_async_copy(block, out.at[pl.ds(i * size, size)], sems.at[6 + i])
        for i in range(out.shape[0] // size)
    ]
    for copy in leaving:
        copy.start()
    for copy in copies[4:]:
        copy.wait()
    lists[:count] = index[...].astype(F32)
    lists[count:] = weight[...]
    for copy in leaving:
        copy.wait()


def extra_kernel(sizes, lists, out):
    _, row, col = position(sizes)
    lines = lax.broadcasted_iota(jnp.int32, (128, 128), 0).astype(F32)
    count = lists.shape[0] // 2
    half = count // 2
    low = low_half((half, 128))
    odd = col % 2 == 1
    both = lists[:, lines_of(col // 2)]
    place = both[:count].astype(jnp.int32)
    place = (((place // 64) ^ row) * 64 + place % 64).astype(F32)
    packed = []
    for value in (place, both[count:]):
        top, bottom = value[:half], value[half:]
        lower = jnp.where(low, top, pltpu.roll(bottom, 64, 1))
        upper = jnp.where(low, pltpu.roll(top, 64, 1), bottom)
        packed.append(jnp.where(odd, upper, lower))
    index, weight = packed

    def build(u):
        line = lines + (u * 128.0 if isinstance(u, int) else (u * 128).astype(F32))
        total = jnp.zeros((128, 128), F32)
        for k in range(half):
            total = total + jnp.where(line == index[k : k + 1], weight[k : k + 1], 0.0)
        turned = total.T
        out[u] = turned[:64] + turned[64:]

    each(out.shape[0], build)


def first_kernel(sizes, piece, *refs):
    n_row, n_col = sizes[0] * sizes[1] * sizes[2], sizes[3]
    extra = refs[:n_col]
    tgt, kernels, places, basis, norm_out, out, cols, *sums = refs[n_col:]
    half = n_row // 2
    n_chunk = n_row * n_col // 2
    me, _, _ = position(sizes)
    total = Sums(1, sums[0] if sums else None)

    def unpack(chunk):
        vec = [
            chunk_parts(piece, chunk, me, n_row, n_col, FIRST, HALF * a, 4)
            for a in range(3)
        ]
        spot = chunk_parts(piece, chunk, me, n_row, n_col, FIRST, 3 * HALF, 2)
        places[chunk] = spot
        for a in range(3):
            basis[chunk, a] = vec[a]
        total.add(chunk, 0, vec, vec)
        write_columns(cols, spot, chunk, vec)

    turned = tgt[...].T
    x = [jnp.broadcast_to(turned[:64, a : a + 1], (64, 128)) for a in range(3)]

    def build(chunk):
        unpack(chunk)
        y = places[chunk]
        d = [x[a] - y[k : k + 1] for a, k in enumerate(ORDER)]
        dist = d[0] * d[0] + d[1] * d[1] + d[2] * d[2]
        root = lax.rsqrt(dist + BLOB_SQ)
        two = (y[3:4] * INV_EIGHT_PI) * root * root * root
        one = (dist + 2.0 * BLOB_SQ) * two
        if isinstance(chunk, int):
            one = one + extra[chunk // half][chunk % half]
        else:
            for o in range(n_col):
                mine = extra[o][chunk % half]
                one = one + jnp.where(chunk // half == o, mine, 0.0)
        moved = [two * part for part in d]
        at = lines_of(chunk)
        for k, pair in enumerate(([one, moved[0]], moved[1:])):
            value = jnp.concatenate(pair, axis=0).T
            high = value.astype(BF16)
            kernels[at, 128 * k : 128 * k + 128] = high
            kernels[at, 256 + 128 * k : 384 + 128 * k] = (value - high.astype(F32)).astype(BF16)

    prod = products(n_chunk, build, cols, kernels)
    norm = jnp.sqrt(total.get(0))
    scale = 1.0 / norm
    norm_out[0] = norm
    norm_out[1] = scale
    write_piece(image_rows(prod, tgt, basis[0], scale), out)


def middle_kernel(sizes, n_base, final, piece, *refs):
    n_row, n_col = sizes[0] * sizes[1] * sizes[2], sizes[3]
    bases, norms = refs[:n_base], refs[n_base : 2 * n_base]
    if final:
        kernels, places, tgt, own, h_out, out, basis, cols, *held = refs[2 * n_base :]
    else:
        kernels, places, tgt, basis, h_out, out, cols, *held = refs[2 * n_base :]
    n_chunk = n_row * n_col // 2
    me, _, _ = position(sizes)
    scales = [norm[norm.shape[0] - 1] for norm in norms]
    cross = [(i, j) for i in range(n_base) for j in range(i)]
    sums = Sums(2 * n_base + 1 + len(cross), held[0] if held else None)

    def unpack(chunk):
        vec = [
            chunk_parts(piece, chunk, me, n_row, n_col, LATER, HALF * a, 4)
            for a in range(3)
        ]
        old = [[base[chunk, a] for a in range(3)] for base in bases]
        for a in range(3):
            basis[chunk, a] = vec[a]
        for j in range(n_base):
            sums.add(chunk, j, vec, old[j])
        for at, (i, j) in enumerate(cross):
            sums.add(chunk, 2 * n_base + 1 + at, old[i], old[j])

    each(n_chunk, unpack)
    gram = {}
    for at, (i, j) in enumerate(cross):
        gram[j, i] = sums.get(2 * n_base + 1 + at) * (scales[i] * scales[j])
    column = []
    for j in range(n_base):
        h = sums.get(j) * scales[j]
        for i in range(j):
            h = h - column[i] * gram[i, j]
        column.append(h)
        h_out[j] = h
    factors = [h * scale for h, scale in zip(column, scales)]

    def columns(chunk):
        old = [[base[chunk, a] for a in range(3)] for base in bases]
        vec = []
        for a in range(3):
            value = basis[chunk, a]
            for j in range(n_base):
                value = value - factors[j] * old[j][a]
            vec.append(value)
            basis[chunk, a] = value
        sums.add(chunk, n_base, vec, vec)
        write_columns(cols, places[chunk], chunk, vec)
        if final:
            for j in range(n_base):
                sums.add(chunk, n_base + 1 + j, vec, old[j])

    prod = products(n_chunk, columns, cols, kernels)
    norm = jnp.sqrt(sums.get(n_base))
    scale = 1.0 / norm
    h_out[n_base] = norm
    images = image_rows(prod, tgt, basis[0], scale)
    if not final:
        h_out[n_base + 1] = scale
        write_piece(images, out)
        return
    every = [*bases, basis]
    for j, base in enumerate(every):
        for a in range(3):
            own[j, a] = base[0, a] * [*scales, scale][j]
    for j in range(n_base):
        gram[j, n_base] = sums.get(n_base + 1 + j) * (scale * scales[j])
    for at, pair in enumerate(PAIRS):
        h_out[n_base + 1 + at] = gram[pair]
    low = low_half((ROWS, 128))
    row = jnp.zeros((ROWS, 128), F32)
    for j in range(ITERS + 1):
        other = images if j == ITERS else [own[j, a] for a in range(3)]
        part = sum(images[a] * other[a] for a in range(3))
        part = row_sum(jnp.where(low, part, 0.0))
        row = row + jnp.where(place_of(j), part, 0.0)
    row = jnp.sum(row, axis=0, keepdims=True)

    def put(m):
        out[pl.ds(m, 1)] = row

    each_wide(out.shape[0], put)


def solve_small(hessen, start_norm, count):
    zero = jnp.zeros_like(start_norm)
    target = [start_norm] + [zero] * count
    cosines = []
    sines = []
    triangle = {}
    for k in range(count):
        column = [hessen[i, k] for i in range(k + 2)]
        for j in range(k):
            first_val = column[j]
            second_val = column[j + 1]
            column[j] = cosines[j] * first_val + sines[j] * second_val
            column[j + 1] = cosines[j] * second_val - sines[j] * first_val
        radius = jnp.sqrt(column[k] * column[k] + column[k + 1] * column[k + 1])
        cosine = column[k] / radius
        sine = column[k + 1] / radius
        cosines.append(cosine)
        sines.append(sine)
        for i in range(k):
            triangle[i, k] = column[i]
        triangle[k, k] = radius
        target[k + 1] = -sine * target[k]
        target[k] = cosine * target[k]
    coeffs = [None] * count
    for k in range(count - 1, -1, -1):
        accum = target[k]
        for i in range(k + 1, count):
            accum = accum - triangle[k, i] * coeffs[i]
        coeffs[k] = accum / triangle[k, k]
    return coeffs


def last_kernel(sums, own, *refs):
    columns = refs[: ITERS - 1]
    norm, out = refs[ITERS - 1 :]
    hessen = {}
    for k in range(ITERS - 1):
        for j in range(k + 2):
            hessen[j, k] = columns[k][j]
    gram = {(j, j): 1.0 for j in range(ITERS)}
    for at, (i, j) in enumerate(PAIRS):
        gram[i, j] = gram[j, i] = columns[-1][ITERS + at]
    row = jnp.broadcast_to(jnp.sum(sums[...], axis=0, keepdims=True), (ROWS, 128))
    inner = [
        jnp.broadcast_to(row_sum(jnp.where(place_of(j), row, 0.0)), (ROWS, 128))
        for j in range(ITERS + 1)
    ]
    square = inner[ITERS]
    for j in range(ITERS):
        h = inner[j]
        for i in range(j):
            h = h - hessen[i, ITERS - 1] * gram[i, j]
        hessen[j, ITERS - 1] = h
    for j in range(ITERS):
        rest = -2.0 * inner[j]
        for i in range(ITERS):
            rest = rest + hessen[i, ITERS - 1] * gram[i, j]
        square = square + hessen[j, ITERS - 1] * rest
    hessen[ITERS, ITERS - 1] = jnp.sqrt(jnp.maximum(square, 0.0))
    coeffs = solve_small(hessen, norm[0], ITERS)
    for a in range(3):
        density = sum(coeffs[k] * own[k, a] for k in range(ITERS))
        out[:HALF, a, :] = density[:HALF, :64]
        out[HALF:, a, :] = density[4 : 4 + HALF, :64]


def call(kernel, outs, scratch, operands, far=(), spread_out=False, flops=0):
    vmem = pl.BlockSpec(memory_space=pltpu.VMEM)
    count = len(operands)
    hbm = pl.BlockSpec(memory_space=pltpu.HBM)
    specs = [hbm if i in far else vmem for i in range(count)]
    moved = sum(x.size * x.dtype.itemsize for x in operands)
    return pl.pallas_call(
        kernel,
        out_shape=[jax.ShapeDtypeStruct(s, t) for s, t in outs],
        in_specs=specs,
        out_specs=[pl.BlockSpec(memory_space=pl.ANY) if spread_out and i == 0 else vmem for i in range(len(outs))],
        scratch_shapes=scratch,
        cost_estimate=pl.CostEstimate(flops=flops, bytes_accessed=moved, transcendentals=0),
        compiler_params=pltpu.CompilerParams(vmem_limit_bytes=48 * 1024 * 1024),
    )(*operands)


def body(sizes, velocity, points, panel_area, self_term, near_index, near_weight):
    n_row, n_col = sizes[0] * sizes[1] * sizes[2], sizes[3]
    n = n_row * n_col
    n_chunk = n // 2
    total = n * 64
    rhs = velocity.shape[0]

    message = ((n * LATER, 128), F32)
    sources = [
        velocity,
        points,
        panel_area[None],
        self_term[None],
        near_index.T,
        near_weight.T,
    ]
    wide, tgt, lists = call(
        pack_kernel,
        [
            ((n * FIRST, 128), F32),
            ((8, 128), F32),
            ((2 * near_index.shape[1], near_index.shape[0]), F32),
        ],
        [pltpu.VMEM(x.shape, x.dtype) for x in sources]
        + [pltpu.VMEM((8 * FIRST, 128), F32), pltpu.SemaphoreType.DMA((6 + n // 8,))],
        [pltpu.with_memory_space_constraint(x, pltpu.HBM) for x in sources],
        far=range(6),
        spread_out=True,
    )
    piece = spread(wide, n)
    near = [lists] + [lax.ppermute(lists, "col", xor_perm(n_col, o)) for o in range(1, n_col)]
    extra = [
        call(
            functools.partial(extra_kernel, sizes),
            [((n_row // 2, 64, 128), F32)],
            [],
            [pair],
            flops=10**8,
        )[0]
        for pair in near
    ]

    vec_shape = (n_chunk, 3, ROWS, 128)
    cols = pltpu.VMEM((64, total), BF16)
    held = [] if n_chunk <= 16 else [pltpu.VMEM((8, ROWS, 128), F32)]
    kernels, places, basis, norm, wide = call(
        functools.partial(first_kernel, sizes),
        [
            ((total, 512), BF16),
            ((n_chunk, 4, 128), F32),
            (vec_shape, F32),
            ((2, ROWS, 128), F32),
            message,
        ],
        [cols, *held],
        [piece, *extra, tgt],
    )
    bases = [basis]
    columns = [norm]
    for k in range(1, ITERS):
        final = k == ITERS - 1
        piece = spread(wide, n)
        main, column, wide = call(
            functools.partial(middle_kernel, sizes, k, final),
            [
                ((ITERS, 3, ROWS, 128) if final else vec_shape, F32),
                ((k + 1 + (len(PAIRS) if final else 1), ROWS, 128), F32),
                ((n, 128), F32) if final else message,
            ],
            [*([pltpu.VMEM(vec_shape, F32)] if final else []), cols, *held],
            [piece, *bases, *columns, kernels, places, tgt],
        )
        bases.append(main)
        columns.append(column)
    sums = spread(wide, n)
    (density,) = call(
        last_kernel, [((rhs, 3, 64), F32)], [], [sums, bases[-1], *columns[1:], columns[0]]
    )
    return density


def solution(mesh):
    n_row, n_col = mesh.shape["row"], mesh.shape["col"]
    sizes = (n_row // 4, 2, 2, n_col)
    split = jax.sharding.Mesh(mesh.devices.reshape(sizes), AXES)
    return jax.shard_map(
        functools.partial(body, sizes),
        mesh=split,
        in_specs=(
            P(None, None, AXES),
            P(None, AXES),
            P(AXES),
            P(AXES),
            P(AXES[:3], "col"),
            P(AXES[:3], "col"),
        ),
        out_specs=P(None, None, AXES),
        check_vma=False,
    )
```

```python
import functools
import math

import jax
import jax.numpy as jnp
from jax import lax
from jax.experimental import pallas as pl
from jax.experimental.pallas import tpu as pltpu
from jax.sharding import PartitionSpec as P

ITERS = 3
BLOB_SQ = 0.0025
INV_EIGHT_PI = 1.0 / (8.0 * math.pi)
ROWS = 8
HALF = 3
FIRST, LATER = 11, 9
ORDER = (0, 2, 1)
AXES = ("top", "mid", "core", "col")
F32 = jnp.float32
BF16 = jnp.bfloat16


def position(sizes):
    top, mid, core, col = (lax.axis_index(axis) for axis in AXES)
    row = (top * sizes[1] + mid) * sizes[2] + core
    return row * sizes[3] + col, row, col


def low_half(shape):
    return lax.broadcasted_iota(jnp.int32, shape, len(shape) - 1) < 64


def xor_perm(n, m):
    return [(d, d ^ m) for d in range(n)]


def spread(rows, n):
    wide = rows.reshape(n, -1, 1, 128)
    return lax.all_to_all(wide, AXES, 0, 0, tiled=True).reshape(rows.shape)


def each(count, step):
    if count <= 16:
        for i in range(count):
            step(i)
    else:
        pl.loop(0, count)(step)


class Sums:
    def __init__(self, count, refs):
        self.refs = refs
        self.parts = [[None] * 4 for _ in range(count)]
        if refs is not None:
            for at in range(count):
                refs[at] = jnp.zeros((ROWS, 128), F32)

    def add(self, chunk, at, left, right):
        part = sum(left[a] * right[a] for a in range(3))
        if self.refs is not None:
            self.refs[at] = self.refs[at] + part
            return
        held = self.parts[at]
        slot = chunk % 4
        held[slot] = part if held[slot] is None else held[slot] + part

    def get(self, at):
        if self.refs is not None:
            total = self.refs[at]
        else:
            held = self.parts[at]
            total = (held[0] + held[1]) + (held[2] + held[3])
        return jnp.broadcast_to(jnp.sum(total, axis=1, keepdims=True), (ROWS, 128))


def chunk_parts(piece, chunk, me, n_row, n_col, size, at, count):
    half = n_row // 2
    o = chunk // half
    u = chunk % half
    early = max(at + count - size, 0)
    even = piece[pl.ds((me ^ ((2 * u) * n_col + o)) * size + at - early, count)]
    odd = piece[pl.ds((me ^ ((2 * u + 1) * n_col + o)) * size + at - early, count)]
    low = low_half((count, 128))
    first = jnp.where(low, even, pltpu.roll(odd, 64, 1))
    second = jnp.where(low, pltpu.roll(even, 64, 1), odd)
    rows = jnp.concatenate([first, second], axis=0)
    return pltpu.roll(rows, ROWS - early, 0) if early else rows


PAIRS = [(i, j) for i in range(ITERS) for j in range(i + 1, ITERS)]


def place_of(j):
    lane = lax.broadcasted_iota(jnp.int32, (ROWS, 128), 1)
    return lane == lax.broadcasted_iota(jnp.int32, (ROWS, 128), 0) * (ITERS + 1) + j


def row_sum(acc):
    return jnp.sum(acc, axis=1, keepdims=True)


def lines_of(chunk):
    if isinstance(chunk, int):
        return pl.ds(chunk * 128, 128)
    return pl.ds(pl.multiple_of(chunk * 128, 128), 128)


def write_columns(cols, y, chunk, f):
    inner = sum(y[k : k + 1] * f[a] for a, k in enumerate(ORDER))
    full = jnp.concatenate([*f, inner], axis=0)
    high = full.astype(BF16)
    at = lines_of(chunk)
    cols[0:32, at] = high
    cols[32:64, at] = (full - high.astype(F32)).astype(BF16)


def contract(cols, kernels):
    prod = jnp.dot(cols, kernels, preferred_element_type=F32)
    return prod[:32, :256] + (prod[32:, :256] + prod[:32, 256:])


def products(n_chunk, columns, cols, kernels):
    if n_chunk <= 16:
        for chunk in range(n_chunk):
            columns(chunk)
        return contract(cols[...], kernels[...])
    pl.loop(0, n_chunk)(columns)

    def turn(i, acc):
        at = pl.ds(pl.multiple_of(i * 2048, 2048), 2048)
        return acc + contract(cols[:, at], kernels[at, :])

    return lax.fori_loop(0, n_chunk // 16, turn, jnp.zeros((32, 256), F32))


def image_rows(prod, targets, own, scale):
    left = [prod[8 * k : 8 * k + 8, :128] for k in range(4)]
    right = [prod[8 * k : 8 * k + 8, 128:] for k in range(4)]
    x = [targets[a : a + 1] for a in range(3)]
    first = x[0] * left[0] + x[1] * left[1] + x[2] * left[2] - left[3]
    other = x[0] * right[0] + x[1] * right[1] + x[2] * right[2] - right[3]
    parts = [pltpu.roll(first, 64, 1), other, pltpu.roll(other, 64, 1)]
    return [(left[a] + parts[a] + targets[3:4] * own[a]) * scale for a in range(3)]


def write_piece(images, out):
    rows = []
    for image in images:
        top, bottom = image[:4], pltpu.roll(image[4:], 64, 1)
        rows.append(jnp.where(low_half((4, 128)), top, bottom))
    message = jnp.concatenate([row[:HALF] for row in rows], axis=0)
    block = jnp.concatenate([message] * 8, axis=0)

    def put(m):
        out[pl.ds(m * 8 * LATER, 8 * LATER)] = block

    each_wide(out.shape[0] // (8 * LATER), put)


def each_wide(count, put):
    if count <= 64:
        for m in range(count):
            put(m)
    else:
        pl.loop(0, count)(put)


def pack_kernel(*refs):
    sources, (out, tgt, lists), held = refs[:6], refs[6:9], refs[9:15]
    block, sems = refs[15:]
    copies = [
        pltpu.make_async_copy(src, dst, sems.at[i])
        for i, (src, dst) in enumerate(zip(sources, held))
    ]
    for copy in copies:
        copy.start()
    for copy in copies[:4]:
        copy.wait()
    velocity, points, area, self_term, index, weight = held
    count = index.shape[0]
    field = velocity[...]
    spot = points[...]
    rows = []
    for a in range(3):
        vec = field[:, a, :]
        rows.append(jnp.concatenate([vec[:HALF], vec[HALF:]], axis=1))
    mine = jnp.concatenate([spot, self_term[...]], axis=0)
    mine = jnp.concatenate([mine, mine], axis=1)
    tgt[...] = jnp.concatenate([mine, mine], axis=0)
    left = jnp.concatenate([spot[0:1], spot[2:3]], axis=0)
    right = jnp.concatenate([spot[1:2], area[...]], axis=0)
    rows.append(jnp.concatenate([left, right], axis=1))
    message = jnp.concatenate(rows, axis=0)
    size = block.shape[0]
    block[...] = jnp.concatenate([message] * 8, axis=0)
    leaving = [
        pltpu.make_async_copy(block, out.at[pl.ds(i * size, size)], sems.at[6 + i])
        for i in range(out.shape[0] // size)
    ]
    for copy in leaving:
        copy.start()
    for copy in copies[4:]:
        copy.wait()
    lists[:count] = index[...].astype(F32)
    lists[count:] = weight[...]
    for copy in leaving:
        copy.wait()


def extra_kernel(sizes, lists, out):
    _, row, col = position(sizes)
    lines = lax.broadcasted_iota(jnp.int32, (128, 128), 0).astype(F32)
    count = lists.shape[0] // 2
    half = count // 2
    low = low_half((half, 128))
    odd = col % 2 == 1
    both = lists[:, lines_of(col // 2)]
    place = both[:count].astype(jnp.int32)
    place = (((place // 64) ^ row) * 64 + place % 64).astype(F32)
    packed = []
    for value in (place, both[count:]):
        top, bottom = value[:half], value[half:]
        lower = jnp.where(low, top, pltpu.roll(bottom, 64, 1))
        upper = jnp.where(low, pltpu.roll(top, 64, 1), bottom)
        packed.append(jnp.where(odd, upper, lower))
    index, weight = packed

    def build(u):
        line = lines + (u * 128.0 if isinstance(u, int) else (u * 128).astype(F32))
        total = jnp.zeros((128, 128), F32)
        for k in range(half):
            total = total + jnp.where(line == index[k : k + 1], weight[k : k + 1], 0.0)
        turned = total.T
        out[u] = turned[:64] + turned[64:]

    each(out.shape[0], build)


def first_kernel(sizes, piece, *refs):
    n_row, n_col = sizes[0] * sizes[1] * sizes[2], sizes[3]
    extra = refs[:n_col]
    tgt, kernels, places, basis, norm_out, out, cols, *sums = refs[n_col:]
    half = n_row // 2
    n_chunk = n_row * n_col // 2
    me, _, _ = position(sizes)
    total = Sums(1, sums[0] if sums else None)

    def unpack(chunk):
        vec = [
            chunk_parts(piece, chunk, me, n_row, n_col, FIRST, HALF * a, 4)
            for a in range(3)
        ]
        spot = chunk_parts(piece, chunk, me, n_row, n_col, FIRST, 3 * HALF, 2)
        places[chunk] = spot
        for a in range(3):
            basis[chunk, a] = vec[a]
        total.add(chunk, 0, vec, vec)
        write_columns(cols, spot, chunk, vec)

    turned = tgt[...].T
    x = [jnp.broadcast_to(turned[:64, a : a + 1], (64, 128)) for a in range(3)]

    def build(chunk):
        unpack(chunk)
        y = places[chunk]
        d = [x[a] - y[k : k + 1] for a, k in enumerate(ORDER)]
        dist = d[0] * d[0] + d[1] * d[1] + d[2] * d[2]
        root = lax.rsqrt(dist + BLOB_SQ)
        two = (y[3:4] * INV_EIGHT_PI) * root * root * root
        one = (dist + 2.0 * BLOB_SQ) * two
        if isinstance(chunk, int):
            one = one + extra[chunk // half][chunk % half]
        else:
            for o in range(n_col):
                mine = extra[o][chunk % half]
                one = one + jnp.where(chunk // half == o, mine, 0.0)
        moved = [two * part for part in d]
        at = lines_of(chunk)
        for k, pair in enumerate(([one, moved[0]], moved[1:])):
            value = jnp.concatenate(pair, axis=0).T
            high = value.astype(BF16)
            kernels[at, 128 * k : 128 * k + 128] = high
            kernels[at, 256 + 128 * k : 384 + 128 * k] = (value - high.astype(F32)).astype(BF16)

    prod = products(n_chunk, build, cols, kernels)
    norm = jnp.sqrt(total.get(0))
    scale = 1.0 / norm
    norm_out[0] = norm
    norm_out[1] = scale
    write_piece(image_rows(prod, tgt, basis[0], scale), out)


def middle_kernel(sizes, n_base, final, piece, *refs):
    n_row, n_col = sizes[0] * sizes[1] * sizes[2], sizes[3]
    bases, norms = refs[:n_base], refs[n_base : 2 * n_base]
    if final:
        kernels, places, tgt, own, h_out, out, basis, cols, *held = refs[2 * n_base :]
    else:
        kernels, places, tgt, basis, h_out, out, cols, *held = refs[2 * n_base :]
    n_chunk = n_row * n_col // 2
    me, _, _ = position(sizes)
    scales = [norm[norm.shape[0] - 1] for norm in norms]
    cross = [(i, j) for i in range(n_base) for j in range(i)]
    sums = Sums(2 * n_base + 1 + len(cross), held[0] if held else None)

    def unpack(chunk):
        vec = [
            chunk_parts(piece, chunk, me, n_row, n_col, LATER, HALF * a, 4)
            for a in range(3)
        ]
        old = [[base[chunk, a] for a in range(3)] for base in bases]
        for a in range(3):
            basis[chunk, a] = vec[a]
        for j in range(n_base):
            sums.add(chunk, j, vec, old[j])
        for at, (i, j) in enumerate(cross):
            sums.add(chunk, 2 * n_base + 1 + at, old[i], old[j])

    each(n_chunk, unpack)
    gram = {}
    for at, (i, j) in enumerate(cross):
        gram[j, i] = sums.get(2 * n_base + 1 + at) * (scales[i] * scales[j])
    column = []
    for j in range(n_base):
        h = sums.get(j) * scales[j]
        for i in range(j):
            h = h - column[i] * gram[i, j]
        column.append(h)
        if not final:
            h_out[j] = h
    factors = [h * scale for h, scale in zip(column, scales)]

    def columns(chunk):
        old = [[base[chunk, a] for a in range(3)] for base in bases]
        vec = []
        for a in range(3):
            value = basis[chunk, a]
            for j in range(n_base):
                value = value - factors[j] * old[j][a]
            vec.append(value)
            basis[chunk, a] = value
        sums.add(chunk, n_base, vec, vec)
        write_columns(cols, places[chunk], chunk, vec)
        if final:
            for j in range(n_base):
                sums.add(chunk, n_base + 1 + j, vec, old[j])

    prod = products(n_chunk, columns, cols, kernels)
    norm = jnp.sqrt(sums.get(n_base))
    scale = 1.0 / norm
    images = image_rows(prod, tgt, basis[0], scale)
    if not final:
        h_out[n_base] = norm
        h_out[n_base + 1] = scale
        write_piece(images, out)
        return
    every = [*bases, basis]
    for j, base in enumerate(every):
        for a in range(3):
            own[j, a] = base[0, a] * [*scales, scale][j]
    for j in range(n_base):
        gram[j, n_base] = sums.get(n_base + 1 + j) * (scale * scales[j])
    hessen = {(i, n_base - 1): value for i, value in enumerate([*column, norm])}
    for k in range(1, n_base):
        for i in range(k + 1):
            hessen[i, k - 1] = norms[k][i]
    known = rotate_known(hessen, norms[0][0], ITERS)
    for at, value in enumerate(known + [gram[pair] for pair in PAIRS]):
        h_out[at] = value
    low = low_half((ROWS, 128))
    row = jnp.zeros((ROWS, 128), F32)
    for j in range(ITERS + 1):
        other = images if j == ITERS else [own[j, a] for a in range(3)]
        part = sum(images[a] * other[a] for a in range(3))
        part = row_sum(jnp.where(low, part, 0.0))
        row = row + jnp.where(place_of(j), part, 0.0)
    row = jnp.broadcast_to(jnp.sum(row, axis=0, keepdims=True), (8, 128))

    def put(m):
        out[pl.ds(m * 8, 8)] = row

    each_wide(out.shape[0] // 8, put)


def rotate_known(hessen, start_norm, count):
    target = [start_norm]
    turns = []
    above = []
    inverses = []
    for k in range(count - 1):
        column = [hessen[i, k] for i in range(k + 2)]
        for j, (cosine, sine) in enumerate(turns):
            first_val, second_val = column[j], column[j + 1]
            column[j] = cosine * first_val + sine * second_val
            column[j + 1] = cosine * second_val - sine * first_val
        inverse = 1.0 / jnp.sqrt(column[k] * column[k] + column[k + 1] * column[k + 1])
        turns.append((column[k] * inverse, column[k + 1] * inverse))
        above += column[:k]
        inverses.append(inverse)
        target.append(-turns[k][1] * target[k])
        target[k] = turns[k][0] * target[k]
    return [value for turn in turns for value in turn] + above + inverses + target


def solve_last(known, column, square, count):
    size = count - 1
    turns, known = known[: 2 * size], known[2 * size :]
    above, known = known[: size * (size - 1) // 2], known[size * (size - 1) // 2 :]
    inverses, target = known[:size], known[size:]
    column = list(column)
    for j in range(size):
        cosine, sine = turns[2 * j], turns[2 * j + 1]
        first_val, second_val = column[j], column[j + 1]
        column[j] = cosine * first_val + sine * second_val
        column[j + 1] = cosine * second_val - sine * first_val
    last = column[size]
    coeffs = [None] * count
    coeffs[size] = target[size] * last / (last * last + square)
    for k in range(size - 1, -1, -1):
        accum = target[k] - column[k] * coeffs[size]
        for i in range(k + 1, size):
            accum = accum - above[i * (i - 1) // 2 + k] * coeffs[i]
        coeffs[k] = accum * inverses[k]
    return coeffs


KNOWN = 2 * (ITERS - 1) + (ITERS - 1) * (ITERS - 2) // 2 + (ITERS - 1) + ITERS


def last_kernel(sums, own, held, out):
    known = [held[i] for i in range(KNOWN)]
    gram = {(j, j): 1.0 for j in range(ITERS)}
    for at, (i, j) in enumerate(PAIRS):
        gram[i, j] = gram[j, i] = held[KNOWN + at]
    row = jnp.broadcast_to(jnp.sum(sums[...], axis=0, keepdims=True), (ROWS, 128))
    inner = [
        jnp.broadcast_to(row_sum(jnp.where(place_of(j), row, 0.0)), (ROWS, 128))
        for j in range(ITERS + 1)
    ]
    column = []
    for j in range(ITERS):
        column.append(inner[j] - sum(column[i] * gram[i, j] for i in range(j)))
    square = inner[ITERS]
    for j in range(ITERS):
        rest = sum(column[i] * gram[i, j] for i in range(ITERS)) - 2.0 * inner[j]
        square = square + column[j] * rest
    coeffs = solve_last(known, column, jnp.maximum(square, 0.0), ITERS)
    for a in range(3):
        density = sum(coeffs[k] * own[k, a] for k in range(ITERS))
        out[:HALF, a, :] = density[:HALF, :64]
        out[HALF:, a, :] = density[4 : 4 + HALF, :64]


def call(kernel, outs, scratch, operands, far=(), spread_out=False, flops=0):
    vmem = pl.BlockSpec(memory_space=pltpu.VMEM)
    count = len(operands)
    hbm = pl.BlockSpec(memory_space=pltpu.HBM)
    specs = [hbm if i in far else vmem for i in range(count)]
    moved = sum(x.size * x.dtype.itemsize for x in operands)
    return pl.pallas_call(
        kernel,
        out_shape=[jax.ShapeDtypeStruct(s, t) for s, t in outs],
        in_specs=specs,
        out_specs=[pl.BlockSpec(memory_space=pl.ANY) if spread_out and i == 0 else vmem for i in range(len(outs))],
        scratch_shapes=scratch,
        cost_estimate=pl.CostEstimate(flops=flops, bytes_accessed=moved, transcendentals=0),
        compiler_params=pltpu.CompilerParams(vmem_limit_bytes=48 * 1024 * 1024),
    )(*operands)


def body(sizes, velocity, points, panel_area, self_term, near_index, near_weight):
    n_row, n_col = sizes[0] * sizes[1] * sizes[2], sizes[3]
    n = n_row * n_col
    n_chunk = n // 2
    total = n * 64
    rhs = velocity.shape[0]

    message = ((n * LATER, 128), F32)
    sources = [
        velocity,
        points,
        panel_area[None],
        self_term[None],
        near_index.T,
        near_weight.T,
    ]
    wide, tgt, lists = call(
        pack_kernel,
        [
            ((n * FIRST, 128), F32),
            ((8, 128), F32),
            ((2 * near_index.shape[1], near_index.shape[0]), F32),
        ],
        [pltpu.VMEM(x.shape, x.dtype) for x in sources]
        + [pltpu.VMEM((8 * FIRST, 128), F32), pltpu.SemaphoreType.DMA((6 + n // 8,))],
        [pltpu.with_memory_space_constraint(x, pltpu.HBM) for x in sources],
        far=range(6),
        spread_out=True,
    )
    piece = spread(wide, n)
    near = [lists] + [lax.ppermute(lists, "col", xor_perm(n_col, o)) for o in range(1, n_col)]
    extra = [
        call(
            functools.partial(extra_kernel, sizes),
            [((n_row // 2, 64, 128), F32)],
            [],
            [pair],
            flops=10**8,
        )[0]
        for pair in near
    ]

    vec_shape = (n_chunk, 3, ROWS, 128)
    cols = pltpu.VMEM((64, total), BF16)
    held = [] if n_chunk <= 16 else [pltpu.VMEM((8, ROWS, 128), F32)]
    kernels, places, basis, norm, wide = call(
        functools.partial(first_kernel, sizes),
        [
            ((total, 512), BF16),
            ((n_chunk, 4, 128), F32),
            (vec_shape, F32),
            ((2, ROWS, 128), F32),
            message,
        ],
        [cols, *held],
        [piece, *extra, tgt],
    )
    bases = [basis]
    columns = [norm]
    for k in range(1, ITERS):
        final = k == ITERS - 1
        piece = spread(wide, n)
        main, column, wide = call(
            functools.partial(middle_kernel, sizes, k, final),
            [
                ((ITERS, 3, ROWS, 128) if final else vec_shape, F32),
                ((KNOWN + len(PAIRS) if final else k + 2, ROWS, 128), F32),
                ((n, 128), F32) if final else message,
            ],
            [*([pltpu.VMEM(vec_shape, F32)] if final else []), cols, *held],
            [piece, *bases, *columns, kernels, places, tgt],
        )
        bases.append(main)
        columns.append(column)
    sums = spread(wide, n)
    (density,) = call(
        last_kernel, [((rhs, 3, 64), F32)], [], [sums, bases[-1], columns[-1]]
    )
    return density


def solution(mesh):
    n_row, n_col = mesh.shape["row"], mesh.shape["col"]
    sizes = (n_row // 4, 2, 2, n_col)
    split = jax.sharding.Mesh(mesh.devices.reshape(sizes), AXES)
    return jax.shard_map(
        functools.partial(body, sizes),
        mesh=split,
        in_specs=(
            P(None, None, AXES),
            P(None, AXES),
            P(AXES),
            P(AXES),
            P(AXES[:3], "col"),
            P(AXES[:3], "col"),
        ),
        out_specs=P(None, None, AXES),
        check_vma=False,
    )
```

```python
import functools
import math

import jax
import jax.numpy as jnp
from jax import lax
from jax.experimental import pallas as pl
from jax.experimental.pallas import tpu as pltpu
from jax.sharding import PartitionSpec as P

ITERS = 3
BLOB_SQ = 0.0025
INV_EIGHT_PI = 1.0 / (8.0 * math.pi)
ROWS = 8
HALF = 3
FIRST, LATER = 11, 9
ORDER = (0, 2, 1)
AXES = ("top", "mid", "core", "col")
F32 = jnp.float32
BF16 = jnp.bfloat16


def position(sizes):
    top, mid, core, col = (lax.axis_index(axis) for axis in AXES)
    row = (top * sizes[1] + mid) * sizes[2] + core
    return row * sizes[3] + col, row, col


def low_half(shape):
    return lax.broadcasted_iota(jnp.int32, shape, len(shape) - 1) < 64


def xor_perm(n, m):
    return [(d, d ^ m) for d in range(n)]


def spread(rows, n):
    wide = rows.reshape(n, -1, 1, 128)
    return lax.all_to_all(wide, AXES, 0, 0, tiled=True).reshape(rows.shape)


def each(count, step):
    if count <= 16:
        for i in range(count):
            step(i)
    else:
        pl.loop(0, count)(step)


class Sums:
    def __init__(self, count, refs):
        self.refs = refs
        self.parts = [[None] * 4 for _ in range(count)]
        if refs is not None:
            for at in range(count):
                refs[at] = jnp.zeros((ROWS, 128), F32)

    def add(self, chunk, at, left, right):
        part = sum(left[a] * right[a] for a in range(3))
        if self.refs is not None:
            self.refs[at] = self.refs[at] + part
            return
        held = self.parts[at]
        slot = chunk % 4
        held[slot] = part if held[slot] is None else held[slot] + part

    def get(self, at):
        if self.refs is not None:
            total = self.refs[at]
        else:
            held = self.parts[at]
            total = (held[0] + held[1]) + (held[2] + held[3])
        return jnp.broadcast_to(jnp.sum(total, axis=1, keepdims=True), (ROWS, 128))


def chunk_parts(piece, chunk, me, n_row, n_col, size, at, count):
    half = n_row // 2
    o = chunk // half
    u = chunk % half
    early = max(at + count - size, 0)
    even = piece[pl.ds((me ^ ((2 * u) * n_col + o)) * size + at - early, count)]
    odd = piece[pl.ds((me ^ ((2 * u + 1) * n_col + o)) * size + at - early, count)]
    low = low_half((count, 128))
    first = jnp.where(low, even, pltpu.roll(odd, 64, 1))
    second = jnp.where(low, pltpu.roll(even, 64, 1), odd)
    rows = jnp.concatenate([first, second], axis=0)
    return pltpu.roll(rows, ROWS - early, 0) if early else rows


PAIRS = [(i, j) for i in range(ITERS) for j in range(i + 1, ITERS)]


def place_of(j):
    lane = lax.broadcasted_iota(jnp.int32, (ROWS, 128), 1)
    return lane == lax.broadcasted_iota(jnp.int32, (ROWS, 128), 0) * (ITERS + 1) + j


def row_sum(acc):
    return jnp.sum(acc, axis=1, keepdims=True)


def lines_of(chunk):
    if isinstance(chunk, int):
        return pl.ds(chunk * 128, 128)
    return pl.ds(pl.multiple_of(chunk * 128, 128), 128)


def write_columns(cols, y, chunk, f):
    inner = sum(y[k : k + 1] * f[a] for a, k in enumerate(ORDER))
    full = jnp.concatenate([*f, inner], axis=0)
    high = full.astype(BF16)
    at = lines_of(chunk)
    cols[0:32, at] = high
    cols[32:64, at] = (full - high.astype(F32)).astype(BF16)


def contract(cols, kernels):
    prod = jnp.dot(cols, kernels, preferred_element_type=F32)
    return prod[:32, :256] + (prod[32:, :256] + prod[:32, 256:])


def products(n_chunk, columns, cols, kernels):
    if n_chunk <= 16:
        for chunk in range(n_chunk):
            columns(chunk)
        return contract(cols[...], kernels[...])
    pl.loop(0, n_chunk)(columns)

    def turn(i, acc):
        at = pl.ds(pl.multiple_of(i * 2048, 2048), 2048)
        return acc + contract(cols[:, at], kernels[at, :])

    return lax.fori_loop(0, n_chunk // 16, turn, jnp.zeros((32, 256), F32))


def image_rows(prod, targets, own, scale):
    left = [prod[8 * k : 8 * k + 8, :128] for k in range(4)]
    right = [prod[8 * k : 8 * k + 8, 128:] for k in range(4)]
    x = [targets[a : a + 1] for a in range(3)]
    first = x[0] * left[0] + x[1] * left[1] + x[2] * left[2] - left[3]
    other = x[0] * right[0] + x[1] * right[1] + x[2] * right[2] - right[3]
    parts = [pltpu.roll(first, 64, 1), other, pltpu.roll(other, 64, 1)]
    return [(left[a] + parts[a] + targets[3:4] * own[a]) * scale for a in range(3)]


def write_piece(images, out):
    rows = []
    for image in images:
        top, bottom = image[:4], pltpu.roll(image[4:], 64, 1)
        rows.append(jnp.where(low_half((4, 128)), top, bottom))
    message = jnp.concatenate([row[:HALF] for row in rows], axis=0)
    block = jnp.concatenate([message] * 8, axis=0)

    def put(m):
        out[pl.ds(m * 8 * LATER, 8 * LATER)] = block

    each_wide(out.shape[0] // (8 * LATER), put)


def each_wide(count, put):
    if count <= 64:
        for m in range(count):
            put(m)
    else:
        pl.loop(0, count)(put)


def pack_kernel(*refs):
    sources, (out, tgt, lists), held = refs[:6], refs[6:9], refs[9:15]
    block, sems = refs[15:]
    copies = [
        pltpu.make_async_copy(src, dst, sems.at[i])
        for i, (src, dst) in enumerate(zip(sources, held))
    ]
    for copy in copies:
        copy.start()
    for copy in copies[:3]:
        copy.wait()
    velocity, points, area, self_term, index, weight = held
    count = index.shape[0]
    rows = [
        jnp.concatenate([velocity[:HALF, a, :], velocity[HALF:, a, :]], axis=1) for a in range(3)
    ]
    spot = points[...]
    left = jnp.concatenate([spot[0:1], spot[2:3]], axis=0)
    right = jnp.concatenate([spot[1:2], area[...]], axis=0)
    rows.append(jnp.concatenate([left, right], axis=1))
    message = jnp.concatenate(rows, axis=0)
    size = block.shape[0]
    block[...] = jnp.concatenate([message] * 8, axis=0)
    leaving = [
        pltpu.make_async_copy(block, out.at[pl.ds(i * size, size)], sems.at[6 + i])
        for i in range(out.shape[0] // size)
    ]
    for copy in leaving:
        copy.start()
    for copy in copies[3:]:
        copy.wait()
    mine = jnp.concatenate([spot, self_term[...]], axis=0)
    mine = jnp.concatenate([mine, mine], axis=1)
    tgt[...] = jnp.concatenate([mine, mine], axis=0)
    lists[:count] = index[...].astype(F32)
    lists[count:] = weight[...]
    for copy in leaving:
        copy.wait()


def extra_kernel(sizes, lists, out):
    _, row, col = position(sizes)
    lines = lax.broadcasted_iota(jnp.int32, (128, 128), 0).astype(F32)
    count = lists.shape[0] // 2
    half = count // 2
    low = low_half((half, 128))
    odd = col % 2 == 1
    both = lists[:, lines_of(col // 2)]
    place = both[:count].astype(jnp.int32)
    place = (((place // 64) ^ row) * 64 + place % 64).astype(F32)
    packed = []
    for value in (place, both[count:]):
        top, bottom = value[:half], value[half:]
        lower = jnp.where(low, top, pltpu.roll(bottom, 64, 1))
        upper = jnp.where(low, pltpu.roll(top, 64, 1), bottom)
        packed.append(jnp.where(odd, upper, lower))
    index, weight = packed

    def build(u):
        line = lines + (u * 128.0 if isinstance(u, int) else (u * 128).astype(F32))
        total = jnp.zeros((128, 128), F32)
        for k in range(half):
            total = total + jnp.where(line == index[k : k + 1], weight[k : k + 1], 0.0)
        turned = total.T
        out[u] = turned[:64] + turned[64:]

    each(out.shape[0], build)


def first_kernel(sizes, piece, *refs):
    n_row, n_col = sizes[0] * sizes[1] * sizes[2], sizes[3]
    extra = refs[:n_col]
    tgt, kernels, places, basis, norm_out, out, cols, *sums = refs[n_col:]
    half = n_row // 2
    n_chunk = n_row * n_col // 2
    me, _, _ = position(sizes)
    total = Sums(1, sums[0] if sums else None)

    def unpack(chunk):
        vec = [
            chunk_parts(piece, chunk, me, n_row, n_col, FIRST, HALF * a, 4)
            for a in range(3)
        ]
        spot = chunk_parts(piece, chunk, me, n_row, n_col, FIRST, 3 * HALF, 2)
        places[chunk] = spot
        for a in range(3):
            basis[chunk, a] = vec[a]
        total.add(chunk, 0, vec, vec)
        write_columns(cols, spot, chunk, vec)

    turned = tgt[...].T
    x = [jnp.broadcast_to(turned[:64, a : a + 1], (64, 128)) for a in range(3)]

    def build(chunk):
        unpack(chunk)
        y = places[chunk]
        d = [x[a] - y[k : k + 1] for a, k in enumerate(ORDER)]
        dist = d[0] * d[0] + d[1] * d[1] + d[2] * d[2]
        root = lax.rsqrt(dist + BLOB_SQ)
        two = (y[3:4] * INV_EIGHT_PI) * root * root * root
        one = (dist + 2.0 * BLOB_SQ) * two
        if isinstance(chunk, int):
            one = one + extra[chunk // half][chunk % half]
        else:
            for o in range(n_col):
                mine = extra[o][chunk % half]
                one = one + jnp.where(chunk // half == o, mine, 0.0)
        moved = [two * part for part in d]
        at = lines_of(chunk)
        for k, pair in enumerate(([one, moved[0]], moved[1:])):
            value = jnp.concatenate(pair, axis=0).T
            high = value.astype(BF16)
            kernels[at, 128 * k : 128 * k + 128] = high
            kernels[at, 256 + 128 * k : 384 + 128 * k] = (value - high.astype(F32)).astype(BF16)

    prod = products(n_chunk, build, cols, kernels)
    norm = jnp.sqrt(total.get(0))
    scale = 1.0 / norm
    norm_out[0] = norm
    norm_out[1] = scale
    write_piece(image_rows(prod, tgt, basis[0], scale), out)


def middle_kernel(sizes, n_base, final, piece, *refs):
    n_row, n_col = sizes[0] * sizes[1] * sizes[2], sizes[3]
    bases, norms = refs[:n_base], refs[n_base : 2 * n_base]
    if final:
        kernels, places, tgt, own, h_out, out, basis, cols, *held = refs[2 * n_base :]
    else:
        kernels, places, tgt, basis, h_out, out, cols, *held = refs[2 * n_base :]
    n_chunk = n_row * n_col // 2
    me, _, _ = position(sizes)
    scales = [norm[norm.shape[0] - 1] for norm in norms]
    cross = [(i, j) for i in range(n_base) for j in range(i)]
    sums = Sums(2 * n_base + 1 + len(cross), held[0] if held else None)

    def unpack(chunk):
        vec = [
            chunk_parts(piece, chunk, me, n_row, n_col, LATER, HALF * a, 4)
            for a in range(3)
        ]
        old = [[base[chunk, a] for a in range(3)] for base in bases]
        for a in range(3):
            basis[chunk, a] = vec[a]
        for j in range(n_base):
            sums.add(chunk, j, vec, old[j])
        for at, (i, j) in enumerate(cross):
            sums.add(chunk, 2 * n_base + 1 + at, old[i], old[j])

    each(n_chunk, unpack)
    gram = {}
    for at, (i, j) in enumerate(cross):
        gram[j, i] = sums.get(2 * n_base + 1 + at) * (scales[i] * scales[j])
    column = []
    for j in range(n_base):
        h = sums.get(j) * scales[j]
        for i in range(j):
            h = h - column[i] * gram[i, j]
        column.append(h)
        if not final:
            h_out[j] = h
    factors = [h * scale for h, scale in zip(column, scales)]

    def columns(chunk):
        old = [[base[chunk, a] for a in range(3)] for base in bases]
        vec = []
        for a in range(3):
            value = basis[chunk, a]
            for j in range(n_base):
                value = value - factors[j] * old[j][a]
            vec.append(value)
            basis[chunk, a] = value
        sums.add(chunk, n_base, vec, vec)
        write_columns(cols, places[chunk], chunk, vec)
        if final:
            for j in range(n_base):
                sums.add(chunk, n_base + 1 + j, vec, old[j])

    prod = products(n_chunk, columns, cols, kernels)
    norm = jnp.sqrt(sums.get(n_base))
    scale = 1.0 / norm
    images = image_rows(prod, tgt, basis[0], scale)
    if not final:
        h_out[n_base] = norm
        h_out[n_base + 1] = scale
        write_piece(images, out)
        return
    every = [*bases, basis]
    for j, base in enumerate(every):
        for a in range(3):
            own[j, a] = base[0, a] * [*scales, scale][j]
    for j in range(n_base):
        gram[j, n_base] = sums.get(n_base + 1 + j) * (scale * scales[j])
    hessen = {(i, n_base - 1): value for i, value in enumerate([*column, norm])}
    for k in range(1, n_base):
        for i in range(k + 1):
            hessen[i, k - 1] = norms[k][i]
    known = rotate_known(hessen, norms[0][0], ITERS)
    for at, value in enumerate(known + [gram[pair] for pair in PAIRS]):
        h_out[at] = value
    low = low_half((ROWS, 128))
    row = jnp.zeros((ROWS, 128), F32)
    for j in range(ITERS + 1):
        other = images if j == ITERS else [own[j, a] for a in range(3)]
        part = sum(images[a] * other[a] for a in range(3))
        part = row_sum(jnp.where(low, part, 0.0))
        row = row + jnp.where(place_of(j), part, 0.0)
    row = jnp.broadcast_to(jnp.sum(row, axis=0, keepdims=True), (8, 128))

    def put(m):
        out[pl.ds(m * 8, 8)] = row

    each_wide(out.shape[0] // 8, put)


def rotate_known(hessen, start_norm, count):
    target = [start_norm]
    turns = []
    above = []
    inverses = []
    for k in range(count - 1):
        column = [hessen[i, k] for i in range(k + 2)]
        for j, (cosine, sine) in enumerate(turns):
            first_val, second_val = column[j], column[j + 1]
            column[j] = cosine * first_val + sine * second_val
            column[j + 1] = cosine * second_val - sine * first_val
        inverse = 1.0 / jnp.sqrt(column[k] * column[k] + column[k + 1] * column[k + 1])
        turns.append((column[k] * inverse, column[k + 1] * inverse))
        above += column[:k]
        inverses.append(inverse)
        target.append(-turns[k][1] * target[k])
        target[k] = turns[k][0] * target[k]
    return [value for turn in turns for value in turn] + above + inverses + target


def solve_last(known, column, square, count):
    size = count - 1
    turns, known = known[: 2 * size], known[2 * size :]
    above, known = known[: size * (size - 1) // 2], known[size * (size - 1) // 2 :]
    inverses, target = known[:size], known[size:]
    column = list(column)
    for j in range(size):
        cosine, sine = turns[2 * j], turns[2 * j + 1]
        first_val, second_val = column[j], column[j + 1]
        column[j] = cosine * first_val + sine * second_val
        column[j + 1] = cosine * second_val - sine * first_val
    last = column[size]
    coeffs = [None] * count
    coeffs[size] = target[size] * last / (last * last + square)
    for k in range(size - 1, -1, -1):
        accum = target[k] - column[k] * coeffs[size]
        for i in range(k + 1, size):
            accum = accum - above[i * (i - 1) // 2 + k] * coeffs[i]
        coeffs[k] = accum * inverses[k]
    return coeffs


KNOWN = 2 * (ITERS - 1) + (ITERS - 1) * (ITERS - 2) // 2 + (ITERS - 1) + ITERS


def last_kernel(sums, own, held, out):
    known = [held[i] for i in range(KNOWN)]
    gram = {(j, j): 1.0 for j in range(ITERS)}
    for at, (i, j) in enumerate(PAIRS):
        gram[i, j] = gram[j, i] = held[KNOWN + at]
    row = jnp.broadcast_to(jnp.sum(sums[...], axis=0, keepdims=True), (ROWS, 128))
    inner = [
        jnp.broadcast_to(row_sum(jnp.where(place_of(j), row, 0.0)), (ROWS, 128))
        for j in range(ITERS + 1)
    ]
    column = []
    for j in range(ITERS):
        column.append(inner[j] - sum(column[i] * gram[i, j] for i in range(j)))
    square = inner[ITERS]
    for j in range(ITERS):
        rest = sum(column[i] * gram[i, j] for i in range(ITERS)) - 2.0 * inner[j]
        square = square + column[j] * rest
    coeffs = solve_last(known, column, jnp.maximum(square, 0.0), ITERS)
    for a in range(3):
        density = sum(coeffs[k] * own[k, a] for k in range(ITERS))
        out[:HALF, a, :] = density[:HALF, :64]
        out[HALF:, a, :] = density[4 : 4 + HALF, :64]


def call(kernel, outs, scratch, operands, far=(), spread_out=False, flops=0):
    vmem = pl.BlockSpec(memory_space=pltpu.VMEM)
    count = len(operands)
    hbm = pl.BlockSpec(memory_space=pltpu.HBM)
    specs = [hbm if i in far else vmem for i in range(count)]
    moved = sum(x.size * x.dtype.itemsize for x in operands)
    return pl.pallas_call(
        kernel,
        out_shape=[jax.ShapeDtypeStruct(s, t) for s, t in outs],
        in_specs=specs,
        out_specs=[pl.BlockSpec(memory_space=pl.ANY) if spread_out and i == 0 else vmem for i in range(len(outs))],
        scratch_shapes=scratch,
        cost_estimate=pl.CostEstimate(flops=flops, bytes_accessed=moved, transcendentals=0),
        compiler_params=pltpu.CompilerParams(vmem_limit_bytes=48 * 1024 * 1024),
    )(*operands)


def body(sizes, velocity, points, panel_area, self_term, near_index, near_weight):
    n_row, n_col = sizes[0] * sizes[1] * sizes[2], sizes[3]
    n = n_row * n_col
    n_chunk = n // 2
    total = n * 64
    rhs = velocity.shape[0]

    message = ((n * LATER, 128), F32)
    sources = [
        velocity,
        points,
        panel_area[None],
        self_term[None],
        near_index.T,
        near_weight.T,
    ]
    wide, tgt, lists = call(
        pack_kernel,
        [
            ((n * FIRST, 128), F32),
            ((8, 128), F32),
            ((2 * near_index.shape[1], near_index.shape[0]), F32),
        ],
        [pltpu.VMEM(x.shape, x.dtype) for x in sources]
        + [pltpu.VMEM((8 * FIRST, 128), F32), pltpu.SemaphoreType.DMA((6 + n // 8,))],
        [pltpu.with_memory_space_constraint(x, pltpu.HBM) for x in sources],
        far=range(6),
        spread_out=True,
    )
    piece = spread(wide, n)
    near = [lists] + [lax.ppermute(lists, "col", xor_perm(n_col, o)) for o in range(1, n_col)]
    extra = [
        call(
            functools.partial(extra_kernel, sizes),
            [((n_row // 2, 64, 128), F32)],
            [],
            [pair],
            flops=10**8,
        )[0]
        for pair in near
    ]

    vec_shape = (n_chunk, 3, ROWS, 128)
    cols = pltpu.VMEM((64, total), BF16)
    held = [] if n_chunk <= 16 else [pltpu.VMEM((8, ROWS, 128), F32)]
    kernels, places, basis, norm, wide = call(
        functools.partial(first_kernel, sizes),
        [
            ((total, 512), BF16),
            ((n_chunk, 4, 128), F32),
            (vec_shape, F32),
            ((2, ROWS, 128), F32),
            message,
        ],
        [cols, *held],
        [piece, *extra, tgt],
    )
    bases = [basis]
    columns = [norm]
    for k in range(1, ITERS):
        final = k == ITERS - 1
        piece = spread(wide, n)
        main, column, wide = call(
            functools.partial(middle_kernel, sizes, k, final),
            [
                ((ITERS, 3, ROWS, 128) if final else vec_shape, F32),
                ((KNOWN + len(PAIRS) if final else k + 2, ROWS, 128), F32),
                ((n, 128), F32) if final else message,
            ],
            [*([pltpu.VMEM(vec_shape, F32)] if final else []), cols, *held],
            [piece, *bases, *columns, kernels, places, tgt],
        )
        bases.append(main)
        columns.append(column)
    sums = spread(wide, n)
    (density,) = call(
        last_kernel, [((rhs, 3, 64), F32)], [], [sums, bases[-1], columns[-1]]
    )
    return density


def solution(mesh):
    n_row, n_col = mesh.shape["row"], mesh.shape["col"]
    sizes = (n_row // 4, 2, 2, n_col)
    split = jax.sharding.Mesh(mesh.devices.reshape(sizes), AXES)
    return jax.shard_map(
        functools.partial(body, sizes),
        mesh=split,
        in_specs=(
            P(None, None, AXES),
            P(None, AXES),
            P(AXES),
            P(AXES),
            P(AXES[:3], "col"),
            P(AXES[:3], "col"),
        ),
        out_specs=P(None, None, AXES),
        check_vma=False,
    )
```

```python
import functools
import math

import jax
import jax.numpy as jnp
from jax import lax
from jax.experimental import pallas as pl
from jax.experimental.pallas import tpu as pltpu
from jax.sharding import PartitionSpec as P

ITERS = 3
BLOB_SQ = 0.0025
INV_EIGHT_PI = 1.0 / (8.0 * math.pi)
ROWS = 8
HALF = 3
FIRST, LATER = 11, 9
ORDER = (0, 2, 1)
AXES = ("top", "mid", "core", "col")
F32 = jnp.float32
BF16 = jnp.bfloat16


def position(sizes):
    top, mid, core, col = (lax.axis_index(axis) for axis in AXES)
    row = (top * sizes[1] + mid) * sizes[2] + core
    return row * sizes[3] + col, row, col


def low_half(shape):
    return lax.broadcasted_iota(jnp.int32, shape, len(shape) - 1) < 64


def xor_perm(n, m):
    return [(d, d ^ m) for d in range(n)]


def spread(rows, n):
    wide = rows.reshape(n, -1, 1, 128)
    return lax.all_to_all(wide, AXES, 0, 0, tiled=True).reshape(rows.shape)


def each(count, step):
    if count <= 16:
        for i in range(count):
            step(i)
    else:
        pl.loop(0, count)(step)


class Sums:
    def __init__(self, count, refs):
        self.refs = refs
        self.parts = [[None] * 4 for _ in range(count)]
        if refs is not None:
            for at in range(count):
                refs[at] = jnp.zeros((ROWS, 128), F32)

    def add(self, chunk, at, left, right):
        part = sum(left[a] * right[a] for a in range(3))
        if self.refs is not None:
            self.refs[at] = self.refs[at] + part
            return
        held = self.parts[at]
        slot = chunk % 4
        held[slot] = part if held[slot] is None else held[slot] + part

    def get(self, at):
        if self.refs is not None:
            total = self.refs[at]
        else:
            held = self.parts[at]
            total = (held[0] + held[1]) + (held[2] + held[3])
        return jnp.broadcast_to(jnp.sum(total, axis=1, keepdims=True), (ROWS, 128))


def chunk_parts(piece, chunk, me, n_row, n_col, size, at, count):
    half = n_row // 2
    o = chunk // half
    u = chunk % half
    early = max(at + count - size, 0)
    even = piece[pl.ds((me ^ ((2 * u) * n_col + o)) * size + at - early, count)]
    odd = piece[pl.ds((me ^ ((2 * u + 1) * n_col + o)) * size + at - early, count)]
    low = low_half((count, 128))
    first = jnp.where(low, even, pltpu.roll(odd, 64, 1))
    second = jnp.where(low, pltpu.roll(even, 64, 1), odd)
    rows = jnp.concatenate([first, second], axis=0)
    return pltpu.roll(rows, ROWS - early, 0) if early else rows


PAIRS = [(i, j) for i in range(ITERS) for j in range(i + 1, ITERS)]


def place_of(j):
    lane = lax.broadcasted_iota(jnp.int32, (ROWS, 128), 1)
    return lane == lax.broadcasted_iota(jnp.int32, (ROWS, 128), 0) * (ITERS + 1) + j


def row_sum(acc):
    return jnp.sum(acc, axis=1, keepdims=True)


def lines_of(chunk):
    if isinstance(chunk, int):
        return pl.ds(chunk * 128, 128)
    return pl.ds(pl.multiple_of(chunk * 128, 128), 128)


def write_columns(cols, y, chunk, f):
    inner = sum(y[k : k + 1] * f[a] for a, k in enumerate(ORDER))
    full = jnp.concatenate([*f, inner], axis=0)
    high = full.astype(BF16)
    at = lines_of(chunk)
    cols[0:32, at] = high
    cols[32:64, at] = (full - high.astype(F32)).astype(BF16)


def contract(cols, kernels):
    first = jnp.dot(cols, kernels[:, :256], preferred_element_type=F32)
    second = jnp.dot(cols[:32], kernels[:, 256:], preferred_element_type=F32)
    return first[:32] + (first[32:] + second)


def products(n_chunk, columns, cols, kernels):
    if n_chunk <= 16:
        for chunk in range(n_chunk):
            columns(chunk)
        return contract(cols[...], kernels[...])
    pl.loop(0, n_chunk)(columns)

    def turn(i, acc):
        at = pl.ds(pl.multiple_of(i * 2048, 2048), 2048)
        return acc + contract(cols[:, at], kernels[at, :])

    return lax.fori_loop(0, n_chunk // 16, turn, jnp.zeros((32, 256), F32))


def image_rows(prod, targets, own, scale):
    left = [prod[8 * k : 8 * k + 8, :128] for k in range(4)]
    right = [prod[8 * k : 8 * k + 8, 128:] for k in range(4)]
    x = [targets[a : a + 1] for a in range(3)]
    first = x[0] * left[0] + x[1] * left[1] + x[2] * left[2] - left[3]
    other = x[0] * right[0] + x[1] * right[1] + x[2] * right[2] - right[3]
    parts = [pltpu.roll(first, 64, 1), other, pltpu.roll(other, 64, 1)]
    return [(left[a] + parts[a] + targets[3:4] * own[a]) * scale for a in range(3)]


def write_piece(images, out):
    rows = []
    for image in images:
        top, bottom = image[:4], pltpu.roll(image[4:], 64, 1)
        rows.append(jnp.where(low_half((4, 128)), top, bottom))
    message = jnp.concatenate([row[:HALF] for row in rows], axis=0)
    block = jnp.concatenate([message] * 8, axis=0)

    def put(m):
        out[pl.ds(m * 8 * LATER, 8 * LATER)] = block

    each_wide(out.shape[0] // (8 * LATER), put)


def each_wide(count, put):
    if count <= 64:
        for m in range(count):
            put(m)
    else:
        pl.loop(0, count)(put)


def pack_kernel(*refs):
    sources, (out, tgt, lists), held = refs[:6], refs[6:9], refs[9:15]
    block, sems = refs[15:]
    copies = [
        pltpu.make_async_copy(src, dst, sems.at[i])
        for i, (src, dst) in enumerate(zip(sources, held))
    ]
    for copy in copies:
        copy.start()
    for copy in copies[:3]:
        copy.wait()
    velocity, points, area, self_term, index, weight = held
    count = index.shape[0]
    rows = [
        jnp.concatenate([velocity[:HALF, a, :], velocity[HALF:, a, :]], axis=1) for a in range(3)
    ]
    spot = points[...]
    left = jnp.concatenate([spot[0:1], spot[2:3]], axis=0)
    right = jnp.concatenate([spot[1:2], area[...]], axis=0)
    rows.append(jnp.concatenate([left, right], axis=1))
    message = jnp.concatenate(rows, axis=0)
    size = block.shape[0]
    block[...] = jnp.concatenate([message] * 8, axis=0)
    leaving = [
        pltpu.make_async_copy(block, out.at[pl.ds(i * size, size)], sems.at[6 + i])
        for i in range(out.shape[0] // size)
    ]
    for copy in leaving:
        copy.start()
    for copy in copies[3:]:
        copy.wait()
    mine = jnp.concatenate([spot, self_term[...]], axis=0)
    mine = jnp.concatenate([mine, mine], axis=1)
    tgt[...] = jnp.concatenate([mine, mine], axis=0)
    lists[:count] = index[...].astype(F32)
    lists[count:] = weight[...]
    for copy in leaving:
        copy.wait()


def extra_kernel(sizes, lists, out):
    _, row, col = position(sizes)
    lines = lax.broadcasted_iota(jnp.int32, (128, 128), 0).astype(F32)
    count = lists.shape[0] // 2
    half = count // 2
    low = low_half((half, 128))
    odd = col % 2 == 1
    both = lists[:, lines_of(col // 2)]
    place = both[:count].astype(jnp.int32)
    place = (((place // 64) ^ row) * 64 + place % 64).astype(F32)
    packed = []
    for value in (place, both[count:]):
        top, bottom = value[:half], value[half:]
        lower = jnp.where(low, top, pltpu.roll(bottom, 64, 1))
        upper = jnp.where(low, pltpu.roll(top, 64, 1), bottom)
        packed.append(jnp.where(odd, upper, lower))
    index, weight = packed

    def build(u):
        line = lines + (u * 128.0 if isinstance(u, int) else (u * 128).astype(F32))
        total = jnp.zeros((128, 128), F32)
        for k in range(half):
            total = total + jnp.where(line == index[k : k + 1], weight[k : k + 1], 0.0)
        turned = total.T
        out[u] = turned[:64] + turned[64:]

    each(out.shape[0], build)


def first_kernel(sizes, piece, *refs):
    n_row, n_col = sizes[0] * sizes[1] * sizes[2], sizes[3]
    extra = refs[:n_col]
    tgt, kernels, places, basis, norm_out, out, cols, *sums = refs[n_col:]
    half = n_row // 2
    n_chunk = n_row * n_col // 2
    me, _, _ = position(sizes)
    total = Sums(1, sums[0] if sums else None)

    def unpack(chunk):
        vec = [
            chunk_parts(piece, chunk, me, n_row, n_col, FIRST, HALF * a, 4)
            for a in range(3)
        ]
        spot = chunk_parts(piece, chunk, me, n_row, n_col, FIRST, 3 * HALF, 2)
        places[chunk] = spot
        for a in range(3):
            basis[chunk, a] = vec[a]
        total.add(chunk, 0, vec, vec)
        write_columns(cols, spot, chunk, vec)

    turned = tgt[...].T
    x = [jnp.broadcast_to(turned[:64, a : a + 1], (64, 128)) for a in range(3)]

    def build(chunk):
        unpack(chunk)
        y = places[chunk]
        d = [x[a] - y[k : k + 1] for a, k in enumerate(ORDER)]
        dist = d[0] * d[0] + d[1] * d[1] + d[2] * d[2]
        root = lax.rsqrt(dist + BLOB_SQ)
        two = (y[3:4] * INV_EIGHT_PI) * root * root * root
        one = (dist + 2.0 * BLOB_SQ) * two
        if isinstance(chunk, int):
            one = one + extra[chunk // half][chunk % half]
        else:
            for o in range(n_col):
                mine = extra[o][chunk % half]
                one = one + jnp.where(chunk // half == o, mine, 0.0)
        moved = [two * part for part in d]
        at = lines_of(chunk)
        for k, pair in enumerate(([one, moved[0]], moved[1:])):
            value = jnp.concatenate(pair, axis=0).T
            high = value.astype(BF16)
            kernels[at, 128 * k : 128 * k + 128] = high
            kernels[at, 256 + 128 * k : 384 + 128 * k] = (value - high.astype(F32)).astype(BF16)

    prod = products(n_chunk, build, cols, kernels)
    norm = jnp.sqrt(total.get(0))
    scale = 1.0 / norm
    norm_out[0] = norm
    norm_out[1] = scale
    write_piece(image_rows(prod, tgt, basis[0], scale), out)


def middle_kernel(sizes, n_base, final, piece, *refs):
    n_row, n_col = sizes[0] * sizes[1] * sizes[2], sizes[3]
    bases, norms = refs[:n_base], refs[n_base : 2 * n_base]
    if final:
        kernels, places, tgt, own, h_out, out, basis, cols, *held = refs[2 * n_base :]
    else:
        kernels, places, tgt, basis, h_out, out, cols, *held = refs[2 * n_base :]
    n_chunk = n_row * n_col // 2
    me, _, _ = position(sizes)
    scales = [norm[norm.shape[0] - 1] for norm in norms]
    cross = [(i, j) for i in range(n_base) for j in range(i)]
    sums = Sums(2 * n_base + 1 + len(cross), held[0] if held else None)

    def unpack(chunk):
        vec = [
            chunk_parts(piece, chunk, me, n_row, n_col, LATER, HALF * a, 4)
            for a in range(3)
        ]
        old = [[base[chunk, a] for a in range(3)] for base in bases]
        for a in range(3):
            basis[chunk, a] = vec[a]
        for j in range(n_base):
            sums.add(chunk, j, vec, old[j])
        for at, (i, j) in enumerate(cross):
            sums.add(chunk, 2 * n_base + 1 + at, old[i], old[j])

    each(n_chunk, unpack)
    gram = {}
    for at, (i, j) in enumerate(cross):
        gram[j, i] = sums.get(2 * n_base + 1 + at) * (scales[i] * scales[j])
    column = []
    for j in range(n_base):
        h = sums.get(j) * scales[j]
        for i in range(j):
            h = h - column[i] * gram[i, j]
        column.append(h)
        if not final:
            h_out[j] = h
    factors = [h * scale for h, scale in zip(column, scales)]

    def columns(chunk):
        old = [[base[chunk, a] for a in range(3)] for base in bases]
        vec = []
        for a in range(3):
            value = basis[chunk, a]
            for j in range(n_base):
                value = value - factors[j] * old[j][a]
            vec.append(value)
            basis[chunk, a] = value
        sums.add(chunk, n_base, vec, vec)
        write_columns(cols, places[chunk], chunk, vec)
        if final:
            for j in range(n_base):
                sums.add(chunk, n_base + 1 + j, vec, old[j])

    prod = products(n_chunk, columns, cols, kernels)
    norm = jnp.sqrt(sums.get(n_base))
    scale = 1.0 / norm
    images = image_rows(prod, tgt, basis[0], scale)
    if not final:
        h_out[n_base] = norm
        h_out[n_base + 1] = scale
        write_piece(images, out)
        return
    every = [*bases, basis]
    for j, base in enumerate(every):
        for a in range(3):
            own[j, a] = base[0, a] * [*scales, scale][j]
    for j in range(n_base):
        gram[j, n_base] = sums.get(n_base + 1 + j) * (scale * scales[j])
    hessen = {(i, n_base - 1): value for i, value in enumerate([*column, norm])}
    for k in range(1, n_base):
        for i in range(k + 1):
            hessen[i, k - 1] = norms[k][i]
    known = rotate_known(hessen, norms[0][0], ITERS)
    for at, value in enumerate(known + [gram[pair] for pair in PAIRS]):
        h_out[at] = value
    low = low_half((ROWS, 128))
    row = jnp.zeros((ROWS, 128), F32)
    for j in range(ITERS + 1):
        other = images if j == ITERS else [own[j, a] for a in range(3)]
        part = sum(images[a] * other[a] for a in range(3))
        part = row_sum(jnp.where(low, part, 0.0))
        row = row + jnp.where(place_of(j), part, 0.0)
    row = jnp.broadcast_to(jnp.sum(row, axis=0, keepdims=True), (8, 128))

    def put(m):
        out[pl.ds(m * 8, 8)] = row

    each_wide(out.shape[0] // 8, put)


def rotate_known(hessen, start_norm, count):
    target = [start_norm]
    turns = []
    above = []
    inverses = []
    for k in range(count - 1):
        column = [hessen[i, k] for i in range(k + 2)]
        for j, (cosine, sine) in enumerate(turns):
            first_val, second_val = column[j], column[j + 1]
            column[j] = cosine * first_val + sine * second_val
            column[j + 1] = cosine * second_val - sine * first_val
        inverse = 1.0 / jnp.sqrt(column[k] * column[k] + column[k + 1] * column[k + 1])
        turns.append((column[k] * inverse, column[k + 1] * inverse))
        above += column[:k]
        inverses.append(inverse)
        target.append(-turns[k][1] * target[k])
        target[k] = turns[k][0] * target[k]
    return [value for turn in turns for value in turn] + above + inverses + target


def solve_last(known, column, square, count):
    size = count - 1
    turns, known = known[: 2 * size], known[2 * size :]
    above, known = known[: size * (size - 1) // 2], known[size * (size - 1) // 2 :]
    inverses, target = known[:size], known[size:]
    column = list(column)
    for j in range(size):
        cosine, sine = turns[2 * j], turns[2 * j + 1]
        first_val, second_val = column[j], column[j + 1]
        column[j] = cosine * first_val + sine * second_val
        column[j + 1] = cosine * second_val - sine * first_val
    last = column[size]
    coeffs = [None] * count
    coeffs[size] = target[size] * last / (last * last + square)
    for k in range(size - 1, -1, -1):
        accum = target[k] - column[k] * coeffs[size]
        for i in range(k + 1, size):
            accum = accum - above[i * (i - 1) // 2 + k] * coeffs[i]
        coeffs[k] = accum * inverses[k]
    return coeffs


KNOWN = 2 * (ITERS - 1) + (ITERS - 1) * (ITERS - 2) // 2 + (ITERS - 1) + ITERS


def last_kernel(sums, own, held, out):
    known = [held[i] for i in range(KNOWN)]
    gram = {(j, j): 1.0 for j in range(ITERS)}
    for at, (i, j) in enumerate(PAIRS):
        gram[i, j] = gram[j, i] = held[KNOWN + at]
    row = jnp.broadcast_to(jnp.sum(sums[...], axis=0, keepdims=True), (ROWS, 128))
    inner = [
        jnp.broadcast_to(row_sum(jnp.where(place_of(j), row, 0.0)), (ROWS, 128))
        for j in range(ITERS + 1)
    ]
    column = []
    for j in range(ITERS):
        column.append(inner[j] - sum(column[i] * gram[i, j] for i in range(j)))
    square = inner[ITERS]
    for j in range(ITERS):
        rest = sum(column[i] * gram[i, j] for i in range(ITERS)) - 2.0 * inner[j]
        square = square + column[j] * rest
    coeffs = solve_last(known, column, jnp.maximum(square, 0.0), ITERS)
    for a in range(3):
        density = sum(coeffs[k] * own[k, a] for k in range(ITERS))
        out[:HALF, a, :] = density[:HALF, :64]
        out[HALF:, a, :] = density[4 : 4 + HALF, :64]


def call(kernel, outs, scratch, operands, far=(), spread_out=False, flops=0):
    vmem = pl.BlockSpec(memory_space=pltpu.VMEM)
    count = len(operands)
    hbm = pl.BlockSpec(memory_space=pltpu.HBM)
    specs = [hbm if i in far else vmem for i in range(count)]
    moved = sum(x.size * x.dtype.itemsize for x in operands)
    return pl.pallas_call(
        kernel,
        out_shape=[jax.ShapeDtypeStruct(s, t) for s, t in outs],
        in_specs=specs,
        out_specs=[pl.BlockSpec(memory_space=pl.ANY) if spread_out and i == 0 else vmem for i in range(len(outs))],
        scratch_shapes=scratch,
        cost_estimate=pl.CostEstimate(flops=flops, bytes_accessed=moved, transcendentals=0),
        compiler_params=pltpu.CompilerParams(vmem_limit_bytes=48 * 1024 * 1024),
    )(*operands)


def body(sizes, velocity, points, panel_area, self_term, near_index, near_weight):
    n_row, n_col = sizes[0] * sizes[1] * sizes[2], sizes[3]
    n = n_row * n_col
    n_chunk = n // 2
    total = n * 64
    rhs = velocity.shape[0]

    message = ((n * LATER, 128), F32)
    sources = [
        velocity,
        points,
        panel_area[None],
        self_term[None],
        near_index.T,
        near_weight.T,
    ]
    wide, tgt, lists = call(
        pack_kernel,
        [
            ((n * FIRST, 128), F32),
            ((8, 128), F32),
            ((2 * near_index.shape[1], near_index.shape[0]), F32),
        ],
        [pltpu.VMEM(x.shape, x.dtype) for x in sources]
        + [pltpu.VMEM((8 * FIRST, 128), F32), pltpu.SemaphoreType.DMA((6 + n // 8,))],
        [pltpu.with_memory_space_constraint(x, pltpu.HBM) for x in sources],
        far=range(6),
        spread_out=True,
    )
    piece = spread(wide, n)
    near = [lists] + [lax.ppermute(lists, "col", xor_perm(n_col, o)) for o in range(1, n_col)]
    extra = [
        call(
            functools.partial(extra_kernel, sizes),
            [((n_row // 2, 64, 128), F32)],
            [],
            [pair],
            flops=10**8,
        )[0]
        for pair in near
    ]

    vec_shape = (n_chunk, 3, ROWS, 128)
    cols = pltpu.VMEM((64, total), BF16)
    held = [] if n_chunk <= 16 else [pltpu.VMEM((8, ROWS, 128), F32)]
    kernels, places, basis, norm, wide = call(
        functools.partial(first_kernel, sizes),
        [
            ((total, 512), BF16),
            ((n_chunk, 4, 128), F32),
            (vec_shape, F32),
            ((2, ROWS, 128), F32),
            message,
        ],
        [cols, *held],
        [piece, *extra, tgt],
    )
    bases = [basis]
    columns = [norm]
    for k in range(1, ITERS):
        final = k == ITERS - 1
        piece = spread(wide, n)
        main, column, wide = call(
            functools.partial(middle_kernel, sizes, k, final),
            [
                ((ITERS, 3, ROWS, 128) if final else vec_shape, F32),
                ((KNOWN + len(PAIRS) if final else k + 2, ROWS, 128), F32),
                ((n, 128), F32) if final else message,
            ],
            [*([pltpu.VMEM(vec_shape, F32)] if final else []), cols, *held],
            [piece, *bases, *columns, kernels, places, tgt],
        )
        bases.append(main)
        columns.append(column)
    sums = spread(wide, n)
    (density,) = call(
        last_kernel, [((rhs, 3, 64), F32)], [], [sums, bases[-1], columns[-1]]
    )
    return density


def solution(mesh):
    n_row, n_col = mesh.shape["row"], mesh.shape["col"]
    sizes = (n_row // 4, 2, 2, n_col)
    split = jax.sharding.Mesh(mesh.devices.reshape(sizes), AXES)
    return jax.shard_map(
        functools.partial(body, sizes),
        mesh=split,
        in_specs=(
            P(None, None, AXES),
            P(None, AXES),
            P(AXES),
            P(AXES),
            P(AXES[:3], "col"),
            P(AXES[:3], "col"),
        ),
        out_specs=P(None, None, AXES),
        check_vma=False,
    )
```

```python
import functools
import math

import jax
import jax.numpy as jnp
from jax import lax
from jax.experimental import pallas as pl
from jax.experimental.pallas import tpu as pltpu
from jax.sharding import PartitionSpec as P

ITERS = 3
BLOB_SQ = 0.0025
INV_EIGHT_PI = 1.0 / (8.0 * math.pi)
ROWS = 8
HALF = 3
FIRST, LATER = 11, 9
ORDER = (0, 2, 1)
AXES = ("top", "mid", "core", "col")
F32 = jnp.float32
BF16 = jnp.bfloat16


def position(sizes):
    top, mid, core, col = (lax.axis_index(axis) for axis in AXES)
    row = (top * sizes[1] + mid) * sizes[2] + core
    return row * sizes[3] + col, row, col


def low_half(shape):
    return lax.broadcasted_iota(jnp.int32, shape, len(shape) - 1) < 64


def xor_perm(n, m):
    return [(d, d ^ m) for d in range(n)]


def spread(rows, n):
    wide = rows.reshape(n, -1, 1, 128)
    return lax.all_to_all(wide, AXES, 0, 0, tiled=True).reshape(rows.shape)


def each(count, step):
    if count <= 16:
        for i in range(count):
            step(i)
    else:
        pl.loop(0, count)(step)


class Sums:
    def __init__(self, count, refs):
        self.refs = refs
        self.parts = [[None] * 4 for _ in range(count)]
        if refs is not None:
            for at in range(count):
                refs[at] = jnp.zeros((ROWS, 128), F32)

    def add(self, chunk, at, left, right):
        part = sum(left[a] * right[a] for a in range(3))
        if self.refs is not None:
            self.refs[at] = self.refs[at] + part
            return
        held = self.parts[at]
        slot = chunk % 4
        held[slot] = part if held[slot] is None else held[slot] + part

    def get(self, at):
        if self.refs is not None:
            total = self.refs[at]
        else:
            held = self.parts[at]
            total = (held[0] + held[1]) + (held[2] + held[3])
        return jnp.broadcast_to(jnp.sum(total, axis=1, keepdims=True), (ROWS, 128))


def chunk_parts(piece, chunk, me, n_row, n_col, size, at, count):
    half = n_row // 2
    o = chunk // half
    u = chunk % half
    early = max(at + count - size, 0)
    even = piece[pl.ds((me ^ ((2 * u) * n_col + o)) * size + at - early, count)]
    odd = piece[pl.ds((me ^ ((2 * u + 1) * n_col + o)) * size + at - early, count)]
    low = low_half((count, 128))
    first = jnp.where(low, even, pltpu.roll(odd, 64, 1))
    second = jnp.where(low, pltpu.roll(even, 64, 1), odd)
    rows = jnp.concatenate([first, second], axis=0)
    return pltpu.roll(rows, ROWS - early, 0) if early else rows


PAIRS = [(i, j) for i in range(ITERS) for j in range(i + 1, ITERS)]


def place_of(j):
    lane = lax.broadcasted_iota(jnp.int32, (ROWS, 128), 1)
    return lane == lax.broadcasted_iota(jnp.int32, (ROWS, 128), 0) * (ITERS + 1) + j


def row_sum(acc):
    return jnp.sum(acc, axis=1, keepdims=True)


def lines_of(chunk):
    if isinstance(chunk, int):
        return pl.ds(chunk * 128, 128)
    return pl.ds(pl.multiple_of(chunk * 128, 128), 128)


def write_columns(cols, y, chunk, f):
    inner = sum(y[k : k + 1] * f[a] for a, k in enumerate(ORDER))
    full = jnp.concatenate([*f, inner], axis=0)
    high = full.astype(BF16)
    at = lines_of(chunk)
    cols[0:32, at] = high
    cols[32:64, at] = (full - high.astype(F32)).astype(BF16)


def contract(cols, kernels):
    first = jnp.dot(cols, kernels[:, :256], preferred_element_type=F32)
    second = jnp.dot(cols[:32], kernels[:, 256:], preferred_element_type=F32)
    return first[:32] + (first[32:] + second)


def products(n_chunk, columns, cols, kernels):
    if n_chunk <= 16:
        for chunk in range(n_chunk):
            columns(chunk)
        return contract(cols[...], kernels[...])
    pl.loop(0, n_chunk)(columns)

    def turn(i, acc):
        at = pl.ds(pl.multiple_of(i * 2048, 2048), 2048)
        return acc + contract(cols[:, at], kernels[at, :])

    return lax.fori_loop(0, n_chunk // 16, turn, jnp.zeros((32, 256), F32))


def image_rows(prod, targets, own, scale):
    left = [prod[8 * k : 8 * k + 8, :128] for k in range(4)]
    right = [prod[8 * k : 8 * k + 8, 128:] for k in range(4)]
    x = [targets[a : a + 1] for a in range(3)]
    first = x[0] * left[0] + x[1] * left[1] + x[2] * left[2] - left[3]
    other = x[0] * right[0] + x[1] * right[1] + x[2] * right[2] - right[3]
    parts = [pltpu.roll(first, 64, 1), other, pltpu.roll(other, 64, 1)]
    return [(left[a] + parts[a] + targets[3:4] * own[a]) * scale for a in range(3)]


def write_piece(images, out):
    rows = []
    for image in images:
        top, bottom = image[:4], pltpu.roll(image[4:], 64, 1)
        rows.append(jnp.where(low_half((4, 128)), top, bottom))
    message = jnp.concatenate([row[:HALF] for row in rows], axis=0)
    block = jnp.concatenate([message] * 8, axis=0)

    def put(m):
        out[pl.ds(m * 8 * LATER, 8 * LATER)] = block

    each_wide(out.shape[0] // (8 * LATER), put)


def each_wide(count, put):
    if count <= 64:
        for m in range(count):
            put(m)
    else:
        pl.loop(0, count)(put)


def pack_kernel(*refs):
    sources, (out, tgt, lists), held = refs[:6], refs[6:9], refs[9:15]
    block, sems = refs[15:]
    copies = [
        pltpu.make_async_copy(src, dst, sems.at[i])
        for i, (src, dst) in enumerate(zip(sources, held))
    ]
    for copy in copies:
        copy.start()
    for copy in copies[:3]:
        copy.wait()
    velocity, points, area, self_term, index, weight = held
    count = index.shape[0]
    rows = [
        jnp.concatenate([velocity[:HALF, a, :], velocity[HALF:, a, :]], axis=1) for a in range(3)
    ]
    spot = points[...]
    left = jnp.concatenate([spot[0:1], spot[2:3]], axis=0)
    right = jnp.concatenate([spot[1:2], area[...]], axis=0)
    rows.append(jnp.concatenate([left, right], axis=1))
    message = jnp.concatenate(rows, axis=0)
    size = block.shape[0]
    block[...] = jnp.concatenate([message] * 8, axis=0)
    leaving = [
        pltpu.make_async_copy(block, out.at[pl.ds(i * size, size)], sems.at[6 + i])
        for i in range(out.shape[0] // size)
    ]
    for copy in leaving:
        copy.start()
    for copy in copies[3:]:
        copy.wait()
    mine = jnp.concatenate([spot, self_term[...]], axis=0)
    mine = jnp.concatenate([mine, mine], axis=1)
    tgt[...] = jnp.concatenate([mine, mine], axis=0)
    lists[:count] = index[...].astype(F32)
    lists[count:] = weight[...]
    for copy in leaving:
        copy.wait()


def extra_kernel(sizes, lists, out):
    _, row, col = position(sizes)
    lines = lax.broadcasted_iota(jnp.int32, (128, 128), 0).astype(F32)
    count = lists.shape[0] // 2
    half = count // 2
    low = low_half((half, 128))
    odd = col % 2 == 1
    both = lists[:, lines_of(col // 2)]
    place = both[:count].astype(jnp.int32)
    place = (((place // 64) ^ row) * 64 + place % 64).astype(F32)
    packed = []
    for value in (place, both[count:]):
        top, bottom = value[:half], value[half:]
        lower = jnp.where(low, top, pltpu.roll(bottom, 64, 1))
        upper = jnp.where(low, pltpu.roll(top, 64, 1), bottom)
        packed.append(jnp.where(odd, upper, lower))
    index, weight = packed

    def build(u):
        line = lines + (u * 128.0 if isinstance(u, int) else (u * 128).astype(F32))
        total = jnp.zeros((128, 128), F32)
        for k in range(half):
            total = total + jnp.where(line == index[k : k + 1], weight[k : k + 1], 0.0)
        turned = total.T
        out[u] = turned[:64] + turned[64:]

    each(out.shape[0], build)


def first_kernel(sizes, piece, *refs):
    n_row, n_col = sizes[0] * sizes[1] * sizes[2], sizes[3]
    extra = refs[:n_col]
    tgt, kernels, places, basis, mine, norm_out, out, cols, *sums = refs[n_col:]
    half = n_row // 2
    n_chunk = n_row * n_col // 2
    me, _, _ = position(sizes)
    total = Sums(1, sums[0] if sums else None)

    def unpack(chunk):
        vec = [
            chunk_parts(piece, chunk, me, n_row, n_col, FIRST, HALF * a, 4)
            for a in range(3)
        ]
        spot = chunk_parts(piece, chunk, me, n_row, n_col, FIRST, 3 * HALF, 2)
        places[chunk] = spot
        for a in range(3):
            basis[chunk, a] = vec[a]
        total.add(chunk, 0, vec, vec)
        write_columns(cols, spot, chunk, vec)

    turned = tgt[...].T
    x = [jnp.broadcast_to(turned[:64, a : a + 1], (64, 128)) for a in range(3)]

    def build(chunk):
        unpack(chunk)
        y = places[chunk]
        d = [x[a] - y[k : k + 1] for a, k in enumerate(ORDER)]
        dist = d[0] * d[0] + d[1] * d[1] + d[2] * d[2]
        root = lax.rsqrt(dist + BLOB_SQ)
        two = (y[3:4] * INV_EIGHT_PI) * root * root * root
        one = (dist + 2.0 * BLOB_SQ) * two
        if isinstance(chunk, int):
            one = one + extra[chunk // half][chunk % half]
        else:
            for o in range(n_col):
                mine = extra[o][chunk % half]
                one = one + jnp.where(chunk // half == o, mine, 0.0)
        moved = [two * part for part in d]
        at = lines_of(chunk)
        for k, pair in enumerate(([one, moved[0]], moved[1:])):
            value = jnp.concatenate(pair, axis=0).T
            high = value.astype(BF16)
            kernels[at, 128 * k : 128 * k + 128] = high
            kernels[at, 256 + 128 * k : 384 + 128 * k] = (value - high.astype(F32)).astype(BF16)

    prod = products(n_chunk, build, cols, kernels)
    norm = jnp.sqrt(total.get(0))
    scale = 1.0 / norm
    norm_out[0] = norm
    norm_out[1] = scale
    images = image_rows(prod, tgt, basis[0], scale)
    for a in range(3):
        mine[a] = images[a]
    write_piece(images, out)


def middle_kernel(sizes, n_base, final, piece, *refs):
    n_row, n_col = sizes[0] * sizes[1] * sizes[2], sizes[3]
    bases, norms, before = (refs[i * n_base : (i + 1) * n_base] for i in range(3))
    if final:
        kernels, places, tgt, own, h_out, out, basis, cols, *held = refs[3 * n_base :]
    else:
        kernels, places, tgt, basis, mine, h_out, out, cols, *held = refs[3 * n_base :]
    n_chunk = n_row * n_col // 2
    me, _, _ = position(sizes)
    scales = [norm[norm.shape[0] - 1] for norm in norms]
    cross = [(i, j) for i in range(n_base) for j in range(i)]
    sums = Sums(2 * n_base + 1 + len(cross), held[0] if held else None)

    def unpack(chunk):
        vec = [
            chunk_parts(piece, chunk, me, n_row, n_col, LATER, HALF * a, 4)
            for a in range(3)
        ]
        old = [[base[chunk, a] for a in range(3)] for base in bases]
        for a in range(3):
            basis[chunk, a] = vec[a]
        write_columns(cols, places[chunk], chunk, vec)
        for j in range(n_base):
            sums.add(chunk, j, vec, old[j])
        for at, (i, j) in enumerate(cross):
            sums.add(chunk, 2 * n_base + 1 + at, old[i], old[j])

    prod = products(n_chunk, unpack, cols, kernels)
    raw = image_rows(prod, tgt, basis[0], 1.0)
    gram = {}
    for at, (i, j) in enumerate(cross):
        gram[j, i] = sums.get(2 * n_base + 1 + at) * (scales[i] * scales[j])
    column = []
    for j in range(n_base):
        h = sums.get(j) * scales[j]
        for i in range(j):
            h = h - column[i] * gram[i, j]
        column.append(h)
        if not final:
            h_out[j] = h
    factors = [h * scale for h, scale in zip(column, scales)]

    def columns(chunk):
        old = [[base[chunk, a] for a in range(3)] for base in bases]
        vec = []
        for a in range(3):
            value = basis[chunk, a]
            for j in range(n_base):
                value = value - factors[j] * old[j][a]
            vec.append(value)
            basis[chunk, a] = value
        sums.add(chunk, n_base, vec, vec)
        if final:
            for j in range(n_base):
                sums.add(chunk, n_base + 1 + j, vec, old[j])

    each(n_chunk, columns)
    norm = jnp.sqrt(sums.get(n_base))
    scale = 1.0 / norm
    images = [
        (raw[a] - sum(column[j] * before[j][a] for j in range(n_base))) * scale
        for a in range(3)
    ]
    if not final:
        for a in range(3):
            mine[a] = images[a]
        h_out[n_base] = norm
        h_out[n_base + 1] = scale
        write_piece(images, out)
        return
    every = [*bases, basis]
    for j, base in enumerate(every):
        for a in range(3):
            own[j, a] = base[0, a] * [*scales, scale][j]
    for j in range(n_base):
        gram[j, n_base] = sums.get(n_base + 1 + j) * (scale * scales[j])
    hessen = {(i, n_base - 1): value for i, value in enumerate([*column, norm])}
    for k in range(1, n_base):
        for i in range(k + 1):
            hessen[i, k - 1] = norms[k][i]
    known = rotate_known(hessen, norms[0][0], ITERS)
    for at, value in enumerate(known + [gram[pair] for pair in PAIRS]):
        h_out[at] = value
    low = low_half((ROWS, 128))
    row = jnp.zeros((ROWS, 128), F32)
    for j in range(ITERS + 1):
        other = images if j == ITERS else [own[j, a] for a in range(3)]
        part = sum(images[a] * other[a] for a in range(3))
        part = row_sum(jnp.where(low, part, 0.0))
        row = row + jnp.where(place_of(j), part, 0.0)
    row = jnp.broadcast_to(jnp.sum(row, axis=0, keepdims=True), (8, 128))

    def put(m):
        out[pl.ds(m * 8, 8)] = row

    each_wide(out.shape[0] // 8, put)


def rotate_known(hessen, start_norm, count):
    target = [start_norm]
    turns = []
    above = []
    inverses = []
    for k in range(count - 1):
        column = [hessen[i, k] for i in range(k + 2)]
        for j, (cosine, sine) in enumerate(turns):
            first_val, second_val = column[j], column[j + 1]
            column[j] = cosine * first_val + sine * second_val
            column[j + 1] = cosine * second_val - sine * first_val
        inverse = 1.0 / jnp.sqrt(column[k] * column[k] + column[k + 1] * column[k + 1])
        turns.append((column[k] * inverse, column[k + 1] * inverse))
        above += column[:k]
        inverses.append(inverse)
        target.append(-turns[k][1] * target[k])
        target[k] = turns[k][0] * target[k]
    return [value for turn in turns for value in turn] + above + inverses + target


def solve_last(known, column, square, count):
    size = count - 1
    turns, known = known[: 2 * size], known[2 * size :]
    above, known = known[: size * (size - 1) // 2], known[size * (size - 1) // 2 :]
    inverses, target = known[:size], known[size:]
    column = list(column)
    for j in range(size):
        cosine, sine = turns[2 * j], turns[2 * j + 1]
        first_val, second_val = column[j], column[j + 1]
        column[j] = cosine * first_val + sine * second_val
        column[j + 1] = cosine * second_val - sine * first_val
    last = column[size]
    coeffs = [None] * count
    coeffs[size] = target[size] * last / (last * last + square)
    for k in range(size - 1, -1, -1):
        accum = target[k] - column[k] * coeffs[size]
        for i in range(k + 1, size):
            accum = accum - above[i * (i - 1) // 2 + k] * coeffs[i]
        coeffs[k] = accum * inverses[k]
    return coeffs


KNOWN = 2 * (ITERS - 1) + (ITERS - 1) * (ITERS - 2) // 2 + (ITERS - 1) + ITERS


def last_kernel(sums, own, held, out):
    known = [held[i] for i in range(KNOWN)]
    gram = {(j, j): 1.0 for j in range(ITERS)}
    for at, (i, j) in enumerate(PAIRS):
        gram[i, j] = gram[j, i] = held[KNOWN + at]
    row = jnp.broadcast_to(jnp.sum(sums[...], axis=0, keepdims=True), (ROWS, 128))
    inner = [
        jnp.broadcast_to(row_sum(jnp.where(place_of(j), row, 0.0)), (ROWS, 128))
        for j in range(ITERS + 1)
    ]
    column = []
    for j in range(ITERS):
        column.append(inner[j] - sum(column[i] * gram[i, j] for i in range(j)))
    square = inner[ITERS]
    for j in range(ITERS):
        rest = sum(column[i] * gram[i, j] for i in range(ITERS)) - 2.0 * inner[j]
        square = square + column[j] * rest
    coeffs = solve_last(known, column, jnp.maximum(square, 0.0), ITERS)
    for a in range(3):
        density = sum(coeffs[k] * own[k, a] for k in range(ITERS))
        out[:HALF, a, :] = density[:HALF, :64]
        out[HALF:, a, :] = density[4 : 4 + HALF, :64]


def call(kernel, outs, scratch, operands, far=(), spread_out=False, flops=0):
    vmem = pl.BlockSpec(memory_space=pltpu.VMEM)
    count = len(operands)
    hbm = pl.BlockSpec(memory_space=pltpu.HBM)
    specs = [hbm if i in far else vmem for i in range(count)]
    moved = sum(x.size * x.dtype.itemsize for x in operands)
    return pl.pallas_call(
        kernel,
        out_shape=[jax.ShapeDtypeStruct(s, t) for s, t in outs],
        in_specs=specs,
        out_specs=[pl.BlockSpec(memory_space=pl.ANY) if spread_out and i == 0 else vmem for i in range(len(outs))],
        scratch_shapes=scratch,
        cost_estimate=pl.CostEstimate(flops=flops, bytes_accessed=moved, transcendentals=0),
        compiler_params=pltpu.CompilerParams(vmem_limit_bytes=48 * 1024 * 1024),
    )(*operands)


def body(sizes, velocity, points, panel_area, self_term, near_index, near_weight):
    n_row, n_col = sizes[0] * sizes[1] * sizes[2], sizes[3]
    n = n_row * n_col
    n_chunk = n // 2
    total = n * 64
    rhs = velocity.shape[0]

    message = ((n * LATER, 128), F32)
    sources = [
        velocity,
        points,
        panel_area[None],
        self_term[None],
        near_index.T,
        near_weight.T,
    ]
    wide, tgt, lists = call(
        pack_kernel,
        [
            ((n * FIRST, 128), F32),
            ((8, 128), F32),
            ((2 * near_index.shape[1], near_index.shape[0]), F32),
        ],
        [pltpu.VMEM(x.shape, x.dtype) for x in sources]
        + [pltpu.VMEM((8 * FIRST, 128), F32), pltpu.SemaphoreType.DMA((6 + n // 8,))],
        [pltpu.with_memory_space_constraint(x, pltpu.HBM) for x in sources],
        far=range(6),
        spread_out=True,
    )
    piece = spread(wide, n)
    near = [lists] + [lax.ppermute(lists, "col", xor_perm(n_col, o)) for o in range(1, n_col)]
    extra = [
        call(
            functools.partial(extra_kernel, sizes),
            [((n_row // 2, 64, 128), F32)],
            [],
            [pair],
            flops=10**8,
        )[0]
        for pair in near
    ]

    vec_shape = (n_chunk, 3, ROWS, 128)
    cols = pltpu.VMEM((64, total), BF16)
    held = [] if n_chunk <= 16 else [pltpu.VMEM((8, ROWS, 128), F32)]
    kernels, places, basis, image, norm, wide = call(
        functools.partial(first_kernel, sizes),
        [
            ((total, 512), BF16),
            ((n_chunk, 4, 128), F32),
            (vec_shape, F32),
            ((3, ROWS, 128), F32),
            ((2, ROWS, 128), F32),
            message,
        ],
        [cols, *held],
        [piece, *extra, tgt],
    )
    bases = [basis]
    columns = [norm]
    images = [image]
    for k in range(1, ITERS):
        final = k == ITERS - 1
        piece = spread(wide, n)
        main, *image, column, wide = call(
            functools.partial(middle_kernel, sizes, k, final),
            [
                ((ITERS, 3, ROWS, 128) if final else vec_shape, F32),
                *([] if final else [((3, ROWS, 128), F32)]),
                ((KNOWN + len(PAIRS) if final else k + 2, ROWS, 128), F32),
                ((n, 128), F32) if final else message,
            ],
            [*([pltpu.VMEM(vec_shape, F32)] if final else []), cols, *held],
            [piece, *bases, *columns, *images, kernels, places, tgt],
        )
        bases.append(main)
        columns.append(column)
        images += image
    sums = spread(wide, n)
    (density,) = call(
        last_kernel, [((rhs, 3, 64), F32)], [], [sums, bases[-1], columns[-1]]
    )
    return density


def solution(mesh):
    n_row, n_col = mesh.shape["row"], mesh.shape["col"]
    sizes = (n_row // 4, 2, 2, n_col)
    split = jax.sharding.Mesh(mesh.devices.reshape(sizes), AXES)
    return jax.shard_map(
        functools.partial(body, sizes),
        mesh=split,
        in_specs=(
            P(None, None, AXES),
            P(None, AXES),
            P(AXES),
            P(AXES),
            P(AXES[:3], "col"),
            P(AXES[:3], "col"),
        ),
        out_specs=P(None, None, AXES),
        check_vma=False,
    )
```
